32 devices in a mesh: row: 4 (over y, x), blk: 8 (over z, core).
Axes of the slice: x: 2, y: 2, z: 4, core: 2. Of those that a mesh axis runs over, the one named last changes fastest.
Arguments:
- tokens: bfloat16 [8, 512, 2048], P('row', 'blk'), may hold values from -6 to 6
- attn_weights: bfloat16 [2048, 8192], P(('row', 'blk')), may hold values from -0.1875 to 0.1875
- mlp_weights: bfloat16 [2048, 2, 8192], P(('row', 'blk')), may hold values from -0.125 to 0.125
- ln1_gain: float32 [2048], replicated, may hold values from 0.5 to 1.5
- ln1_bias: float32 [2048], replicated, may hold values from -1 to 1
- ln2_gain: float32 [2048], replicated, may hold values from 0.5 to 1.5
- ln2_bias: float32 [2048], replicated, may hold values from -1 to 1
- qkv_bias: float32 [6144], replicated, may hold values from -1 to 1
- dense_bias: float32 [2048], replicated, may hold values from -1 to 1
- up_bias: float32 [8192], replicated, may hold values from -2.5 to 2.5
- down_bias: float32 [2048], replicated, may hold values from -1 to 1
- doc_lengths: int32 [8, 4], P('row'), may hold values from 1 to 447, as said below
- cotangent: bfloat16 [8, 512, 2048], P('row', 'blk'), may hold values from -6 to 6
Outputs:
- layer_out: bfloat16 [8, 512, 2048], P('row', 'blk')
- tokens_grad: bfloat16 [8, 512, 2048], P('row', 'blk')
- attn_weights_grad: float32 [2048, 8192], P(('row', 'blk'))
- mlp_weights_grad: float32 [2048, 2, 8192], P(('row', 'blk'))
- ln1_gain_grad: float32 [2048], replicated
- ln1_bias_grad: float32 [2048], replicated
- ln2_gain_grad: float32 [2048], replicated
- ln2_bias_grad: float32 [2048], replicated
- qkv_bias_grad: float32 [6144], replicated
- dense_bias_grad: float32 [2048], replicated
- up_bias_grad: float32 [8192], replicated
- down_bias_grad: float32 [2048], replicated
The draws below stay inside these ranges and needn't reach their ends.
Inputs may be any that keep to these rules, and one draw needn't show every extreme that they name: `doc_lengths`: each row's 4 lengths are whole numbers that sum to 512; in every group of 2 rows held by one index of row, one row holds a document of length 447 that starts within the first 64 positions and ends within the last 64 positions, and that row ends with a document of length 1.
All inputs are finite; a program needn't handle non-finite values.
Results may differ from the reference program's by a relative error of at most 0.013.
Values may be sent and summed in bfloat16 or wider, within the bound.
No kernel may reach another device: no remote copies, remote signals or barrier semaphores. Data moves between devices by JAX's collectives and lax.ppermute only.
A program may use at most 704 MiB of HBM per device.

```python
import jax
import jax.numpy as jnp
from jax import lax

D = 2048
H = 8
HD = 256
FF = 8192
ROT = 64
R_DEV = 2
SPAN = 64
ROWS = 8
LEN = 512


def draw_doc_lengths(key, part):
    key = jax.random.fold_in(key, 11)
    pick_key, head_key, first_key, second_key, third_key = jax.random.split(key, 5)
    groups = ROWS // R_DEV
    chosen = jax.random.randint(pick_key, (groups,), 0, R_DEV)
    row_ids = jnp.arange(ROWS, dtype=jnp.int32)
    is_long = row_ids % R_DEV == jnp.repeat(chosen, R_DEV)
    head = jax.random.randint(head_key, (ROWS,), 1, SPAN).astype(jnp.int32)
    tail = (SPAN - head).astype(jnp.int32)
    last = jnp.ones((ROWS,), jnp.int32)
    middle = jnp.full((ROWS,), LEN - SPAN - 1, jnp.int32)
    long_rows = jnp.stack([head, middle, tail, last], 1).astype(jnp.int32)
    third = LEN // 3
    cut_one = jax.random.randint(first_key, (ROWS,), 1, third + 1).astype(jnp.int32)
    cut_two = jax.random.randint(second_key, (ROWS,), third + 1, 2 * third + 1).astype(jnp.int32)
    cut_three = jax.random.randint(third_key, (ROWS,), 2 * third + 1, LEN).astype(jnp.int32)
    other_rows = jnp.stack([cut_one, cut_two - cut_one, cut_three - cut_two, LEN - cut_three], 1).astype(jnp.int32)
    return jnp.where(is_long[:, None], long_rows, other_rows).astype(jnp.int32)


def block_levels(rng, extent, cuts, low, high):
    def one(axis_at, shards_of):
        draws = jax.random.uniform(jax.random.fold_in(jax.random.fold_in(rng, 6), axis_at), (shards_of,), jnp.float32, low / len(cuts), high / len(cuts))
        return jnp.repeat(jnp.exp(draws), extent[axis_at] // shards_of).reshape((-1,) + (1,) * (len(extent) - axis_at - 1))

    factor_of = one(*cuts[0])
    for cut in cuts[1:]:
        factor_of = factor_of * one(*cut)
    return factor_of


def gaussian(own_key, dims, width, limit, cuts=(), kind=jnp.bfloat16):
    drawn = width * jax.random.normal(own_key, dims, jnp.float32)
    if cuts:
        drawn = drawn * block_levels(own_key, dims, cuts, -0.22, 0.18)
    return jnp.clip(drawn, -limit, limit).astype(kind)


def setup_inputs(seed: int = 0) -> dict:
    key_list = jax.random.split(jax.random.key(seed), 14)
    tokens = gaussian(key_list[0], (ROWS, LEN, D), 1.0, 6.0, ((0, 4), (1, 8)))
    attn_weights = gaussian(key_list[1], (D, 4 * D), (D // 2) ** -0.5, 0.1875, ((0, 32),))
    mlp_weights = gaussian(key_list[2], (D, 2, FF), D ** -0.5, 0.125, ((0, 32),))
    ln1_gain = jnp.clip(1.0 + 0.1 * jax.random.normal(key_list[3], (D,), jnp.float32), 0.5, 1.5)
    ln1_bias = gaussian(key_list[4], (D,), 0.2, 1.0, (), jnp.float32)
    ln2_gain = jnp.clip(1.0 + 0.1 * jax.random.normal(key_list[5], (D,), jnp.float32), 0.5, 1.5)
    ln2_bias = gaussian(key_list[6], (D,), 0.2, 1.0, (), jnp.float32)
    qkv_bias = gaussian(key_list[7], (3 * D,), 0.2, 1.0, (), jnp.float32)
    dense_bias = gaussian(key_list[8], (D,), 0.2, 1.0, (), jnp.float32)
    up_bias = gaussian(key_list[9], (FF,), 0.5, 2.5, (), jnp.float32)
    down_bias = gaussian(key_list[10], (D,), 0.2, 1.0, (), jnp.float32)
    doc_lengths = draw_doc_lengths(jax.random.fold_in(key_list[13], 71), 0)
    cotangent = gaussian(key_list[12], (ROWS, LEN, D), 1.0, 6.0, ((0, 4), (1, 8)))
    return {"tokens": tokens, "attn_weights": attn_weights, "mlp_weights": mlp_weights, "ln1_gain": ln1_gain, "ln1_bias": ln1_bias, "ln2_gain": ln2_gain, "ln2_bias": ln2_bias, "qkv_bias": qkv_bias, "dense_bias": dense_bias, "up_bias": up_bias, "down_bias": down_bias, "doc_lengths": doc_lengths, "cotangent": cotangent}


EPSILON = 1e-05
MASKED = -1e+30
HIGH = lax.Precision.HIGHEST

@jax.custom_vjp
def low(v):
    return lax.optimization_barrier(v.astype(jnp.bfloat16)).astype(jnp.float32)

@jax.custom_vjp
def low_back(v):
    return v

def low_keep(v):
    return (low(v), None)

def low_pass(kept, grad):
    return (grad,)

def back_keep(v):
    return (v, None)

def back_low(kept, grad):
    return (low(grad),)
low.defvjp(low_keep, low_pass)
low_back.defvjp(back_keep, back_low)

def layer_norm(field, gain, bias):
    average = lax.optimization_barrier(jnp.mean(field, -1, keepdims=True))
    centred = field - average
    spread_sq = lax.optimization_barrier(jnp.mean(centred * centred, -1, keepdims=True))
    return centred * lax.rsqrt(spread_sq + EPSILON) * gain + bias

def rotate(field, cosine, sine_vals):
    half_dims = ROT // 2
    lower_half = field[..., :half_dims]
    upper_half = field[..., half_dims:ROT]
    return jnp.concatenate([lower_half * cosine - upper_half * sine_vals, upper_half * cosine + lower_half * sine_vals, field[..., ROT:]], -1)

def one_row(params, x_row, lengths):
    attn_w, mlp_w, gain1, bias1, gain2, bias2, bias_qkv, bias_dense, bias_up, bias_down = params
    places = jnp.arange(LEN, dtype=jnp.int32)
    doc_ends = jnp.cumsum(lengths).astype(jnp.int32)
    starts = doc_ends - lengths
    doc_ids = lax.optimization_barrier(jnp.sum((places[:, None] >= doc_ends[None, :]).astype(jnp.int32), 1))
    positions = places - starts[doc_ids]
    allowed = (doc_ids[:, None] == doc_ids[None, :]) & (places[None, :] <= places[:, None])
    inverse = 10000.0 ** (-2.0 * jnp.arange(ROT // 2, dtype=jnp.float32) / ROT)
    angles = positions.astype(jnp.float32)[:, None] * inverse[None, :]
    cosine = jnp.cos(angles)[:, None, :]
    sine_vals = jnp.sin(angles)[:, None, :]
    normed1 = low(layer_norm(x_row, gain1, bias1))
    qkv_proj = low_back(jnp.dot(normed1, attn_w[:, :3 * D], precision=HIGH) + bias_qkv).reshape(LEN, 3, H, HD)
    queries = low(rotate(qkv_proj[:, 0], cosine, sine_vals) * HD ** (-0.5))
    keys_rot = low(rotate(qkv_proj[:, 1], cosine, sine_vals))
    values = low(qkv_proj[:, 2])
    scores = low_back(jnp.einsum('qhd,khd->hqk', queries, keys_rot, precision=HIGH))
    scores = jnp.where(allowed[None], scores, MASKED)
    weights = low(jax.nn.softmax(scores, axis=-1))
    attended = jnp.einsum('hqk,khd->qhd', weights, values, precision=HIGH).reshape(LEN, D)
    attended = low_back(low(attended))
    attn_out = jnp.dot(attended, attn_w[:, 3 * D:], precision=HIGH) + bias_dense
    normed2 = low(layer_norm(x_row, gain2, bias2))
    pre_act = low_back(jnp.dot(normed2, mlp_w[:, 0, :], precision=HIGH) + bias_up)
    hidden = low(jax.nn.gelu(pre_act, approximate=False))
    mlp_out = jnp.dot(hidden, mlp_w[:, 1, :].T, precision=HIGH) + bias_down
    return x_row + attn_out + mlp_out

def reference(tokens, attn_weights, mlp_weights, ln1_gain, ln1_bias, ln2_gain, ln2_bias, qkv_bias, dense_bias, up_bias, down_bias, doc_lengths, cotangent):
    params = tuple((a.astype(jnp.float32) for a in (attn_weights, mlp_weights, ln1_gain, ln1_bias, ln2_gain, ln2_bias, qkv_bias, dense_bias, up_bias, down_bias)))
    row_fn = jax.checkpoint(one_row)

    def forward(inputs, params):
        return lax.map(lambda row_pair: row_fn(params, row_pair[0], row_pair[1]), (inputs, doc_lengths))
    layer_out, pull = jax.vjp(forward, tokens.astype(jnp.float32), params)
    input_grad, grads = pull(cotangent.astype(jnp.float32))
    return (layer_out.astype(jnp.bfloat16), input_grad.astype(jnp.bfloat16), grads[0], grads[1], grads[2], grads[3], grads[4], grads[5], grads[6], grads[7], grads[8], grads[9])
```

```python
import math

import jax
import jax.numpy as jnp
import numpy as np
from jax import lax
from jax.sharding import PartitionSpec as P

HD = 256
ROT = 64
EPSILON = 1e-05
MASKED = -1e30
BF = jnp.bfloat16
F32 = jnp.float32


def rotate(field, cosine, sine_vals):
    half_dims = ROT // 2
    lower_half = field[..., :half_dims]
    upper_half = field[..., half_dims:ROT]
    return jnp.concatenate(
        [
            lower_half * cosine - upper_half * sine_vals,
            upper_half * cosine + lower_half * sine_vals,
            field[..., ROT:],
        ],
        -1,
    )


def dot(left, right, left_dim, right_dim):
    return lax.dot_general(
        left, right, (((left_dim,), (right_dim,)), ((), ())), preferred_element_type=F32
    )


def batched(spec, left, right):
    return jnp.einsum(spec, left, right, preferred_element_type=F32)


class Plan:
    def __init__(self, rows, blks, heads):
        self.rows = rows
        self.blks = blks
        self.share = blks // heads
        self.per_row = heads // rows
        self.group = blks // self.per_row
        self.heads = [
            (b % self.group) // self.share * self.per_row + b // self.group for b in range(blks)
        ]
        self.first = [self.heads.index(h) for h in range(heads)]
        self.groups = [
            list(range(i * self.group, (i + 1) * self.group)) for i in range(self.per_row)
        ]


def spread_columns(pieces, plan):
    mine = lax.all_to_all(pieces.transpose(1, 0, 2), "blk", 0, 0)
    return lax.all_gather(mine.reshape(-1, mine.shape[-1]), "row", axis=0, tiled=True)


def collect_columns(grad, plan):
    summed = lax.psum_scatter(grad, "row", scatter_dimension=0, tiled=True)
    return lax.all_to_all(summed.reshape(plan.blks, -1, grad.shape[-1]), "blk", 0, 0)


def shards(
    plan,
    tokens,
    attn_weights,
    mlp_weights,
    ln1_gain,
    ln1_bias,
    ln2_gain,
    ln2_bias,
    qkv_bias,
    dense_bias,
    up_bias,
    down_bias,
    doc_lengths,
    cotangent,
):
    row_count, shard_len, width = tokens.shape
    depth = attn_weights.shape[0]
    heads = width // HD
    hidden_width = mlp_weights.shape[-1]
    blks = plan.blks
    me = lax.axis_index("blk")
    length = shard_len * blks
    count = row_count * length
    head_of = jnp.asarray(plan.heads, jnp.int32)[me]
    part = me % plan.share
    own_rows = row_count // plan.share

    x_all = lax.all_gather(tokens, "blk", axis=1, tiled=True)
    up_w = spread_columns(mlp_weights[:, 0].reshape(depth, blks, -1), plan)
    g_all = lax.all_gather(cotangent, "blk", axis=1, tiled=True)
    down_w = spread_columns(mlp_weights[:, 1].reshape(depth, blks, -1), plan)
    qkv_cols = attn_weights[:, : 3 * width].reshape(depth, 3, heads, HD)
    qkv_cols = qkv_cols[:, :, np.array(plan.heads)].transpose(0, 2, 1, 3)
    qkv_w = spread_columns(qkv_cols.reshape(depth, blks, 3 * HD), plan)
    out_rows = lax.all_gather(attn_weights[:, 3 * width :], "row", axis=0)
    out_rows = jnp.repeat(out_rows, plan.share, axis=0)
    out_w = lax.all_to_all(out_rows, "blk", 0, 0, axis_index_groups=plan.groups)
    out_w = out_w.reshape(HD, width)

    field = x_all.reshape(count, width).astype(F32)
    average = jnp.mean(field, -1, keepdims=True)
    centred = field - average
    rstd = lax.rsqrt(jnp.mean(centred * centred, -1, keepdims=True) + EPSILON)
    standard = centred * rstd
    normed1 = (standard * ln1_gain + ln1_bias).astype(BF)
    normed2 = (standard * ln2_gain + ln2_bias).astype(BF)
    grad_all = g_all.reshape(count, width)

    up_b = lax.dynamic_slice_in_dim(up_bias, me * (hidden_width // blks), hidden_width // blks)
    pre = dot(normed2, up_w, 1, 0) + up_b
    cdf = 0.5 * (1.0 + lax.erf(pre * math.sqrt(0.5)))
    hidden = (pre * cdf).astype(BF)
    slope = cdf + pre * (jnp.exp(-0.5 * pre * pre) * (1.0 / math.sqrt(2.0 * math.pi)))
    pre_grad = (dot(grad_all, down_w, 1, 0) * slope).astype(BF)
    up_g = dot(normed2, pre_grad, 0, 0)
    down_g = dot(grad_all, hidden, 0, 0)
    up_back = collect_columns(up_g.astype(BF), plan)
    down_back = collect_columns(down_g.astype(BF), plan)
    mlp_term = dot(hidden, down_w, 1, 1)
    normed2_grad = dot(pre_grad, up_w, 1, 1)
    up_sum = jnp.sum(pre_grad.astype(F32), 0)
    gain2_part = jnp.sum(up_w.astype(F32) * up_g, 1)
    bias2_part = jnp.sum(up_w.astype(F32) * up_sum, 1)

    lengths = lax.dynamic_slice_in_dim(doc_lengths, part * own_rows, own_rows, 0)
    doc_ends = jnp.cumsum(lengths, axis=-1)
    starts = doc_ends - lengths
    places = jnp.arange(length, dtype=jnp.int32)
    doc_ids = jnp.sum((places[None, :, None] >= doc_ends[:, None, :]).astype(jnp.int32), -1)
    picked = doc_ids[:, :, None] == jnp.arange(lengths.shape[-1], dtype=jnp.int32)
    positions = places - jnp.sum(jnp.where(picked, starts[:, None, :], 0), -1)
    inverse = 10000.0 ** (-2.0 * jnp.arange(ROT // 2, dtype=F32) / ROT)
    angles = positions.astype(F32)[..., None] * inverse
    cosine = jnp.cos(angles)
    sine_vals = jnp.sin(angles)
    allowed = (doc_ids[:, :, None] == doc_ids[:, None, :]) & (
        places[None, None, :] <= places[None, :, None]
    )
    scale = HD ** (-0.5)

    def own(field):
        return lax.dynamic_slice_in_dim(field, part * own_rows * length, own_rows * length, 0)

    own_normed1 = own(normed1)
    own_grad = own(grad_all)
    qkv_b = lax.dynamic_index_in_dim(qkv_bias.reshape(3, heads, HD), head_of, 1, keepdims=False)
    qkv = (dot(own_normed1, qkv_w, 1, 0) + qkv_b.reshape(-1)).reshape(own_rows, length, 3, HD)
    queries = (rotate(qkv[:, :, 0], cosine, sine_vals) * scale).astype(BF)
    keys = rotate(qkv[:, :, 1], cosine, sine_vals).astype(BF)
    values = qkv[:, :, 2].astype(BF)
    scores = jnp.where(allowed, batched("rqd,rkd->rqk", queries, keys), MASKED)
    weights = jnp.where(allowed, jnp.exp(scores - jnp.max(scores, -1, keepdims=True)), 0.0)
    weights = weights / jnp.sum(weights, -1, keepdims=True)
    weights_low = weights.astype(BF)
    attended = batched("rqk,rkd->rqd", weights_low, values).astype(BF)
    heads_grad = dot(own_grad, out_w, 1, 1).astype(BF).reshape(own_rows, length, HD)
    deltas = jnp.sum(heads_grad.astype(F32) * attended.astype(F32), -1, keepdims=True)
    weight_grad = batched("rqd,rkd->rqk", heads_grad, values)
    score_grad = (weights * (weight_grad - deltas)).astype(BF)
    query_grad = batched("rqk,rkd->rqd", score_grad, keys)
    key_grad = batched("rqk,rqd->rkd", score_grad, queries)
    value_grad = batched("rqk,rqd->rkd", weights_low, heads_grad)
    qkv_grad = jnp.concatenate(
        [
            rotate(query_grad * scale, cosine, -sine_vals),
            rotate(key_grad, cosine, -sine_vals),
            value_grad,
        ],
        -1,
    ).reshape(own_rows * length, 3 * HD)
    qkv_grad = qkv_grad.astype(BF)
    attended = attended.reshape(own_rows * length, HD)
    qkv_g = dot(own_normed1, qkv_grad, 0, 0)
    out_g = dot(attended, own_grad, 0, 0)
    qkv_back = collect_columns(qkv_g.astype(BF), plan)
    out_send = out_g.astype(BF).reshape(plan.group, depth, width)
    out_back = lax.all_to_all(out_send, "blk", 0, 0, axis_index_groups=plan.groups)
    out_back = out_back.reshape(plan.rows, plan.share, depth, width)
    if plan.share > 1:
        out_back = jnp.sum(out_back.astype(F32), 1, keepdims=True).astype(BF)
    out_back = lax.psum_scatter(out_back[:, 0], "row", scatter_dimension=0, tiled=False)
    qkv_sum = jnp.sum(qkv_grad.astype(F32), 0)
    gain1_part = jnp.sum(qkv_w.astype(F32) * qkv_g, 1)
    bias1_part = jnp.sum(qkv_w.astype(F32) * qkv_sum, 1)

    def spread_rows(field):
        if plan.share == 1:
            return field
        whole = jnp.zeros((count, width), F32)
        return lax.dynamic_update_slice_in_dim(whole, field, part * own_rows * length, 0)

    out_term = (mlp_term + spread_rows(dot(attended, out_w, 1, 0))).astype(BF)
    out_term = lax.psum_scatter(
        out_term.reshape(row_count, length, width), "blk", scatter_dimension=1, tiled=True
    )
    layer_out = (
        tokens.astype(F32) + out_term.astype(F32) + (dense_bias + down_bias)
    ).astype(BF)
    norm_term = spread_rows(dot(qkv_grad, qkv_w, 1, 1)) * ln1_gain + normed2_grad * ln2_gain
    norm_term = lax.psum_scatter(
        norm_term.astype(BF).reshape(row_count, length, width),
        "blk",
        scatter_dimension=1,
        tiled=True,
    ).astype(F32)
    mine = tokens.astype(F32)
    mine = mine - jnp.mean(mine, -1, keepdims=True)
    mine_rstd = lax.rsqrt(jnp.mean(mine * mine, -1, keepdims=True) + EPSILON)
    mine = mine * mine_rstd
    tokens_grad = (
        cotangent.astype(F32)
        + mine_rstd
        * (
            norm_term
            - jnp.mean(norm_term, -1, keepdims=True)
            - mine * jnp.mean(norm_term * mine, -1, keepdims=True)
        )
    ).astype(BF)

    qkv_cols = qkv_back.astype(F32)
    if plan.share > 1:
        qkv_cols = jnp.sum(qkv_cols.reshape(heads, plan.share, depth, 3 * HD), 1)
    order = np.argsort(plan.heads[:: plan.share])
    qkv_cols = qkv_cols[order].reshape(heads, depth, 3, HD).transpose(1, 2, 0, 3)
    attn_weights_grad = jnp.concatenate(
        [qkv_cols.reshape(depth, 3 * width), out_back.astype(F32)], 1
    )
    mlp_weights_grad = jnp.stack(
        [
            up_back.astype(F32).transpose(1, 0, 2).reshape(depth, hidden_width),
            down_back.astype(F32).transpose(1, 0, 2).reshape(depth, hidden_width),
        ],
        1,
    )

    qkv_slot = jnp.zeros((3, heads, HD), F32)
    qkv_slot = lax.dynamic_update_slice_in_dim(qkv_slot, qkv_sum.reshape(3, 1, HD), head_of, 1)
    up_slot = jnp.zeros((hidden_width,), F32)
    up_slot = lax.dynamic_update_slice_in_dim(up_slot, up_sum, me * (hidden_width // blks), 0)
    gain1, bias1, gain2, bias2, qkv_total, up_total, out_total = lax.psum(
        (
            gain1_part,
            bias1_part,
            gain2_part,
            bias2_part,
            qkv_slot.reshape(-1),
            up_slot,
            jnp.sum(cotangent.astype(F32), (0, 1)),
        ),
        ("row", "blk"),
    )
    return (
        layer_out,
        tokens_grad,
        attn_weights_grad,
        mlp_weights_grad,
        (gain1 - ln1_bias * bias1) / ln1_gain,
        bias1,
        (gain2 - ln2_bias * bias2) / ln2_gain,
        bias2,
        qkv_total,
        out_total,
        up_total,
        out_total,
    )


def solution(mesh):
    rows, blks = mesh.shape["row"], mesh.shape["blk"]

    def run(*arrays):
        plan = Plan(rows, blks, arrays[0].shape[-1] // HD)
        placed = (
            P("row", "blk", None),
            P(("row", "blk"), None),
            P(("row", "blk"), None, None),
            P(),
            P(),
            P(),
            P(),
            P(),
            P(),
            P(),
            P(),
            P("row", None),
            P("row", "blk", None),
        )
        return jax.shard_map(
            lambda *local: shards(plan, *local),
            mesh=mesh,
            in_specs=placed,
            out_specs=(
                P("row", "blk", None),
                P("row", "blk", None),
                P(("row", "blk"), None),
                P(("row", "blk"), None, None),
                P(),
                P(),
                P(),
                P(),
                P(),
                P(),
                P(),
                P(),
            ),
            check_vma=False,
        )(*arrays)

    return run
```

```python
import math

import jax
import jax.numpy as jnp
import numpy as np
from jax import lax
from jax.sharding import PartitionSpec as P

HD = 256
ROT = 64
EPSILON = 1e-05
MASKED = -1e30
BF = jnp.bfloat16
F32 = jnp.float32


def rotate(field, cosine, sine_vals):
    half_dims = ROT // 2
    lower_half = field[..., :half_dims]
    upper_half = field[..., half_dims:ROT]
    return jnp.concatenate(
        [
            lower_half * cosine - upper_half * sine_vals,
            upper_half * cosine + lower_half * sine_vals,
            field[..., ROT:],
        ],
        -1,
    )


def dot(left, right, left_dim, right_dim):
    return lax.dot_general(
        left, right, (((left_dim,), (right_dim,)), ((), ())), preferred_element_type=F32
    )


def batched(spec, left, right):
    return jnp.einsum(spec, left, right, preferred_element_type=F32)


class Plan:
    def __init__(self, rows, blks, heads):
        self.rows = rows
        self.blks = blks
        self.share = blks // heads
        self.per_row = heads // rows
        self.group = blks // self.per_row
        self.groups = [
            list(range(i * self.group, (i + 1) * self.group)) for i in range(self.per_row)
        ]


def swap(field, axis, size, bit):
    return lax.ppermute(field, axis, [(i, i ^ bit) for i in range(size)])


def bits_of(size):
    return [1 << i for i in range(size.bit_length() - 1)]


def total(field, plan):
    for axis, size in (("row", plan.rows), ("blk", plan.blks)):
        for bit in bits_of(size):
            field = field + swap(field, axis, size, bit)
    return field


def turn(field, axis, plan):
    me = lax.axis_index("row")
    part = field.shape[axis] // plan.rows
    return jnp.concatenate(
        [
            lax.dynamic_slice_in_dim(field, (me ^ k) * part, part, axis)
            for k in range(plan.rows)
        ],
        axis,
    )


def halves(field):
    middle = field.shape[0] // 2
    return field[:middle], field[middle:]


def gather_rows(piece, plan):
    bits = bits_of(plan.rows)
    both = []
    for half, order in zip(halves(piece), (bits, bits[::-1])):
        got = {0: half}
        for bit in order:
            got.update({k ^ bit: swap(v, "row", plan.rows, bit) for k, v in got.items()})
        both.append(got)
    return jnp.concatenate([got[k] for k in range(plan.rows) for got in both], 0)


def scatter_rows(terms, plan):
    bits = bits_of(plan.rows)
    out = []
    for i, order in enumerate((bits, bits[::-1])):
        held = {k: halves(terms[k])[i] for k in range(plan.rows)}
        for bit in order:
            sent = {k: held.pop(k) for k in list(held) if k & bit}
            for k, v in sent.items():
                held[k ^ bit] = held[k ^ bit] + swap(v.astype(BF), "row", plan.rows, bit).astype(F32)
        out.append(held[0])
    return jnp.concatenate(out, 0)


def spread_columns(pieces, plan):
    mine = lax.all_to_all(pieces, "blk", 0, 0)
    return gather_rows(mine.reshape(-1, mine.shape[-1]), plan)


def collect_columns(grad, plan):
    summed = scatter_rows(jnp.split(grad, plan.rows, 0), plan).astype(BF)
    return lax.all_to_all(summed.reshape(plan.blks, -1, grad.shape[-1]), "blk", 0, 0)


def shards(
    plan,
    tokens,
    attn_weights,
    mlp_weights,
    ln1_gain,
    ln1_bias,
    ln2_gain,
    ln2_bias,
    qkv_bias,
    dense_bias,
    up_bias,
    down_bias,
    doc_lengths,
    cotangent,
):
    row_count, shard_len, width = tokens.shape
    depth = attn_weights.shape[0]
    heads = width // HD
    hidden_width = mlp_weights.shape[-1]
    blks = plan.blks
    me = lax.axis_index("blk")
    length = shard_len * blks
    count = row_count * length
    head_of = me % plan.group // plan.share * plan.per_row + me // plan.group
    part = me % plan.share
    own_rows = row_count // plan.share

    tokens_turned = turn(tokens, 2, plan)
    grad_turned = turn(cotangent, 2, plan)
    gain1, bias1 = turn(ln1_gain, 0, plan), turn(ln1_bias, 0, plan)
    gain2, bias2 = turn(ln2_gain, 0, plan), turn(ln2_bias, 0, plan)
    x_all = lax.all_gather(tokens_turned, "blk", axis=1, tiled=True)

    def by_block(field):
        return field.reshape(depth, blks, -1).transpose(1, 0, 2)

    up_w = spread_columns(by_block(mlp_weights[:, 0]), plan)
    g_all = lax.all_gather(grad_turned, "blk", axis=1, tiled=True)
    down_w = spread_columns(by_block(mlp_weights[:, 1]), plan)
    qkv_cols = attn_weights[:, : 3 * width].reshape(depth, 3, plan.rows, plan.per_row, HD)
    qkv_cols = jnp.repeat(qkv_cols.transpose(3, 2, 0, 1, 4), plan.share, 1)
    qkv_w = spread_columns(qkv_cols.reshape(blks, depth, 3 * HD), plan)
    out_own = attn_weights[:, 3 * width :]
    out_rows = jnp.concatenate(
        [out_own] + [swap(out_own, "row", plan.rows, k) for k in range(1, plan.rows)], 0
    )
    out_rows = turn(out_rows, 0, plan).reshape(plan.rows, depth, width)
    out_rows = jnp.repeat(out_rows, plan.share, axis=0)
    out_w = lax.all_to_all(out_rows, "blk", 0, 0, axis_index_groups=plan.groups)
    out_w = turn(out_w.reshape(HD, width), 1, plan)

    field = x_all.reshape(count, width).astype(F32)
    average = jnp.mean(field, -1, keepdims=True)
    centred = field - average
    rstd = lax.rsqrt(jnp.mean(centred * centred, -1, keepdims=True) + EPSILON)
    standard = centred * rstd
    normed1 = (standard * gain1 + bias1).astype(BF)
    normed2 = (standard * gain2 + bias2).astype(BF)
    grad_all = g_all.reshape(count, width)

    up_b = lax.dynamic_slice_in_dim(up_bias, me * (hidden_width // blks), hidden_width // blks)
    pre = dot(normed2, up_w, 1, 0) + up_b
    cdf = 0.5 * (1.0 + lax.erf(pre * math.sqrt(0.5)))
    hidden = (pre * cdf).astype(BF)
    slope = cdf + pre * (jnp.exp(-0.5 * pre * pre) * (1.0 / math.sqrt(2.0 * math.pi)))
    pre_grad = (dot(grad_all, down_w, 1, 0) * slope).astype(BF)
    up_g = dot(normed2, pre_grad, 0, 0)
    down_g = dot(grad_all, hidden, 0, 0)
    up_back = collect_columns(up_g, plan)
    down_back = collect_columns(down_g, plan)
    mlp_term = dot(hidden, down_w, 1, 1)
    normed2_grad = dot(pre_grad, up_w, 1, 1)
    up_sum = jnp.sum(pre_grad.astype(F32), 0)
    gain2_part = jnp.sum(up_w.astype(F32) * up_g, 1)
    bias2_part = jnp.sum(up_w.astype(F32) * up_sum, 1)

    lengths = lax.dynamic_slice_in_dim(doc_lengths, part * own_rows, own_rows, 0)
    doc_ends = jnp.cumsum(lengths, axis=-1)
    starts = doc_ends - lengths
    places = jnp.arange(length, dtype=jnp.int32)
    doc_ids = jnp.sum((places[None, :, None] >= doc_ends[:, None, :]).astype(jnp.int32), -1)
    picked = doc_ids[:, :, None] == jnp.arange(lengths.shape[-1], dtype=jnp.int32)
    positions = places - jnp.sum(jnp.where(picked, starts[:, None, :], 0), -1)
    inverse = 10000.0 ** (-2.0 * jnp.arange(ROT // 2, dtype=F32) / ROT)
    angles = positions.astype(F32)[..., None] * inverse
    cosine = jnp.cos(angles)
    sine_vals = jnp.sin(angles)
    allowed = (doc_ids[:, :, None] == doc_ids[:, None, :]) & (
        places[None, None, :] <= places[None, :, None]
    )
    scale = HD ** (-0.5)

    def own(field):
        return lax.dynamic_slice_in_dim(field, part * own_rows * length, own_rows * length, 0)

    own_normed1 = own(normed1)
    own_grad = own(grad_all)
    qkv_b = lax.dynamic_index_in_dim(qkv_bias.reshape(3, heads, HD), head_of, 1, keepdims=False)
    qkv = (dot(own_normed1, qkv_w, 1, 0) + qkv_b.reshape(-1)).reshape(own_rows, length, 3, HD)
    queries = (rotate(qkv[:, :, 0], cosine, sine_vals) * scale).astype(BF)
    keys = rotate(qkv[:, :, 1], cosine, sine_vals).astype(BF)
    values = qkv[:, :, 2].astype(BF)
    scores = jnp.where(allowed, batched("rqd,rkd->rqk", queries, keys), MASKED)
    weights = jnp.where(allowed, jnp.exp(scores - jnp.max(scores, -1, keepdims=True)), 0.0)
    weights = weights / jnp.sum(weights, -1, keepdims=True)
    weights_low = weights.astype(BF)
    attended = batched("rqk,rkd->rqd", weights_low, values).astype(BF)
    heads_grad = dot(own_grad, out_w, 1, 1).astype(BF).reshape(own_rows, length, HD)
    deltas = jnp.sum(heads_grad.astype(F32) * attended.astype(F32), -1, keepdims=True)
    weight_grad = batched("rqd,rkd->rqk", heads_grad, values)
    score_grad = (weights * (weight_grad - deltas)).astype(BF)
    query_grad = batched("rqk,rkd->rqd", score_grad, keys)
    key_grad = batched("rqk,rqd->rkd", score_grad, queries)
    value_grad = batched("rqk,rqd->rkd", weights_low, heads_grad)
    qkv_grad = jnp.concatenate(
        [
            rotate(query_grad * scale, cosine, -sine_vals),
            rotate(key_grad, cosine, -sine_vals),
            value_grad,
        ],
        -1,
    ).reshape(own_rows * length, 3 * HD)
    qkv_grad = qkv_grad.astype(BF)
    attended = attended.reshape(own_rows * length, HD)
    qkv_g = dot(own_normed1, qkv_grad, 0, 0)
    out_g = dot(attended, own_grad, 0, 0)
    qkv_back = collect_columns(qkv_g, plan)
    out_send = turn(out_g.astype(BF), 1, plan).reshape(plan.group, depth, width)
    out_back = lax.all_to_all(out_send, "blk", 0, 0, axis_index_groups=plan.groups)
    out_back = out_back.reshape(plan.rows, plan.share, depth, width).astype(F32)
    out_back = turn(jnp.sum(out_back, 1), 0, plan)
    out_back = out_back[0] + sum(
        swap(out_back[k].astype(BF), "row", plan.rows, k).astype(F32)
        for k in range(1, plan.rows)
    )
    qkv_sum = jnp.sum(qkv_grad.astype(F32), 0)
    gain1_part = jnp.sum(qkv_w.astype(F32) * qkv_g, 1)
    bias1_part = jnp.sum(qkv_w.astype(F32) * qkv_sum, 1)

    def spread_rows(field):
        if plan.share == 1:
            return field
        whole = jnp.zeros((count, width), F32)
        return lax.dynamic_update_slice_in_dim(whole, field, part * own_rows * length, 0)

    out_term = (mlp_term + spread_rows(dot(attended, out_w, 1, 0))).astype(BF)
    out_term = lax.psum_scatter(
        out_term.reshape(row_count, length, width), "blk", scatter_dimension=1, tiled=True
    )
    layer_out = (
        tokens.astype(F32) + turn(out_term, 2, plan).astype(F32) + (dense_bias + down_bias)
    ).astype(BF)
    norm_term = spread_rows(dot(qkv_grad, qkv_w, 1, 1)) * gain1 + normed2_grad * gain2
    norm_term = lax.psum_scatter(
        norm_term.astype(BF).reshape(row_count, length, width),
        "blk",
        scatter_dimension=1,
        tiled=True,
    )
    norm_term = turn(norm_term, 2, plan).astype(F32)
    mine = tokens.astype(F32)
    mine = mine - jnp.mean(mine, -1, keepdims=True)
    mine_rstd = lax.rsqrt(jnp.mean(mine * mine, -1, keepdims=True) + EPSILON)
    mine = mine * mine_rstd
    tokens_grad = (
        cotangent.astype(F32)
        + mine_rstd
        * (
            norm_term
            - jnp.mean(norm_term, -1, keepdims=True)
            - mine * jnp.mean(norm_term * mine, -1, keepdims=True)
        )
    ).astype(BF)

    qkv_cols = qkv_back.reshape(plan.per_row, plan.rows, plan.share, depth, 3, HD)
    qkv_cols = jnp.sum(qkv_cols.astype(F32), 2).transpose(2, 3, 1, 0, 4)
    attn_weights_grad = jnp.concatenate(
        [qkv_cols.reshape(depth, 3 * width), out_back], 1
    )
    mlp_weights_grad = jnp.stack(
        [
            up_back.astype(F32).transpose(1, 0, 2).reshape(depth, hidden_width),
            down_back.astype(F32).transpose(1, 0, 2).reshape(depth, hidden_width),
        ],
        1,
    )

    qkv_slot = jnp.zeros((3, heads, HD), F32)
    qkv_slot = lax.dynamic_update_slice_in_dim(qkv_slot, qkv_sum.reshape(3, 1, HD), head_of, 1)
    up_slot = jnp.zeros((hidden_width,), F32)
    up_slot = lax.dynamic_update_slice_in_dim(up_slot, up_sum, me * (hidden_width // blks), 0)
    parts = [
        turn(gain1_part, 0, plan),
        turn(bias1_part, 0, plan),
        turn(gain2_part, 0, plan),
        turn(bias2_part, 0, plan),
        qkv_slot.reshape(-1),
        up_slot,
        jnp.sum(cotangent.astype(F32), (0, 1)),
    ]
    ends = np.cumsum([p.shape[0] for p in parts])[:-1]
    sums = jnp.split(total(jnp.concatenate(parts), plan), ends)
    gain1_sum, bias1_sum, gain2_sum, bias2_sum, qkv_total, up_total, out_total = sums
    return (
        layer_out,
        tokens_grad,
        attn_weights_grad,
        mlp_weights_grad,
        (gain1_sum - ln1_bias * bias1_sum) / ln1_gain,
        bias1_sum,
        (gain2_sum - ln2_bias * bias2_sum) / ln2_gain,
        bias2_sum,
        qkv_total,
        out_total,
        up_total,
        out_total,
    )


def solution(mesh):
    rows, blks = mesh.shape["row"], mesh.shape["blk"]

    def run(*arrays):
        plan = Plan(rows, blks, arrays[0].shape[-1] // HD)
        placed = (
            P("row", "blk", None),
            P(("row", "blk"), None),
            P(("row", "blk"), None, None),
            P(),
            P(),
            P(),
            P(),
            P(),
            P(),
            P(),
            P(),
            P("row", None),
            P("row", "blk", None),
        )
        return jax.shard_map(
            lambda *local: shards(plan, *local),
            mesh=mesh,
            in_specs=placed,
            out_specs=(
                P("row", "blk", None),
                P("row", "blk", None),
                P(("row", "blk"), None),
                P(("row", "blk"), None, None),
                P(),
                P(),
                P(),
                P(),
                P(),
                P(),
                P(),
                P(),
            ),
            check_vma=False,
        )(*arrays)

    return run
```

```python
import functools
import math

import jax
import jax.numpy as jnp
import numpy as np
from jax import lax
from jax.experimental import pallas as pl
from jax.experimental.pallas import tpu as pltpu
from jax.sharding import PartitionSpec as P

HD = 256
ROT = 64
LANES = 128
BLOCK = 256
EPSILON = 1e-05
MASKED = -1e30
BF = jnp.bfloat16
F32 = jnp.float32
VMEM_LIMIT = 48 * 2**20


class Plan:
    def __init__(self, rows, blks, heads):
        self.rows = rows
        self.blks = blks
        self.share = blks // heads
        self.per_row = heads // rows
        self.group = blks // self.per_row
        self.groups = [
            list(range(i * self.group, (i + 1) * self.group)) for i in range(self.per_row)
        ]


def swap(field, axis, size, bit):
    return lax.ppermute(field, axis, [(i, i ^ bit) for i in range(size)])


def bits_of(size):
    return [1 << i for i in range(size.bit_length() - 1)]


def orders(plan):
    bits = bits_of(plan.rows)
    return bits, bits[::-1]


def total(field, plan):
    for axis, size in (("row", plan.rows), ("blk", plan.blks)):
        for bit in bits_of(size):
            field = field + swap(field, axis, size, bit)
    return field


def turn(field, axis, plan):
    me = lax.axis_index("row")
    part = field.shape[axis] // plan.rows
    return jnp.concatenate(
        [
            lax.dynamic_slice_in_dim(field, (me ^ k) * part, part, axis)
            for k in range(plan.rows)
        ],
        axis,
    )


def gather_row(piece, order, plan):
    got = {0: piece}
    for bit in order:
        got.update({k ^ bit: swap(v, "row", plan.rows, bit) for k, v in got.items()})
    return [got[k] for k in range(plan.rows)]


def scatter_row(terms, order, plan):
    held = dict(enumerate(terms))
    for bit in order:
        sent = {k: held.pop(k) for k in list(held) if k & bit}
        for k, v in sent.items():
            got = swap(v.astype(BF), "row", plan.rows, bit)
            held[k ^ bit] = held[k ^ bit].astype(F32) + got.astype(F32)
    return held[0].astype(BF)


def spread_columns(units, plan):
    out = []
    for unit, order in zip(units, orders(plan)):
        mine = lax.all_to_all(unit, "blk", 0, 0)
        out.append(gather_row(mine.reshape(-1, mine.shape[-1]), order, plan))
    return out


def collect_columns(units, plan):
    out = []
    for terms, order in zip(units, orders(plan)):
        summed = scatter_row(terms, order, plan)
        summed = summed.reshape(plan.blks, -1, summed.shape[-1])
        out.append(lax.all_to_all(summed, "blk", 0, 0))
    return out


def dot(left, right, left_dim, right_dim):
    return lax.dot_general(
        left, right, (((left_dim,), (right_dim,)), ((), ())), preferred_element_type=F32
    )


def whole(array):
    return pl.BlockSpec(array.shape, lambda *i: (0,) * array.ndim)


def call(body, grid, in_specs, out_specs, out_shape, flops, moved, operands):
    return pl.pallas_call(
        body,
        grid=grid,
        in_specs=in_specs,
        out_specs=out_specs,
        out_shape=out_shape,
        compiler_params=pltpu.CompilerParams(vmem_limit_bytes=VMEM_LIMIT),
        cost_estimate=pl.CostEstimate(flops=flops, bytes_accessed=moved, transcendentals=0),
    )(*operands)


def norm_kernel(x_ref, g1_ref, b1_ref, g2_ref, b2_ref, a1_ref, a2_ref):
    field = x_ref[...].astype(F32)
    centred = field - jnp.mean(field, -1, keepdims=True)
    standard = centred * lax.rsqrt(jnp.mean(centred * centred, -1, keepdims=True) + EPSILON)
    a1_ref[...] = (standard * g1_ref[...] + b1_ref[...]).astype(BF)
    a2_ref[...] = (standard * g2_ref[...] + b2_ref[...]).astype(BF)


def norms(x, gain1, bias1, gain2, bias2):
    count, width = x.shape
    block = pl.BlockSpec((BLOCK, width), lambda i: (i, 0))
    row = pl.BlockSpec((1, width), lambda i: (0, 0))
    return call(
        norm_kernel,
        (count // BLOCK,),
        [block] + [row] * 4,
        [block] * 2,
        [jax.ShapeDtypeStruct(x.shape, BF)] * 2,
        20 * count * width,
        6 * count * width,
        [x] + [v.reshape(1, width) for v in (gain1, bias1, gain2, bias2)],
    )


def times_pieces(left, pieces):
    depth = pieces[0].shape[0]
    out = None
    for k, piece in enumerate(pieces):
        term = dot(left[:, k * depth : (k + 1) * depth], piece[...], 1, 0)
        out = term if out is None else out + term
    return out


def up_kernel(count, a_ref, b_ref, *refs):
    pieces, (h_ref, s_ref) = refs[:-2], refs[-2:]
    left = a_ref[...]
    half = h_ref.shape[1] // 2
    for i in range(2):
        cols = slice(i * half, (i + 1) * half)
        pre = times_pieces(left, pieces[i * count : (i + 1) * count]) + b_ref[:, cols]
        cdf = 0.5 * (1.0 + lax.erf(pre * math.sqrt(0.5)))
        h_ref[:, cols] = (pre * cdf).astype(BF)
        s_ref[:, cols] = cdf + pre * (
            jnp.exp(-0.5 * pre * pre) * (1.0 / math.sqrt(2.0 * math.pi))
        )


def feed_up(normed, bias, units):
    count, width = normed.shape
    hidden = bias.shape[0]
    pieces = units[0] + units[1]
    block = pl.BlockSpec((BLOCK, hidden), lambda i: (i, 0))
    return call(
        functools.partial(up_kernel, len(units[0])),
        (count // BLOCK,),
        [
            pl.BlockSpec((BLOCK, width), lambda i: (i, 0)),
            pl.BlockSpec((1, hidden), lambda i: (0, 0)),
        ]
        + [whole(p) for p in pieces],
        [block, block],
        [jax.ShapeDtypeStruct((count, hidden), t) for t in (BF, F32)],
        2 * count * width * hidden,
        2 * count * width + 6 * count * hidden + 2 * width * hidden,
        [normed, bias.reshape(1, hidden)] + pieces,
    )


def slope_kernel(count, g_ref, s_ref, *refs):
    pieces, (p_ref, sum_ref) = refs[:-2], refs[-2:]
    left = g_ref[...]
    half = p_ref.shape[1] // 2

    @pl.when(pl.program_id(0) == 0)
    def _():
        sum_ref[...] = jnp.zeros_like(sum_ref)

    for i in range(2):
        cols = slice(i * half, (i + 1) * half)
        grad = times_pieces(left, pieces[i * count : (i + 1) * count]) * s_ref[:, cols]
        grad = grad.astype(BF)
        p_ref[:, cols] = grad
        sum_ref[:, cols] += jnp.sum(grad.astype(F32), 0, keepdims=True)


def feed_slope(grad, slope, units):
    count, width = grad.shape
    hidden = slope.shape[1]
    pieces = units[0] + units[1]
    block = pl.BlockSpec((BLOCK, hidden), lambda i: (i, 0))
    return call(
        functools.partial(slope_kernel, len(units[0])),
        (count // BLOCK,),
        [pl.BlockSpec((BLOCK, width), lambda i: (i, 0)), block] + [whole(p) for p in pieces],
        [block, pl.BlockSpec((1, hidden), lambda i: (0, 0))],
        [
            jax.ShapeDtypeStruct((count, hidden), BF),
            jax.ShapeDtypeStruct((1, hidden), F32),
        ],
        2 * count * width * hidden,
        2 * count * width + 6 * count * hidden + 2 * width * hidden,
        [grad, slope] + pieces,
    )


def lane_sum(field):
    return sum(field[:, i : i + LANES] for i in range(0, field.shape[1], LANES))


def weight_kernel(rows, with_sums, l_ref, r_ref, *refs):
    step = pl.program_id(0)
    half = r_ref.shape[1] // 2
    if with_sums:
        sum_ref, pieces, refs = refs[0], refs[1 : 1 + 2 * rows], refs[1 + 2 * rows :]
        parts = refs[2 * rows :]
    left = l_ref[...]
    for i in range(2):
        cols = slice(i * half, (i + 1) * half)
        grad = dot(left, r_ref[:, cols], 0, 0)
        for k in range(rows):

            @pl.when(step == k)
            def _(i=i, k=k, grad=grad, cols=cols):
                refs[i * rows + k][...] = grad.astype(BF)
                if with_sums:
                    piece = pieces[i * rows + k][...].astype(F32)
                    gain = lane_sum(piece * grad)
                    bias = lane_sum(piece * sum_ref[:, cols])
                    if i == 0:
                        parts[0][...] = gain
                        parts[1][...] = bias
                    else:
                        parts[0][...] += gain
                        parts[1][...] += bias


def weight_grad(left, right, rows, sums=None, units=None):
    count, width = left.shape
    columns = right.shape[1]
    depth = width // rows
    chunk = jax.ShapeDtypeStruct((depth, columns // 2), BF)
    pieces = units[0] + units[1] if units else []
    in_specs = [pl.BlockSpec((count, depth), lambda k: (0, k)), whole(right)]
    out_shape = [chunk] * (2 * rows)
    out_specs = [whole(chunk)] * (2 * rows)
    operands = [left, right]
    if units:
        in_specs += [whole(sums)] + [whole(p) for p in pieces]
        operands += [sums] + pieces
        out_shape += [jax.ShapeDtypeStruct((width, LANES), F32)] * 2
        out_specs += [pl.BlockSpec((depth, LANES), lambda k: (k, 0))] * 2
    out = call(
        functools.partial(weight_kernel, rows, bool(units)),
        (rows,),
        in_specs,
        out_specs,
        out_shape,
        2 * count * width * columns,
        2 * (count * (width + columns) + width * columns),
        operands,
    )
    return [out[:rows], out[rows : 2 * rows]] + [jnp.sum(v, 1) for v in out[2 * rows :]]


def back_kernel(rows, with_gains, l_ref, s_ref, *refs):
    refs, out_ref = refs[:-1], refs[-1]
    pieces = refs[: 2 * rows]
    half = l_ref.shape[1] // 2
    depth = out_ref.shape[1] // rows
    if with_gains:
        sides, (g2_ref, g1_ref) = refs[2 * rows : 4 * rows], refs[4 * rows :]
        side_half = s_ref.shape[1] // 2
    for k in range(rows):
        cols = slice(k * depth, (k + 1) * depth)
        term = dot(l_ref[:, :half], pieces[k][...], 1, 1)
        term += dot(l_ref[:, half:], pieces[rows + k][...], 1, 1)
        if with_gains:
            side = dot(s_ref[:, :side_half], sides[k][...], 1, 1)
            side += dot(s_ref[:, side_half:], sides[rows + k][...], 1, 1)
            term = term * g2_ref[:, cols] + side * g1_ref[:, cols]
        else:
            term += dot(s_ref[...], refs[2 * rows][:, cols], 1, 0)
        out_ref[:, cols] = term.astype(BF)


def back(left, units, side, other, width, gains=None):
    count = left.shape[0]
    rows = len(units[0])
    operands = [left, side] + units[0] + units[1] + other
    in_specs = [
        pl.BlockSpec((BLOCK, left.shape[1]), lambda i: (i, 0)),
        pl.BlockSpec((BLOCK, side.shape[1]), lambda i: (i, 0)),
    ] + [whole(p) for p in operands[2:]]
    if gains:
        operands += [v.reshape(1, width) for v in gains]
        in_specs += [pl.BlockSpec((1, width), lambda i: (0, 0))] * 2
    columns = left.shape[1] + side.shape[1]
    return call(
        functools.partial(back_kernel, rows, bool(gains)),
        (count // BLOCK,),
        in_specs,
        pl.BlockSpec((BLOCK, width), lambda i: (i, 0)),
        jax.ShapeDtypeStruct((count, width), BF),
        2 * count * width * columns,
        2 * (count * (width + columns) + width * columns),
        operands,
    )


def turned(field, cosine, minus, plus):
    head = field[:, :LANES]
    half = ROT // 2
    head = (
        head * cosine
        + pltpu.roll(head, LANES - half, 1) * minus
        + pltpu.roll(head, half, 1) * plus
    )
    return jnp.concatenate([head, field[:, LANES:]], 1)


def head_kernel(
    rows, a_ref, g_ref, w_ref, b_ref, c_ref, m_ref, p_ref, dq_ref, dk_ref, *refs
):
    pieces, (o_ref, grad_ref, sum_ref) = refs[:-3], refs[-3:]
    left = a_ref[...]
    scale = HD ** (-0.5)
    qkv = jnp.concatenate(
        [times_pieces(left, pieces[:rows]), times_pieces(left, pieces[rows:])], 1
    )
    qkv = qkv + b_ref[...]
    cosine, minus, plus = c_ref[0], m_ref[0], p_ref[0]
    queries = (turned(qkv[:, :HD], cosine, minus, plus) * scale).astype(BF)
    keys = turned(qkv[:, HD : 2 * HD], cosine, minus, plus).astype(BF)
    values = qkv[:, 2 * HD :].astype(BF)
    length = left.shape[0]
    spot = lax.broadcasted_iota(jnp.int32, (length, length), 0)
    other = lax.broadcasted_iota(jnp.int32, (length, length), 1)
    allowed = (dq_ref[0] == dk_ref[0]) & (other <= spot)
    scores = jnp.where(allowed, dot(queries, keys, 1, 1), MASKED)
    weights = jnp.exp(scores - jnp.max(scores, -1, keepdims=True))
    weights = jnp.where(allowed, weights, 0.0)
    weights = weights / jnp.sum(weights, -1, keepdims=True)
    weights_low = weights.astype(BF)
    attended = dot(weights_low, values, 1, 0).astype(BF)
    o_ref[...] = attended
    heads_grad = dot(g_ref[...], w_ref[...], 1, 1).astype(BF)
    deltas = jnp.sum(heads_grad.astype(F32) * attended.astype(F32), -1, keepdims=True)
    weight_grad_ = dot(heads_grad, values, 1, 1)
    score_grad = (weights * (weight_grad_ - deltas)).astype(BF)
    query_grad = dot(score_grad, keys, 1, 0) * scale
    key_grad = dot(score_grad, queries, 0, 0)
    value_grad = dot(weights_low, heads_grad, 0, 0)
    grad = jnp.concatenate(
        [
            turned(query_grad, cosine, -minus, -plus),
            turned(key_grad, cosine, -minus, -plus),
            value_grad,
        ],
        1,
    ).astype(BF)
    grad_ref[...] = grad

    @pl.when(pl.program_id(0) == 0)
    def _():
        sum_ref[...] = jnp.zeros_like(sum_ref)

    sum_ref[...] += jnp.sum(grad.astype(F32), 0, keepdims=True)


def one_head(normed, grad, out_w, bias, tables, doc_ids, units, length):
    count, width = normed.shape
    pieces = units[0] + units[1]
    columns = 3 * HD
    field = pl.BlockSpec((length, width), lambda r: (r, 0))
    table = pl.BlockSpec((1, length, LANES), lambda r: (r, 0, 0))
    return call(
        functools.partial(head_kernel, len(units[0])),
        (count // length,),
        [field, field, whole(out_w), pl.BlockSpec((1, columns), lambda r: (0, 0))]
        + [table] * 3
        + [
            pl.BlockSpec((1, length, 1), lambda r: (r, 0, 0)),
            pl.BlockSpec((1, 1, length), lambda r: (r, 0, 0)),
        ]
        + [whole(p) for p in pieces],
        [
            pl.BlockSpec((length, HD), lambda r: (r, 0)),
            pl.BlockSpec((length, columns), lambda r: (r, 0)),
            pl.BlockSpec((1, columns), lambda r: (0, 0)),
        ],
        [
            jax.ShapeDtypeStruct((count, HD), BF),
            jax.ShapeDtypeStruct((count, columns), BF),
            jax.ShapeDtypeStruct((1, columns), F32),
        ],
        2 * count * (width * (columns + HD) + 7 * length * HD),
        2 * (count * (2 * width + columns + HD) + width * (columns + HD)),
        [normed, grad, out_w, bias.reshape(1, columns)]
        + list(tables)
        + [doc_ids[:, :, None], doc_ids[:, None, :]]
        + pieces,
    )


def shards(
    plan,
    tokens,
    attn_weights,
    mlp_weights,
    ln1_gain,
    ln1_bias,
    ln2_gain,
    ln2_bias,
    qkv_bias,
    dense_bias,
    up_bias,
    down_bias,
    doc_lengths,
    cotangent,
):
    row_count, shard_len, width = tokens.shape
    depth = attn_weights.shape[0]
    heads = width // HD
    rows, blks = plan.rows, plan.blks
    hidden_width = mlp_weights.shape[-1]
    own_hidden = hidden_width // blks
    me = lax.axis_index("blk")
    length = shard_len * blks
    count = row_count * length
    head_of = me % plan.group // plan.share * plan.per_row + me // plan.group
    part = me % plan.share
    own_rows = row_count // plan.share

    gain1, bias1 = turn(ln1_gain, 0, plan), turn(ln1_bias, 0, plan)
    gain2, bias2 = turn(ln2_gain, 0, plan), turn(ln2_bias, 0, plan)
    x_all = lax.all_gather(turn(tokens, 2, plan), "blk", axis=1, tiled=True)
    x_all = x_all.reshape(count, width)
    g_all = lax.all_gather(turn(cotangent, 2, plan), "blk", axis=1, tiled=True)
    g_all = g_all.reshape(count, width)
    pick = np.zeros((2 * depth, 2 * depth), np.float32)
    pick[np.arange(2 * depth), np.arange(2 * depth) % depth * 2 + np.arange(2 * depth) // depth] = 1
    both = dot(jnp.asarray(pick, BF), mlp_weights.reshape(2 * depth, hidden_width), 1, 0)
    both = both.astype(BF).reshape(2, depth, blks, 2, own_hidden // 2).transpose(0, 3, 2, 1, 4)
    up_units = spread_columns([both[0, 0], both[0, 1]], plan)
    down_units = spread_columns([both[1, 0], both[1, 1]], plan)
    qkv_cols = attn_weights[:, : 3 * width].reshape(depth, 3, rows, plan.per_row, HD)
    qkv_cols = jnp.repeat(qkv_cols.transpose(3, 2, 0, 1, 4), plan.share, 1)
    qkv_cols = qkv_cols.reshape(blks, depth, 2, 3 * HD // 2)
    qkv_units = spread_columns([qkv_cols[:, :, 0], qkv_cols[:, :, 1]], plan)
    out_own = attn_weights[:, 3 * width :]
    out_rows = jnp.stack([out_own] + [swap(out_own, "row", rows, k) for k in range(1, rows)])
    out_rows = jnp.repeat(turn(out_rows, 0, plan), plan.share, axis=0)
    out_w = lax.all_to_all(out_rows, "blk", 0, 0, axis_index_groups=plan.groups)
    out_w = turn(out_w.reshape(HD, width), 1, plan)

    normed1, normed2 = norms(x_all, gain1, bias1, gain2, bias2)
    up_b = lax.dynamic_slice_in_dim(up_bias, me * own_hidden, own_hidden)
    hidden, slope = feed_up(normed2, up_b, up_units)
    down_g = weight_grad(g_all, hidden, rows)
    down_back = collect_columns(down_g[:2], plan)
    pre_grad, up_sum = feed_slope(g_all, slope, down_units)
    *up_g, gain2_part, bias2_part = weight_grad(normed2, pre_grad, rows, up_sum, up_units)
    up_back = collect_columns(up_g, plan)

    lengths = lax.dynamic_slice_in_dim(doc_lengths, part * own_rows, own_rows, 0)
    doc_ends = jnp.cumsum(lengths, axis=-1)
    starts = doc_ends - lengths
    places = jnp.arange(length, dtype=jnp.int32)
    doc_ids = jnp.sum((places[None, :, None] >= doc_ends[:, None, :]).astype(jnp.int32), -1)
    picked = doc_ids[:, :, None] == jnp.arange(lengths.shape[-1], dtype=jnp.int32)
    positions = places - jnp.sum(jnp.where(picked, starts[:, None, :], 0), -1)
    lane = jnp.arange(LANES)
    inverse = 10000.0 ** (-2.0 * (lane % (ROT // 2)).astype(F32) / ROT)
    angles = positions.astype(F32)[..., None] * inverse
    sine = jnp.sin(angles)
    tables = (
        jnp.where(lane < ROT, jnp.cos(angles), 1.0),
        jnp.where(lane < ROT // 2, -sine, 0.0),
        jnp.where((lane >= ROT // 2) & (lane < ROT), sine, 0.0),
    )

    def own(field):
        if plan.share == 1:
            return field
        return lax.dynamic_slice_in_dim(field, part * own_rows * length, own_rows * length, 0)

    def spread_rows(field):
        if plan.share == 1:
            return field
        zeros = jnp.zeros((count, field.shape[1]), field.dtype)
        return lax.dynamic_update_slice_in_dim(zeros, field, part * own_rows * length, 0)

    own_normed1 = own(normed1)
    own_grad = own(g_all)
    qkv_b = lax.dynamic_index_in_dim(qkv_bias.reshape(3, heads, HD), head_of, 1, keepdims=False)
    attended, qkv_grad, qkv_sum = one_head(
        own_normed1, own_grad, out_w, qkv_b.reshape(-1), tables, doc_ids, qkv_units, length
    )
    *qkv_g, gain1_part, bias1_part = weight_grad(own_normed1, qkv_grad, rows, qkv_sum, qkv_units)
    qkv_back = collect_columns(qkv_g, plan)
    out_g = dot(attended, own_grad, 0, 0)
    out_send = turn(out_g.astype(BF), 1, plan).reshape(plan.group, depth, width)
    out_back = lax.all_to_all(out_send, "blk", 0, 0, axis_index_groups=plan.groups)
    out_back = out_back.reshape(rows, plan.share, depth, width).astype(F32)
    out_back = turn(jnp.sum(out_back, 1), 0, plan)
    out_back = out_back[0] + sum(
        swap(out_back[k].astype(BF), "row", rows, k).astype(F32) for k in range(1, rows)
    )

    def sum_blocks(field):
        field = field.reshape(row_count, length, width)
        field = lax.psum_scatter(field, "blk", scatter_dimension=1, tiled=True)
        return turn(field, 2, plan).astype(F32)

    out_term = sum_blocks(back(hidden, down_units, spread_rows(attended), [out_w], width))
    layer_out = (tokens.astype(F32) + out_term + (dense_bias + down_bias)).astype(BF)
    norm_term = sum_blocks(
        back(
            pre_grad,
            up_units,
            spread_rows(qkv_grad),
            qkv_units[0] + qkv_units[1],
            width,
            (gain2, gain1),
        )
    )
    mine = tokens.astype(F32)
    mine = mine - jnp.mean(mine, -1, keepdims=True)
    mine_rstd = lax.rsqrt(jnp.mean(mine * mine, -1, keepdims=True) + EPSILON)
    mine = mine * mine_rstd
    tokens_grad = (
        cotangent.astype(F32)
        + mine_rstd
        * (
            norm_term
            - jnp.mean(norm_term, -1, keepdims=True)
            - mine * jnp.mean(norm_term * mine, -1, keepdims=True)
        )
    ).astype(BF)

    qkv_cols = jnp.stack(qkv_back, 2)
    qkv_cols = qkv_cols.reshape(plan.per_row, rows, plan.share, depth, 3, HD)
    qkv_cols = jnp.sum(qkv_cols.astype(F32), 2).transpose(2, 3, 1, 0, 4)
    attn_weights_grad = jnp.concatenate([qkv_cols.reshape(depth, 3 * width), out_back], 1)
    mlp_weights_grad = jnp.stack(
        [
            jnp.stack(units).astype(F32).transpose(2, 1, 0, 3).reshape(depth, hidden_width)
            for units in (up_back, down_back)
        ],
        1,
    )

    qkv_slot = jnp.zeros((3, heads, HD), F32)
    qkv_slot = lax.dynamic_update_slice_in_dim(qkv_slot, qkv_sum.reshape(3, 1, HD), head_of, 1)
    up_slot = jnp.zeros((hidden_width,), F32)
    up_slot = lax.dynamic_update_slice_in_dim(up_slot, up_sum.reshape(-1), me * own_hidden, 0)
    parts = [
        turn(gain1_part, 0, plan),
        turn(bias1_part, 0, plan),
        turn(gain2_part, 0, plan),
        turn(bias2_part, 0, plan),
        qkv_slot.reshape(-1),
        up_slot,
        jnp.sum(cotangent.astype(F32), (0, 1)),
    ]
    ends = np.cumsum([p.shape[0] for p in parts])[:-1]
    sums = jnp.split(total(jnp.concatenate(parts), plan), ends)
    gain1_sum, bias1_sum, gain2_sum, bias2_sum, qkv_total, up_total, out_total = sums
    return (
        layer_out,
        tokens_grad,
        attn_weights_grad,
        mlp_weights_grad,
        (gain1_sum - ln1_bias * bias1_sum) / ln1_gain,
        bias1_sum,
        (gain2_sum - ln2_bias * bias2_sum) / ln2_gain,
        bias2_sum,
        qkv_total,
        out_total,
        up_total,
        out_total,
    )


def solution(mesh):
    rows, blks = mesh.shape["row"], mesh.shape["blk"]
    vector = P()
    tokens = P("row", "blk", None)
    attn = P(("row", "blk"), None)
    mlp = P(("row", "blk"), None, None)

    def run(*arrays):
        plan = Plan(rows, blks, arrays[0].shape[-1] // HD)
        return jax.shard_map(
            functools.partial(shards, plan),
            mesh=mesh,
            in_specs=(tokens, attn, mlp) + (vector,) * 8 + (P("row", None), tokens),
            out_specs=(tokens, tokens, attn, mlp) + (vector,) * 8,
            check_vma=False,
        )(*arrays)

    return run
```

```python
import functools
import math

import jax
import jax.numpy as jnp
import numpy as np
from jax import lax
from jax.experimental import pallas as pl
from jax.experimental.pallas import tpu as pltpu
from jax.sharding import PartitionSpec as P

HD = 256
ROT = 64
LANES = 128
BLOCK = 256
EPSILON = 1e-05
MASKED = -1e30
BF = jnp.bfloat16
F32 = jnp.float32
VMEM_LIMIT = 48 * 2**20


class Plan:
    def __init__(self, rows, blks, heads):
        self.rows = rows
        self.blks = blks
        self.share = blks // heads
        self.per_row = heads // rows
        self.group = blks // self.per_row
        self.groups = [
            list(range(i * self.group, (i + 1) * self.group)) for i in range(self.per_row)
        ]


def after(field, *others):
    return lax.optimization_barrier((field,) + others)[0]


def swap(field, axis, size, bit):
    return lax.ppermute(field, axis, [(i, i ^ bit) for i in range(size)])


def bits_of(size):
    return [1 << i for i in range(size.bit_length() - 1)]


def total(field, plan):
    for axis, size in (("row", plan.rows), ("blk", plan.blks)):
        for bit in bits_of(size):
            field = field + swap(field, axis, size, bit)
    return field


def near(k):
    return k & (k - 1) == 0


def orders(plan):
    bits = bits_of(plan.rows)
    return bits, bits[::-1]


def half_of(field, h):
    middle = field.shape[0] // 2
    return field[h * middle : (h + 1) * middle]


def parts_of(rows, depth):
    out = []
    for k in range(rows):
        if near(k):
            out.append((k * depth, depth))
        else:
            out += [(k * depth, depth // 2), (k * depth + depth // 2, depth // 2)]
    return out


class Gather:
    def __init__(self, own, plan):
        self.plan = plan
        self.whole = {0: own}
        for bit in bits_of(plan.rows):
            self.whole[bit] = swap(own, "row", plan.rows, bit)

    def first(self):
        return [v for k, v in self.whole.items() if k]

    def finish(self):
        plan = self.plan
        halves = []
        for h, order in enumerate(orders(plan)):
            got = {0: None}
            for bit in order:
                for k in list(got):
                    if k == 0:
                        got[bit] = half_of(self.whole[bit], h)
                    else:
                        got[k ^ bit] = swap(got[k], "row", plan.rows, bit)
            halves.append(got)
        out = []
        for k in range(plan.rows):
            out += [self.whole[k]] if near(k) else [half[k] for half in halves]
        return out


class Scatter:
    def __init__(self, pieces, plan):
        self.plan = plan
        pieces = iter(pieces)
        self.whole, far = {}, [{}, {}]
        for k in range(plan.rows):
            if near(k):
                self.whole[k] = next(pieces)
            else:
                far[0][k], far[1][k] = next(pieces), next(pieces)
        self.got = []
        for h, order in enumerate(orders(plan)):
            held = far[h]
            for bit in order:
                for k in [k for k in held if k & bit]:
                    term = swap(held.pop(k), "row", plan.rows, bit)
                    if near(k ^ bit):
                        self.got.append((k ^ bit, h, term))
                    else:
                        held[k ^ bit] = (held[k ^ bit].astype(F32) + term.astype(F32)).astype(BF)

    def first(self):
        return [term for _, _, term in self.got]

    def finish(self, *others):
        whole = dict(self.whole)
        for k, h, term in self.got:
            middle = whole[k].shape[0] // 2
            both = half_of(whole[k], h).astype(F32) + term.astype(F32)
            whole[k] = lax.dynamic_update_slice(whole[k], both.astype(BF), (h * middle, 0))
        out = whole[0].astype(F32)
        for bit in bits_of(self.plan.rows):
            field = after(whole[bit], *others) if others else whole[bit]
            out = out + swap(field, "row", self.plan.rows, bit).astype(F32)
        return out.astype(BF)


def dot(left, right, left_dim, right_dim):
    return lax.dot_general(
        left, right, (((left_dim,), (right_dim,)), ((), ())), preferred_element_type=F32
    )


def whole(array):
    return pl.BlockSpec(array.shape, lambda *i: (0,) * len(array.shape))


def like(shape, kind=BF):
    return jax.ShapeDtypeStruct(shape, kind)


def call(body, turns, grid, in_specs, out_specs, out_shape, operands, flops=0):
    moved = sum(v.size * v.dtype.itemsize for v in operands)
    moved += sum(math.prod(v.shape) * jnp.dtype(v.dtype).itemsize for v in out_shape)
    return pl.pallas_call(
        body,
        grid_spec=pltpu.PrefetchScalarGridSpec(
            num_scalar_prefetch=1, grid=(grid,), in_specs=in_specs, out_specs=out_specs
        ),
        out_shape=out_shape,
        compiler_params=pltpu.CompilerParams(vmem_limit_bytes=VMEM_LIMIT),
        cost_estimate=pl.CostEstimate(flops=flops, bytes_accessed=moved, transcendentals=0),
    )(turns, *operands)


def rows_block(columns, block=BLOCK):
    return pl.BlockSpec((block, columns), lambda i, t: (i, 0))


def turn_kernel(t_ref, x_ref, g_ref, v_ref, xo_ref, go_ref, vo_ref, s_ref):
    xo_ref[...] = x_ref[...]
    go_ref[...] = g_ref[...]
    vo_ref[...] = v_ref[...]
    s_ref[...] = jnp.sum(g_ref[...].astype(F32), 0, keepdims=True)


def turn_in(turns, x, g, vectors):
    rows = turns.shape[0]
    part = x.shape[1] // rows

    def specs(array, turned):
        index = (lambda k, t: (0, t[k])) if turned else (lambda k, t: (0, k))
        return pl.BlockSpec((array.shape[0], part), index)

    total_shape = like((1, x.shape[1]), F32)
    return call(
        turn_kernel,
        turns,
        rows,
        [specs(v, True) for v in (x, g, vectors)],
        [specs(v, False) for v in (x, g, vectors)] + [specs(total_shape, True)],
        [like(v.shape, v.dtype) for v in (x, g, vectors)] + [total_shape],
        [x, g, vectors],
    )


def split_kernel(t_ref, w_ref, u_ref, d_ref):
    u_ref[0] = w_ref[:, 0, :]
    d_ref[0] = w_ref[:, 1, :]


def split_mlp(turns, weights, blks):
    depth, _, hidden = weights.shape
    part = hidden // blks
    block = pl.BlockSpec((1, depth, part), lambda b, t: (b, 0, 0))
    return call(
        split_kernel,
        turns,
        blks,
        [pl.BlockSpec((depth, 2, part), lambda b, t: (0, 0, b))],
        [block] * 2,
        [like((blks, depth, part))] * 2,
        [weights],
    )


def join_kernel(t_ref, u_ref, d_ref, o_ref):
    o_ref[:, 0, :] = u_ref[0].astype(F32)
    o_ref[:, 1, :] = d_ref[0].astype(F32)


def join_mlp(turns, up, down):
    blks, depth, part = up.shape
    block = pl.BlockSpec((1, depth, part), lambda b, t: (b, 0, 0))
    return call(
        join_kernel,
        turns,
        blks,
        [block] * 2,
        [pl.BlockSpec((depth, 2, part), lambda b, t: (0, 0, b))],
        [like((depth, 2, blks * part), F32)],
        [up, down],
    )[0]


def split_attn_kernel(t_ref, q_ref, k_ref, v_ref, o_ref, qkv_ref, out_ref):
    for i, ref in enumerate((q_ref, k_ref, v_ref)):
        qkv_ref[0, :, i * HD : (i + 1) * HD] = ref[...]
    out_ref[...] = o_ref[...]


def split_attn(turns, weights, plan, width):
    depth = weights.shape[0]
    heads = width // HD
    part = width // plan.blks

    def head(i):
        def index(b, t):
            h = b % plan.group // plan.share * plan.per_row + b // plan.group
            return 0, i * heads + h

        return pl.BlockSpec((depth, HD), index)

    return call(
        split_attn_kernel,
        turns,
        plan.blks,
        [head(i) for i in range(3)] + [pl.BlockSpec((depth, part), lambda b, t: (0, 3 * plan.blks + b))],
        [
            pl.BlockSpec((1, depth, 3 * HD), lambda b, t: (b, 0, 0)),
            pl.BlockSpec((depth, part), lambda b, t: (0, b)),
        ],
        [like((plan.blks, depth, 3 * HD)), like((depth, width))],
        [weights] * 4,
    )


def join_attn_kernel(columns, t_ref, *refs):
    *parts, out_ref, o_ref = refs
    step = pl.program_id(0)

    @pl.when(step < columns)
    def _():
        o_ref[...] = sum(ref[0].astype(F32) for ref in parts)

    @pl.when(step >= columns)
    def _():
        o_ref[...] = out_ref[...]


def join_attn(turns, qkv, out, plan):
    depth, width = out.shape
    heads = width // HD

    def copy(i):
        def index(j, t):
            at = jnp.minimum(j, 3 * heads - 1)
            h = at % heads
            return h % plan.per_row * plan.group + h // plan.per_row * plan.share + i, 0, at // heads

        return pl.BlockSpec((1, depth, HD), index)

    return call(
        functools.partial(join_attn_kernel, 3 * heads),
        turns,
        4 * heads,
        [copy(i) for i in range(plan.share)]
        + [pl.BlockSpec((depth, HD), lambda j, t: (0, jnp.maximum(j - 3 * heads, 0)))],
        [pl.BlockSpec((depth, HD), lambda j, t: (0, j))],
        [like((depth, 4 * width), F32)],
        [qkv] * plan.share + [out],
    )[0]


def place_kernel(share, t_ref, *refs):
    for k, ref in enumerate(refs[:-1]):

        @pl.when(pl.program_id(0) == k)
        def _(ref=ref):
            for i in range(share):
                refs[-1][i] = ref[...]


def place(turns, pieces, share):
    depth, width = pieces[0].shape
    return call(
        functools.partial(place_kernel, share),
        turns,
        len(pieces),
        [whole(p) for p in pieces],
        [pl.BlockSpec((share, depth, width), lambda k, t: (t[k], 0, 0))],
        [like((len(pieces) * share, depth, width))],
        pieces,
    )[0]


def norm_kernel(t_ref, x_ref, v_ref, a1_ref, a2_ref):
    field = x_ref[...].astype(F32)
    centred = field - jnp.mean(field, -1, keepdims=True)
    standard = centred * lax.rsqrt(jnp.mean(centred * centred, -1, keepdims=True) + EPSILON)
    a1_ref[...] = (standard * v_ref[0:1] + v_ref[1:2]).astype(BF)
    a2_ref[...] = (standard * v_ref[2:3] + v_ref[3:4]).astype(BF)


def norms(turns, x, vectors):
    count, width = x.shape
    return call(
        norm_kernel,
        turns,
        count // BLOCK,
        [rows_block(width), whole(vectors)],
        [rows_block(width)] * 2,
        [like(x.shape)] * 2,
        [x, vectors],
        20 * count * width,
    )


def times_pieces(left, pieces):
    out, start = None, 0
    for piece in pieces:
        depth = piece.shape[0]
        term = dot(left[:, start : start + depth], piece[...], 1, 0)
        out = term if out is None else out + term
        start += depth
    return out


def up_kernel(t_ref, a_ref, b_ref, *refs):
    pieces, (h_ref, s_ref) = refs[:-2], refs[-2:]
    pre = times_pieces(a_ref[...], pieces) + b_ref[...]
    cdf = 0.5 * (1.0 + lax.erf(pre * math.sqrt(0.5)))
    h_ref[...] = (pre * cdf).astype(BF)
    s_ref[...] = cdf + pre * (jnp.exp(-0.5 * pre * pre) * (1.0 / math.sqrt(2.0 * math.pi)))


def feed_up(turns, normed, bias, pieces):
    count, width = normed.shape
    hidden = bias.shape[0]
    return call(
        up_kernel,
        turns,
        count // BLOCK,
        [rows_block(width), pl.BlockSpec((1, hidden), lambda i, t: (0, 0))]
        + [whole(p) for p in pieces],
        [rows_block(hidden)] * 2,
        [like((count, hidden)), like((count, hidden), F32)],
        [normed, bias.reshape(1, hidden)] + pieces,
        2 * count * width * hidden,
    )


def slope_kernel(t_ref, g_ref, s_ref, *refs):
    pieces, (p_ref, sum_ref) = refs[:-2], refs[-2:]

    @pl.when(pl.program_id(0) == 0)
    def _():
        sum_ref[...] = jnp.zeros_like(sum_ref)

    grad = (times_pieces(g_ref[...], pieces) * s_ref[...]).astype(BF)
    p_ref[...] = grad
    sum_ref[...] += jnp.sum(grad.astype(F32), 0, keepdims=True)


def feed_slope(turns, grad, slope, pieces):
    count, width = grad.shape
    hidden = slope.shape[1]
    return call(
        slope_kernel,
        turns,
        count // BLOCK,
        [rows_block(width), rows_block(hidden)] + [whole(p) for p in pieces],
        [rows_block(hidden), pl.BlockSpec((1, hidden), lambda i, t: (0, 0))],
        [like((count, hidden)), like((1, hidden), F32)],
        [grad, slope] + pieces,
        2 * count * width * hidden,
    )


def lane_sum(field):
    return sum(field[:, i : i + LANES] for i in range(0, field.shape[1], LANES))


def weight_kernel(rows, layout, with_sums, t_ref, l_ref, r_ref, *refs):
    step = pl.program_id(0)
    depth = l_ref.shape[1]
    if with_sums:
        sum_ref, pieces, refs = refs[0], refs[1 : 1 + len(layout)], refs[1 + len(layout) :]
        parts_ref = refs[-1]
    grad = dot(l_ref[...], r_ref[...], 0, 0)
    for k in range(rows):

        @pl.when(step == k)
        def _(k=k):
            for i, (start, size) in enumerate(layout):
                if start // depth != k:
                    continue
                at = slice(start - k * depth, start - k * depth + size)
                refs[i][...] = grad[at].astype(BF)
                if with_sums:
                    piece = pieces[i][...].astype(F32)
                    parts_ref[0, at] = lane_sum(piece * grad[at])
                    parts_ref[1, at] = lane_sum(piece * sum_ref[...])


def weight_grad(turns, left, right, sums=None, pieces=()):
    rows = turns.shape[0]
    count, width = left.shape
    columns = right.shape[1]
    depth = width // rows
    layout = parts_of(rows, depth)
    out_shape = [like((size, columns)) for _, size in layout]
    out_specs = [whole(v) for v in out_shape]
    operands = [left, right]
    if pieces:
        operands += [sums] + pieces
        out_shape.append(like((2, width, LANES), F32))
        out_specs.append(pl.BlockSpec((2, depth, LANES), lambda k, t: (0, t[k], 0)))
    out = call(
        functools.partial(weight_kernel, rows, layout, bool(pieces)),
        turns,
        rows,
        [pl.BlockSpec((count, depth), lambda k, t: (0, k))] + [whole(v) for v in operands[1:]],
        out_specs,
        out_shape,
        operands,
        2 * count * width * columns,
    )
    if pieces:
        return out[:-1], jnp.sum(out[-1], -1)
    return out


def out_kernel(t_ref, o_ref, g_ref, w_ref):
    w_ref[...] = dot(o_ref[...], g_ref[...], 0, 0).astype(BF)


def out_grad(turns, attended, grad):
    rows = turns.shape[0]
    count, width = grad.shape
    part = width // rows
    return call(
        out_kernel,
        turns,
        rows,
        [whole(attended), pl.BlockSpec((count, part), lambda k, t: (0, k))],
        [pl.BlockSpec((HD, part), lambda k, t: (0, t[k]))],
        [like((HD, width))],
        [attended, grad],
        2 * count * width * HD,
    )[0]


def turned_columns(t_ref, w_ref, start, size, depth):
    at = t_ref[start // depth] * depth + start % depth
    return w_ref[:, pl.ds(pl.multiple_of(at, LANES), size)]


def sum_kernel(layout, depth, t_ref, h_ref, o_ref, w_ref, *refs):
    pieces, y_ref = refs[:-1], refs[-1]
    for piece, (start, size) in zip(pieces, layout):
        term = dot(h_ref[...], piece[...], 1, 1)
        term += dot(o_ref[...], turned_columns(t_ref, w_ref, start, size, depth), 1, 0)
        y_ref[:, start : start + size] = term.astype(BF)


def out_sum(turns, hidden, pieces, attended, out_w):
    rows = turns.shape[0]
    count = hidden.shape[0]
    width = out_w.shape[1]
    return call(
        functools.partial(sum_kernel, parts_of(rows, width // rows), width // rows),
        turns,
        count // BLOCK,
        [rows_block(hidden.shape[1]), rows_block(HD), whole(out_w)] + [whole(p) for p in pieces],
        [rows_block(width)],
        [like((count, width))],
        [hidden, attended, out_w] + pieces,
        2 * count * width * (hidden.shape[1] + HD),
    )[0]


def back_kernel(layout, t_ref, p_ref, q_ref, v_ref, *refs):
    pieces, c_ref = refs[:-1], refs[-1]
    count = len(layout)
    for up, qkv, (start, size) in zip(pieces[:count], pieces[count:], layout):
        cols = slice(start, start + size)
        term = dot(p_ref[...], up[...], 1, 1) * v_ref[2:3, cols]
        term += dot(q_ref[...], qkv[...], 1, 1) * v_ref[0:1, cols]
        c_ref[:, cols] = term.astype(BF)


def norm_back(turns, pre_grad, up_pieces, qkv_grad, qkv_pieces, vectors):
    rows = turns.shape[0]
    count = pre_grad.shape[0]
    width = vectors.shape[1]
    columns = pre_grad.shape[1] + qkv_grad.shape[1]
    return call(
        functools.partial(back_kernel, parts_of(rows, width // rows)),
        turns,
        count // BLOCK,
        [rows_block(pre_grad.shape[1]), rows_block(qkv_grad.shape[1]), whole(vectors)]
        + [whole(p) for p in up_pieces + qkv_pieces],
        [rows_block(width)],
        [like((count, width))],
        [pre_grad, qkv_grad, vectors] + up_pieces + qkv_pieces,
        2 * count * width * columns,
    )[0]


def turned(field, cosine, minus, plus):
    head = field[:, :LANES]
    half = ROT // 2
    head = (
        head * cosine
        + pltpu.roll(head, LANES - half, 1) * minus
        + pltpu.roll(head, half, 1) * plus
    )
    return jnp.concatenate([head, field[:, LANES:]], 1)


def allowed_pairs(length, dq_ref, dk_ref):
    spot = lax.broadcasted_iota(jnp.int32, (length, length), 0)
    other = lax.broadcasted_iota(jnp.int32, (length, length), 1)
    return (dq_ref[0] == dk_ref[0]) & (other <= spot)


def forward_kernel(t_ref, a_ref, b_ref, c_ref, m_ref, p_ref, dq_ref, dk_ref, *refs):
    pieces, (qkv_ref, o_ref, lse_ref) = refs[:-3], refs[-3:]
    qkv = times_pieces(a_ref[...], pieces) + b_ref[...]
    tables = c_ref[0], m_ref[0], p_ref[0]
    queries = (turned(qkv[:, :HD], *tables) * HD ** (-0.5)).astype(BF)
    keys = turned(qkv[:, HD : 2 * HD], *tables).astype(BF)
    values = qkv[:, 2 * HD :].astype(BF)
    for i, field in enumerate((queries, keys, values)):
        qkv_ref[:, i * HD : (i + 1) * HD] = field
    allowed = allowed_pairs(a_ref.shape[0], dq_ref, dk_ref)
    scores = jnp.where(allowed, dot(queries, keys, 1, 1), MASKED)
    largest = jnp.max(scores, -1, keepdims=True)
    weights = jnp.where(allowed, jnp.exp(scores - largest), 0.0)
    mass = jnp.sum(weights, -1, keepdims=True)
    o_ref[...] = dot((weights / mass).astype(BF), values, 1, 0).astype(BF)
    lse_ref[...] = largest + jnp.log(mass)


def backward_kernel(
    parts, t_ref, g_ref, w_ref, qkv_ref, o_ref, lse_ref, c_ref, m_ref, p_ref, dq_ref, dk_ref,
    grad_ref, sum_ref,
):
    queries, keys, values = (qkv_ref[:, i * HD : (i + 1) * HD] for i in range(3))
    tables = c_ref[0], -m_ref[0], -p_ref[0]
    depth = w_ref.shape[1] // parts
    heads_grad = None
    for k in range(parts):
        cols = slice(k * depth, (k + 1) * depth)
        term = dot(g_ref[:, cols], turned_columns(t_ref, w_ref, k * depth, depth, depth), 1, 1)
        heads_grad = term if heads_grad is None else heads_grad + term
    heads_grad = heads_grad.astype(BF)
    allowed = allowed_pairs(g_ref.shape[0], dq_ref, dk_ref)
    scores = jnp.where(allowed, dot(queries, keys, 1, 1), MASKED)
    weights = jnp.where(allowed, jnp.exp(scores - lse_ref[...]), 0.0)
    deltas = jnp.sum(heads_grad.astype(F32) * o_ref[...].astype(F32), -1, keepdims=True)
    score_grad = (weights * (dot(heads_grad, values, 1, 1) - deltas)).astype(BF)
    query_grad = dot(score_grad, keys, 1, 0) * HD ** (-0.5)
    key_grad = dot(score_grad, queries, 0, 0)
    value_grad = dot(weights.astype(BF), heads_grad, 0, 0)
    fields = turned(query_grad, *tables), turned(key_grad, *tables), value_grad

    @pl.when(pl.program_id(0) == 0)
    def _():
        sum_ref[...] = jnp.zeros_like(sum_ref)

    for i, field in enumerate(fields):
        field = field.astype(BF)
        cols = slice(i * HD, (i + 1) * HD)
        grad_ref[:, cols] = field
        sum_ref[:, cols] += jnp.sum(field.astype(F32), 0, keepdims=True)


def pair_specs(length):
    table = pl.BlockSpec((1, length, LANES), lambda r, t: (r, 0, 0))
    return [table] * 3 + [
        pl.BlockSpec((1, length, 1), lambda r, t: (r, 0, 0)),
        pl.BlockSpec((1, 1, length), lambda r, t: (r, 0, 0)),
    ]


def head_forward(turns, normed, bias, pairs, pieces, length):
    count, width = normed.shape
    columns = 3 * HD
    return call(
        forward_kernel,
        turns,
        count // length,
        [rows_block(width, length), pl.BlockSpec((1, columns), lambda r, t: (0, 0))]
        + pair_specs(length)
        + [whole(p) for p in pieces],
        [rows_block(columns, length), rows_block(HD, length), rows_block(1, length)],
        [like((count, columns)), like((count, HD)), like((count, 1), F32)],
        [normed, bias.reshape(1, columns)] + pairs + pieces,
        2 * count * (width * columns + 2 * length * HD),
    )


def head_backward(turns, grad, out_w, qkv, attended, lse, pairs, length):
    count, width = grad.shape
    columns = 3 * HD
    return call(
        functools.partial(backward_kernel, turns.shape[0]),
        turns,
        count // length,
        [
            rows_block(width, length),
            whole(out_w),
            rows_block(columns, length),
            rows_block(HD, length),
            rows_block(1, length),
        ]
        + pair_specs(length),
        [rows_block(columns, length), pl.BlockSpec((1, columns), lambda r, t: (0, 0))],
        [like((count, columns)), like((1, columns), F32)],
        [grad, out_w, qkv, attended, lse] + pairs,
        2 * count * (width * HD + 5 * length * HD),
    )


def finish_kernel(rows, with_norm, t_ref, x_ref, s_ref, o_ref, out_ref):
    depth = x_ref.shape[1] // rows
    term = s_ref[...].astype(F32)
    if with_norm:
        centred = x_ref[...].astype(F32)
        centred = centred - jnp.mean(centred, -1, keepdims=True)
        rstd = lax.rsqrt(jnp.mean(centred * centred, -1, keepdims=True) + EPSILON)
        centred = centred * rstd
        term = term - jnp.mean(term, -1, keepdims=True) - centred * jnp.mean(
            term * centred, -1, keepdims=True
        )
        field = o_ref[...].astype(F32) + rstd * term
    else:
        field = x_ref[...].astype(F32) + term + o_ref[4:5]
    for k in range(rows):
        at = pl.multiple_of(t_ref[k] * depth, LANES)
        out_ref[:, pl.ds(at, depth)] = field[:, k * depth : (k + 1) * depth].astype(BF)


def finish(turns, x, term, other, with_norm):
    return call(
        functools.partial(finish_kernel, turns.shape[0], with_norm),
        turns,
        1,
        [whole(v) for v in (x, term, other)],
        [whole(x)],
        [like(x.shape)],
        [x, term, other],
    )[0]


def shards(
    plan,
    tokens,
    attn_weights,
    mlp_weights,
    ln1_gain,
    ln1_bias,
    ln2_gain,
    ln2_bias,
    qkv_bias,
    dense_bias,
    up_bias,
    down_bias,
    doc_lengths,
    cotangent,
):
    row_count, shard_len, width = tokens.shape
    depth = attn_weights.shape[0]
    heads = width // HD
    rows, blks = plan.rows, plan.blks
    own_hidden = mlp_weights.shape[-1] // blks
    me = lax.axis_index("blk")
    length = shard_len * blks
    count = row_count * length
    head_of = me % plan.group // plan.share * plan.per_row + me // plan.group
    part = me % plan.share
    own_rows = row_count // plan.share
    turns = lax.axis_index("row") ^ jnp.arange(rows, dtype=jnp.int32)

    def exchange(field, groups=None):
        return lax.all_to_all(field, "blk", 0, 0, axis_index_groups=groups)

    def collect(field):
        return exchange(field.reshape(blks, -1, field.shape[-1]))

    def gather_blocks(field):
        field = field.reshape(row_count, shard_len, width)
        return lax.all_gather(field, "blk", axis=1, tiled=True).reshape(count, width)

    def sum_blocks(field):
        field = field.reshape(row_count, length, width)
        field = lax.psum_scatter(field, "blk", scatter_dimension=1, tiled=True)
        return field.reshape(row_count * shard_len, width)

    qkv_send, out_own = split_attn(turns, attn_weights, plan, width)
    out_rows = place(
        turns, [out_own] + [swap(out_own, "row", rows, k) for k in range(1, rows)], plan.share
    )
    up_send, down_send = split_mlp(turns, mlp_weights, blks)
    zeros = jnp.zeros((3, width), F32)
    vectors = jnp.stack([ln1_gain, ln1_bias, ln2_gain, ln2_bias, dense_bias + down_bias])
    x_own, g_own, vectors, g_sum = turn_in(
        turns,
        tokens.reshape(row_count * shard_len, width),
        cotangent.reshape(row_count * shard_len, width),
        jnp.concatenate([vectors, zeros]),
    )
    qkv_mine = exchange(qkv_send)
    qkv_gather = Gather(qkv_mine.reshape(-1, 3 * HD), plan)
    up_mine = exchange(after(up_send, qkv_mine))
    up_gather = Gather(up_mine.reshape(-1, own_hidden), plan)
    down_mine = exchange(after(down_send, up_mine, *qkv_gather.first()))
    down_gather = Gather(down_mine.reshape(-1, own_hidden), plan)
    x_all = gather_blocks(after(x_own, down_mine))
    qkv_pieces = qkv_gather.finish()
    out_w = exchange(after(out_rows, down_mine, *up_gather.first(), qkv_pieces[-1]), plan.groups)
    out_w = out_w.reshape(HD, width)
    g_all = gather_blocks(after(g_own, out_w))
    up_pieces = up_gather.finish()

    lengths = lax.dynamic_slice_in_dim(doc_lengths, part * own_rows, own_rows, 0)
    doc_ends = jnp.cumsum(lengths, axis=-1)
    starts = doc_ends - lengths
    places = jnp.arange(length, dtype=jnp.int32)
    doc_ids = jnp.sum((places[None, :, None] >= doc_ends[:, None, :]).astype(jnp.int32), -1)
    picked = doc_ids[:, :, None] == jnp.arange(lengths.shape[-1], dtype=jnp.int32)
    positions = places - jnp.sum(jnp.where(picked, starts[:, None, :], 0), -1)
    lane = jnp.arange(LANES)
    inverse = 10000.0 ** (-2.0 * (lane % (ROT // 2)).astype(F32) / ROT)
    angles = positions.astype(F32)[..., None] * inverse
    sine = jnp.sin(angles)
    pairs = [
        jnp.where(lane < ROT, jnp.cos(angles), 1.0),
        jnp.where(lane < ROT // 2, -sine, 0.0),
        jnp.where((lane >= ROT // 2) & (lane < ROT), sine, 0.0),
        doc_ids[:, :, None],
        doc_ids[:, None, :],
    ]

    def own(field):
        if plan.share == 1:
            return field
        return lax.dynamic_slice_in_dim(field, part * own_rows * length, own_rows * length, 0)

    def spread(field):
        if plan.share == 1:
            return field
        blank = jnp.zeros((count, field.shape[1]), field.dtype)
        return lax.dynamic_update_slice_in_dim(blank, field, part * own_rows * length, 0)

    normed1, normed2 = norms(turns, x_all, vectors)
    up_b = lax.dynamic_slice_in_dim(up_bias, me * own_hidden, own_hidden)
    qkv_b = lax.dynamic_index_in_dim(qkv_bias.reshape(3, heads, HD), head_of, 1, keepdims=False)
    hidden, slope = feed_up(turns, normed2, up_b, up_pieces)
    own_normed1 = own(after(normed1, hidden))
    qkv, attended, lse = head_forward(
        turns, own_normed1, qkv_b.reshape(-1), pairs, qkv_pieces, length
    )
    down_pieces = down_gather.finish()
    out_term = out_sum(turns, hidden, down_pieces, spread(attended), out_w)
    out_total = sum_blocks(out_term)

    g_all = after(g_all, out_term)
    down_g = weight_grad(turns, g_all, hidden)
    down_scatter = Scatter(down_g, plan)
    pre_grad, up_sum = feed_slope(turns, after(g_all, down_g[0]), slope, down_pieces)
    own_grad = own(after(g_all, pre_grad))
    qkv_grad, qkv_sum = head_backward(
        turns, own_grad, out_w, qkv, attended, lse, pairs, length
    )
    norm_term = norm_back(
        turns,
        after(pre_grad, qkv_grad, *down_scatter.first()),
        up_pieces,
        spread(qkv_grad),
        qkv_pieces,
        vectors,
    )
    norm_total = sum_blocks(norm_term)
    down_back = collect(down_scatter.finish())
    up_g, up_parts = weight_grad(
        turns, after(normed2, norm_term), pre_grad, up_sum, up_pieces
    )
    up_scatter = Scatter(up_g, plan)
    qkv_g, qkv_parts = weight_grad(
        turns, after(own_normed1, up_g[0]), qkv_grad, qkv_sum, qkv_pieces
    )
    qkv_scatter = Scatter(qkv_g, plan)
    out_g = out_grad(turns, after(attended, qkv_g[0]), own_grad)
    out_back = exchange(after(out_g, down_back).reshape(plan.group, depth, width), plan.groups)
    out_back = out_back.reshape(rows, plan.share, depth, width)
    if plan.share > 1:
        out_back = jnp.sum(out_back.astype(F32), 1, keepdims=True).astype(BF)
    out_back = out_back[:, 0]
    out_back = [lax.dynamic_index_in_dim(out_back, turns[k], 0, False) for k in range(rows)]
    out_back = out_back[0].astype(F32) + sum(
        swap(out_back[k], "row", rows, k).astype(F32) for k in range(1, rows)
    )
    up_total = up_scatter.finish(down_back)
    up_back = collect(up_total)
    qkv_back = collect(after(qkv_scatter.finish(up_total), up_back))

    qkv_slot = jnp.zeros((3, heads, HD), F32)
    qkv_slot = lax.dynamic_update_slice_in_dim(qkv_slot, qkv_sum.reshape(3, 1, HD), head_of, 1)
    up_slot = jnp.zeros((blks, own_hidden), F32)
    up_slot = lax.dynamic_update_slice_in_dim(up_slot, up_sum, me, 0)
    terms = [qkv_parts, up_parts, g_sum, qkv_slot, up_slot]
    sizes = [width] * 5 + [3 * width, mlp_weights.shape[-1]]
    sums = total(jnp.concatenate([v.reshape(-1) for v in terms]), plan)
    gain1, bias1, gain2, bias2, g_total, qkv_total, up_bias_grad = jnp.split(
        sums, np.cumsum(sizes)[:-1]
    )

    layer_out = finish(turns, x_own, out_total, vectors, False)
    tokens_grad = finish(turns, x_own, norm_total, g_own, True)
    return (
        layer_out.reshape(tokens.shape),
        tokens_grad.reshape(tokens.shape),
        join_attn(turns, qkv_back, out_back, plan),
        join_mlp(turns, up_back, down_back),
        (gain1 - ln1_bias * bias1) / ln1_gain,
        bias1,
        (gain2 - ln2_bias * bias2) / ln2_gain,
        bias2,
        qkv_total,
        g_total,
        up_bias_grad,
        g_total,
    )


def solution(mesh):
    rows, blks = mesh.shape["row"], mesh.shape["blk"]
    vector = P()
    tokens = P("row", "blk", None)
    attn = P(("row", "blk"), None)
    mlp = P(("row", "blk"), None, None)

    def run(*arrays):
        plan = Plan(rows, blks, arrays[0].shape[-1] // HD)
        return jax.shard_map(
            functools.partial(shards, plan),
            mesh=mesh,
            in_specs=(tokens, attn, mlp) + (vector,) * 8 + (P("row", None), tokens),
            out_specs=(tokens, tokens, attn, mlp) + (vector,) * 8,
            check_vma=False,
        )(*arrays)

    return run
```

```python
import functools
import math

import jax
import jax.numpy as jnp
import numpy as np
from jax import lax
from jax.experimental import pallas as pl
from jax.experimental.pallas import tpu as pltpu
from jax.sharding import PartitionSpec as P

HD = 256
ROT = 64
LANES = 128
BLOCK = 256
EPSILON = 1e-05
MASKED = -1e30
BF = jnp.bfloat16
F32 = jnp.float32
VMEM_LIMIT = 48 * 2**20


class Plan:
    def __init__(self, rows, blks, heads):
        self.rows = rows
        self.blks = blks
        self.share = blks // heads
        self.per_row = heads // rows
        self.group = blks // self.per_row
        self.groups = [
            list(range(i * self.group, (i + 1) * self.group)) for i in range(self.per_row)
        ]


def after(field, *others):
    return lax.optimization_barrier((field,) + others)[0] if others else field


def swap(field, axis, size, bit):
    return lax.ppermute(field, axis, [(i, i ^ bit) for i in range(size)])


def bits_of(size):
    return [1 << i for i in range(size.bit_length() - 1)]


def total(field, plan):
    for axis, size in (("row", plan.rows), ("blk", plan.blks)):
        for bit in bits_of(size):
            field = field + swap(field, axis, size, bit)
    return field


def near(k):
    return k & (k - 1) == 0


def orders(plan):
    bits = bits_of(plan.rows)
    return bits, bits[::-1]


def half_of(field, h):
    middle = field.shape[0] // 2
    return field[h * middle : (h + 1) * middle]


def parts_of(rows, depth):
    out = []
    for k in range(rows):
        if near(k):
            out.append((k * depth, depth))
        else:
            out += [(k * depth, depth // 2), (k * depth + depth // 2, depth // 2)]
    return out


class Gather:
    def __init__(self, own, plan):
        self.plan = plan
        self.whole = {0: own}
        for bit in bits_of(plan.rows):
            self.whole[bit] = swap(own, "row", plan.rows, bit)

    def first(self):
        return [v for k, v in self.whole.items() if k]

    def finish(self, *others):
        plan = self.plan
        halves = []
        for h, order in enumerate(orders(plan)):
            got = {0: None}
            for bit in order:
                for k in list(got):
                    if k == 0:
                        got[bit] = half_of(after(self.whole[bit], *others), h)
                    else:
                        got[k ^ bit] = swap(got[k], "row", plan.rows, bit)
            halves.append(got)
        out = []
        for k in range(plan.rows):
            out += [self.whole[k]] if near(k) else [half[k] for half in halves]
        return out


class Scatter:
    def __init__(self, pieces, plan):
        self.plan = plan
        pieces = iter(pieces)
        self.whole, far = {}, [{}, {}]
        for k in range(plan.rows):
            if near(k):
                self.whole[k] = next(pieces)
            else:
                far[0][k], far[1][k] = next(pieces), next(pieces)
        self.got = []
        for h, order in enumerate(orders(plan)):
            held = far[h]
            for bit in order:
                for k in [k for k in held if k & bit]:
                    term = swap(held.pop(k), "row", plan.rows, bit)
                    if near(k ^ bit):
                        self.got.append((k ^ bit, h, term))
                    else:
                        held[k ^ bit] = (held[k ^ bit].astype(F32) + term.astype(F32)).astype(BF)

    def first(self):
        return [term for _, _, term in self.got]

    def finish(self, *others):
        whole = dict(self.whole)
        for k, h, term in self.got:
            middle = whole[k].shape[0] // 2
            both = half_of(whole[k], h).astype(F32) + term.astype(F32)
            whole[k] = lax.dynamic_update_slice(whole[k], both.astype(BF), (h * middle, 0))
        out = whole[0].astype(F32)
        for bit in bits_of(self.plan.rows):
            field = after(whole[bit], *others)
            out = out + swap(field, "row", self.plan.rows, bit).astype(F32)
        return out.astype(BF)


def dot(left, right, left_dim, right_dim):
    return lax.dot_general(
        left, right, (((left_dim,), (right_dim,)), ((), ())), preferred_element_type=F32
    )


def whole(array):
    return pl.BlockSpec(array.shape, lambda *i: (0,) * len(array.shape))


def like(shape, kind=BF):
    return jax.ShapeDtypeStruct(shape, kind)


def call(body, turns, grid, in_specs, out_specs, out_shape, operands, flops=0):
    moved = sum(v.size * v.dtype.itemsize for v in operands)
    moved += sum(math.prod(v.shape) * jnp.dtype(v.dtype).itemsize for v in out_shape)
    return pl.pallas_call(
        body,
        grid_spec=pltpu.PrefetchScalarGridSpec(
            num_scalar_prefetch=1, grid=(grid,), in_specs=in_specs, out_specs=out_specs
        ),
        out_shape=out_shape,
        compiler_params=pltpu.CompilerParams(vmem_limit_bytes=VMEM_LIMIT),
        cost_estimate=pl.CostEstimate(flops=flops, bytes_accessed=moved, transcendentals=0),
    )(turns, *operands)


def rows_block(columns, block=BLOCK):
    return pl.BlockSpec((block, columns), lambda i, t: (i, 0))


def turn_kernel(t_ref, x_ref, g_ref, v_ref, xo_ref, go_ref, vo_ref, s_ref):
    xo_ref[...] = x_ref[...]
    go_ref[...] = g_ref[...]
    vo_ref[...] = v_ref[...]
    s_ref[...] = jnp.sum(g_ref[...].astype(F32), 0, keepdims=True)


def turn_in(turns, x, g, vectors):
    rows = turns.shape[0]
    part = x.shape[1] // rows

    def specs(array, turned):
        index = (lambda k, t: (0, t[k])) if turned else (lambda k, t: (0, k))
        return pl.BlockSpec((array.shape[0], part), index)

    total_shape = like((1, x.shape[1]), F32)
    return call(
        turn_kernel,
        turns,
        rows,
        [specs(v, True) for v in (x, g, vectors)],
        [specs(v, False) for v in (x, g, vectors)] + [specs(total_shape, True)],
        [like(v.shape, v.dtype) for v in (x, g, vectors)] + [total_shape],
        [x, g, vectors],
    )


def split_kernel(t_ref, w_ref, u_ref, d_ref):
    u_ref[0] = w_ref[:, 0, :]
    d_ref[0] = w_ref[:, 1, :]


def split_mlp(turns, weights, blks):
    depth, _, hidden = weights.shape
    part = hidden // blks
    block = pl.BlockSpec((1, depth, part), lambda b, t: (b, 0, 0))
    return call(
        split_kernel,
        turns,
        blks,
        [pl.BlockSpec((depth, 2, part), lambda b, t: (0, 0, b))],
        [block] * 2,
        [like((blks, depth, part))] * 2,
        [weights],
    )


def join_kernel(t_ref, u_ref, d_ref, o_ref):
    o_ref[:, 0, :] = u_ref[0].astype(F32)
    o_ref[:, 1, :] = d_ref[0].astype(F32)


def join_mlp(turns, up, down):
    blks, depth, part = up.shape
    block = pl.BlockSpec((1, depth, part), lambda b, t: (b, 0, 0))
    return call(
        join_kernel,
        turns,
        blks,
        [block] * 2,
        [pl.BlockSpec((depth, 2, part), lambda b, t: (0, 0, b))],
        [like((depth, 2, blks * part), F32)],
        [up, down],
    )[0]


def split_attn_kernel(t_ref, q_ref, k_ref, v_ref, o_ref, qkv_ref, out_ref):
    for i, ref in enumerate((q_ref, k_ref, v_ref)):
        qkv_ref[0, :, i * HD : (i + 1) * HD] = ref[...]
    out_ref[...] = o_ref[...]


def split_attn(turns, weights, plan, width):
    depth = weights.shape[0]
    heads = width // HD
    part = width // plan.blks

    def head(i):
        def index(b, t):
            h = b % plan.group // plan.share * plan.per_row + b // plan.group
            return 0, i * heads + h

        return pl.BlockSpec((depth, HD), index)

    return call(
        split_attn_kernel,
        turns,
        plan.blks,
        [head(i) for i in range(3)] + [pl.BlockSpec((depth, part), lambda b, t: (0, 3 * plan.blks + b))],
        [
            pl.BlockSpec((1, depth, 3 * HD), lambda b, t: (b, 0, 0)),
            pl.BlockSpec((depth, part), lambda b, t: (0, b)),
        ],
        [like((plan.blks, depth, 3 * HD)), like((depth, width))],
        [weights] * 4,
    )


def join_attn_kernel(plan, t_ref, qkv_ref, out_ref, o_ref):
    step = pl.program_id(0)
    heads = o_ref.shape[1] // HD

    @pl.when(step < 3)
    def _():
        at = pl.ds(pl.multiple_of(step * HD, HD), HD)
        for h in range(heads):
            first = h % plan.per_row * plan.group + h // plan.per_row * plan.share
            o_ref[:, h * HD : (h + 1) * HD] = sum(
                qkv_ref[first + i, :, at].astype(F32) for i in range(plan.share)
            )

    @pl.when(step == 3)
    def _():
        o_ref[...] = out_ref[...]


def join_attn(turns, qkv, out, plan):
    depth, width = out.shape
    return call(
        functools.partial(join_attn_kernel, plan),
        turns,
        4,
        [whole(qkv), whole(out)],
        [pl.BlockSpec((depth, width), lambda j, t: (0, j))],
        [like((depth, 4 * width), F32)],
        [qkv, out],
    )[0]


def place_kernel(share, t_ref, *refs):
    for k, ref in enumerate(refs[:-1]):

        @pl.when(pl.program_id(0) == k)
        def _(ref=ref):
            for i in range(share):
                refs[-1][i] = ref[...]


def place(turns, pieces, share):
    depth, width = pieces[0].shape
    return call(
        functools.partial(place_kernel, share),
        turns,
        len(pieces),
        [whole(p) for p in pieces],
        [pl.BlockSpec((share, depth, width), lambda k, t: (t[k], 0, 0))],
        [like((len(pieces) * share, depth, width))],
        pieces,
    )[0]


def norm_kernel(t_ref, x_ref, v_ref, a1_ref, a2_ref):
    field = x_ref[...].astype(F32)
    centred = field - jnp.mean(field, -1, keepdims=True)
    standard = centred * lax.rsqrt(jnp.mean(centred * centred, -1, keepdims=True) + EPSILON)
    a1_ref[...] = (standard * v_ref[0:1] + v_ref[1:2]).astype(BF)
    a2_ref[...] = (standard * v_ref[2:3] + v_ref[3:4]).astype(BF)


def norms(turns, x, vectors):
    count, width = x.shape
    return call(
        norm_kernel,
        turns,
        count // BLOCK,
        [rows_block(width), whole(vectors)],
        [rows_block(width)] * 2,
        [like(x.shape)] * 2,
        [x, vectors],
        20 * count * width,
    )


def times_pieces(left, pieces):
    out, start = None, 0
    for piece in pieces:
        depth = piece.shape[0]
        term = dot(left[:, start : start + depth], piece[...], 1, 0)
        out = term if out is None else out + term
        start += depth
    return out


def up_kernel(t_ref, a_ref, b_ref, *refs):
    pieces, (h_ref, s_ref) = refs[:-2], refs[-2:]
    pre = times_pieces(a_ref[...], pieces) + b_ref[...]
    cdf = 0.5 * (1.0 + lax.erf(pre * math.sqrt(0.5)))
    h_ref[...] = (pre * cdf).astype(BF)
    s_ref[...] = cdf + pre * (jnp.exp(-0.5 * pre * pre) * (1.0 / math.sqrt(2.0 * math.pi)))


def feed_up(turns, normed, bias, pieces):
    count, width = normed.shape
    hidden = bias.shape[0]
    return call(
        up_kernel,
        turns,
        count // BLOCK,
        [rows_block(width), pl.BlockSpec((1, hidden), lambda i, t: (0, 0))]
        + [whole(p) for p in pieces],
        [rows_block(hidden)] * 2,
        [like((count, hidden)), like((count, hidden), F32)],
        [normed, bias.reshape(1, hidden)] + pieces,
        2 * count * width * hidden,
    )


def slope_kernel(t_ref, g_ref, s_ref, *refs):
    pieces, (p_ref, sum_ref) = refs[:-2], refs[-2:]

    @pl.when(pl.program_id(0) == 0)
    def _():
        sum_ref[...] = jnp.zeros_like(sum_ref)

    grad = (times_pieces(g_ref[...], pieces) * s_ref[...]).astype(BF)
    p_ref[...] = grad
    sum_ref[...] += jnp.sum(grad.astype(F32), 0, keepdims=True)


def feed_slope(turns, grad, slope, pieces):
    count, width = grad.shape
    hidden = slope.shape[1]
    return call(
        slope_kernel,
        turns,
        count // BLOCK,
        [rows_block(width), rows_block(hidden)] + [whole(p) for p in pieces],
        [rows_block(hidden), pl.BlockSpec((1, hidden), lambda i, t: (0, 0))],
        [like((count, hidden)), like((1, hidden), F32)],
        [grad, slope] + pieces,
        2 * count * width * hidden,
    )


def lane_sum(field):
    return sum(field[:, i : i + LANES] for i in range(0, field.shape[1], LANES))


def weight_kernel(rows, layout, with_sums, t_ref, l_ref, r_ref, *refs):
    step = pl.program_id(0)
    depth = l_ref.shape[1]
    if with_sums:
        sum_ref, pieces, refs = refs[0], refs[1 : 1 + len(layout)], refs[1 + len(layout) :]
        parts_ref = refs[-1]
    grad = dot(l_ref[...], r_ref[...], 0, 0)
    for k in range(rows):

        @pl.when(step == k)
        def _(k=k):
            for i, (start, size) in enumerate(layout):
                if start // depth != k:
                    continue
                at = slice(start - k * depth, start - k * depth + size)
                refs[i][...] = grad[at].astype(BF)
                if with_sums:
                    piece = pieces[i][...].astype(F32)
                    parts_ref[0, at] = lane_sum(piece * grad[at])
                    parts_ref[1, at] = lane_sum(piece * sum_ref[...])


def weight_grad(turns, left, right, sums=None, pieces=()):
    rows = turns.shape[0]
    count, width = left.shape
    columns = right.shape[1]
    depth = width // rows
    layout = parts_of(rows, depth)
    out_shape = [like((size, columns)) for _, size in layout]
    out_specs = [whole(v) for v in out_shape]
    operands = [left, right]
    if pieces:
        operands += [sums] + pieces
        out_shape.append(like((2, width, LANES), F32))
        out_specs.append(pl.BlockSpec((2, depth, LANES), lambda k, t: (0, t[k], 0)))
    out = call(
        functools.partial(weight_kernel, rows, layout, bool(pieces)),
        turns,
        rows,
        [pl.BlockSpec((count, depth), lambda k, t: (0, k))] + [whole(v) for v in operands[1:]],
        out_specs,
        out_shape,
        operands,
        2 * count * width * columns,
    )
    if pieces:
        return out[:-1], jnp.sum(out[-1], -1)
    return out


def out_kernel(t_ref, o_ref, g_ref, w_ref):
    w_ref[...] = dot(o_ref[...], g_ref[...], 0, 0).astype(BF)


def out_grad(turns, attended, grad):
    rows = turns.shape[0]
    count, width = grad.shape
    part = width // rows
    return call(
        out_kernel,
        turns,
        rows,
        [whole(attended), pl.BlockSpec((count, part), lambda k, t: (0, k))],
        [pl.BlockSpec((HD, part), lambda k, t: (0, t[k]))],
        [like((HD, width))],
        [attended, grad],
        2 * count * width * HD,
    )[0]


def turned_columns(t_ref, w_ref, start, size, depth):
    at = t_ref[start // depth] * depth + start % depth
    return w_ref[:, pl.ds(pl.multiple_of(at, LANES), size)]


def sum_kernel(layout, depth, t_ref, h_ref, o_ref, w_ref, *refs):
    pieces, y_ref = refs[:-1], refs[-1]
    for piece, (start, size) in zip(pieces, layout):
        term = dot(h_ref[...], piece[...], 1, 1)
        term += dot(o_ref[...], turned_columns(t_ref, w_ref, start, size, depth), 1, 0)
        y_ref[:, start : start + size] = term.astype(BF)


def out_sum(turns, hidden, pieces, attended, out_w):
    rows = turns.shape[0]
    count = hidden.shape[0]
    width = out_w.shape[1]
    return call(
        functools.partial(sum_kernel, parts_of(rows, width // rows), width // rows),
        turns,
        count // BLOCK,
        [rows_block(hidden.shape[1]), rows_block(HD), whole(out_w)] + [whole(p) for p in pieces],
        [rows_block(width)],
        [like((count, width))],
        [hidden, attended, out_w] + pieces,
        2 * count * width * (hidden.shape[1] + HD),
    )[0]


def back_kernel(layout, t_ref, p_ref, q_ref, v_ref, *refs):
    pieces, c_ref = refs[:-1], refs[-1]
    count = len(layout)
    for up, qkv, (start, size) in zip(pieces[:count], pieces[count:], layout):
        cols = slice(start, start + size)
        term = dot(p_ref[...], up[...], 1, 1) * v_ref[2:3, cols]
        term += dot(q_ref[...], qkv[...], 1, 1) * v_ref[0:1, cols]
        c_ref[:, cols] = term.astype(BF)


def norm_back(turns, pre_grad, up_pieces, qkv_grad, qkv_pieces, vectors):
    rows = turns.shape[0]
    count = pre_grad.shape[0]
    width = vectors.shape[1]
    columns = pre_grad.shape[1] + qkv_grad.shape[1]
    return call(
        functools.partial(back_kernel, parts_of(rows, width // rows)),
        turns,
        count // BLOCK,
        [rows_block(pre_grad.shape[1]), rows_block(qkv_grad.shape[1]), whole(vectors)]
        + [whole(p) for p in up_pieces + qkv_pieces],
        [rows_block(width)],
        [like((count, width))],
        [pre_grad, qkv_grad, vectors] + up_pieces + qkv_pieces,
        2 * count * width * columns,
    )[0]


def turned(field, cosine, minus, plus):
    head = field[:, :LANES]
    half = ROT // 2
    head = (
        head * cosine
        + pltpu.roll(head, LANES - half, 1) * minus
        + pltpu.roll(head, half, 1) * plus
    )
    return jnp.concatenate([head, field[:, LANES:]], 1)


def allowed_pairs(length, dq_ref, dk_ref):
    spot = lax.broadcasted_iota(jnp.int32, (length, length), 0)
    other = lax.broadcasted_iota(jnp.int32, (length, length), 1)
    return (dq_ref[0] == dk_ref[0]) & (other <= spot)


def forward_kernel(t_ref, a_ref, b_ref, c_ref, m_ref, p_ref, dq_ref, dk_ref, *refs):
    pieces, (qkv_ref, o_ref, lse_ref) = refs[:-3], refs[-3:]
    qkv = times_pieces(a_ref[...], pieces) + b_ref[...]
    tables = c_ref[0], m_ref[0], p_ref[0]
    queries = (turned(qkv[:, :HD], *tables) * HD ** (-0.5)).astype(BF)
    keys = turned(qkv[:, HD : 2 * HD], *tables).astype(BF)
    values = qkv[:, 2 * HD :].astype(BF)
    for i, field in enumerate((queries, keys, values)):
        qkv_ref[:, i * HD : (i + 1) * HD] = field
    allowed = allowed_pairs(a_ref.shape[0], dq_ref, dk_ref)
    scores = jnp.where(allowed, dot(queries, keys, 1, 1), MASKED)
    largest = jnp.max(scores, -1, keepdims=True)
    weights = jnp.where(allowed, jnp.exp(scores - largest), 0.0)
    mass = jnp.sum(weights, -1, keepdims=True)
    o_ref[...] = dot((weights / mass).astype(BF), values, 1, 0).astype(BF)
    lse_ref[...] = largest + jnp.log(mass)


def backward_kernel(
    parts, t_ref, g_ref, w_ref, qkv_ref, o_ref, lse_ref, c_ref, m_ref, p_ref, dq_ref, dk_ref,
    grad_ref, sum_ref,
):
    queries, keys, values = (qkv_ref[:, i * HD : (i + 1) * HD] for i in range(3))
    tables = c_ref[0], -m_ref[0], -p_ref[0]
    depth = w_ref.shape[1] // parts
    heads_grad = None
    for k in range(parts):
        cols = slice(k * depth, (k + 1) * depth)
        term = dot(g_ref[:, cols], turned_columns(t_ref, w_ref, k * depth, depth, depth), 1, 1)
        heads_grad = term if heads_grad is None else heads_grad + term
    heads_grad = heads_grad.astype(BF)
    allowed = allowed_pairs(g_ref.shape[0], dq_ref, dk_ref)
    scores = jnp.where(allowed, dot(queries, keys, 1, 1), MASKED)
    weights = jnp.where(allowed, jnp.exp(scores - lse_ref[...]), 0.0)
    deltas = jnp.sum(heads_grad.astype(F32) * o_ref[...].astype(F32), -1, keepdims=True)
    score_grad = (weights * (dot(heads_grad, values, 1, 1) - deltas)).astype(BF)
    query_grad = dot(score_grad, keys, 1, 0) * HD ** (-0.5)
    key_grad = dot(score_grad, queries, 0, 0)
    value_grad = dot(weights.astype(BF), heads_grad, 0, 0)
    fields = turned(query_grad, *tables), turned(key_grad, *tables), value_grad

    @pl.when(pl.program_id(0) == 0)
    def _():
        sum_ref[...] = jnp.zeros_like(sum_ref)

    for i, field in enumerate(fields):
        field = field.astype(BF)
        cols = slice(i * HD, (i + 1) * HD)
        grad_ref[:, cols] = field
        sum_ref[:, cols] += jnp.sum(field.astype(F32), 0, keepdims=True)


def pair_specs(length):
    table = pl.BlockSpec((1, length, LANES), lambda r, t: (r, 0, 0))
    return [table] * 3 + [
        pl.BlockSpec((1, length, 1), lambda r, t: (r, 0, 0)),
        pl.BlockSpec((1, 1, length), lambda r, t: (r, 0, 0)),
    ]


def head_forward(turns, normed, bias, pairs, pieces, length):
    count, width = normed.shape
    columns = 3 * HD
    return call(
        forward_kernel,
        turns,
        count // length,
        [rows_block(width, length), pl.BlockSpec((1, columns), lambda r, t: (0, 0))]
        + pair_specs(length)
        + [whole(p) for p in pieces],
        [rows_block(columns, length), rows_block(HD, length), rows_block(1, length)],
        [like((count, columns)), like((count, HD)), like((count, 1), F32)],
        [normed, bias.reshape(1, columns)] + pairs + pieces,
        2 * count * (width * columns + 2 * length * HD),
    )


def head_backward(turns, grad, out_w, qkv, attended, lse, pairs, length):
    count, width = grad.shape
    columns = 3 * HD
    return call(
        functools.partial(backward_kernel, turns.shape[0]),
        turns,
        count // length,
        [
            rows_block(width, length),
            whole(out_w),
            rows_block(columns, length),
            rows_block(HD, length),
            rows_block(1, length),
        ]
        + pair_specs(length),
        [rows_block(columns, length), pl.BlockSpec((1, columns), lambda r, t: (0, 0))],
        [like((count, columns)), like((1, columns), F32)],
        [grad, out_w, qkv, attended, lse] + pairs,
        2 * count * (width * HD + 5 * length * HD),
    )


def finish_kernel(rows, with_norm, t_ref, x_ref, s_ref, o_ref, out_ref):
    depth = x_ref.shape[1] // rows
    term = s_ref[...].astype(F32)
    if with_norm:
        centred = x_ref[...].astype(F32)
        centred = centred - jnp.mean(centred, -1, keepdims=True)
        rstd = lax.rsqrt(jnp.mean(centred * centred, -1, keepdims=True) + EPSILON)
        centred = centred * rstd
        term = term - jnp.mean(term, -1, keepdims=True) - centred * jnp.mean(
            term * centred, -1, keepdims=True
        )
        field = o_ref[...].astype(F32) + rstd * term
    else:
        field = x_ref[...].astype(F32) + term + o_ref[4:5]
    for k in range(rows):
        at = pl.multiple_of(t_ref[k] * depth, LANES)
        out_ref[:, pl.ds(at, depth)] = field[:, k * depth : (k + 1) * depth].astype(BF)


def finish(turns, x, term, other, with_norm):
    return call(
        functools.partial(finish_kernel, turns.shape[0], with_norm),
        turns,
        1,
        [whole(v) for v in (x, term, other)],
        [whole(x)],
        [like(x.shape)],
        [x, term, other],
    )[0]


def shards(
    plan,
    tokens,
    attn_weights,
    mlp_weights,
    ln1_gain,
    ln1_bias,
    ln2_gain,
    ln2_bias,
    qkv_bias,
    dense_bias,
    up_bias,
    down_bias,
    doc_lengths,
    cotangent,
):
    row_count, shard_len, width = tokens.shape
    depth = attn_weights.shape[0]
    heads = width // HD
    rows, blks = plan.rows, plan.blks
    own_hidden = mlp_weights.shape[-1] // blks
    me = lax.axis_index("blk")
    length = shard_len * blks
    count = row_count * length
    head_of = me % plan.group // plan.share * plan.per_row + me // plan.group
    part = me % plan.share
    own_rows = row_count // plan.share
    turns = lax.axis_index("row") ^ jnp.arange(rows, dtype=jnp.int32)

    def exchange(field, groups=None):
        return lax.all_to_all(field, "blk", 0, 0, axis_index_groups=groups)

    def collect(field):
        return exchange(field.reshape(blks, -1, field.shape[-1]))

    def gather_blocks(field):
        field = field.reshape(row_count, shard_len, width)
        return lax.all_gather(field, "blk", axis=1, tiled=True).reshape(count, width)

    def sum_blocks(field):
        field = field.reshape(row_count, length, width)
        field = lax.psum_scatter(field, "blk", scatter_dimension=1, tiled=True)
        return field.reshape(row_count * shard_len, width)

    zeros = jnp.zeros((3, width), F32)
    vectors = jnp.stack([ln1_gain, ln1_bias, ln2_gain, ln2_bias, dense_bias + down_bias])
    x_own, g_own, vectors, g_sum = turn_in(
        turns,
        tokens.reshape(row_count * shard_len, width),
        cotangent.reshape(row_count * shard_len, width),
        jnp.concatenate([vectors, zeros]),
    )
    x_all = gather_blocks(x_own)
    qkv_send, out_own = split_attn(turns, after(attn_weights, x_own), plan, width)
    qkv_mine = exchange(qkv_send)
    out_rows = place(
        turns, [out_own] + [swap(out_own, "row", rows, k) for k in range(1, rows)], plan.share
    )
    up_send, down_send = split_mlp(turns, after(mlp_weights, qkv_send), blks)
    up_mine = exchange(after(up_send, qkv_mine, out_rows))
    qkv_gather = Gather(qkv_mine.reshape(-1, 3 * HD), plan)
    qkv_pieces = qkv_gather.finish()
    out_w = exchange(after(out_rows, up_mine, *qkv_gather.first()), plan.groups)
    down_mine = exchange(after(down_send, out_w, *qkv_pieces))
    out_w = out_w.reshape(HD, width)
    normed1, normed2 = norms(turns, x_all, vectors)
    up_gather = Gather(up_mine.reshape(-1, own_hidden), plan)
    up_pieces = up_gather.finish(normed2)
    down_gather = Gather(after(down_mine, *up_pieces).reshape(-1, own_hidden), plan)
    g_all = gather_blocks(after(g_own, down_mine))

    lengths = lax.dynamic_slice_in_dim(doc_lengths, part * own_rows, own_rows, 0)
    doc_ends = jnp.cumsum(lengths, axis=-1)
    starts = doc_ends - lengths
    places = jnp.arange(length, dtype=jnp.int32)
    doc_ids = jnp.sum((places[None, :, None] >= doc_ends[:, None, :]).astype(jnp.int32), -1)
    picked = doc_ids[:, :, None] == jnp.arange(lengths.shape[-1], dtype=jnp.int32)
    positions = places - jnp.sum(jnp.where(picked, starts[:, None, :], 0), -1)
    lane = jnp.arange(LANES)
    inverse = 10000.0 ** (-2.0 * (lane % (ROT // 2)).astype(F32) / ROT)
    angles = positions.astype(F32)[..., None] * inverse
    sine = jnp.sin(angles)
    pairs = [
        jnp.where(lane < ROT, jnp.cos(angles), 1.0),
        jnp.where(lane < ROT // 2, -sine, 0.0),
        jnp.where((lane >= ROT // 2) & (lane < ROT), sine, 0.0),
        doc_ids[:, :, None],
        doc_ids[:, None, :],
    ]

    def own(field):
        if plan.share == 1:
            return field
        return lax.dynamic_slice_in_dim(field, part * own_rows * length, own_rows * length, 0)

    def spread(field):
        if plan.share == 1:
            return field
        blank = jnp.zeros((count, field.shape[1]), field.dtype)
        return lax.dynamic_update_slice_in_dim(blank, field, part * own_rows * length, 0)

    up_b = lax.dynamic_slice_in_dim(up_bias, me * own_hidden, own_hidden)
    qkv_b = lax.dynamic_index_in_dim(qkv_bias.reshape(3, heads, HD), head_of, 1, keepdims=False)
    hidden, slope = feed_up(turns, normed2, up_b, up_pieces)
    own_normed1 = own(after(normed1, hidden))
    qkv, attended, lse = head_forward(
        turns, own_normed1, qkv_b.reshape(-1), pairs, qkv_pieces, length
    )
    down_pieces = down_gather.finish(attended)
    out_term = out_sum(turns, hidden, down_pieces, spread(attended), out_w)
    out_total = sum_blocks(out_term)

    g_all = after(g_all, out_term)
    down_g = weight_grad(turns, g_all, hidden)
    down_scatter = Scatter(down_g, plan)
    pre_grad, up_sum = feed_slope(turns, after(g_all, down_g[0]), slope, down_pieces)
    own_grad = own(after(g_all, pre_grad))
    qkv_grad, qkv_sum = head_backward(
        turns, own_grad, out_w, qkv, attended, lse, pairs, length
    )
    qkv_g, qkv_parts = weight_grad(
        turns, after(own_normed1, qkv_grad, *down_scatter.first()), qkv_grad, qkv_sum, qkv_pieces
    )
    qkv_scatter = Scatter(qkv_g, plan)
    norm_term = norm_back(
        turns,
        after(pre_grad, qkv_g[0]),
        up_pieces,
        spread(qkv_grad),
        qkv_pieces,
        vectors,
    )
    norm_total = sum_blocks(norm_term)
    down_total = down_scatter.finish()
    down_back = collect(down_total)
    up_g, up_parts = weight_grad(
        turns, after(normed2, norm_term, down_total), pre_grad, up_sum, up_pieces
    )
    up_scatter = Scatter(up_g, plan)
    out_g = out_grad(turns, after(attended, up_g[0]), own_grad)
    qkv_total = qkv_scatter.finish(down_total)
    qkv_back = collect(after(qkv_total, down_back, out_g, *up_scatter.first()))
    up_total = up_scatter.finish(qkv_total, down_back)
    out_back = exchange(after(out_g, qkv_back).reshape(plan.group, depth, width), plan.groups)
    up_back = collect(after(up_total, out_back))
    out_back = out_back.reshape(rows, plan.share, depth, width)
    if plan.share > 1:
        out_back = jnp.sum(out_back.astype(F32), 1, keepdims=True).astype(BF)
    out_back = out_back[:, 0]
    out_back = [lax.dynamic_index_in_dim(out_back, turns[k], 0, False) for k in range(rows)]
    out_back = out_back[0].astype(F32) + sum(
        swap(out_back[k], "row", rows, k).astype(F32) for k in range(1, rows)
    )

    qkv_slot = jnp.zeros((3, heads, HD), F32)
    qkv_slot = lax.dynamic_update_slice_in_dim(qkv_slot, qkv_sum.reshape(3, 1, HD), head_of, 1)
    up_slot = jnp.zeros((blks, own_hidden), F32)
    up_slot = lax.dynamic_update_slice_in_dim(up_slot, up_sum, me, 0)
    terms = [qkv_parts, up_parts, g_sum, qkv_slot, up_slot]
    sizes = [width] * 5 + [3 * width, mlp_weights.shape[-1]]
    sums = total(jnp.concatenate([v.reshape(-1) for v in terms]), plan)
    gain1, bias1, gain2, bias2, g_total, qkv_bias_grad, up_bias_grad = jnp.split(
        sums, np.cumsum(sizes)[:-1]
    )

    layer_out = finish(turns, x_own, out_total, vectors, False)
    tokens_grad = finish(turns, x_own, norm_total, g_own, True)
    return (
        layer_out.reshape(tokens.shape),
        tokens_grad.reshape(tokens.shape),
        join_attn(turns, qkv_back, out_back, plan),
        join_mlp(turns, up_back, down_back),
        (gain1 - ln1_bias * bias1) / ln1_gain,
        bias1,
        (gain2 - ln2_bias * bias2) / ln2_gain,
        bias2,
        qkv_bias_grad,
        g_total,
        up_bias_grad,
        g_total,
    )


def solution(mesh):
    rows, blks = mesh.shape["row"], mesh.shape["blk"]
    vector = P()
    tokens = P("row", "blk", None)
    attn = P(("row", "blk"), None)
    mlp = P(("row", "blk"), None, None)

    def run(*arrays):
        plan = Plan(rows, blks, arrays[0].shape[-1] // HD)
        return jax.shard_map(
            functools.partial(shards, plan),
            mesh=mesh,
            in_specs=(tokens, attn, mlp) + (vector,) * 8 + (P("row", None), tokens),
            out_specs=(tokens, tokens, attn, mlp) + (vector,) * 8,
            check_vma=False,
        )(*arrays)

    return run
```

```python
import functools
import math

import jax
import jax.numpy as jnp
import numpy as np
from jax import lax
from jax.experimental import pallas as pl
from jax.experimental.pallas import tpu as pltpu
from jax.sharding import PartitionSpec as P

HD = 256
ROT = 64
LANES = 128
BLOCK = 256
EPSILON = 1e-05
MASKED = -1e30
BF = jnp.bfloat16
F32 = jnp.float32
VMEM_LIMIT = 48 * 2**20


class Plan:
    def __init__(self, rows, blks, heads):
        self.rows = rows
        self.blks = blks
        self.share = blks // heads
        self.per_row = heads // rows
        self.group = blks // self.per_row
        self.groups = [
            list(range(i * self.group, (i + 1) * self.group)) for i in range(self.per_row)
        ]
        self.to_heads = []
        for row in range(rows):
            for blk in range(blks):
                first, place = blk // self.group * self.group, blk % self.group
                target = first + row * self.share + place % self.share
                self.to_heads.append((row * blks + blk, place // self.share * blks + target))


def after(field, *others):
    return lax.optimization_barrier((field,) + others)[0] if others else field


def swap(field, axis, size, bit):
    return lax.ppermute(field, axis, [(i, i ^ bit) for i in range(size)])


def bits_of(size):
    return [1 << i for i in range(size.bit_length() - 1)]


def total(field, plan):
    for axis, size in (("row", plan.rows), ("blk", plan.blks)):
        for bit in bits_of(size):
            field = field + swap(field, axis, size, bit)
    return field


def near(k):
    return k & (k - 1) == 0


def orders(plan):
    bits = bits_of(plan.rows)
    return bits, bits[::-1]


def half_of(field, h):
    middle = field.shape[0] // 2
    return field[h * middle : (h + 1) * middle]


def parts_of(rows, depth):
    out = []
    for k in range(rows):
        if near(k):
            out.append((k * depth, depth))
        else:
            out += [(k * depth, depth // 2), (k * depth + depth // 2, depth // 2)]
    return out


class Gather:
    def __init__(self, own, plan):
        self.plan = plan
        self.whole = {0: own}
        for bit in bits_of(plan.rows):
            self.whole[bit] = swap(own, "row", plan.rows, bit)

    def first(self):
        return [v for k, v in self.whole.items() if k]

    def finish(self, *others):
        plan = self.plan
        halves = []
        for h, order in enumerate(orders(plan)):
            got = {0: None}
            for bit in order:
                for k in list(got):
                    if k == 0:
                        got[bit] = half_of(after(self.whole[bit], *others), h)
                    else:
                        got[k ^ bit] = swap(got[k], "row", plan.rows, bit)
            halves.append(got)
        out = []
        for k in range(plan.rows):
            out += [self.whole[k]] if near(k) else [half[k] for half in halves]
        return out


class Scatter:
    def __init__(self, pieces, plan):
        self.plan = plan
        pieces = iter(pieces)
        self.whole, far = {}, [{}, {}]
        for k in range(plan.rows):
            if near(k):
                self.whole[k] = next(pieces)
            else:
                far[0][k], far[1][k] = next(pieces), next(pieces)
        self.got = []
        for h, order in enumerate(orders(plan)):
            held = far[h]
            for bit in order:
                for k in [k for k in held if k & bit]:
                    term = swap(held.pop(k), "row", plan.rows, bit)
                    if near(k ^ bit):
                        self.got.append((k ^ bit, h, term))
                    else:
                        held[k ^ bit] = (held[k ^ bit].astype(F32) + term.astype(F32)).astype(BF)

    def first(self):
        return [term for _, _, term in self.got]

    def second(self, *others):
        for k, h, term in self.got:
            term = after(term, *others)
            middle = self.whole[k].shape[0] // 2
            both = half_of(self.whole[k], h).astype(F32) + term.astype(F32)
            self.whole[k] = lax.dynamic_update_slice(self.whole[k], both.astype(BF), (h * middle, 0))
        return [v for k, v in self.whole.items() if k]

    def finish(self, *others):
        out = after(self.whole[0], *others).astype(F32)
        for bit in bits_of(self.plan.rows):
            out = out + swap(self.whole[bit], "row", self.plan.rows, bit).astype(F32)
        return out.astype(BF)


def dot(left, right, left_dim, right_dim):
    return lax.dot_general(
        left, right, (((left_dim,), (right_dim,)), ((), ())), preferred_element_type=F32
    )


def whole(array):
    return pl.BlockSpec(array.shape, lambda *i: (0,) * len(array.shape))


def like(shape, kind=BF):
    return jax.ShapeDtypeStruct(shape, kind)


def call(body, turns, grid, in_specs, out_specs, out_shape, operands, flops=0):
    moved = sum(v.size * v.dtype.itemsize for v in operands)
    moved += sum(math.prod(v.shape) * jnp.dtype(v.dtype).itemsize for v in out_shape)
    return pl.pallas_call(
        body,
        grid_spec=pltpu.PrefetchScalarGridSpec(
            num_scalar_prefetch=1, grid=(grid,), in_specs=in_specs, out_specs=out_specs
        ),
        out_shape=out_shape,
        compiler_params=pltpu.CompilerParams(vmem_limit_bytes=VMEM_LIMIT),
        cost_estimate=pl.CostEstimate(flops=flops, bytes_accessed=moved, transcendentals=0),
    )(turns, *operands)


def rows_block(columns, block=BLOCK):
    return pl.BlockSpec((block, columns), lambda i, t: (i, 0))


def turn_kernel(t_ref, x_ref, g_ref, v_ref, xo_ref, go_ref, vo_ref, s_ref):
    xo_ref[...] = x_ref[...]
    go_ref[...] = g_ref[...]
    vo_ref[...] = v_ref[...]
    s_ref[...] = jnp.sum(g_ref[...].astype(F32), 0, keepdims=True)


def turn_in(turns, x, g, vectors):
    rows = turns.shape[0]
    part = x.shape[1] // rows

    def specs(array, turned):
        index = (lambda k, t: (0, t[k])) if turned else (lambda k, t: (0, k))
        return pl.BlockSpec((array.shape[0], part), index)

    total_shape = like((1, x.shape[1]), F32)
    return call(
        turn_kernel,
        turns,
        rows,
        [specs(v, True) for v in (x, g, vectors)],
        [specs(v, False) for v in (x, g, vectors)] + [specs(total_shape, True)],
        [like(v.shape, v.dtype) for v in (x, g, vectors)] + [total_shape],
        [x, g, vectors],
    )


def split_kernel(t_ref, w_ref, u_ref, d_ref):
    u_ref[0] = w_ref[:, 0, :]
    d_ref[0] = w_ref[:, 1, :]


def split_mlp(turns, weights, blks):
    depth, _, hidden = weights.shape
    part = hidden // blks
    block = pl.BlockSpec((1, depth, part), lambda b, t: (b, 0, 0))
    return call(
        split_kernel,
        turns,
        blks,
        [pl.BlockSpec((depth, 2, part), lambda b, t: (0, 0, b))],
        [block] * 2,
        [like((blks, depth, part))] * 2,
        [weights],
    )


def join_kernel(t_ref, u_ref, d_ref, o_ref):
    o_ref[:, 0, :] = u_ref[0].astype(F32)
    o_ref[:, 1, :] = d_ref[0].astype(F32)


def join_mlp(turns, up, down):
    blks, depth, part = up.shape
    block = pl.BlockSpec((1, depth, part), lambda b, t: (b, 0, 0))
    return call(
        join_kernel,
        turns,
        blks,
        [block] * 2,
        [pl.BlockSpec((depth, 2, part), lambda b, t: (0, 0, b))],
        [like((depth, 2, blks * part), F32)],
        [up, down],
    )[0]


def split_attn_kernel(t_ref, q_ref, k_ref, v_ref, o_ref, qkv_ref, out_ref):
    for i, ref in enumerate((q_ref, k_ref, v_ref)):
        qkv_ref[0, :, i * HD : (i + 1) * HD] = ref[...]
    out_ref[...] = o_ref[...]


def split_attn(turns, weights, plan, width):
    depth = weights.shape[0]
    heads = width // HD
    part = width // plan.blks

    def head(i):
        def index(b, t):
            h = b % plan.group // plan.share * plan.per_row + b // plan.group
            return 0, i * heads + h

        return pl.BlockSpec((depth, HD), index)

    return call(
        split_attn_kernel,
        turns,
        plan.blks,
        [head(i) for i in range(3)] + [pl.BlockSpec((depth, part), lambda b, t: (0, 3 * plan.blks + b))],
        [
            pl.BlockSpec((1, depth, 3 * HD), lambda b, t: (b, 0, 0)),
            pl.BlockSpec((depth, part), lambda b, t: (0, b)),
        ],
        [like((plan.blks, depth, 3 * HD)), like((depth, width))],
        [weights] * 4,
    )


def join_attn_kernel(plan, t_ref, qkv_ref, out_ref, o_ref):
    step = pl.program_id(0)
    heads = o_ref.shape[1] // HD

    @pl.when(step < 3)
    def _():
        at = pl.ds(pl.multiple_of(step * HD, HD), HD)
        for h in range(heads):
            first = h % plan.per_row * plan.group + h // plan.per_row * plan.share
            o_ref[:, h * HD : (h + 1) * HD] = sum(
                qkv_ref[first + i, :, at].astype(F32) for i in range(plan.share)
            )

    @pl.when(step == 3)
    def _():
        o_ref[...] = out_ref[...]


def join_attn(turns, qkv, out, plan):
    depth, width = out.shape
    return call(
        functools.partial(join_attn_kernel, plan),
        turns,
        4,
        [whole(qkv), whole(out)],
        [pl.BlockSpec((depth, width), lambda j, t: (0, j))],
        [like((depth, 4 * width), F32)],
        [qkv, out],
    )[0]


def norm_kernel(t_ref, x_ref, v_ref, a1_ref, a2_ref):
    field = x_ref[...].astype(F32)
    centred = field - jnp.mean(field, -1, keepdims=True)
    standard = centred * lax.rsqrt(jnp.mean(centred * centred, -1, keepdims=True) + EPSILON)
    a1_ref[...] = (standard * v_ref[0:1] + v_ref[1:2]).astype(BF)
    a2_ref[...] = (standard * v_ref[2:3] + v_ref[3:4]).astype(BF)


def norms(turns, x, vectors):
    count, width = x.shape
    return call(
        norm_kernel,
        turns,
        count // BLOCK,
        [rows_block(width), whole(vectors)],
        [rows_block(width)] * 2,
        [like(x.shape)] * 2,
        [x, vectors],
        20 * count * width,
    )


def times_pieces(left, pieces):
    out, start = None, 0
    for piece in pieces:
        depth = piece.shape[0]
        term = dot(left[:, start : start + depth], piece[...], 1, 0)
        out = term if out is None else out + term
        start += depth
    return out


def up_kernel(t_ref, a_ref, b_ref, *refs):
    pieces, (h_ref, s_ref) = refs[:-2], refs[-2:]
    pre = times_pieces(a_ref[...], pieces) + b_ref[...]
    cdf = 0.5 * (1.0 + lax.erf(pre * math.sqrt(0.5)))
    h_ref[...] = (pre * cdf).astype(BF)
    s_ref[...] = cdf + pre * (jnp.exp(-0.5 * pre * pre) * (1.0 / math.sqrt(2.0 * math.pi)))


def feed_up(turns, normed, bias, pieces):
    count, width = normed.shape
    hidden = bias.shape[0]
    return call(
        up_kernel,
        turns,
        count // BLOCK,
        [rows_block(width), pl.BlockSpec((1, hidden), lambda i, t: (0, 0))]
        + [whole(p) for p in pieces],
        [rows_block(hidden)] * 2,
        [like((count, hidden)), like((count, hidden), F32)],
        [normed, bias.reshape(1, hidden)] + pieces,
        2 * count * width * hidden,
    )


def slope_kernel(t_ref, g_ref, s_ref, *refs):
    pieces, (p_ref, sum_ref) = refs[:-2], refs[-2:]

    @pl.when(pl.program_id(0) == 0)
    def _():
        sum_ref[...] = jnp.zeros_like(sum_ref)

    grad = (times_pieces(g_ref[...], pieces) * s_ref[...]).astype(BF)
    p_ref[...] = grad
    sum_ref[...] += jnp.sum(grad.astype(F32), 0, keepdims=True)


def feed_slope(turns, grad, slope, pieces):
    count, width = grad.shape
    hidden = slope.shape[1]
    return call(
        slope_kernel,
        turns,
        count // BLOCK,
        [rows_block(width), rows_block(hidden)] + [whole(p) for p in pieces],
        [rows_block(hidden), pl.BlockSpec((1, hidden), lambda i, t: (0, 0))],
        [like((count, hidden)), like((1, hidden), F32)],
        [grad, slope] + pieces,
        2 * count * width * hidden,
    )


def lane_sum(field):
    return sum(field[:, i : i + LANES] for i in range(0, field.shape[1], LANES))


def weight_kernel(rows, layout, with_sums, t_ref, l_ref, r_ref, *refs):
    step = pl.program_id(0)
    depth = l_ref.shape[1]
    if with_sums:
        sum_ref, pieces, refs = refs[0], refs[1 : 1 + len(layout)], refs[1 + len(layout) :]
        parts_ref = refs[-1]
    grad = dot(l_ref[...], r_ref[...], 0, 0)
    for k in range(rows):

        @pl.when(step == k)
        def _(k=k):
            for i, (start, size) in enumerate(layout):
                if start // depth != k:
                    continue
                at = slice(start - k * depth, start - k * depth + size)
                refs[i][...] = grad[at].astype(BF)
                if with_sums:
                    piece = pieces[i][...].astype(F32)
                    parts_ref[0, at] = lane_sum(piece * grad[at])
                    parts_ref[1, at] = lane_sum(piece * sum_ref[...])


def weight_grad(turns, left, right, sums=None, pieces=()):
    rows = turns.shape[0]
    count, width = left.shape
    columns = right.shape[1]
    depth = width // rows
    layout = parts_of(rows, depth)
    out_shape = [like((size, columns)) for _, size in layout]
    out_specs = [whole(v) for v in out_shape]
    operands = [left, right]
    if pieces:
        operands += [sums] + pieces
        out_shape.append(like((2, width, LANES), F32))
        out_specs.append(pl.BlockSpec((2, depth, LANES), lambda k, t: (0, t[k], 0)))
    out = call(
        functools.partial(weight_kernel, rows, layout, bool(pieces)),
        turns,
        rows,
        [pl.BlockSpec((count, depth), lambda k, t: (0, k))] + [whole(v) for v in operands[1:]],
        out_specs,
        out_shape,
        operands,
        2 * count * width * columns,
    )
    if pieces:
        return out[:-1], jnp.sum(out[-1], -1)
    return out


def out_kernel(t_ref, o_ref, g_ref, w_ref):
    w_ref[...] = dot(o_ref[...], g_ref[...], 0, 0).astype(BF)


def out_grad(turns, attended, grad):
    rows = turns.shape[0]
    count, width = grad.shape
    part = width // rows
    return call(
        out_kernel,
        turns,
        rows,
        [whole(attended), pl.BlockSpec((count, part), lambda k, t: (0, k))],
        [pl.BlockSpec((HD, part), lambda k, t: (0, t[k]))],
        [like((HD, width))],
        [attended, grad],
        2 * count * width * HD,
    )[0]


def turned_columns(t_ref, w_ref, start, size, depth):
    at = t_ref[start // depth] * depth + start % depth
    return w_ref[:, pl.ds(pl.multiple_of(at, LANES), size)]


def sum_kernel(layout, depth, t_ref, h_ref, o_ref, w_ref, *refs):
    pieces, y_ref = refs[:-1], refs[-1]
    for piece, (start, size) in zip(pieces, layout):
        term = dot(h_ref[...], piece[...], 1, 1)
        term += dot(o_ref[...], turned_columns(t_ref, w_ref, start, size, depth), 1, 0)
        y_ref[:, start : start + size] = term.astype(BF)


def out_sum(turns, hidden, pieces, attended, out_w):
    rows = turns.shape[0]
    count = hidden.shape[0]
    width = out_w.shape[1]
    return call(
        functools.partial(sum_kernel, parts_of(rows, width // rows), width // rows),
        turns,
        count // BLOCK,
        [rows_block(hidden.shape[1]), rows_block(HD), whole(out_w)] + [whole(p) for p in pieces],
        [rows_block(width)],
        [like((count, width))],
        [hidden, attended, out_w] + pieces,
        2 * count * width * (hidden.shape[1] + HD),
    )[0]


def back_kernel(layout, t_ref, p_ref, q_ref, v_ref, *refs):
    pieces, c_ref = refs[:-1], refs[-1]
    count = len(layout)
    for up, qkv, (start, size) in zip(pieces[:count], pieces[count:], layout):
        cols = slice(start, start + size)
        term = dot(p_ref[...], up[...], 1, 1) * v_ref[2:3, cols]
        term += dot(q_ref[...], qkv[...], 1, 1) * v_ref[0:1, cols]
        c_ref[:, cols] = term.astype(BF)


def norm_back(turns, pre_grad, up_pieces, qkv_grad, qkv_pieces, vectors):
    rows = turns.shape[0]
    count = pre_grad.shape[0]
    width = vectors.shape[1]
    columns = pre_grad.shape[1] + qkv_grad.shape[1]
    return call(
        functools.partial(back_kernel, parts_of(rows, width // rows)),
        turns,
        count // BLOCK,
        [rows_block(pre_grad.shape[1]), rows_block(qkv_grad.shape[1]), whole(vectors)]
        + [whole(p) for p in up_pieces + qkv_pieces],
        [rows_block(width)],
        [like((count, width))],
        [pre_grad, qkv_grad, vectors] + up_pieces + qkv_pieces,
        2 * count * width * columns,
    )[0]


def turned(field, cosine, minus, plus):
    head = field[:, :LANES]
    half = ROT // 2
    head = (
        head * cosine
        + pltpu.roll(head, LANES - half, 1) * minus
        + pltpu.roll(head, half, 1) * plus
    )
    return jnp.concatenate([head, field[:, LANES:]], 1)


def allowed_pairs(length, dq_ref, dk_ref):
    spot = lax.broadcasted_iota(jnp.int32, (length, length), 0)
    other = lax.broadcasted_iota(jnp.int32, (length, length), 1)
    return (dq_ref[0] == dk_ref[0]) & (other <= spot)


def forward_kernel(t_ref, a_ref, b_ref, c_ref, m_ref, p_ref, dq_ref, dk_ref, *refs):
    pieces, (qkv_ref, o_ref, lse_ref) = refs[:-3], refs[-3:]
    qkv = times_pieces(a_ref[...], pieces) + b_ref[...]
    tables = c_ref[0], m_ref[0], p_ref[0]
    queries = (turned(qkv[:, :HD], *tables) * HD ** (-0.5)).astype(BF)
    keys = turned(qkv[:, HD : 2 * HD], *tables).astype(BF)
    values = qkv[:, 2 * HD :].astype(BF)
    for i, field in enumerate((queries, keys, values)):
        qkv_ref[:, i * HD : (i + 1) * HD] = field
    allowed = allowed_pairs(a_ref.shape[0], dq_ref, dk_ref)
    scores = jnp.where(allowed, dot(queries, keys, 1, 1), MASKED)
    largest = jnp.max(scores, -1, keepdims=True)
    weights = jnp.where(allowed, jnp.exp(scores - largest), 0.0)
    mass = jnp.sum(weights, -1, keepdims=True)
    o_ref[...] = dot((weights / mass).astype(BF), values, 1, 0).astype(BF)
    lse_ref[...] = largest + jnp.log(mass)


def backward_kernel(
    parts, t_ref, g_ref, w_ref, qkv_ref, o_ref, lse_ref, c_ref, m_ref, p_ref, dq_ref, dk_ref,
    grad_ref, sum_ref,
):
    queries, keys, values = (qkv_ref[:, i * HD : (i + 1) * HD] for i in range(3))
    tables = c_ref[0], -m_ref[0], -p_ref[0]
    depth = w_ref.shape[1] // parts
    heads_grad = None
    for k in range(parts):
        cols = slice(k * depth, (k + 1) * depth)
        term = dot(g_ref[:, cols], turned_columns(t_ref, w_ref, k * depth, depth, depth), 1, 1)
        heads_grad = term if heads_grad is None else heads_grad + term
    heads_grad = heads_grad.astype(BF)
    allowed = allowed_pairs(g_ref.shape[0], dq_ref, dk_ref)
    scores = jnp.where(allowed, dot(queries, keys, 1, 1), MASKED)
    weights = jnp.where(allowed, jnp.exp(scores - lse_ref[...]), 0.0)
    deltas = jnp.sum(heads_grad.astype(F32) * o_ref[...].astype(F32), -1, keepdims=True)
    score_grad = (weights * (dot(heads_grad, values, 1, 1) - deltas)).astype(BF)
    query_grad = dot(score_grad, keys, 1, 0) * HD ** (-0.5)
    key_grad = dot(score_grad, queries, 0, 0)
    value_grad = dot(weights.astype(BF), heads_grad, 0, 0)
    fields = turned(query_grad, *tables), turned(key_grad, *tables), value_grad

    @pl.when(pl.program_id(0) == 0)
    def _():
        sum_ref[...] = jnp.zeros_like(sum_ref)

    for i, field in enumerate(fields):
        field = field.astype(BF)
        cols = slice(i * HD, (i + 1) * HD)
        grad_ref[:, cols] = field
        sum_ref[:, cols] += jnp.sum(field.astype(F32), 0, keepdims=True)


def pair_specs(length):
    table = pl.BlockSpec((1, length, LANES), lambda r, t: (r, 0, 0))
    return [table] * 3 + [
        pl.BlockSpec((1, length, 1), lambda r, t: (r, 0, 0)),
        pl.BlockSpec((1, 1, length), lambda r, t: (r, 0, 0)),
    ]


def head_forward(turns, normed, bias, pairs, pieces, length):
    count, width = normed.shape
    columns = 3 * HD
    return call(
        forward_kernel,
        turns,
        count // length,
        [rows_block(width, length), pl.BlockSpec((1, columns), lambda r, t: (0, 0))]
        + pair_specs(length)
        + [whole(p) for p in pieces],
        [rows_block(columns, length), rows_block(HD, length), rows_block(1, length)],
        [like((count, columns)), like((count, HD)), like((count, 1), F32)],
        [normed, bias.reshape(1, columns)] + pairs + pieces,
        2 * count * (width * columns + 2 * length * HD),
    )


def head_backward(turns, grad, out_w, qkv, attended, lse, pairs, length):
    count, width = grad.shape
    columns = 3 * HD
    return call(
        functools.partial(backward_kernel, turns.shape[0]),
        turns,
        count // length,
        [
            rows_block(width, length),
            whole(out_w),
            rows_block(columns, length),
            rows_block(HD, length),
            rows_block(1, length),
        ]
        + pair_specs(length),
        [rows_block(columns, length), pl.BlockSpec((1, columns), lambda r, t: (0, 0))],
        [like((count, columns)), like((1, columns), F32)],
        [grad, out_w, qkv, attended, lse] + pairs,
        2 * count * (width * HD + 5 * length * HD),
    )


def finish_kernel(rows, with_norm, t_ref, x_ref, s_ref, o_ref, out_ref):
    depth = x_ref.shape[1] // rows
    term = s_ref[...].astype(F32)
    if with_norm:
        centred = x_ref[...].astype(F32)
        centred = centred - jnp.mean(centred, -1, keepdims=True)
        rstd = lax.rsqrt(jnp.mean(centred * centred, -1, keepdims=True) + EPSILON)
        centred = centred * rstd
        term = term - jnp.mean(term, -1, keepdims=True) - centred * jnp.mean(
            term * centred, -1, keepdims=True
        )
        field = o_ref[...].astype(F32) + rstd * term
    else:
        field = x_ref[...].astype(F32) + term + o_ref[4:5]
    for k in range(rows):
        at = pl.multiple_of(t_ref[k] * depth, LANES)
        out_ref[:, pl.ds(at, depth)] = field[:, k * depth : (k + 1) * depth].astype(BF)


def finish(turns, x, term, other, with_norm):
    return call(
        functools.partial(finish_kernel, turns.shape[0], with_norm),
        turns,
        1,
        [whole(v) for v in (x, term, other)],
        [whole(x)],
        [like(x.shape)],
        [x, term, other],
    )[0]


def shards(
    plan,
    tokens,
    attn_weights,
    mlp_weights,
    ln1_gain,
    ln1_bias,
    ln2_gain,
    ln2_bias,
    qkv_bias,
    dense_bias,
    up_bias,
    down_bias,
    doc_lengths,
    cotangent,
):
    row_count, shard_len, width = tokens.shape
    depth = attn_weights.shape[0]
    heads = width // HD
    rows, blks = plan.rows, plan.blks
    own_hidden = mlp_weights.shape[-1] // blks
    me = lax.axis_index("blk")
    length = shard_len * blks
    count = row_count * length
    head_of = me % plan.group // plan.share * plan.per_row + me // plan.group
    part = me % plan.share
    own_rows = row_count // plan.share
    turns = lax.axis_index("row") ^ jnp.arange(rows, dtype=jnp.int32)

    def exchange(field):
        return lax.all_to_all(field, "blk", 0, 0)

    def collect(field):
        return exchange(field.reshape(blks, -1, field.shape[-1]))

    def gather_blocks(field):
        field = field.reshape(row_count, shard_len, width)
        return lax.all_gather(field, "blk", axis=1, tiled=True).reshape(count, width)

    def sum_blocks(field):
        field = field.reshape(row_count, length, width)
        field = lax.psum_scatter(field, "blk", scatter_dimension=1, tiled=True)
        return field.reshape(row_count * shard_len, width)

    zeros = jnp.zeros((3, width), F32)
    vectors = jnp.stack([ln1_gain, ln1_bias, ln2_gain, ln2_bias, dense_bias + down_bias])
    x_own, g_own, vectors, g_sum = turn_in(
        turns,
        tokens.reshape(row_count * shard_len, width),
        cotangent.reshape(row_count * shard_len, width),
        jnp.concatenate([vectors, zeros]),
    )
    qkv_send, out_own = split_attn(turns, attn_weights, plan, width)
    out_w = lax.all_gather(out_own, "blk", axis=0, tiled=True, axis_index_groups=plan.groups)
    x_all = gather_blocks(after(x_own, out_w))
    out_w = lax.ppermute(out_w, ("row", "blk"), plan.to_heads)
    qkv_mine = exchange(qkv_send)
    up_send, down_send = split_mlp(turns, after(mlp_weights, qkv_send), blks)
    up_mine = exchange(after(up_send, qkv_mine, out_w))
    qkv_gather = Gather(qkv_mine.reshape(-1, 3 * HD), plan)
    down_mine = exchange(after(down_send, up_mine, *qkv_gather.first()))
    up_gather = Gather(after(up_mine, *qkv_gather.first()).reshape(-1, own_hidden), plan)
    qkv_pieces = qkv_gather.finish(up_mine)
    joined = (down_mine, qkv_pieces[-2], qkv_pieces[-1], *up_gather.first())
    g_all = gather_blocks(after(g_own, *joined))
    down_gather = Gather(after(*joined).reshape(-1, own_hidden), plan)
    up_pieces = up_gather.finish(down_mine)
    normed1, normed2 = norms(turns, after(x_all, *joined), vectors)

    lengths = lax.dynamic_slice_in_dim(doc_lengths, part * own_rows, own_rows, 0)
    doc_ends = jnp.cumsum(lengths, axis=-1)
    starts = doc_ends - lengths
    places = jnp.arange(length, dtype=jnp.int32)
    doc_ids = jnp.sum((places[None, :, None] >= doc_ends[:, None, :]).astype(jnp.int32), -1)
    picked = doc_ids[:, :, None] == jnp.arange(lengths.shape[-1], dtype=jnp.int32)
    positions = places - jnp.sum(jnp.where(picked, starts[:, None, :], 0), -1)
    lane = jnp.arange(LANES)
    inverse = 10000.0 ** (-2.0 * (lane % (ROT // 2)).astype(F32) / ROT)
    angles = positions.astype(F32)[..., None] * inverse
    sine = jnp.sin(angles)
    pairs = [
        jnp.where(lane < ROT, jnp.cos(angles), 1.0),
        jnp.where(lane < ROT // 2, -sine, 0.0),
        jnp.where((lane >= ROT // 2) & (lane < ROT), sine, 0.0),
        doc_ids[:, :, None],
        doc_ids[:, None, :],
    ]

    def own(field):
        if plan.share == 1:
            return field
        return lax.dynamic_slice_in_dim(field, part * own_rows * length, own_rows * length, 0)

    def spread(field):
        if plan.share == 1:
            return field
        blank = jnp.zeros((count, field.shape[1]), field.dtype)
        return lax.dynamic_update_slice_in_dim(blank, field, part * own_rows * length, 0)

    up_b = lax.dynamic_slice_in_dim(up_bias, me * own_hidden, own_hidden)
    qkv_b = lax.dynamic_index_in_dim(qkv_bias.reshape(3, heads, HD), head_of, 1, keepdims=False)
    own_normed1 = own(normed1)
    qkv, attended, lse = head_forward(
        turns, own_normed1, qkv_b.reshape(-1), pairs, qkv_pieces, length
    )
    joined = (attended, up_pieces[-2], up_pieces[-1], *down_gather.first())
    hidden, slope = feed_up(turns, after(normed2, *joined), up_b, up_pieces)
    down_pieces = down_gather.finish(*joined)
    out_term = out_sum(turns, hidden, down_pieces, spread(attended), out_w)
    out_total = sum_blocks(out_term)

    g_all = after(g_all, out_term)
    down_g = weight_grad(turns, g_all, hidden)
    down_scatter = Scatter(down_g, plan)
    pre_grad, up_sum = feed_slope(turns, after(g_all, down_g[0]), slope, down_pieces)
    own_grad = own(after(g_all, *down_scatter.second(pre_grad)))
    qkv_grad, qkv_sum = head_backward(
        turns, own_grad, out_w, qkv, attended, lse, pairs, length
    )
    qkv_g, qkv_parts = weight_grad(turns, own_normed1, qkv_grad, qkv_sum, qkv_pieces)
    qkv_scatter = Scatter(qkv_g, plan)
    down_total = down_scatter.finish(qkv_g[0])
    down_back = collect(down_total)
    norm_term = norm_back(
        turns, after(pre_grad, down_total), up_pieces, spread(qkv_grad), qkv_pieces, vectors
    )
    norm_total = sum_blocks(norm_term)
    up_g, up_parts = weight_grad(
        turns, after(normed2, *qkv_scatter.second(norm_term)), pre_grad, up_sum, up_pieces
    )
    up_scatter = Scatter(up_g, plan)
    qkv_total = qkv_scatter.finish(up_g[0], down_back)
    out_g = out_grad(turns, after(attended, qkv_total), own_grad)
    out_back = lax.ppermute(out_g, ("row", "blk"), [(d, s) for s, d in plan.to_heads])
    qkv_back = collect(after(qkv_total, *up_scatter.second(out_g)))
    up_total = up_scatter.finish(qkv_back, out_back)
    up_back = collect(up_total)
    out_back = lax.psum_scatter(
        out_back, "blk", scatter_dimension=0, tiled=True, axis_index_groups=plan.groups
    )

    qkv_slot = jnp.zeros((3, heads, HD), F32)
    qkv_slot = lax.dynamic_update_slice_in_dim(qkv_slot, qkv_sum.reshape(3, 1, HD), head_of, 1)
    up_slot = jnp.zeros((blks, own_hidden), F32)
    up_slot = lax.dynamic_update_slice_in_dim(up_slot, up_sum, me, 0)
    terms = [qkv_parts, up_parts, g_sum, qkv_slot, up_slot]
    sizes = [width] * 5 + [3 * width, mlp_weights.shape[-1]]
    sums = total(jnp.concatenate([v.reshape(-1) for v in terms]), plan)
    gain1, bias1, gain2, bias2, g_total, qkv_bias_grad, up_bias_grad = jnp.split(
        sums, np.cumsum(sizes)[:-1]
    )

    layer_out = finish(turns, x_own, out_total, vectors, False)
    tokens_grad = finish(turns, x_own, norm_total, g_own, True)
    return (
        layer_out.reshape(tokens.shape),
        tokens_grad.reshape(tokens.shape),
        join_attn(turns, qkv_back, out_back.astype(F32), plan),
        join_mlp(turns, up_back, down_back),
        (gain1 - ln1_bias * bias1) / ln1_gain,
        bias1,
        (gain2 - ln2_bias * bias2) / ln2_gain,
        bias2,
        qkv_bias_grad,
        g_total,
        up_bias_grad,
        g_total,
    )


def solution(mesh):
    rows, blks = mesh.shape["row"], mesh.shape["blk"]
    vector = P()
    tokens = P("row", "blk", None)
    attn = P(("row", "blk"), None)
    mlp = P(("row", "blk"), None, None)

    def run(*arrays):
        plan = Plan(rows, blks, arrays[0].shape[-1] // HD)
        return jax.shard_map(
            functools.partial(shards, plan),
            mesh=mesh,
            in_specs=(tokens, attn, mlp) + (vector,) * 8 + (P("row", None), tokens),
            out_specs=(tokens, tokens, attn, mlp) + (vector,) * 8,
            check_vma=False,
        )(*arrays)

    return run
```

```python
import functools
import math

import jax
import jax.numpy as jnp
import numpy as np
from jax import lax
from jax.experimental import pallas as pl
from jax.experimental.pallas import tpu as pltpu
from jax.sharding import PartitionSpec as P

HD = 256
ROT = 64
LANES = 128
BLOCK = 256
EPSILON = 1e-05
MASKED = -1e30
BF = jnp.bfloat16
F32 = jnp.float32
VMEM_LIMIT = 48 * 2**20


class Plan:
    def __init__(self, rows, blks, heads):
        self.rows = rows
        self.blks = blks
        self.share = blks // heads
        self.per_row = heads // rows
        self.group = blks // self.per_row
        self.groups = [
            list(range(i * self.group, (i + 1) * self.group)) for i in range(self.per_row)
        ]


def after(field, *others):
    return lax.optimization_barrier((field,) + others)[0] if others else field


def swap(field, axis, size, bit):
    return lax.ppermute(field, axis, [(i, i ^ bit) for i in range(size)])


def bits_of(size):
    return [1 << i for i in range(size.bit_length() - 1)]


def swap_group(field, plan, bits):
    return lax.ppermute(field, "blk", [(i, i ^ bits) for i in range(plan.blks)])


def near(k):
    return k & (k - 1) == 0


def orders(plan):
    bits = bits_of(plan.rows)
    return bits, bits[::-1]


def half_of(field, h):
    middle = field.shape[0] // 2
    return field[h * middle : (h + 1) * middle]


def parts_of(rows, depth):
    out = []
    for k in range(rows):
        if near(k):
            out.append((k * depth, depth))
        else:
            out += [(k * depth, depth // 2), (k * depth + depth // 2, depth // 2)]
    return out


class Gather:
    def __init__(self, own, plan):
        self.plan = plan
        self.whole = {0: own}
        for bit in bits_of(plan.rows):
            self.whole[bit] = swap(own, "row", plan.rows, bit)

    def first(self):
        return [v for k, v in self.whole.items() if k]

    def finish(self, *others):
        plan = self.plan
        halves = []
        for h, order in enumerate(orders(plan)):
            got = {0: None}
            for bit in order:
                for k in list(got):
                    if k == 0:
                        got[bit] = half_of(after(self.whole[bit], *others), h)
                    else:
                        got[k ^ bit] = swap(got[k], "row", plan.rows, bit)
            halves.append(got)
        out = []
        for k in range(plan.rows):
            out += [self.whole[k]] if near(k) else [half[k] for half in halves]
        return out


class Scatter:
    def __init__(self, pieces, plan):
        self.plan = plan
        pieces = iter(pieces)
        self.whole, far = {}, [{}, {}]
        for k in range(plan.rows):
            if near(k):
                self.whole[k] = next(pieces)
            else:
                far[0][k], far[1][k] = next(pieces), next(pieces)
        self.got = []
        for h, order in enumerate(orders(plan)):
            held = far[h]
            for bit in order:
                for k in [k for k in held if k & bit]:
                    term = swap(held.pop(k), "row", plan.rows, bit)
                    if near(k ^ bit):
                        self.got.append((k ^ bit, h, term))
                    else:
                        held[k ^ bit] = (held[k ^ bit].astype(F32) + term.astype(F32)).astype(BF)

    def first(self):
        return [term for _, _, term in self.got]

    def second(self, *others):
        for k, h, term in self.got:
            term = after(term, *others)
            middle = self.whole[k].shape[0] // 2
            both = half_of(self.whole[k], h).astype(F32) + term.astype(F32)
            self.whole[k] = lax.dynamic_update_slice(self.whole[k], both.astype(BF), (h * middle, 0))
        return [v for k, v in self.whole.items() if k]

    def finish(self, *others):
        out = after(self.whole[0], *others).astype(F32)
        for bit in bits_of(self.plan.rows):
            out = out + swap(self.whole[bit], "row", self.plan.rows, bit).astype(F32)
        return out.astype(BF)


def dot(left, right, left_dim, right_dim):
    return lax.dot_general(
        left, right, (((left_dim,), (right_dim,)), ((), ())), preferred_element_type=F32
    )


def whole(array):
    return pl.BlockSpec(array.shape, lambda *i: (0,) * len(array.shape))


def like(shape, kind=BF):
    return jax.ShapeDtypeStruct(shape, kind)


def call(body, turns, grid, in_specs, out_specs, out_shape, operands, flops=0):
    moved = sum(v.size * v.dtype.itemsize for v in operands)
    moved += sum(math.prod(v.shape) * jnp.dtype(v.dtype).itemsize for v in out_shape)
    return pl.pallas_call(
        body,
        grid_spec=pltpu.PrefetchScalarGridSpec(
            num_scalar_prefetch=1, grid=(grid,), in_specs=in_specs, out_specs=out_specs
        ),
        out_shape=out_shape,
        compiler_params=pltpu.CompilerParams(vmem_limit_bytes=VMEM_LIMIT),
        cost_estimate=pl.CostEstimate(flops=flops, bytes_accessed=moved, transcendentals=0),
    )(turns, *operands)


def rows_block(columns, block=BLOCK):
    return pl.BlockSpec((block, columns), lambda i, t: (i, 0))


def turn_kernel(t_ref, x_ref, g_ref, v_ref, xo_ref, go_ref, vo_ref, s_ref):
    xo_ref[...] = x_ref[...]
    go_ref[...] = g_ref[...]
    vo_ref[...] = v_ref[...]
    s_ref[...] = jnp.sum(g_ref[...].astype(F32), 0, keepdims=True)


def turn_in(turns, x, g, vectors):
    rows = turns.shape[0]
    part = x.shape[1] // rows

    def specs(array, turned):
        index = (lambda k, t: (0, t[k])) if turned else (lambda k, t: (0, k))
        return pl.BlockSpec((array.shape[0], part), index)

    total_shape = like((1, x.shape[1]), F32)
    return call(
        turn_kernel,
        turns,
        rows,
        [specs(v, True) for v in (x, g, vectors)],
        [specs(v, False) for v in (x, g, vectors)] + [specs(total_shape, True)],
        [like(v.shape, v.dtype) for v in (x, g, vectors)] + [total_shape],
        [x, g, vectors],
    )


def split_kernel(t_ref, w_ref, u_ref, d_ref):
    u_ref[0] = w_ref[:, 0, :]
    d_ref[0] = w_ref[:, 1, :]


def split_mlp(turns, weights, blks):
    depth, _, hidden = weights.shape
    part = hidden // blks
    block = pl.BlockSpec((1, depth, part), lambda b, t: (b, 0, 0))
    return call(
        split_kernel,
        turns,
        blks,
        [pl.BlockSpec((depth, 2, part), lambda b, t: (0, 0, b))],
        [block] * 2,
        [like((blks, depth, part))] * 2,
        [weights],
    )


def join_kernel(t_ref, u_ref, d_ref, o_ref):
    o_ref[:, 0, :] = u_ref[0].astype(F32)
    o_ref[:, 1, :] = d_ref[0].astype(F32)


def join_mlp(turns, up, down):
    blks, depth, part = up.shape
    block = pl.BlockSpec((1, depth, part), lambda b, t: (b, 0, 0))
    return call(
        join_kernel,
        turns,
        blks,
        [block] * 2,
        [pl.BlockSpec((depth, 2, part), lambda b, t: (0, 0, b))],
        [like((depth, 2, blks * part), F32)],
        [up, down],
    )[0]


def split_attn_kernel(t_ref, q_ref, k_ref, v_ref, o_ref, qkv_ref, out_ref):
    for i, ref in enumerate((q_ref, k_ref, v_ref)):
        qkv_ref[0, :, i * HD : (i + 1) * HD] = ref[...]
    out_ref[...] = o_ref[...]


def split_attn(turns, weights, plan, width):
    depth = weights.shape[0]
    heads = width // HD
    part = width // plan.blks

    def head(i):
        def index(b, t):
            h = b % plan.group // plan.share * plan.per_row + b // plan.group
            return 0, i * heads + h

        return pl.BlockSpec((depth, HD), index)

    return call(
        split_attn_kernel,
        turns,
        plan.blks,
        [head(i) for i in range(3)] + [pl.BlockSpec((depth, part), lambda b, t: (0, 3 * plan.blks + b))],
        [
            pl.BlockSpec((1, depth, 3 * HD), lambda b, t: (b, 0, 0)),
            pl.BlockSpec((depth, part), lambda b, t: (0, b)),
        ],
        [like((plan.blks, depth, 3 * HD)), like((depth, width))],
        [weights] * 4,
    )


def join_attn_kernel(plan, t_ref, qkv_ref, out_ref, o_ref):
    step = pl.program_id(0)
    heads = o_ref.shape[1] // HD

    @pl.when(step < 3)
    def _():
        at = pl.ds(pl.multiple_of(step * HD, HD), HD)
        for h in range(heads):
            first = h % plan.per_row * plan.group + h // plan.per_row * plan.share
            o_ref[:, h * HD : (h + 1) * HD] = sum(
                qkv_ref[first + i, :, at].astype(F32) for i in range(plan.share)
            )

    @pl.when(step == 3)
    def _():
        o_ref[...] = out_ref[...]


def join_attn(turns, qkv, out, plan):
    depth, width = out.shape
    return call(
        functools.partial(join_attn_kernel, plan),
        turns,
        4,
        [whole(qkv), whole(out)],
        [pl.BlockSpec((depth, width), lambda j, t: (0, j))],
        [like((depth, 4 * width), F32)],
        [qkv, out],
    )[0]


def pick_kernel(count, t_ref, *refs):
    pieces, outs = refs[:count], refs[count:]
    share = t_ref.shape[0] // len(outs)
    for n, out in enumerate(outs):
        for i in range(share):
            for k, piece in enumerate(pieces):

                @pl.when(t_ref[n * share + i] == k)
                def _(i=i, out=out, piece=piece):
                    out[...] = piece[...] if i == 0 else out[...] + piece[...]


def pick(table, pieces, count):
    return call(
        functools.partial(pick_kernel, len(pieces)),
        table,
        1,
        [whole(p) for p in pieces],
        [whole(pieces[0])] * count,
        [like(pieces[0].shape)] * count,
        pieces,
    )


def place_kernel(t_ref, *refs):
    *pieces, out_ref = refs
    for k, piece in enumerate(pieces):
        depth = piece.shape[0]
        out_ref[pl.ds(pl.multiple_of(t_ref[k] * depth, depth), depth)] = piece[...]


def place(table, pieces):
    depth, width = pieces[0].shape
    shape = like((len(pieces) * depth, width))
    return call(place_kernel, table, 1, [whole(p) for p in pieces], [whole(shape)], [shape], pieces)[0]


def norm_kernel(t_ref, x_ref, v_ref, a1_ref, a2_ref):
    field = x_ref[...].astype(F32)
    centred = field - jnp.mean(field, -1, keepdims=True)
    standard = centred * lax.rsqrt(jnp.mean(centred * centred, -1, keepdims=True) + EPSILON)
    a1_ref[...] = (standard * v_ref[0:1] + v_ref[1:2]).astype(BF)
    a2_ref[...] = (standard * v_ref[2:3] + v_ref[3:4]).astype(BF)


def norms(turns, x, vectors):
    count, width = x.shape
    return call(
        norm_kernel,
        turns,
        count // BLOCK,
        [rows_block(width), whole(vectors)],
        [rows_block(width)] * 2,
        [like(x.shape)] * 2,
        [x, vectors],
        20 * count * width,
    )


def times_pieces(left, pieces):
    out, start = None, 0
    for piece in pieces:
        depth = piece.shape[0]
        term = dot(left[:, start : start + depth], piece[...], 1, 0)
        out = term if out is None else out + term
        start += depth
    return out


def up_kernel(t_ref, a_ref, b_ref, *refs):
    pieces, (h_ref, s_ref) = refs[:-2], refs[-2:]
    pre = times_pieces(a_ref[...], pieces) + b_ref[...]
    cdf = 0.5 * (1.0 + lax.erf(pre * math.sqrt(0.5)))
    h_ref[...] = (pre * cdf).astype(BF)
    s_ref[...] = cdf + pre * (jnp.exp(-0.5 * pre * pre) * (1.0 / math.sqrt(2.0 * math.pi)))


def feed_up(turns, normed, bias, pieces):
    count, width = normed.shape
    hidden = bias.shape[0]
    return call(
        up_kernel,
        turns,
        count // BLOCK,
        [rows_block(width), pl.BlockSpec((1, hidden), lambda i, t: (0, 0))]
        + [whole(p) for p in pieces],
        [rows_block(hidden)] * 2,
        [like((count, hidden)), like((count, hidden), F32)],
        [normed, bias.reshape(1, hidden)] + pieces,
        2 * count * width * hidden,
    )


def slope_kernel(t_ref, g_ref, s_ref, *refs):
    pieces, (p_ref, sum_ref) = refs[:-2], refs[-2:]

    @pl.when(pl.program_id(0) == 0)
    def _():
        sum_ref[...] = jnp.zeros_like(sum_ref)

    grad = (times_pieces(g_ref[...], pieces) * s_ref[...]).astype(BF)
    p_ref[...] = grad
    sum_ref[...] += jnp.sum(grad.astype(F32), 0, keepdims=True)


def feed_slope(turns, grad, slope, pieces):
    count, width = grad.shape
    hidden = slope.shape[1]
    return call(
        slope_kernel,
        turns,
        count // BLOCK,
        [rows_block(width), rows_block(hidden)] + [whole(p) for p in pieces],
        [rows_block(hidden), pl.BlockSpec((1, hidden), lambda i, t: (0, 0))],
        [like((count, hidden)), like((1, hidden), F32)],
        [grad, slope] + pieces,
        2 * count * width * hidden,
    )


def lane_sum(field):
    return sum(field[:, i : i + LANES] for i in range(0, field.shape[1], LANES))


def weight_kernel(rows, layout, with_sums, t_ref, l_ref, r_ref, *refs):
    step = pl.program_id(0)
    depth = l_ref.shape[1]
    if with_sums:
        sum_ref, pieces, refs = refs[0], refs[1 : 1 + len(layout)], refs[1 + len(layout) :]
        parts_ref = refs[-1]
    grad = dot(l_ref[...], r_ref[...], 0, 0)
    for k in range(rows):

        @pl.when(step == k)
        def _(k=k):
            for i, (start, size) in enumerate(layout):
                if start // depth != k:
                    continue
                at = slice(start - k * depth, start - k * depth + size)
                refs[i][...] = grad[at].astype(BF)
                if with_sums:
                    piece = pieces[i][...].astype(F32)
                    parts_ref[0, at] = lane_sum(piece * grad[at])
                    parts_ref[1, at] = lane_sum(piece * sum_ref[...])


def weight_grad(turns, left, right, sums=None, pieces=()):
    rows = turns.shape[0]
    count, width = left.shape
    columns = right.shape[1]
    depth = width // rows
    layout = parts_of(rows, depth)
    out_shape = [like((size, columns)) for _, size in layout]
    out_specs = [whole(v) for v in out_shape]
    operands = [left, right]
    if pieces:
        operands += [sums] + pieces
        out_shape.append(like((2, width, LANES), F32))
        out_specs.append(pl.BlockSpec((2, depth, LANES), lambda k, t: (0, t[k], 0)))
    out = call(
        functools.partial(weight_kernel, rows, layout, bool(pieces)),
        turns,
        rows,
        [pl.BlockSpec((count, depth), lambda k, t: (0, k))] + [whole(v) for v in operands[1:]],
        out_specs,
        out_shape,
        operands,
        2 * count * width * columns,
    )
    if pieces:
        return out[:-1], jnp.sum(out[-1], -1)
    return out


def out_kernel(rows, t_ref, o_ref, g_ref, *refs):
    *outs, grad_ref = refs
    depth = outs[0].shape[0]
    grad_ref[...] = dot(o_ref[...], g_ref[...], 0, 0)
    for j, out in enumerate(outs):
        at = pl.multiple_of(t_ref[rows + j] * depth, depth)
        out[...] = grad_ref[pl.ds(at, depth)].astype(BF)


def out_grad(turns, places, attended, grad):
    rows, group = turns.shape[0], places.shape[0]
    count, width = grad.shape
    part = width // rows
    depth = HD // group
    return pl.pallas_call(
        functools.partial(out_kernel, rows),
        grid_spec=pltpu.PrefetchScalarGridSpec(
            num_scalar_prefetch=1,
            grid=(rows,),
            in_specs=[whole(attended), pl.BlockSpec((count, part), lambda k, t: (0, k))],
            out_specs=[pl.BlockSpec((depth, part), lambda k, t: (0, t[k]))] * group,
            scratch_shapes=[pltpu.VMEM((HD, part), F32)],
        ),
        out_shape=[like((depth, width))] * group,
        compiler_params=pltpu.CompilerParams(vmem_limit_bytes=VMEM_LIMIT),
        cost_estimate=pl.CostEstimate(
            flops=2 * count * width * HD,
            bytes_accessed=2 * (count * (width + HD) + width * HD),
            transcendentals=0,
        ),
    )(jnp.concatenate([turns, places]), attended, grad)


def turned_columns(t_ref, w_ref, start, size, depth):
    at = t_ref[start // depth] * depth + start % depth
    return w_ref[:, pl.ds(pl.multiple_of(at, LANES), size)]


def sum_kernel(layout, depth, t_ref, h_ref, o_ref, w_ref, *refs):
    pieces, y_ref = refs[:-1], refs[-1]
    for piece, (start, size) in zip(pieces, layout):
        term = dot(h_ref[...], piece[...], 1, 1)
        term += dot(o_ref[...], turned_columns(t_ref, w_ref, start, size, depth), 1, 0)
        y_ref[:, start : start + size] = term.astype(BF)


def out_sum(turns, hidden, pieces, attended, out_w):
    rows = turns.shape[0]
    count = hidden.shape[0]
    width = out_w.shape[1]
    return call(
        functools.partial(sum_kernel, parts_of(rows, width // rows), width // rows),
        turns,
        count // BLOCK,
        [rows_block(hidden.shape[1]), rows_block(HD), whole(out_w)] + [whole(p) for p in pieces],
        [rows_block(width)],
        [like((count, width))],
        [hidden, attended, out_w] + pieces,
        2 * count * width * (hidden.shape[1] + HD),
    )[0]


def back_kernel(layout, t_ref, p_ref, q_ref, v_ref, *refs):
    pieces, c_ref = refs[:-1], refs[-1]
    count = len(layout)
    for up, qkv, (start, size) in zip(pieces[:count], pieces[count:], layout):
        cols = slice(start, start + size)
        term = dot(p_ref[...], up[...], 1, 1) * v_ref[2:3, cols]
        term += dot(q_ref[...], qkv[...], 1, 1) * v_ref[0:1, cols]
        c_ref[:, cols] = term.astype(BF)


def norm_back(turns, pre_grad, up_pieces, qkv_grad, qkv_pieces, vectors):
    rows = turns.shape[0]
    count = pre_grad.shape[0]
    width = vectors.shape[1]
    columns = pre_grad.shape[1] + qkv_grad.shape[1]
    return call(
        functools.partial(back_kernel, parts_of(rows, width // rows)),
        turns,
        count // BLOCK,
        [rows_block(pre_grad.shape[1]), rows_block(qkv_grad.shape[1]), whole(vectors)]
        + [whole(p) for p in up_pieces + qkv_pieces],
        [rows_block(width)],
        [like((count, width))],
        [pre_grad, qkv_grad, vectors] + up_pieces + qkv_pieces,
        2 * count * width * columns,
    )[0]


def turned(field, cosine, minus, plus):
    head = field[:, :LANES]
    half = ROT // 2
    head = (
        head * cosine
        + pltpu.roll(head, LANES - half, 1) * minus
        + pltpu.roll(head, half, 1) * plus
    )
    return jnp.concatenate([head, field[:, LANES:]], 1)


def allowed_pairs(length, dq_ref, dk_ref):
    spot = lax.broadcasted_iota(jnp.int32, (length, length), 0)
    other = lax.broadcasted_iota(jnp.int32, (length, length), 1)
    return (dq_ref[0] == dk_ref[0]) & (other <= spot)


def forward_kernel(t_ref, a_ref, b_ref, c_ref, m_ref, p_ref, dq_ref, dk_ref, *refs):
    pieces, (qkv_ref, o_ref, lse_ref) = refs[:-3], refs[-3:]
    qkv = times_pieces(a_ref[...], pieces) + b_ref[...]
    tables = c_ref[0], m_ref[0], p_ref[0]
    queries = (turned(qkv[:, :HD], *tables) * HD ** (-0.5)).astype(BF)
    keys = turned(qkv[:, HD : 2 * HD], *tables).astype(BF)
    values = qkv[:, 2 * HD :].astype(BF)
    for i, field in enumerate((queries, keys, values)):
        qkv_ref[:, i * HD : (i + 1) * HD] = field
    allowed = allowed_pairs(a_ref.shape[0], dq_ref, dk_ref)
    scores = jnp.where(allowed, dot(queries, keys, 1, 1), MASKED)
    largest = jnp.max(scores, -1, keepdims=True)
    weights = jnp.where(allowed, jnp.exp(scores - largest), 0.0)
    mass = jnp.sum(weights, -1, keepdims=True)
    o_ref[...] = dot((weights / mass).astype(BF), values, 1, 0).astype(BF)
    lse_ref[...] = largest + jnp.log(mass)


def backward_kernel(
    parts, t_ref, g_ref, w_ref, qkv_ref, o_ref, lse_ref, c_ref, m_ref, p_ref, dq_ref, dk_ref,
    grad_ref, sum_ref,
):
    queries, keys, values = (qkv_ref[:, i * HD : (i + 1) * HD] for i in range(3))
    tables = c_ref[0], -m_ref[0], -p_ref[0]
    depth = w_ref.shape[1] // parts
    heads_grad = None
    for k in range(parts):
        cols = slice(k * depth, (k + 1) * depth)
        term = dot(g_ref[:, cols], turned_columns(t_ref, w_ref, k * depth, depth, depth), 1, 1)
        heads_grad = term if heads_grad is None else heads_grad + term
    heads_grad = heads_grad.astype(BF)
    allowed = allowed_pairs(g_ref.shape[0], dq_ref, dk_ref)
    scores = jnp.where(allowed, dot(queries, keys, 1, 1), MASKED)
    weights = jnp.where(allowed, jnp.exp(scores - lse_ref[...]), 0.0)
    deltas = jnp.sum(heads_grad.astype(F32) * o_ref[...].astype(F32), -1, keepdims=True)
    score_grad = (weights * (dot(heads_grad, values, 1, 1) - deltas)).astype(BF)
    query_grad = dot(score_grad, keys, 1, 0) * HD ** (-0.5)
    key_grad = dot(score_grad, queries, 0, 0)
    value_grad = dot(weights.astype(BF), heads_grad, 0, 0)
    fields = turned(query_grad, *tables), turned(key_grad, *tables), value_grad

    @pl.when(pl.program_id(0) == 0)
    def _():
        sum_ref[...] = jnp.zeros_like(sum_ref)

    for i, field in enumerate(fields):
        field = field.astype(BF)
        cols = slice(i * HD, (i + 1) * HD)
        grad_ref[:, cols] = field
        sum_ref[:, cols] += jnp.sum(field.astype(F32), 0, keepdims=True)


def pair_specs(length):
    table = pl.BlockSpec((1, length, LANES), lambda r, t: (r, 0, 0))
    return [table] * 3 + [
        pl.BlockSpec((1, length, 1), lambda r, t: (r, 0, 0)),
        pl.BlockSpec((1, 1, length), lambda r, t: (r, 0, 0)),
    ]


def head_forward(turns, normed, bias, pairs, pieces, length):
    count, width = normed.shape
    columns = 3 * HD
    return call(
        forward_kernel,
        turns,
        count // length,
        [rows_block(width, length), pl.BlockSpec((1, columns), lambda r, t: (0, 0))]
        + pair_specs(length)
        + [whole(p) for p in pieces],
        [rows_block(columns, length), rows_block(HD, length), rows_block(1, length)],
        [like((count, columns)), like((count, HD)), like((count, 1), F32)],
        [normed, bias.reshape(1, columns)] + pairs + pieces,
        2 * count * (width * columns + 2 * length * HD),
    )


def head_backward(turns, grad, out_w, qkv, attended, lse, pairs, length):
    count, width = grad.shape
    columns = 3 * HD
    return call(
        functools.partial(backward_kernel, turns.shape[0]),
        turns,
        count // length,
        [
            rows_block(width, length),
            whole(out_w),
            rows_block(columns, length),
            rows_block(HD, length),
            rows_block(1, length),
        ]
        + pair_specs(length),
        [rows_block(columns, length), pl.BlockSpec((1, columns), lambda r, t: (0, 0))],
        [like((count, columns)), like((1, columns), F32)],
        [grad, out_w, qkv, attended, lse] + pairs,
        2 * count * (width * HD + 5 * length * HD),
    )


def finish_kernel(rows, with_norm, t_ref, x_ref, s_ref, o_ref, out_ref):
    depth = x_ref.shape[1] // rows
    term = s_ref[...].astype(F32)
    if with_norm:
        centred = x_ref[...].astype(F32)
        centred = centred - jnp.mean(centred, -1, keepdims=True)
        rstd = lax.rsqrt(jnp.mean(centred * centred, -1, keepdims=True) + EPSILON)
        centred = centred * rstd
        term = term - jnp.mean(term, -1, keepdims=True) - centred * jnp.mean(
            term * centred, -1, keepdims=True
        )
        field = o_ref[...].astype(F32) + rstd * term
    else:
        field = x_ref[...].astype(F32) + term + o_ref[4:5]
    for k in range(rows):
        at = pl.multiple_of(t_ref[k] * depth, LANES)
        out_ref[:, pl.ds(at, depth)] = field[:, k * depth : (k + 1) * depth].astype(BF)


def finish(turns, x, term, other, with_norm):
    return call(
        functools.partial(finish_kernel, turns.shape[0], with_norm),
        turns,
        1,
        [whole(v) for v in (x, term, other)],
        [whole(x)],
        [like(x.shape)],
        [x, term, other],
    )[0]


def shards(
    plan,
    tokens,
    attn_weights,
    mlp_weights,
    ln1_gain,
    ln1_bias,
    ln2_gain,
    ln2_bias,
    qkv_bias,
    dense_bias,
    up_bias,
    down_bias,
    doc_lengths,
    cotangent,
):
    row_count, shard_len, width = tokens.shape
    depth = attn_weights.shape[0]
    heads = width // HD
    rows, blks = plan.rows, plan.blks
    own_hidden = mlp_weights.shape[-1] // blks
    me = lax.axis_index("blk")
    length = shard_len * blks
    count = row_count * length
    head_of = me % plan.group // plan.share * plan.per_row + me // plan.group
    part = me % plan.share
    own_rows = row_count // plan.share
    row = lax.axis_index("row")
    turns = row ^ jnp.arange(rows, dtype=jnp.int32)
    places = me % plan.group ^ jnp.arange(plan.group, dtype=jnp.int32)

    def exchange(field):
        return lax.all_to_all(field, "blk", 0, 0)

    def collect(field):
        return exchange(field.reshape(blks, -1, field.shape[-1]))

    def gather_blocks(field):
        field = field.reshape(row_count, shard_len, width)
        return lax.all_gather(field, "blk", axis=1, tiled=True).reshape(count, width)

    def sum_blocks(field):
        field = field.reshape(row_count, length, width)
        field = lax.psum_scatter(field, "blk", scatter_dimension=1, tiled=True)
        return field.reshape(row_count * shard_len, width)

    zeros = jnp.zeros((3, width), F32)
    vectors = jnp.stack([ln1_gain, ln1_bias, ln2_gain, ln2_bias, dense_bias + down_bias])
    x_own, g_own, vectors, g_sum = turn_in(
        turns,
        tokens.reshape(row_count * shard_len, width),
        cotangent.reshape(row_count * shard_len, width),
        jnp.concatenate([vectors, zeros]),
    )
    x_all = gather_blocks(x_own)
    qkv_send, out_own = split_attn(turns, attn_weights, plan, width)
    qkv_mine = exchange(qkv_send)
    out_send = pick(
        row ^ places // plan.share,
        [out_own] + [swap(out_own, "row", rows, k) for k in range(1, rows)],
        plan.group,
    )
    up_send, down_send = split_mlp(turns, after(mlp_weights, qkv_send), blks)
    up_mine = exchange(after(up_send, qkv_mine, out_send[0]))
    qkv_gather = Gather(qkv_mine.reshape(-1, 3 * HD), plan)
    out_got = [out_send[0]] + [
        swap_group(after(out_send[j], qkv_mine), plan, j) for j in range(1, plan.group)
    ]
    down_mine = exchange(after(down_send, up_mine, *out_got[1:], *qkv_gather.first()))
    out_w = place(places, out_got)
    up_gather = Gather(after(up_mine, *qkv_gather.first()).reshape(-1, own_hidden), plan)
    qkv_pieces = qkv_gather.finish(up_mine)
    joined = (down_mine, qkv_pieces[-2], qkv_pieces[-1], *up_gather.first())
    g_all = gather_blocks(after(g_own, *joined))
    down_gather = Gather(after(*joined).reshape(-1, own_hidden), plan)
    up_pieces = up_gather.finish(down_mine)
    normed1, normed2 = norms(turns, after(x_all, *joined), vectors)

    lengths = lax.dynamic_slice_in_dim(doc_lengths, part * own_rows, own_rows, 0)
    doc_ends = jnp.cumsum(lengths, axis=-1)
    starts = doc_ends - lengths
    spots = jnp.arange(length, dtype=jnp.int32)
    doc_ids = jnp.sum((spots[None, :, None] >= doc_ends[:, None, :]).astype(jnp.int32), -1)
    picked = doc_ids[:, :, None] == jnp.arange(lengths.shape[-1], dtype=jnp.int32)
    positions = spots - jnp.sum(jnp.where(picked, starts[:, None, :], 0), -1)
    lane = jnp.arange(LANES)
    inverse = 10000.0 ** (-2.0 * (lane % (ROT // 2)).astype(F32) / ROT)
    angles = positions.astype(F32)[..., None] * inverse
    sine = jnp.sin(angles)
    pairs = [
        jnp.where(lane < ROT, jnp.cos(angles), 1.0),
        jnp.where(lane < ROT // 2, -sine, 0.0),
        jnp.where((lane >= ROT // 2) & (lane < ROT), sine, 0.0),
        doc_ids[:, :, None],
        doc_ids[:, None, :],
    ]

    def own(field):
        if plan.share == 1:
            return field
        return lax.dynamic_slice_in_dim(field, part * own_rows * length, own_rows * length, 0)

    def spread(field):
        if plan.share == 1:
            return field
        blank = jnp.zeros((count, field.shape[1]), field.dtype)
        return lax.dynamic_update_slice_in_dim(blank, field, part * own_rows * length, 0)

    up_b = lax.dynamic_slice_in_dim(up_bias, me * own_hidden, own_hidden)
    qkv_b = lax.dynamic_index_in_dim(qkv_bias.reshape(3, heads, HD), head_of, 1, keepdims=False)
    own_normed1 = own(normed1)
    qkv, attended, lse = head_forward(
        turns, own_normed1, qkv_b.reshape(-1), pairs, qkv_pieces, length
    )
    joined = (attended, up_pieces[-2], up_pieces[-1], *down_gather.first())
    hidden, slope = feed_up(turns, after(normed2, *joined), up_b, up_pieces)
    down_pieces = down_gather.finish(*joined)
    out_term = out_sum(turns, hidden, down_pieces, spread(attended), out_w)
    out_total = sum_blocks(out_term)

    g_all = after(g_all, out_term)
    down_g = weight_grad(turns, g_all, hidden)
    down_scatter = Scatter(down_g, plan)
    pre_grad, up_sum = feed_slope(turns, after(g_all, down_g[0]), slope, down_pieces)
    own_grad = own(after(g_all, *down_scatter.second(pre_grad)))
    qkv_grad, qkv_sum = head_backward(
        turns, own_grad, out_w, qkv, attended, lse, pairs, length
    )
    qkv_g, qkv_parts = weight_grad(turns, own_normed1, qkv_grad, qkv_sum, qkv_pieces)
    qkv_scatter = Scatter(qkv_g, plan)
    down_total = down_scatter.finish(qkv_g[0])
    down_back = collect(down_total)
    norm_term = norm_back(
        turns, after(pre_grad, down_total), up_pieces, spread(qkv_grad), qkv_pieces, vectors
    )
    norm_total = sum_blocks(norm_term)
    up_g, up_parts = weight_grad(
        turns, after(normed2, *qkv_scatter.second(norm_term)), pre_grad, up_sum, up_pieces
    )
    up_scatter = Scatter(up_g, plan)
    out_g = out_grad(turns, places, after(attended, up_g[0]), own_grad)
    out_got = [out_g[0]] + [swap_group(out_g[j], plan, j) for j in range(1, plan.group)]
    qkv_total = qkv_scatter.finish(out_g[0], down_back)
    up_second = up_scatter.second(qkv_total, *out_got[1:])
    qkv_back = collect(after(qkv_total, *up_second))
    holders = turns[:, None] * plan.share + jnp.arange(plan.share, dtype=jnp.int32)
    out_send = pick((me % plan.group ^ holders).reshape(-1), out_got, rows)
    out_back = out_send[0].astype(F32) + sum(
        swap(after(out_send[k], *up_second), "row", rows, k).astype(F32) for k in range(1, rows)
    )
    up_total = up_scatter.finish(qkv_back, out_back)
    up_back = collect(up_total)

    terms = [v.reshape(-1) for v in (qkv_parts, up_parts, g_sum, qkv_sum, up_sum)]
    used = sum(v.size for v in terms)
    terms.append(jnp.zeros((-used % (8 * LANES),), F32))
    sums = jnp.concatenate(terms).reshape(-1, LANES)
    sums = lax.all_gather(sums, ("row", "blk"), axis=0, tiled=True).reshape(rows, blks, -1)
    gain1, bias1, gain2, bias2, g_total = jnp.split(
        jnp.sum(sums[:, :, : 5 * width], (0, 1)), 5
    )
    sums = jnp.sum(sums[:, :, 5 * width : used], 0)
    qkv_bias_grad = sums[:, : 3 * HD].reshape(plan.per_row, rows, plan.share, 3, HD)
    qkv_bias_grad = jnp.sum(qkv_bias_grad, 2).transpose(2, 1, 0, 3).reshape(-1)
    up_bias_grad = sums[:, 3 * HD :].reshape(-1)

    layer_out = finish(turns, x_own, out_total, vectors, False)
    tokens_grad = finish(turns, x_own, norm_total, g_own, True)
    return (
        layer_out.reshape(tokens.shape),
        tokens_grad.reshape(tokens.shape),
        join_attn(turns, qkv_back, out_back, plan),
        join_mlp(turns, up_back, down_back),
        (gain1 - ln1_bias * bias1) / ln1_gain,
        bias1,
        (gain2 - ln2_bias * bias2) / ln2_gain,
        bias2,
        qkv_bias_grad,
        g_total,
        up_bias_grad,
        g_total,
    )


def solution(mesh):
    rows, blks = mesh.shape["row"], mesh.shape["blk"]
    vector = P()
    tokens = P("row", "blk", None)
    attn = P(("row", "blk"), None)
    mlp = P(("row", "blk"), None, None)

    def run(*arrays):
        plan = Plan(rows, blks, arrays[0].shape[-1] // HD)
        return jax.shard_map(
            functools.partial(shards, plan),
            mesh=mesh,
            in_specs=(tokens, attn, mlp) + (vector,) * 8 + (P("row", None), tokens),
            out_specs=(tokens, tokens, attn, mlp) + (vector,) * 8,
            check_vma=False,
        )(*arrays)

    return run
```

```python
import functools
import math

import jax
import jax.numpy as jnp
import numpy as np
from jax import lax
from jax.experimental import pallas as pl
from jax.experimental.pallas import tpu as pltpu
from jax.sharding import PartitionSpec as P

HD = 256
ROT = 64
LANES = 128
BLOCK = 256
EPSILON = 1e-05
MASKED = -1e30
BF = jnp.bfloat16
F32 = jnp.float32
VMEM_LIMIT = 60 * 2**20


class Plan:
    def __init__(self, rows, blks, heads):
        self.rows = rows
        self.blks = blks
        self.share = blks // heads
        self.per_row = heads // rows
        self.group = blks // self.per_row
        self.groups = [
            list(range(i * self.group, (i + 1) * self.group)) for i in range(self.per_row)
        ]


def after(field, *others):
    return lax.optimization_barrier((field,) + others)[0] if others else field


def swap(field, axis, size, bit):
    return lax.ppermute(field, axis, [(i, i ^ bit) for i in range(size)])


def bits_of(size):
    return [1 << i for i in range(size.bit_length() - 1)]


def swap_group(field, plan, bits):
    return lax.ppermute(field, "blk", [(i, i ^ bits) for i in range(plan.blks)])


def near(k):
    return k & (k - 1) == 0


def orders(plan):
    bits = bits_of(plan.rows)
    return bits, bits[::-1]


def half_of(field, h):
    middle = field.shape[0] // 2
    return field[h * middle : (h + 1) * middle]


def parts_of(rows, depth):
    out = []
    for k in range(rows):
        if near(k):
            out.append((k * depth, depth))
        else:
            out += [(k * depth, depth // 2), (k * depth + depth // 2, depth // 2)]
    return out


class Gather:
    def __init__(self, own, plan):
        self.plan = plan
        self.whole = {0: own}
        for bit in bits_of(plan.rows):
            self.whole[bit] = swap(own, "row", plan.rows, bit)

    def first(self):
        return [v for k, v in self.whole.items() if k]

    def finish(self, *others):
        plan = self.plan
        halves = []
        for h, order in enumerate(orders(plan)):
            got = {0: None}
            for bit in order:
                for k in list(got):
                    if k == 0:
                        got[bit] = half_of(after(self.whole[bit], *others), h)
                    else:
                        got[k ^ bit] = swap(got[k], "row", plan.rows, bit)
            halves.append(got)
        out = []
        for k in range(plan.rows):
            out += [self.whole[k]] if near(k) else [half[k] for half in halves]
        return out


class Scatter:
    def __init__(self, pieces, plan):
        self.plan = plan
        pieces = iter(pieces)
        self.whole, far = {}, [{}, {}]
        for k in range(plan.rows):
            if near(k):
                self.whole[k] = next(pieces)
            else:
                far[0][k], far[1][k] = next(pieces), next(pieces)
        self.got = []
        for h, order in enumerate(orders(plan)):
            held = far[h]
            for bit in order:
                for k in [k for k in held if k & bit]:
                    term = swap(held.pop(k), "row", plan.rows, bit)
                    if near(k ^ bit):
                        self.got.append((k ^ bit, h, term))
                    else:
                        held[k ^ bit] = (held[k ^ bit].astype(F32) + term.astype(F32)).astype(BF)

    def first(self):
        return [term for _, _, term in self.got]

    def second(self, turns, *others):
        got = [(k, h, after(term, *others)) for k, h, term in self.got]
        while got:
            first = {}
            for item in got:
                first.setdefault(item[0], item)
            got = [item for item in got if all(item is not v for v in first.values())]
            sums = add_halves(turns, [(self.whole[k], h, term) for k, h, term in first.values()])
            self.whole.update(zip(first, sums))
        return [v for k, v in self.whole.items() if k]

    def finish(self, turns, count, *others):
        terms = [after(self.whole[0], *others)]
        for bit in bits_of(self.plan.rows):
            terms.append(swap(self.whole[bit], "row", self.plan.rows, bit))
        return add_wholes(turns, terms, count)


def dot(left, right, left_dim, right_dim):
    return lax.dot_general(
        left, right, (((left_dim,), (right_dim,)), ((), ())), preferred_element_type=F32
    )


def whole(array):
    return pl.BlockSpec(array.shape, lambda *i: (0,) * len(array.shape))


def like(shape, kind=BF):
    return jax.ShapeDtypeStruct(shape, kind)


def call(body, turns, grid, in_specs, out_specs, out_shape, operands, flops=0):
    moved = sum(v.size * v.dtype.itemsize for v in operands)
    moved += sum(math.prod(v.shape) * jnp.dtype(v.dtype).itemsize for v in out_shape)
    return pl.pallas_call(
        body,
        grid_spec=pltpu.PrefetchScalarGridSpec(
            num_scalar_prefetch=1, grid=(grid,), in_specs=in_specs, out_specs=out_specs
        ),
        out_shape=out_shape,
        compiler_params=pltpu.CompilerParams(vmem_limit_bytes=VMEM_LIMIT),
        cost_estimate=pl.CostEstimate(flops=flops, bytes_accessed=moved, transcendentals=0),
    )(turns, *operands)


def rows_block(columns, block=BLOCK):
    return pl.BlockSpec((block, columns), lambda i, t: (i, 0))


def halves_kernel(count, t_ref, *refs):
    for i in range(count):
        into, term, out = refs[i], refs[count + i], refs[2 * count + i]
        out[...] = (into[...].astype(F32) + term[...].astype(F32)).astype(BF)


def add_halves(turns, items):
    count = len(items)
    depth, width = items[0][2].shape
    parts = 2
    into = [pl.BlockSpec((depth, width // parts), lambda i, t, h=h: (h, i)) for _, h, _ in items]
    term = pl.BlockSpec((depth, width // parts), lambda i, t: (0, i))
    return pl.pallas_call(
        functools.partial(halves_kernel, count),
        grid_spec=pltpu.PrefetchScalarGridSpec(
            num_scalar_prefetch=1, grid=(parts,), in_specs=into + [term] * count, out_specs=into
        ),
        out_shape=[like(v.shape) for v, _, _ in items],
        input_output_aliases={1 + i: i for i in range(count)},
        compiler_params=pltpu.CompilerParams(vmem_limit_bytes=VMEM_LIMIT),
        cost_estimate=pl.CostEstimate(
            flops=0, bytes_accessed=6 * depth * width * count, transcendentals=0
        ),
    )(turns, *[v for v, _, _ in items], *[v for _, _, v in items])


def wholes_kernel(count, t_ref, *refs):
    total = sum(ref[...].astype(F32) for ref in refs[:count]).astype(BF)
    outs = refs[count:]
    part = total.shape[1] // len(outs)
    for i, out in enumerate(outs):
        out[...] = total[:, i * part : (i + 1) * part]


def add_wholes(turns, terms, count):
    depth, width = terms[0].shape
    return call(
        functools.partial(wholes_kernel, len(terms)),
        turns,
        4,
        [rows_block(width, depth // 4)] * len(terms),
        [rows_block(width // count, depth // 4)] * count,
        [like((depth, width // count))] * count,
        terms,
    )


def turn_kernel(t_ref, x_ref, g_ref, v_ref, xo_ref, go_ref, vo_ref, s_ref):
    xo_ref[...] = x_ref[...]
    go_ref[...] = g_ref[...]
    vo_ref[...] = v_ref[...]
    s_ref[...] = jnp.sum(g_ref[...].astype(F32), 0, keepdims=True)


def turn_in(turns, x, g, vectors):
    rows = turns.shape[0]
    part = x.shape[1] // rows

    def specs(array, turned):
        index = (lambda k, t: (0, t[k])) if turned else (lambda k, t: (0, k))
        return pl.BlockSpec((array.shape[0], part), index)

    total_shape = like((1, x.shape[1]), F32)
    return call(
        turn_kernel,
        turns,
        rows,
        [specs(v, True) for v in (x, g, vectors)],
        [specs(v, False) for v in (x, g, vectors)] + [specs(total_shape, True)],
        [like(v.shape, v.dtype) for v in (x, g, vectors)] + [total_shape],
        [x, g, vectors],
    )


def split_kernel(t_ref, w_ref, u_ref, d_ref):
    u_ref[0] = w_ref[:, 0, :]
    d_ref[0] = w_ref[:, 1, :]


def split_mlp(turns, weights, blks):
    depth, _, hidden = weights.shape
    part = hidden // blks
    block = pl.BlockSpec((1, depth, part), lambda b, t: (b, 0, 0))
    return call(
        split_kernel,
        turns,
        blks,
        [pl.BlockSpec((depth, 2, part), lambda b, t: (0, 0, b))],
        [block] * 2,
        [like((blks, depth, part))] * 2,
        [weights],
    )


def join_kernel(count, t_ref, *refs):
    *parts, o_ref = refs
    part = parts[0].shape[2]
    for i, ref in enumerate(parts):
        side, at = divmod(i, count)
        o_ref[:, side, at * part : (at + 1) * part] = ref[0].astype(F32)


def join_mlp(turns, up, down):
    blks, depth, part = up[0].shape
    count = len(up)
    block = pl.BlockSpec((1, depth, part), lambda b, t: (b, 0, 0))
    return call(
        functools.partial(join_kernel, count),
        turns,
        blks,
        [block] * (2 * count),
        [pl.BlockSpec((depth, 2, count * part), lambda b, t: (0, 0, b))],
        [like((depth, 2, blks * count * part), F32)],
        up + down,
    )[0]


def split_attn_kernel(t_ref, q_ref, k_ref, v_ref, o_ref, qkv_ref, out_ref):
    for i, ref in enumerate((q_ref, k_ref, v_ref)):
        qkv_ref[0, :, i * HD : (i + 1) * HD] = ref[...]
    out_ref[...] = o_ref[...]


def split_attn(turns, weights, plan, width):
    depth = weights.shape[0]
    heads = width // HD
    part = width // plan.blks

    def head(i):
        def index(b, t):
            h = b % plan.group // plan.share * plan.per_row + b // plan.group
            return 0, i * heads + h

        return pl.BlockSpec((depth, HD), index)

    return call(
        split_attn_kernel,
        turns,
        plan.blks,
        [head(i) for i in range(3)] + [pl.BlockSpec((depth, part), lambda b, t: (0, 3 * plan.blks + b))],
        [
            pl.BlockSpec((1, depth, 3 * HD), lambda b, t: (b, 0, 0)),
            pl.BlockSpec((depth, part), lambda b, t: (0, b)),
        ],
        [like((plan.blks, depth, 3 * HD)), like((depth, width))],
        [weights] * 4,
    )


def join_attn_kernel(plan, t_ref, qkv_ref, out_ref, o_ref):
    step = pl.program_id(0)
    heads = o_ref.shape[1] // HD

    @pl.when(step < 3)
    def _():
        at = pl.ds(pl.multiple_of(step * HD, HD), HD)
        for h in range(heads):
            first = h % plan.per_row * plan.group + h // plan.per_row * plan.share
            o_ref[:, h * HD : (h + 1) * HD] = sum(
                qkv_ref[first + i, :, at].astype(F32) for i in range(plan.share)
            )

    @pl.when(step == 3)
    def _():
        o_ref[...] = out_ref[...]


def join_attn(turns, qkv, out, plan):
    depth, width = out.shape
    return call(
        functools.partial(join_attn_kernel, plan),
        turns,
        4,
        [whole(qkv), whole(out)],
        [pl.BlockSpec((depth, width), lambda j, t: (0, j))],
        [like((depth, 4 * width), F32)],
        [qkv, out],
    )[0]


def pick_kernel(count, t_ref, *refs):
    pieces, outs = refs[:count], refs[count:]
    share = t_ref.shape[0] // len(outs)
    for n, out in enumerate(outs):
        for i in range(share):
            for k, piece in enumerate(pieces):

                @pl.when(t_ref[n * share + i] == k)
                def _(i=i, out=out, piece=piece):
                    out[...] = piece[...] if i == 0 else out[...] + piece[...]


def pick(table, pieces, count):
    return call(
        functools.partial(pick_kernel, len(pieces)),
        table,
        1,
        [whole(p) for p in pieces],
        [whole(pieces[0])] * count,
        [like(pieces[0].shape)] * count,
        pieces,
    )


def place_kernel(t_ref, *refs):
    *pieces, out_ref = refs
    for k, piece in enumerate(pieces):
        depth = piece.shape[0]
        out_ref[pl.ds(pl.multiple_of(t_ref[k] * depth, depth), depth)] = piece[...]


def place(table, pieces):
    depth, width = pieces[0].shape
    shape = like((len(pieces) * depth, width))
    return call(place_kernel, table, 1, [whole(p) for p in pieces], [whole(shape)], [shape], pieces)[0]


def norm_kernel(t_ref, x_ref, v_ref, a1_ref, a2_ref):
    field = x_ref[...].astype(F32)
    centred = field - jnp.mean(field, -1, keepdims=True)
    standard = centred * lax.rsqrt(jnp.mean(centred * centred, -1, keepdims=True) + EPSILON)
    a1_ref[...] = (standard * v_ref[0:1] + v_ref[1:2]).astype(BF)
    a2_ref[...] = (standard * v_ref[2:3] + v_ref[3:4]).astype(BF)


def norms(turns, x, vectors):
    count, width = x.shape
    return call(
        norm_kernel,
        turns,
        count // BLOCK,
        [rows_block(width), whole(vectors)],
        [rows_block(width)] * 2,
        [like(x.shape)] * 2,
        [x, vectors],
        20 * count * width,
    )


def times_pieces(left, pieces):
    out, start = None, 0
    for piece in pieces:
        depth = piece.shape[0]
        term = dot(left[:, start : start + depth], piece[...], 1, 0)
        out = term if out is None else out + term
        start += depth
    return out


def up_kernel(t_ref, a_ref, b_ref, *refs):
    pieces, (h_ref, s_ref) = refs[:-2], refs[-2:]
    pre = times_pieces(a_ref[...], pieces) + b_ref[...]
    cdf = 0.5 * (1.0 + lax.erf(pre * math.sqrt(0.5)))
    h_ref[...] = (pre * cdf).astype(BF)
    s_ref[...] = cdf + pre * (jnp.exp(-0.5 * pre * pre) * (1.0 / math.sqrt(2.0 * math.pi)))


def feed_up(turns, normed, bias, pieces):
    count, width = normed.shape
    hidden = bias.shape[0]
    return call(
        up_kernel,
        turns,
        count // BLOCK,
        [rows_block(width), pl.BlockSpec((1, hidden), lambda i, t: (0, 0))]
        + [whole(p) for p in pieces],
        [rows_block(hidden)] * 2,
        [like((count, hidden)), like((count, hidden), F32)],
        [normed, bias.reshape(1, hidden)] + pieces,
        2 * count * width * hidden,
    )


def slope_kernel(t_ref, g_ref, s_ref, *refs):
    pieces, (p_ref, sum_ref) = refs[:-2], refs[-2:]

    @pl.when(pl.program_id(0) == 0)
    def _():
        sum_ref[...] = jnp.zeros_like(sum_ref)

    grad = (times_pieces(g_ref[...], pieces) * s_ref[...]).astype(BF)
    p_ref[...] = grad
    sum_ref[...] += jnp.sum(grad.astype(F32), 0, keepdims=True)


def feed_slope(turns, grad, slope, pieces):
    count, width = grad.shape
    hidden = slope.shape[1]
    return call(
        slope_kernel,
        turns,
        count // BLOCK,
        [rows_block(width), rows_block(hidden)] + [whole(p) for p in pieces],
        [rows_block(hidden), pl.BlockSpec((1, hidden), lambda i, t: (0, 0))],
        [like((count, hidden)), like((1, hidden), F32)],
        [grad, slope] + pieces,
        2 * count * width * hidden,
    )


def lane_sum(field):
    return sum(field[:, i : i + LANES] for i in range(0, field.shape[1], LANES))


def weight_kernel(rows, layout, with_sums, t_ref, l_ref, r_ref, *refs):
    step = pl.program_id(0)
    depth = l_ref.shape[1]
    if with_sums:
        sum_ref, pieces, refs = refs[0], refs[1 : 1 + len(layout)], refs[1 + len(layout) :]
        parts_ref = refs[-1]
    grad = dot(l_ref[...], r_ref[...], 0, 0)
    for k in range(rows):

        @pl.when(step == k)
        def _(k=k):
            for i, (start, size) in enumerate(layout):
                if start // depth != k:
                    continue
                at = slice(start - k * depth, start - k * depth + size)
                refs[i][...] = grad[at].astype(BF)
                if with_sums:
                    piece = pieces[i][...].astype(F32)
                    parts_ref[0, at] = lane_sum(piece * grad[at])
                    parts_ref[1, at] = lane_sum(piece * sum_ref[...])


def weight_grad(turns, left, right, sums=None, pieces=()):
    rows = turns.shape[0]
    count, width = left.shape
    columns = right.shape[1]
    depth = width // rows
    layout = parts_of(rows, depth)
    out_shape = [like((size, columns)) for _, size in layout]
    out_specs = [whole(v) for v in out_shape]
    operands = [left, right]
    if pieces:
        operands += [sums] + pieces
        out_shape.append(like((2, width, LANES), F32))
        out_specs.append(pl.BlockSpec((2, depth, LANES), lambda k, t: (0, t[k], 0)))
    out = call(
        functools.partial(weight_kernel, rows, layout, bool(pieces)),
        turns,
        rows,
        [pl.BlockSpec((count, depth), lambda k, t: (0, k))] + [whole(v) for v in operands[1:]],
        out_specs,
        out_shape,
        operands,
        2 * count * width * columns,
    )
    if pieces:
        return out[:-1], out[-1]
    return out


def out_kernel(rows, t_ref, o_ref, g_ref, *refs):
    *outs, grad_ref = refs
    depth = outs[0].shape[0]
    grad_ref[...] = dot(o_ref[...], g_ref[...], 0, 0)
    for j, out in enumerate(outs):
        at = pl.multiple_of(t_ref[rows + j] * depth, depth)
        out[...] = grad_ref[pl.ds(at, depth)].astype(BF)


def out_grad(turns, places, attended, grad):
    rows, group = turns.shape[0], places.shape[0]
    count, width = grad.shape
    part = width // rows
    depth = HD // group
    return pl.pallas_call(
        functools.partial(out_kernel, rows),
        grid_spec=pltpu.PrefetchScalarGridSpec(
            num_scalar_prefetch=1,
            grid=(rows,),
            in_specs=[whole(attended), pl.BlockSpec((count, part), lambda k, t: (0, k))],
            out_specs=[pl.BlockSpec((depth, part), lambda k, t: (0, t[k]))] * group,
            scratch_shapes=[pltpu.VMEM((HD, part), F32)],
        ),
        out_shape=[like((depth, width))] * group,
        compiler_params=pltpu.CompilerParams(vmem_limit_bytes=VMEM_LIMIT),
        cost_estimate=pl.CostEstimate(
            flops=2 * count * width * HD,
            bytes_accessed=2 * (count * (width + HD) + width * HD),
            transcendentals=0,
        ),
    )(jnp.concatenate([turns, places]), attended, grad)


def turned_columns(t_ref, w_ref, start, size, depth):
    at = t_ref[start // depth] * depth + start % depth
    return w_ref[:, pl.ds(pl.multiple_of(at, LANES), size)]


def sum_kernel(layout, depth, t_ref, h_ref, o_ref, w_ref, *refs):
    pieces, y_ref = refs[:-1], refs[-1]
    for piece, (start, size) in zip(pieces, layout):
        term = dot(h_ref[...], piece[...], 1, 1)
        term += dot(o_ref[...], turned_columns(t_ref, w_ref, start, size, depth), 1, 0)
        y_ref[:, start : start + size] = term.astype(BF)


def out_sum(turns, hidden, pieces, attended, out_w):
    rows = turns.shape[0]
    count = hidden.shape[0]
    width = out_w.shape[1]
    return call(
        functools.partial(sum_kernel, parts_of(rows, width // rows), width // rows),
        turns,
        count // BLOCK,
        [rows_block(hidden.shape[1]), rows_block(HD), whole(out_w)] + [whole(p) for p in pieces],
        [rows_block(width)],
        [like((count, width))],
        [hidden, attended, out_w] + pieces,
        2 * count * width * (hidden.shape[1] + HD),
    )[0]


def back_kernel(layout, t_ref, p_ref, q_ref, v_ref, *refs):
    pieces, c_ref = refs[:-1], refs[-1]
    count = len(layout)
    for up, qkv, (start, size) in zip(pieces[:count], pieces[count:], layout):
        cols = slice(start, start + size)
        term = dot(p_ref[...], up[...], 1, 1) * v_ref[2:3, cols]
        term += dot(q_ref[...], qkv[...], 1, 1) * v_ref[0:1, cols]
        c_ref[:, cols] = term.astype(BF)


def norm_back(turns, pre_grad, up_pieces, qkv_grad, qkv_pieces, vectors):
    rows = turns.shape[0]
    count = pre_grad.shape[0]
    width = vectors.shape[1]
    columns = pre_grad.shape[1] + qkv_grad.shape[1]
    return call(
        functools.partial(back_kernel, parts_of(rows, width // rows)),
        turns,
        count // BLOCK,
        [rows_block(pre_grad.shape[1]), rows_block(qkv_grad.shape[1]), whole(vectors)]
        + [whole(p) for p in up_pieces + qkv_pieces],
        [rows_block(width)],
        [like((count, width))],
        [pre_grad, qkv_grad, vectors] + up_pieces + qkv_pieces,
        2 * count * width * columns,
    )[0]


def turned(field, cosine, minus, plus):
    head = field[:, :LANES]
    half = ROT // 2
    head = (
        head * cosine
        + pltpu.roll(head, LANES - half, 1) * minus
        + pltpu.roll(head, half, 1) * plus
    )
    return jnp.concatenate([head, field[:, LANES:]], 1)


def allowed_pairs(length, dq_ref, dk_ref):
    spot = lax.broadcasted_iota(jnp.int32, (length, length), 0)
    other = lax.broadcasted_iota(jnp.int32, (length, length), 1)
    return (dq_ref[0] == dk_ref[0]) & (other <= spot)


def forward_kernel(t_ref, a_ref, b_ref, c_ref, m_ref, p_ref, dq_ref, dk_ref, *refs):
    pieces, (qkv_ref, o_ref, lse_ref) = refs[:-3], refs[-3:]
    qkv = times_pieces(a_ref[...], pieces) + b_ref[...]
    tables = c_ref[0], m_ref[0], p_ref[0]
    queries = (turned(qkv[:, :HD], *tables) * HD ** (-0.5)).astype(BF)
    keys = turned(qkv[:, HD : 2 * HD], *tables).astype(BF)
    values = qkv[:, 2 * HD :].astype(BF)
    for i, field in enumerate((queries, keys, values)):
        qkv_ref[:, i * HD : (i + 1) * HD] = field
    allowed = allowed_pairs(a_ref.shape[0], dq_ref, dk_ref)
    scores = jnp.where(allowed, dot(queries, keys, 1, 1), MASKED)
    largest = jnp.max(scores, -1, keepdims=True)
    weights = jnp.where(allowed, jnp.exp(scores - largest), 0.0)
    mass = jnp.sum(weights, -1, keepdims=True)
    o_ref[...] = dot((weights / mass).astype(BF), values, 1, 0).astype(BF)
    lse_ref[...] = largest + jnp.log(mass)


def backward_kernel(
    parts, t_ref, g_ref, w_ref, qkv_ref, o_ref, lse_ref, c_ref, m_ref, p_ref, dq_ref, dk_ref,
    grad_ref, sum_ref,
):
    queries, keys, values = (qkv_ref[:, i * HD : (i + 1) * HD] for i in range(3))
    tables = c_ref[0], -m_ref[0], -p_ref[0]
    depth = w_ref.shape[1] // parts
    heads_grad = None
    for k in range(parts):
        cols = slice(k * depth, (k + 1) * depth)
        term = dot(g_ref[:, cols], turned_columns(t_ref, w_ref, k * depth, depth, depth), 1, 1)
        heads_grad = term if heads_grad is None else heads_grad + term
    heads_grad = heads_grad.astype(BF)
    allowed = allowed_pairs(g_ref.shape[0], dq_ref, dk_ref)
    scores = jnp.where(allowed, dot(queries, keys, 1, 1), MASKED)
    weights = jnp.where(allowed, jnp.exp(scores - lse_ref[...]), 0.0)
    deltas = jnp.sum(heads_grad.astype(F32) * o_ref[...].astype(F32), -1, keepdims=True)
    score_grad = (weights * (dot(heads_grad, values, 1, 1) - deltas)).astype(BF)
    query_grad = dot(score_grad, keys, 1, 0) * HD ** (-0.5)
    key_grad = dot(score_grad, queries, 0, 0)
    value_grad = dot(weights.astype(BF), heads_grad, 0, 0)
    fields = turned(query_grad, *tables), turned(key_grad, *tables), value_grad

    @pl.when(pl.program_id(0) == 0)
    def _():
        sum_ref[...] = jnp.zeros_like(sum_ref)

    for i, field in enumerate(fields):
        field = field.astype(BF)
        cols = slice(i * HD, (i + 1) * HD)
        grad_ref[:, cols] = field
        sum_ref[:, cols] += jnp.sum(field.astype(F32), 0, keepdims=True)


def pair_specs(length):
    table = pl.BlockSpec((1, length, LANES), lambda r, t: (r, 0, 0))
    return [table] * 3 + [
        pl.BlockSpec((1, length, 1), lambda r, t: (r, 0, 0)),
        pl.BlockSpec((1, 1, length), lambda r, t: (r, 0, 0)),
    ]


def head_forward(turns, normed, bias, pairs, pieces, length):
    count, width = normed.shape
    columns = 3 * HD
    return call(
        forward_kernel,
        turns,
        count // length,
        [rows_block(width, length), pl.BlockSpec((1, columns), lambda r, t: (0, 0))]
        + pair_specs(length)
        + [whole(p) for p in pieces],
        [rows_block(columns, length), rows_block(HD, length), rows_block(1, length)],
        [like((count, columns)), like((count, HD)), like((count, 1), F32)],
        [normed, bias.reshape(1, columns)] + pairs + pieces,
        2 * count * (width * columns + 2 * length * HD),
    )


def head_backward(turns, grad, out_w, qkv, attended, lse, pairs, length):
    count, width = grad.shape
    columns = 3 * HD
    return call(
        functools.partial(backward_kernel, turns.shape[0]),
        turns,
        count // length,
        [
            rows_block(width, length),
            whole(out_w),
            rows_block(columns, length),
            rows_block(HD, length),
            rows_block(1, length),
        ]
        + pair_specs(length),
        [rows_block(columns, length), pl.BlockSpec((1, columns), lambda r, t: (0, 0))],
        [like((count, columns)), like((1, columns), F32)],
        [grad, out_w, qkv, attended, lse] + pairs,
        2 * count * (width * HD + 5 * length * HD),
    )


def finish_kernel(rows, with_norm, t_ref, x_ref, s_ref, o_ref, out_ref):
    depth = x_ref.shape[1] // rows
    term = s_ref[...].astype(F32)
    if with_norm:
        centred = x_ref[...].astype(F32)
        centred = centred - jnp.mean(centred, -1, keepdims=True)
        rstd = lax.rsqrt(jnp.mean(centred * centred, -1, keepdims=True) + EPSILON)
        centred = centred * rstd
        term = term - jnp.mean(term, -1, keepdims=True) - centred * jnp.mean(
            term * centred, -1, keepdims=True
        )
        field = o_ref[...].astype(F32) + rstd * term
    else:
        field = x_ref[...].astype(F32) + term + o_ref[4:5]
    for k in range(rows):
        at = pl.multiple_of(t_ref[k] * depth, LANES)
        out_ref[:, pl.ds(at, depth)] = field[:, k * depth : (k + 1) * depth].astype(BF)


def finish(turns, x, term, other, with_norm):
    return call(
        functools.partial(finish_kernel, turns.shape[0], with_norm),
        turns,
        1,
        [whole(v) for v in (x, term, other)],
        [whole(x)],
        [like(x.shape)],
        [x, term, other],
    )[0]


def shards(
    plan,
    tokens,
    attn_weights,
    mlp_weights,
    ln1_gain,
    ln1_bias,
    ln2_gain,
    ln2_bias,
    qkv_bias,
    dense_bias,
    up_bias,
    down_bias,
    doc_lengths,
    cotangent,
):
    row_count, shard_len, width = tokens.shape
    depth = attn_weights.shape[0]
    heads = width // HD
    rows, blks = plan.rows, plan.blks
    own_hidden = mlp_weights.shape[-1] // blks
    me = lax.axis_index("blk")
    length = shard_len * blks
    count = row_count * length
    head_of = me % plan.group // plan.share * plan.per_row + me // plan.group
    part = me % plan.share
    own_rows = row_count // plan.share
    row = lax.axis_index("row")
    turns = row ^ jnp.arange(rows, dtype=jnp.int32)
    places = me % plan.group ^ jnp.arange(plan.group, dtype=jnp.int32)

    def exchange(field):
        return lax.all_to_all(field, "blk", 0, 0)

    def collect(field):
        return exchange(field.reshape(blks, -1, field.shape[-1]))

    def gather_blocks(field):
        field = field.reshape(row_count, shard_len, width)
        return lax.all_gather(field, "blk", axis=1, tiled=True).reshape(count, width)

    def sum_blocks(field):
        field = field.reshape(row_count, length, width)
        field = lax.psum_scatter(field, "blk", scatter_dimension=1, tiled=True)
        return field.reshape(row_count * shard_len, width)

    zeros = jnp.zeros((3, width), F32)
    vectors = jnp.stack([ln1_gain, ln1_bias, ln2_gain, ln2_bias, dense_bias + down_bias])
    x_own, g_own, vectors, g_sum = turn_in(
        turns,
        tokens.reshape(row_count * shard_len, width),
        cotangent.reshape(row_count * shard_len, width),
        jnp.concatenate([vectors, zeros]),
    )
    qkv_send, out_own = split_attn(turns, attn_weights, plan, width)
    qkv_mine = exchange(qkv_send)
    out_send = pick(
        row ^ places // plan.share,
        [out_own] + [swap(out_own, "row", rows, k) for k in range(1, rows)],
        plan.group,
    )
    up_send, down_send = split_mlp(turns, after(mlp_weights, qkv_send), blks)
    up_mine = exchange(after(up_send, qkv_mine, out_send[0]))
    x_all = gather_blocks(after(x_own, up_mine))
    qkv_gather = Gather(qkv_mine.reshape(-1, 3 * HD), plan)
    out_got = [out_send[0]] + [
        swap_group(after(out_send[j], qkv_mine), plan, j) for j in range(1, plan.group)
    ]
    down_mine = exchange(after(down_send, up_mine, *out_got[1:], *qkv_gather.first()))
    out_w = place(places, out_got)
    up_gather = Gather(after(up_mine, *qkv_gather.first()).reshape(-1, own_hidden), plan)
    qkv_pieces = qkv_gather.finish(up_mine)
    joined = (down_mine, qkv_pieces[-2], qkv_pieces[-1], *up_gather.first())
    g_all = gather_blocks(after(g_own, *joined))
    down_gather = Gather(after(*joined).reshape(-1, own_hidden), plan)
    up_pieces = up_gather.finish(down_mine)
    normed1, normed2 = norms(turns, after(x_all, *joined), vectors)

    lengths = lax.dynamic_slice_in_dim(doc_lengths, part * own_rows, own_rows, 0)
    doc_ends = jnp.cumsum(lengths, axis=-1)
    starts = doc_ends - lengths
    spots = jnp.arange(length, dtype=jnp.int32)
    doc_ids = jnp.sum((spots[None, :, None] >= doc_ends[:, None, :]).astype(jnp.int32), -1)
    picked = doc_ids[:, :, None] == jnp.arange(lengths.shape[-1], dtype=jnp.int32)
    positions = spots - jnp.sum(jnp.where(picked, starts[:, None, :], 0), -1)
    lane = jnp.arange(LANES)
    inverse = 10000.0 ** (-2.0 * (lane % (ROT // 2)).astype(F32) / ROT)
    angles = positions.astype(F32)[..., None] * inverse
    sine = jnp.sin(angles)
    pairs = [
        jnp.where(lane < ROT, jnp.cos(angles), 1.0),
        jnp.where(lane < ROT // 2, -sine, 0.0),
        jnp.where((lane >= ROT // 2) & (lane < ROT), sine, 0.0),
        doc_ids[:, :, None],
        doc_ids[:, None, :],
    ]

    def own(field):
        if plan.share == 1:
            return field
        return lax.dynamic_slice_in_dim(field, part * own_rows * length, own_rows * length, 0)

    def spread(field):
        if plan.share == 1:
            return field
        blank = jnp.zeros((count, field.shape[1]), field.dtype)
        return lax.dynamic_update_slice_in_dim(blank, field, part * own_rows * length, 0)

    up_b = lax.dynamic_slice_in_dim(up_bias, me * own_hidden, own_hidden)
    qkv_b = lax.dynamic_index_in_dim(qkv_bias.reshape(3, heads, HD), head_of, 1, keepdims=False)
    own_normed1 = own(normed1)
    qkv, attended, lse = head_forward(
        turns, own_normed1, qkv_b.reshape(-1), pairs, qkv_pieces, length
    )
    joined = (attended, up_pieces[-2], up_pieces[-1], *down_gather.first())
    hidden, slope = feed_up(turns, after(normed2, *joined), up_b, up_pieces)
    down_pieces = down_gather.finish(*joined)
    out_term = out_sum(turns, hidden, down_pieces, spread(attended), out_w)
    out_total = sum_blocks(out_term)

    g_all = after(g_all, out_term)
    down_g = weight_grad(turns, g_all, hidden)
    down_scatter = Scatter(down_g, plan)
    pre_grad, up_sum = feed_slope(turns, after(g_all, down_g[0]), slope, down_pieces)
    down_second = down_scatter.second(turns, pre_grad)
    up_g, up_parts = weight_grad(
        turns, after(normed2, *down_second), pre_grad, up_sum, up_pieces
    )
    up_scatter = Scatter(up_g, plan)
    own_grad = own(after(g_all, up_g[0]))
    qkv_grad, qkv_sum = head_backward(
        turns, own_grad, out_w, qkv, attended, lse, pairs, length
    )
    down_total = down_scatter.finish(turns, 2, qkv_grad)
    down_back = [collect(down_total[0])]
    norm_term = norm_back(
        turns, after(pre_grad, down_total[0]), up_pieces, spread(qkv_grad), qkv_pieces, vectors
    )
    norm_total = sum_blocks(norm_term)
    up_second = up_scatter.second(turns, norm_term)
    joined = (down_back[0], norm_term, *up_second)
    down_back.append(collect(after(down_total[1], *joined)))
    qkv_g, qkv_parts = weight_grad(
        turns, after(own_normed1, *joined), qkv_grad, qkv_sum, qkv_pieces
    )
    qkv_scatter = Scatter(qkv_g, plan)
    up_total = up_scatter.finish(turns, 2, qkv_g[0])
    up_back = [collect(after(up_total[0], down_back[1]))]
    out_g = out_grad(turns, places, after(attended, up_total[0]), own_grad)
    out_got = [out_g[0]] + [swap_group(out_g[j], plan, j) for j in range(1, plan.group)]
    qkv_second = qkv_scatter.second(turns, out_g[0])
    up_back.append(collect(after(up_total[1], up_back[0], *qkv_second)))
    qkv_total = qkv_scatter.finish(turns, 1, *out_got[1:])[0]
    qkv_back = collect(after(qkv_total, up_back[1]))
    holders = turns[:, None] * plan.share + jnp.arange(plan.share, dtype=jnp.int32)
    out_send = pick((me % plan.group ^ holders).reshape(-1), out_got, rows)
    out_back = out_send[0].astype(F32) + sum(
        swap(out_send[k], "row", rows, k).astype(F32) for k in range(1, rows)
    )

    terms = [after(v, norm_total) for v in (qkv_parts, up_parts)]
    terms = [jnp.sum(v, -1) for v in terms] + [g_sum, qkv_sum, up_sum]
    terms = [v.reshape(-1) for v in terms]
    used = sum(v.size for v in terms)
    terms.append(jnp.zeros((-used % (8 * LANES),), F32))
    sums = jnp.concatenate(terms).reshape(-1, LANES)
    sums = lax.all_gather(sums, ("row", "blk"), axis=0, tiled=True).reshape(rows, blks, -1)
    gain1, bias1, gain2, bias2, g_total = jnp.split(
        jnp.sum(sums[:, :, : 5 * width], (0, 1)), 5
    )
    sums = jnp.sum(sums[:, :, 5 * width : used], 0)
    qkv_bias_grad = sums[:, : 3 * HD].reshape(plan.per_row, rows, plan.share, 3, HD)
    qkv_bias_grad = jnp.sum(qkv_bias_grad, 2).transpose(2, 1, 0, 3).reshape(-1)
    up_bias_grad = sums[:, 3 * HD :].reshape(-1)

    layer_out = finish(turns, x_own, out_total, vectors, False)
    tokens_grad = finish(turns, x_own, norm_total, g_own, True)
    return (
        layer_out.reshape(tokens.shape),
        tokens_grad.reshape(tokens.shape),
        join_attn(turns, qkv_back, out_back, plan),
        join_mlp(turns, up_back, down_back),
        (gain1 - ln1_bias * bias1) / ln1_gain,
        bias1,
        (gain2 - ln2_bias * bias2) / ln2_gain,
        bias2,
        qkv_bias_grad,
        g_total,
        up_bias_grad,
        g_total,
    )


def solution(mesh):
    rows, blks = mesh.shape["row"], mesh.shape["blk"]
    vector = P()
    tokens = P("row", "blk", None)
    attn = P(("row", "blk"), None)
    mlp = P(("row", "blk"), None, None)

    def run(*arrays):
        plan = Plan(rows, blks, arrays[0].shape[-1] // HD)
        return jax.shard_map(
            functools.partial(shards, plan),
            mesh=mesh,
            in_specs=(tokens, attn, mlp) + (vector,) * 8 + (P("row", None), tokens),
            out_specs=(tokens, tokens, attn, mlp) + (vector,) * 8,
            check_vma=False,
        )(*arrays)

    return run
```

```python
import functools
import math

import jax
import jax.numpy as jnp
import numpy as np
from jax import lax
from jax.experimental import pallas as pl
from jax.experimental.pallas import tpu as pltpu
from jax.sharding import PartitionSpec as P

HD = 256
ROT = 64
LANES = 128
BLOCK = 256
EPSILON = 1e-05
MASKED = -1e30
BF = jnp.bfloat16
F32 = jnp.float32
COST = 100
VMEM_LIMIT = 56 * 2**20


class Plan:
    def __init__(self, rows, blks, heads):
        self.rows = rows
        self.blks = blks
        self.share = blks // heads
        self.per_row = heads // rows
        self.group = blks // self.per_row
        self.groups = [
            list(range(i * self.group, (i + 1) * self.group)) for i in range(self.per_row)
        ]


def after(field, *others):
    return lax.optimization_barrier((field,) + others)[0] if others else field


def swap(field, axis, size, bit):
    return lax.ppermute(field, axis, [(i, i ^ bit) for i in range(size)])


def bits_of(size):
    return [1 << i for i in range(size.bit_length() - 1)]


def swap_group(field, plan, bits):
    return lax.ppermute(field, "blk", [(i, i ^ bits) for i in range(plan.blks)])


def near(k):
    return k & (k - 1) == 0


def orders(plan):
    bits = bits_of(plan.rows)
    return bits, bits[::-1]


def half_of(field, h):
    middle = field.shape[0] // 2
    return field[h * middle : (h + 1) * middle]


def parts_of(rows, depth):
    out = []
    for k in range(rows):
        if near(k):
            out.append((k * depth, depth))
        else:
            out += [(k * depth, depth // 2), (k * depth + depth // 2, depth // 2)]
    return out


class Gather:
    def __init__(self, own, plan):
        self.plan = plan
        self.whole = {0: own}
        for bit in bits_of(plan.rows):
            self.whole[bit] = swap(own, "row", plan.rows, bit)

    def first(self):
        return [v for k, v in self.whole.items() if k]

    def finish(self, *others):
        plan = self.plan
        halves = []
        for h, order in enumerate(orders(plan)):
            got = {0: None}
            for bit in order:
                for k in list(got):
                    if k == 0:
                        got[bit] = half_of(after(self.whole[bit], *others), h)
                    else:
                        got[k ^ bit] = swap(got[k], "row", plan.rows, bit)
            halves.append(got)
        out = []
        for k in range(plan.rows):
            out += [self.whole[k]] if near(k) else [half[k] for half in halves]
        return out


class Scatter:
    def __init__(self, pieces, plan):
        self.plan = plan
        pieces = iter(pieces)
        self.whole, far = {}, [{}, {}]
        for k in range(plan.rows):
            if near(k):
                self.whole[k] = next(pieces)
            else:
                far[0][k], far[1][k] = next(pieces), next(pieces)
        self.got = []
        for h, order in enumerate(orders(plan)):
            held = far[h]
            for bit in order:
                for k in [k for k in held if k & bit]:
                    term = swap(held.pop(k), "row", plan.rows, bit)
                    if near(k ^ bit):
                        self.got.append((k ^ bit, h, term))
                    else:
                        held[k ^ bit] = (held[k ^ bit].astype(F32) + term.astype(F32)).astype(BF)

    def first(self):
        return [term for _, _, term in self.got]

    def second(self, turns, *others):
        got = [(k, h, after(term, *others)) for k, h, term in self.got]
        while got:
            first = {}
            for item in got:
                first.setdefault(item[0], item)
            got = [item for item in got if all(item is not v for v in first.values())]
            sums = add_halves(turns, [(self.whole[k], h, term) for k, h, term in first.values()])
            self.whole.update(zip(first, sums))
        return [v for k, v in self.whole.items() if k]

    def finish(self, turns, *others):
        terms = [after(self.whole[0], *others)]
        for bit in bits_of(self.plan.rows):
            terms.append(swap(self.whole[bit], "row", self.plan.rows, bit))
        return add_wholes(turns, terms)


def dot(left, right, left_dim, right_dim):
    return lax.dot_general(
        left, right, (((left_dim,), (right_dim,)), ((), ())), preferred_element_type=F32
    )


def whole(array):
    return pl.BlockSpec(array.shape, lambda *i: (0,) * len(array.shape))


def like(shape, kind=BF):
    return jax.ShapeDtypeStruct(shape, kind)


def call(body, turns, grid, in_specs, out_specs, out_shape, operands, flops=0):
    moved = sum(v.size * v.dtype.itemsize for v in operands)
    moved += sum(math.prod(v.shape) * jnp.dtype(v.dtype).itemsize for v in out_shape)
    return pl.pallas_call(
        body,
        name=getattr(body, "func", body).__name__,
        grid_spec=pltpu.PrefetchScalarGridSpec(
            num_scalar_prefetch=1, grid=(grid,), in_specs=in_specs, out_specs=out_specs
        ),
        out_shape=out_shape,
        compiler_params=pltpu.CompilerParams(vmem_limit_bytes=VMEM_LIMIT),
        cost_estimate=pl.CostEstimate(
            flops=flops // COST, bytes_accessed=moved // COST, transcendentals=0
        ),
    )(turns, *operands)


def rows_block(columns, block=BLOCK):
    return pl.BlockSpec((block, columns), lambda i, t: (i, 0))


def halves_kernel(count, t_ref, *refs):
    for i in range(count):
        into, term, out = refs[i], refs[count + i], refs[2 * count + i]
        out[...] = (into[...].astype(F32) + term[...].astype(F32)).astype(BF)


def add_halves(turns, items):
    count = len(items)
    depth, width = items[0][2].shape
    parts = 2
    into = [pl.BlockSpec((depth, width // parts), lambda i, t, h=h: (h, i)) for _, h, _ in items]
    term = pl.BlockSpec((depth, width // parts), lambda i, t: (0, i))
    return pl.pallas_call(
        functools.partial(halves_kernel, count),
        name="halves_kernel",
        grid_spec=pltpu.PrefetchScalarGridSpec(
            num_scalar_prefetch=1, grid=(parts,), in_specs=into + [term] * count, out_specs=into
        ),
        out_shape=[like(v.shape) for v, _, _ in items],
        input_output_aliases={1 + i: i for i in range(count)},
        compiler_params=pltpu.CompilerParams(vmem_limit_bytes=VMEM_LIMIT),
        cost_estimate=pl.CostEstimate(
            flops=0, bytes_accessed=6 * depth * width * count // COST, transcendentals=0
        ),
    )(turns, *[v for v, _, _ in items], *[v for _, _, v in items])


def wholes_kernel(t_ref, *refs):
    refs[-1][...] = sum(ref[...].astype(F32) for ref in refs[:-1]).astype(BF)


def add_wholes(turns, terms):
    depth, width = terms[0].shape
    block = rows_block(width, depth // 4)
    shape = like((depth, width))
    return call(wholes_kernel, turns, 4, [block] * len(terms), [block], [shape], terms)[0]


def turn_kernel(t_ref, x_ref, g_ref, v_ref, xo_ref, go_ref, vo_ref, s_ref):
    xo_ref[...] = x_ref[...]
    go_ref[...] = g_ref[...]
    vo_ref[...] = v_ref[...]
    s_ref[...] = jnp.sum(g_ref[...].astype(F32), 0, keepdims=True)


def turn_in(turns, x, g, vectors):
    rows = turns.shape[0]
    part = x.shape[1] // rows

    def specs(array, turned):
        index = (lambda k, t: (0, t[k])) if turned else (lambda k, t: (0, k))
        return pl.BlockSpec((array.shape[0], part), index)

    total_shape = like((1, x.shape[1]), F32)
    return call(
        turn_kernel,
        turns,
        rows,
        [specs(v, True) for v in (x, g, vectors)],
        [specs(v, False) for v in (x, g, vectors)] + [specs(total_shape, True)],
        [like(v.shape, v.dtype) for v in (x, g, vectors)] + [total_shape],
        [x, g, vectors],
    )


def split_kernel(t_ref, w_ref, u_ref, d_ref):
    u_ref[0] = w_ref[:, 0, :]
    d_ref[0] = w_ref[:, 1, :]


def split_mlp(turns, weights, blks):
    depth, _, hidden = weights.shape
    part = hidden // blks
    block = pl.BlockSpec((1, depth, part), lambda b, t: (b, 0, 0))
    return call(
        split_kernel,
        turns,
        blks,
        [pl.BlockSpec((depth, 2, part), lambda b, t: (0, 0, b))],
        [block] * 2,
        [like((blks, depth, part))] * 2,
        [weights],
    )


def join_kernel(t_ref, u_ref, d_ref, o_ref):
    o_ref[:, 0, :] = u_ref[0].astype(F32)
    o_ref[:, 1, :] = d_ref[0].astype(F32)


def join_mlp(turns, up, down):
    blks, depth, part = up.shape
    block = pl.BlockSpec((1, depth, part), lambda b, t: (b, 0, 0))
    return call(
        join_kernel,
        turns,
        blks,
        [block] * 2,
        [pl.BlockSpec((depth, 2, part), lambda b, t: (0, 0, b))],
        [like((depth, 2, blks * part), F32)],
        [up, down],
    )[0]


def split_attn_kernel(t_ref, q_ref, k_ref, v_ref, o_ref, qkv_ref, out_ref):
    for i, ref in enumerate((q_ref, k_ref, v_ref)):
        qkv_ref[0, :, i * HD : (i + 1) * HD] = ref[...]
    out_ref[...] = o_ref[...]


def split_attn(turns, weights, plan, width):
    depth = weights.shape[0]
    heads = width // HD
    part = width // plan.blks

    def head(i):
        def index(b, t):
            h = b % plan.group // plan.share * plan.per_row + b // plan.group
            return 0, i * heads + h

        return pl.BlockSpec((depth, HD), index)

    return call(
        split_attn_kernel,
        turns,
        plan.blks,
        [head(i) for i in range(3)] + [pl.BlockSpec((depth, part), lambda b, t: (0, 3 * plan.blks + b))],
        [
            pl.BlockSpec((1, depth, 3 * HD), lambda b, t: (b, 0, 0)),
            pl.BlockSpec((depth, part), lambda b, t: (0, b)),
        ],
        [like((plan.blks, depth, 3 * HD)), like((depth, width))],
        [weights] * 4,
    )


def join_attn_kernel(plan, t_ref, qkv_ref, out_ref, o_ref):
    step = pl.program_id(0)
    heads = o_ref.shape[1] // HD

    @pl.when(step < 3)
    def _():
        at = pl.ds(pl.multiple_of(step * HD, HD), HD)
        for h in range(heads):
            first = h % plan.per_row * plan.group + h // plan.per_row * plan.share
            o_ref[:, h * HD : (h + 1) * HD] = sum(
                qkv_ref[first + i, :, at].astype(F32) for i in range(plan.share)
            )

    @pl.when(step == 3)
    def _():
        o_ref[...] = out_ref[...]


def join_attn(turns, qkv, out, plan):
    depth, width = out.shape
    return call(
        functools.partial(join_attn_kernel, plan),
        turns,
        4,
        [whole(qkv), whole(out)],
        [pl.BlockSpec((depth, width), lambda j, t: (0, j))],
        [like((depth, 4 * width), F32)],
        [qkv, out],
    )[0]


def pick_kernel(count, t_ref, *refs):
    pieces, outs = refs[:count], refs[count:]
    share = t_ref.shape[0] // len(outs)
    for n, out in enumerate(outs):
        for i in range(share):
            for k, piece in enumerate(pieces):

                @pl.when(t_ref[n * share + i] == k)
                def _(i=i, out=out, piece=piece):
                    out[...] = piece[...] if i == 0 else out[...] + piece[...]


def pick(table, pieces, count):
    return call(
        functools.partial(pick_kernel, len(pieces)),
        table,
        1,
        [whole(p) for p in pieces],
        [whole(pieces[0])] * count,
        [like(pieces[0].shape)] * count,
        pieces,
    )


def place_kernel(t_ref, *refs):
    *pieces, out_ref = refs
    for k, piece in enumerate(pieces):
        depth = piece.shape[0]
        out_ref[pl.ds(pl.multiple_of(t_ref[k] * depth, depth), depth)] = piece[...]


def place(table, pieces):
    depth, width = pieces[0].shape
    shape = like((len(pieces) * depth, width))
    return call(place_kernel, table, 1, [whole(p) for p in pieces], [whole(shape)], [shape], pieces)[0]


def norm_kernel(t_ref, x_ref, v_ref, a1_ref, a2_ref):
    field = x_ref[...].astype(F32)
    centred = field - jnp.mean(field, -1, keepdims=True)
    standard = centred * lax.rsqrt(jnp.mean(centred * centred, -1, keepdims=True) + EPSILON)
    a1_ref[...] = (standard * v_ref[0:1] + v_ref[1:2]).astype(BF)
    a2_ref[...] = (standard * v_ref[2:3] + v_ref[3:4]).astype(BF)


def norms(turns, x, vectors):
    count, width = x.shape
    return call(
        norm_kernel,
        turns,
        count // BLOCK,
        [rows_block(width), whole(vectors)],
        [rows_block(width)] * 2,
        [like(x.shape)] * 2,
        [x, vectors],
        20 * count * width,
    )


def times_pieces(left, pieces):
    out, start = None, 0
    for piece in pieces:
        depth = piece.shape[0]
        term = dot(left[:, start : start + depth], piece[...], 1, 0)
        out = term if out is None else out + term
        start += depth
    return out


def up_kernel(t_ref, a_ref, b_ref, *refs):
    pieces, (h_ref, s_ref) = refs[:-2], refs[-2:]
    pre = times_pieces(a_ref[...], pieces) + b_ref[...]
    cdf = 0.5 * (1.0 + lax.erf(pre * math.sqrt(0.5)))
    h_ref[...] = (pre * cdf).astype(BF)
    s_ref[...] = cdf + pre * (jnp.exp(-0.5 * pre * pre) * (1.0 / math.sqrt(2.0 * math.pi)))


def feed_up(turns, normed, bias, pieces):
    count, width = normed.shape
    hidden = bias.shape[0]
    return call(
        up_kernel,
        turns,
        count // BLOCK,
        [rows_block(width), pl.BlockSpec((1, hidden), lambda i, t: (0, 0))]
        + [whole(p) for p in pieces],
        [rows_block(hidden)] * 2,
        [like((count, hidden)), like((count, hidden), F32)],
        [normed, bias.reshape(1, hidden)] + pieces,
        2 * count * width * hidden,
    )


def slope_kernel(t_ref, g_ref, s_ref, *refs):
    pieces, (p_ref, sum_ref) = refs[:-2], refs[-2:]

    @pl.when(pl.program_id(0) == 0)
    def _():
        sum_ref[...] = jnp.zeros_like(sum_ref)

    grad = (times_pieces(g_ref[...], pieces) * s_ref[...]).astype(BF)
    p_ref[...] = grad
    sum_ref[...] += jnp.sum(grad.astype(F32), 0, keepdims=True)


def feed_slope(turns, grad, slope, pieces):
    count, width = grad.shape
    hidden = slope.shape[1]
    return call(
        slope_kernel,
        turns,
        count // BLOCK,
        [rows_block(width), rows_block(hidden)] + [whole(p) for p in pieces],
        [rows_block(hidden), pl.BlockSpec((1, hidden), lambda i, t: (0, 0))],
        [like((count, hidden)), like((1, hidden), F32)],
        [grad, slope] + pieces,
        2 * count * width * hidden,
    )


def lane_sum(field):
    return sum(field[:, i : i + LANES] for i in range(0, field.shape[1], LANES))


def weight_kernel(rows, layout, with_sums, t_ref, l_ref, r_ref, *refs):
    step = pl.program_id(0)
    depth = l_ref.shape[1]
    if with_sums:
        sum_ref, pieces, refs = refs[0], refs[1 : 1 + len(layout)], refs[1 + len(layout) :]
        parts_ref = refs[-1]
    grad = dot(l_ref[...], r_ref[...], 0, 0)
    for k in range(rows):

        @pl.when(step == k)
        def _(k=k):
            for i, (start, size) in enumerate(layout):
                if start // depth != k:
                    continue
                at = slice(start - k * depth, start - k * depth + size)
                refs[i][...] = grad[at].astype(BF)
                if with_sums:
                    piece = pieces[i][...].astype(F32)
                    parts_ref[0, at] = lane_sum(piece * grad[at])
                    parts_ref[1, at] = lane_sum(piece * sum_ref[...])


def weight_grad(turns, left, right, sums=None, pieces=()):
    rows = turns.shape[0]
    count, width = left.shape
    columns = right.shape[1]
    depth = width // rows
    layout = parts_of(rows, depth)
    out_shape = [like((size, columns)) for _, size in layout]
    out_specs = [whole(v) for v in out_shape]
    operands = [left, right]
    if pieces:
        operands += [sums] + pieces
        out_shape.append(like((2, width, LANES), F32))
        out_specs.append(pl.BlockSpec((2, depth, LANES), lambda k, t: (0, t[k], 0)))
    out = call(
        functools.partial(weight_kernel, rows, layout, bool(pieces)),
        turns,
        rows,
        [pl.BlockSpec((count, depth), lambda k, t: (0, k))] + [whole(v) for v in operands[1:]],
        out_specs,
        out_shape,
        operands,
        2 * count * width * columns,
    )
    if pieces:
        return out[:-1], out[-1]
    return out


def out_kernel(rows, t_ref, o_ref, g_ref, *refs):
    *outs, grad_ref = refs
    depth = outs[0].shape[0]
    grad_ref[...] = dot(o_ref[...], g_ref[...], 0, 0)
    for j, out in enumerate(outs):
        at = pl.multiple_of(t_ref[rows + j] * depth, depth)
        out[...] = grad_ref[pl.ds(at, depth)].astype(BF)


def out_grad(turns, places, attended, grad):
    rows, group = turns.shape[0], places.shape[0]
    count, width = grad.shape
    part = width // rows
    depth = HD // group
    return pl.pallas_call(
        functools.partial(out_kernel, rows),
        name="out_kernel",
        grid_spec=pltpu.PrefetchScalarGridSpec(
            num_scalar_prefetch=1,
            grid=(rows,),
            in_specs=[whole(attended), pl.BlockSpec((count, part), lambda k, t: (0, k))],
            out_specs=[pl.BlockSpec((depth, part), lambda k, t: (0, t[k]))] * group,
            scratch_shapes=[pltpu.VMEM((HD, part), F32)],
        ),
        out_shape=[like((depth, width))] * group,
        compiler_params=pltpu.CompilerParams(vmem_limit_bytes=VMEM_LIMIT),
        cost_estimate=pl.CostEstimate(
            flops=2 * count * width * HD // COST,
            bytes_accessed=2 * (count * (width + HD) + width * HD) // COST,
            transcendentals=0,
        ),
    )(jnp.concatenate([turns, places]), attended, grad)


def turned_columns(t_ref, w_ref, start, size, depth):
    at = t_ref[start // depth] * depth + start % depth
    return w_ref[:, pl.ds(pl.multiple_of(at, LANES), size)]


def sum_kernel(layout, depth, t_ref, h_ref, o_ref, w_ref, *refs):
    pieces, y_ref = refs[:-1], refs[-1]
    for piece, (start, size) in zip(pieces, layout):
        term = dot(h_ref[...], piece[...], 1, 1)
        term += dot(o_ref[...], turned_columns(t_ref, w_ref, start, size, depth), 1, 0)
        y_ref[:, start : start + size] = term.astype(BF)


def out_sum(turns, hidden, pieces, attended, out_w):
    rows = turns.shape[0]
    count = hidden.shape[0]
    width = out_w.shape[1]
    return call(
        functools.partial(sum_kernel, parts_of(rows, width // rows), width // rows),
        turns,
        count // BLOCK,
        [rows_block(hidden.shape[1]), rows_block(HD), whole(out_w)] + [whole(p) for p in pieces],
        [rows_block(width)],
        [like((count, width))],
        [hidden, attended, out_w] + pieces,
        2 * count * width * (hidden.shape[1] + HD),
    )[0]


def back_kernel(layout, t_ref, p_ref, q_ref, v_ref, *refs):
    pieces, c_ref = refs[:-1], refs[-1]
    count = len(layout)
    for up, qkv, (start, size) in zip(pieces[:count], pieces[count:], layout):
        cols = slice(start, start + size)
        term = dot(p_ref[...], up[...], 1, 1) * v_ref[2:3, cols]
        term += dot(q_ref[...], qkv[...], 1, 1) * v_ref[0:1, cols]
        c_ref[:, cols] = term.astype(BF)


def norm_back(turns, pre_grad, up_pieces, qkv_grad, qkv_pieces, vectors):
    rows = turns.shape[0]
    count = pre_grad.shape[0]
    width = vectors.shape[1]
    columns = pre_grad.shape[1] + qkv_grad.shape[1]
    return call(
        functools.partial(back_kernel, parts_of(rows, width // rows)),
        turns,
        count // BLOCK,
        [rows_block(pre_grad.shape[1]), rows_block(qkv_grad.shape[1]), whole(vectors)]
        + [whole(p) for p in up_pieces + qkv_pieces],
        [rows_block(width)],
        [like((count, width))],
        [pre_grad, qkv_grad, vectors] + up_pieces + qkv_pieces,
        2 * count * width * columns,
    )[0]


def turned(field, cosine, minus, plus):
    head = field[:, :LANES]
    half = ROT // 2
    head = (
        head * cosine
        + pltpu.roll(head, LANES - half, 1) * minus
        + pltpu.roll(head, half, 1) * plus
    )
    return jnp.concatenate([head, field[:, LANES:]], 1)


def allowed_pairs(length, dq_ref, dk_ref):
    spot = lax.broadcasted_iota(jnp.int32, (length, length), 0)
    other = lax.broadcasted_iota(jnp.int32, (length, length), 1)
    return (dq_ref[0] == dk_ref[0]) & (other <= spot)


def forward_kernel(t_ref, a_ref, b_ref, c_ref, m_ref, p_ref, dq_ref, dk_ref, *refs):
    pieces, (qkv_ref, o_ref, lse_ref) = refs[:-3], refs[-3:]
    qkv = times_pieces(a_ref[...], pieces) + b_ref[...]
    tables = c_ref[0], m_ref[0], p_ref[0]
    queries = (turned(qkv[:, :HD], *tables) * HD ** (-0.5)).astype(BF)
    keys = turned(qkv[:, HD : 2 * HD], *tables).astype(BF)
    values = qkv[:, 2 * HD :].astype(BF)
    for i, field in enumerate((queries, keys, values)):
        qkv_ref[:, i * HD : (i + 1) * HD] = field
    allowed = allowed_pairs(a_ref.shape[0], dq_ref, dk_ref)
    scores = jnp.where(allowed, dot(queries, keys, 1, 1), MASKED)
    largest = jnp.max(scores, -1, keepdims=True)
    weights = jnp.where(allowed, jnp.exp(scores - largest), 0.0)
    mass = jnp.sum(weights, -1, keepdims=True)
    o_ref[...] = dot((weights / mass).astype(BF), values, 1, 0).astype(BF)
    lse_ref[...] = largest + jnp.log(mass)


def backward_kernel(
    parts, t_ref, g_ref, w_ref, qkv_ref, o_ref, lse_ref, c_ref, m_ref, p_ref, dq_ref, dk_ref,
    grad_ref, sum_ref,
):
    queries, keys, values = (qkv_ref[:, i * HD : (i + 1) * HD] for i in range(3))
    tables = c_ref[0], -m_ref[0], -p_ref[0]
    depth = w_ref.shape[1] // parts
    heads_grad = None
    for k in range(parts):
        cols = slice(k * depth, (k + 1) * depth)
        term = dot(g_ref[:, cols], turned_columns(t_ref, w_ref, k * depth, depth, depth), 1, 1)
        heads_grad = term if heads_grad is None else heads_grad + term
    heads_grad = heads_grad.astype(BF)
    allowed = allowed_pairs(g_ref.shape[0], dq_ref, dk_ref)
    scores = jnp.where(allowed, dot(queries, keys, 1, 1), MASKED)
    weights = jnp.where(allowed, jnp.exp(scores - lse_ref[...]), 0.0)
    deltas = jnp.sum(heads_grad.astype(F32) * o_ref[...].astype(F32), -1, keepdims=True)
    score_grad = (weights * (dot(heads_grad, values, 1, 1) - deltas)).astype(BF)
    query_grad = dot(score_grad, keys, 1, 0) * HD ** (-0.5)
    key_grad = dot(score_grad, queries, 0, 0)
    value_grad = dot(weights.astype(BF), heads_grad, 0, 0)
    fields = turned(query_grad, *tables), turned(key_grad, *tables), value_grad

    @pl.when(pl.program_id(0) == 0)
    def _():
        sum_ref[...] = jnp.zeros_like(sum_ref)

    for i, field in enumerate(fields):
        field = field.astype(BF)
        cols = slice(i * HD, (i + 1) * HD)
        grad_ref[:, cols] = field
        sum_ref[:, cols] += jnp.sum(field.astype(F32), 0, keepdims=True)


def pair_specs(length):
    table = pl.BlockSpec((1, length, LANES), lambda r, t: (r, 0, 0))
    return [table] * 3 + [
        pl.BlockSpec((1, length, 1), lambda r, t: (r, 0, 0)),
        pl.BlockSpec((1, 1, length), lambda r, t: (r, 0, 0)),
    ]


def head_forward(turns, normed, bias, pairs, pieces, length):
    count, width = normed.shape
    columns = 3 * HD
    return call(
        forward_kernel,
        turns,
        count // length,
        [rows_block(width, length), pl.BlockSpec((1, columns), lambda r, t: (0, 0))]
        + pair_specs(length)
        + [whole(p) for p in pieces],
        [rows_block(columns, length), rows_block(HD, length), rows_block(1, length)],
        [like((count, columns)), like((count, HD)), like((count, 1), F32)],
        [normed, bias.reshape(1, columns)] + pairs + pieces,
        2 * count * (width * columns + 2 * length * HD),
    )


def head_backward(turns, grad, out_w, qkv, attended, lse, pairs, length):
    count, width = grad.shape
    columns = 3 * HD
    return call(
        functools.partial(backward_kernel, turns.shape[0]),
        turns,
        count // length,
        [
            rows_block(width, length),
            whole(out_w),
            rows_block(columns, length),
            rows_block(HD, length),
            rows_block(1, length),
        ]
        + pair_specs(length),
        [rows_block(columns, length), pl.BlockSpec((1, columns), lambda r, t: (0, 0))],
        [like((count, columns)), like((1, columns), F32)],
        [grad, out_w, qkv, attended, lse] + pairs,
        2 * count * (width * HD + 5 * length * HD),
    )


def finish_kernel(rows, with_norm, t_ref, x_ref, s_ref, o_ref, out_ref):
    depth = x_ref.shape[1] // rows
    term = s_ref[...].astype(F32)
    if with_norm:
        centred = x_ref[...].astype(F32)
        centred = centred - jnp.mean(centred, -1, keepdims=True)
        rstd = lax.rsqrt(jnp.mean(centred * centred, -1, keepdims=True) + EPSILON)
        centred = centred * rstd
        term = term - jnp.mean(term, -1, keepdims=True) - centred * jnp.mean(
            term * centred, -1, keepdims=True
        )
        field = o_ref[...].astype(F32) + rstd * term
    else:
        field = x_ref[...].astype(F32) + term + o_ref[4:5]
    for k in range(rows):
        at = pl.multiple_of(t_ref[k] * depth, LANES)
        out_ref[:, pl.ds(at, depth)] = field[:, k * depth : (k + 1) * depth].astype(BF)


def finish(turns, x, term, other, with_norm):
    return call(
        functools.partial(finish_kernel, turns.shape[0], with_norm),
        turns,
        1,
        [whole(v) for v in (x, term, other)],
        [whole(x)],
        [like(x.shape)],
        [x, term, other],
    )[0]


def shards(
    plan,
    tokens,
    attn_weights,
    mlp_weights,
    ln1_gain,
    ln1_bias,
    ln2_gain,
    ln2_bias,
    qkv_bias,
    dense_bias,
    up_bias,
    down_bias,
    doc_lengths,
    cotangent,
):
    row_count, shard_len, width = tokens.shape
    depth = attn_weights.shape[0]
    heads = width // HD
    rows, blks = plan.rows, plan.blks
    own_hidden = mlp_weights.shape[-1] // blks
    me = lax.axis_index("blk")
    length = shard_len * blks
    count = row_count * length
    head_of = me % plan.group // plan.share * plan.per_row + me // plan.group
    part = me % plan.share
    own_rows = row_count // plan.share
    row = lax.axis_index("row")
    turns = row ^ jnp.arange(rows, dtype=jnp.int32)
    places = me % plan.group ^ jnp.arange(plan.group, dtype=jnp.int32)

    def exchange(field):
        return lax.all_to_all(field, "blk", 0, 0)

    def collect(field):
        return exchange(field.reshape(blks, -1, field.shape[-1]))

    def gather_blocks(field):
        field = field.reshape(row_count, shard_len, width)
        return lax.all_gather(field, "blk", axis=1, tiled=True).reshape(count, width)

    def sum_blocks(field):
        field = field.reshape(row_count, length, width)
        field = lax.psum_scatter(field, "blk", scatter_dimension=1, tiled=True)
        return field.reshape(row_count * shard_len, width)

    zeros = jnp.zeros((3, width), F32)
    vectors = jnp.stack([ln1_gain, ln1_bias, ln2_gain, ln2_bias, dense_bias + down_bias])
    x_own, g_own, vectors, g_sum = turn_in(
        turns,
        tokens.reshape(row_count * shard_len, width),
        cotangent.reshape(row_count * shard_len, width),
        jnp.concatenate([vectors, zeros]),
    )
    qkv_send, out_own = split_attn(turns, attn_weights, plan, width)
    qkv_mine = exchange(qkv_send)
    out_send = pick(
        row ^ places // plan.share,
        [out_own] + [swap(out_own, "row", rows, k) for k in range(1, rows)],
        plan.group,
    )
    up_send, down_send = split_mlp(turns, after(mlp_weights, qkv_send), blks)
    up_mine = exchange(after(up_send, qkv_mine, out_send[0]))
    x_all = gather_blocks(after(x_own, qkv_mine))
    qkv_gather = Gather(qkv_mine.reshape(-1, 3 * HD), plan)
    out_got = [out_send[0]] + [
        swap_group(after(out_send[j], qkv_mine), plan, j) for j in range(1, plan.group)
    ]
    down_mine = exchange(after(down_send, up_mine, *out_got[1:], *qkv_gather.first()))
    out_w = place(places, out_got)
    up_gather = Gather(after(up_mine, *qkv_gather.first()).reshape(-1, own_hidden), plan)
    qkv_pieces = qkv_gather.finish(up_mine)
    joined = (down_mine, qkv_pieces[-2], qkv_pieces[-1], *up_gather.first())
    g_all = gather_blocks(after(g_own, *joined))
    down_gather = Gather(after(*joined).reshape(-1, own_hidden), plan)
    up_pieces = up_gather.finish(down_mine)
    normed1, normed2 = norms(turns, after(x_all, *joined), vectors)

    lengths = lax.dynamic_slice_in_dim(doc_lengths, part * own_rows, own_rows, 0)
    doc_ends = jnp.cumsum(lengths, axis=-1)
    starts = doc_ends - lengths
    spots = jnp.arange(length, dtype=jnp.int32)
    doc_ids = jnp.sum((spots[None, :, None] >= doc_ends[:, None, :]).astype(jnp.int32), -1)
    picked = doc_ids[:, :, None] == jnp.arange(lengths.shape[-1], dtype=jnp.int32)
    positions = spots - jnp.sum(jnp.where(picked, starts[:, None, :], 0), -1)
    lane = jnp.arange(LANES)
    inverse = 10000.0 ** (-2.0 * (lane % (ROT // 2)).astype(F32) / ROT)
    angles = positions.astype(F32)[..., None] * inverse
    sine = jnp.sin(angles)
    pairs = [
        jnp.where(lane < ROT, jnp.cos(angles), 1.0),
        jnp.where(lane < ROT // 2, -sine, 0.0),
        jnp.where((lane >= ROT // 2) & (lane < ROT), sine, 0.0),
        doc_ids[:, :, None],
        doc_ids[:, None, :],
    ]

    def own(field):
        if plan.share == 1:
            return field
        return lax.dynamic_slice_in_dim(field, part * own_rows * length, own_rows * length, 0)

    def spread(field):
        if plan.share == 1:
            return field
        blank = jnp.zeros((count, field.shape[1]), field.dtype)
        return lax.dynamic_update_slice_in_dim(blank, field, part * own_rows * length, 0)

    up_b = lax.dynamic_slice_in_dim(up_bias, me * own_hidden, own_hidden)
    qkv_b = lax.dynamic_index_in_dim(qkv_bias.reshape(3, heads, HD), head_of, 1, keepdims=False)
    own_normed1 = own(normed1)
    qkv, attended, lse = head_forward(
        turns, own_normed1, qkv_b.reshape(-1), pairs, qkv_pieces, length
    )
    joined = (attended, up_pieces[-2], up_pieces[-1], *down_gather.first())
    hidden, slope = feed_up(turns, after(normed2, *joined), up_b, up_pieces)
    down_pieces = down_gather.finish(*joined)
    out_term = out_sum(turns, hidden, down_pieces, spread(attended), out_w)
    out_total = sum_blocks(out_term)

    g_all = after(g_all, out_term)
    down_g = weight_grad(turns, g_all, hidden)
    down_scatter = Scatter(down_g, plan)
    pre_grad, up_sum = feed_slope(turns, after(g_all, down_g[0]), slope, down_pieces)
    down_second = down_scatter.second(turns, pre_grad)
    up_g, up_parts = weight_grad(
        turns, after(normed2, *down_second), pre_grad, up_sum, up_pieces
    )
    up_scatter = Scatter(up_g, plan)
    own_grad = own(after(g_all, up_g[0]))
    qkv_grad, qkv_sum = head_backward(
        turns, own_grad, out_w, qkv, attended, lse, pairs, length
    )
    down_total = down_scatter.finish(turns, qkv_grad)
    down_back = collect(down_total)
    norm_term = norm_back(
        turns, after(pre_grad, down_total, out_total), up_pieces, spread(qkv_grad), qkv_pieces, vectors
    )
    norm_total = sum_blocks(norm_term)
    up_second = up_scatter.second(turns, norm_term)
    qkv_g, qkv_parts = weight_grad(
        turns, after(own_normed1, *up_second), qkv_grad, qkv_sum, qkv_pieces
    )
    qkv_scatter = Scatter(qkv_g, plan)
    out_g = out_grad(turns, places, after(attended, qkv_g[0], down_back), own_grad)
    out_got = [out_g[0]] + [swap_group(out_g[j], plan, j) for j in range(1, plan.group)]
    up_total = up_scatter.finish(turns, out_g[0])
    up_back = collect(after(up_total, down_back))
    qkv_second = qkv_scatter.second(turns, out_g[0])
    qkv_total = qkv_scatter.finish(turns, up_total, *out_got[1:])
    qkv_back = collect(after(qkv_total, up_back, norm_total))
    holders = turns[:, None] * plan.share + jnp.arange(plan.share, dtype=jnp.int32)
    out_send = pick((me % plan.group ^ holders).reshape(-1), out_got, rows)
    out_back = out_send[0].astype(F32) + sum(
        swap(out_send[k], "row", rows, k).astype(F32) for k in range(1, rows)
    )

    terms = [after(v, norm_total) for v in (qkv_parts, up_parts)]
    terms = [jnp.sum(v, -1) for v in terms] + [g_sum, qkv_sum, up_sum]
    terms = [v.reshape(-1) for v in terms]
    used = sum(v.size for v in terms)
    terms.append(jnp.zeros((-used % (8 * LANES),), F32))
    sums = jnp.concatenate(terms).reshape(-1, LANES)
    sums = lax.all_gather(sums, ("row", "blk"), axis=0, tiled=True).reshape(rows, blks, -1)
    gain1, bias1, gain2, bias2, g_total = jnp.split(
        jnp.sum(sums[:, :, : 5 * width], (0, 1)), 5
    )
    sums = jnp.sum(sums[:, :, 5 * width : used], 0)
    qkv_bias_grad = sums[:, : 3 * HD].reshape(plan.per_row, rows, plan.share, 3, HD)
    qkv_bias_grad = jnp.sum(qkv_bias_grad, 2).transpose(2, 1, 0, 3).reshape(-1)
    up_bias_grad = sums[:, 3 * HD :].reshape(-1)

    layer_out = finish(turns, x_own, out_total, vectors, False)
    tokens_grad = finish(turns, x_own, norm_total, g_own, True)
    return (
        layer_out.reshape(tokens.shape),
        tokens_grad.reshape(tokens.shape),
        join_attn(turns, qkv_back, out_back, plan),
        join_mlp(turns, up_back, down_back),
        (gain1 - ln1_bias * bias1) / ln1_gain,
        bias1,
        (gain2 - ln2_bias * bias2) / ln2_gain,
        bias2,
        qkv_bias_grad,
        g_total,
        up_bias_grad,
        g_total,
    )


def solution(mesh):
    rows, blks = mesh.shape["row"], mesh.shape["blk"]
    vector = P()
    tokens = P("row", "blk", None)
    attn = P(("row", "blk"), None)
    mlp = P(("row", "blk"), None, None)

    def run(*arrays):
        plan = Plan(rows, blks, arrays[0].shape[-1] // HD)
        return jax.shard_map(
            functools.partial(shards, plan),
            mesh=mesh,
            in_specs=(tokens, attn, mlp) + (vector,) * 8 + (P("row", None), tokens),
            out_specs=(tokens, tokens, attn, mlp) + (vector,) * 8,
            check_vma=False,
        )(*arrays)

    return run
```

```python
import functools
import math

import jax
import jax.numpy as jnp
import numpy as np
from jax import lax
from jax.experimental import pallas as pl
from jax.experimental.pallas import tpu as pltpu
from jax.sharding import PartitionSpec as P

HD = 256
ROT = 64
LANES = 128
BLOCK = 256
EPSILON = 1e-05
MASKED = -1e30
BF = jnp.bfloat16
F32 = jnp.float32
COST = 100
VMEM_LIMIT = 56 * 2**20


class Plan:
    def __init__(self, rows, blks, heads):
        self.rows = rows
        self.blks = blks
        self.share = blks // heads
        self.per_row = heads // rows
        self.group = blks // self.per_row
        self.groups = [
            list(range(i * self.group, (i + 1) * self.group)) for i in range(self.per_row)
        ]


def after(field, *others):
    return lax.optimization_barrier((field,) + others)[0] if others else field


def swap(field, axis, size, bit):
    return lax.ppermute(field, axis, [(i, i ^ bit) for i in range(size)])


def bits_of(size):
    return [1 << i for i in range(size.bit_length() - 1)]


def swap_group(field, plan, bits):
    return lax.ppermute(field, "blk", [(i, i ^ bits) for i in range(plan.blks)])


def near(k):
    return k & (k - 1) == 0


def orders(plan):
    bits = bits_of(plan.rows)
    return bits, bits[::-1]


def half_of(field, h):
    middle = field.shape[0] // 2
    return field[h * middle : (h + 1) * middle]


def parts_of(rows, depth):
    out = []
    for k in range(rows):
        if near(k):
            out.append((k * depth, depth))
        else:
            out += [(k * depth, depth // 2), (k * depth + depth // 2, depth // 2)]
    return out


class Gather:
    def __init__(self, own, plan):
        self.plan = plan
        self.whole = {0: own}
        for bit in bits_of(plan.rows):
            self.whole[bit] = swap(own, "row", plan.rows, bit)

    def first(self):
        return [v for k, v in self.whole.items() if k]

    def finish(self, *others):
        plan = self.plan
        halves = []
        for h, order in enumerate(orders(plan)):
            got = {0: None}
            for bit in order:
                for k in list(got):
                    if k == 0:
                        got[bit] = half_of(after(self.whole[bit], *others), h)
                    else:
                        got[k ^ bit] = swap(got[k], "row", plan.rows, bit)
            halves.append(got)
        out = []
        for k in range(plan.rows):
            out += [self.whole[k]] if near(k) else [half[k] for half in halves]
        return out


class Scatter:
    def __init__(self, pieces, plan):
        self.plan = plan
        pieces = iter(pieces)
        self.whole, far = {}, [{}, {}]
        for k in range(plan.rows):
            if near(k):
                self.whole[k] = next(pieces)
            else:
                far[0][k], far[1][k] = next(pieces), next(pieces)
        self.got = []
        for h, order in enumerate(orders(plan)):
            held = far[h]
            for bit in order:
                for k in [k for k in held if k & bit]:
                    term = swap(held.pop(k), "row", plan.rows, bit)
                    if near(k ^ bit):
                        self.got.append((k ^ bit, h, term))
                    else:
                        held[k ^ bit] = (held[k ^ bit].astype(F32) + term.astype(F32)).astype(BF)

    def first(self):
        return [term for _, _, term in self.got]

    def second(self, turns, *others):
        got = [(k, h, after(term, *others)) for k, h, term in self.got]
        while got:
            first = {}
            for item in got:
                first.setdefault(item[0], item)
            got = [item for item in got if all(item is not v for v in first.values())]
            sums = add_halves(turns, [(self.whole[k], h, term) for k, h, term in first.values()])
            self.whole.update(zip(first, sums))
        return [v for k, v in self.whole.items() if k]

    def finish(self, turns, *others):
        terms = [after(self.whole[0], *others)]
        for bit in bits_of(self.plan.rows):
            terms.append(swap(self.whole[bit], "row", self.plan.rows, bit))
        return add_wholes(turns, terms)


def dot(left, right, left_dim, right_dim):
    return lax.dot_general(
        left, right, (((left_dim,), (right_dim,)), ((), ())), preferred_element_type=F32
    )


def whole(array):
    return pl.BlockSpec(array.shape, lambda *i: (0,) * len(array.shape))


def like(shape, kind=BF):
    return jax.ShapeDtypeStruct(shape, kind)


def call(body, turns, grid, in_specs, out_specs, out_shape, operands, flops=0):
    moved = sum(v.size * v.dtype.itemsize for v in operands)
    moved += sum(math.prod(v.shape) * jnp.dtype(v.dtype).itemsize for v in out_shape)
    return pl.pallas_call(
        body,
        name=getattr(body, "func", body).__name__,
        grid_spec=pltpu.PrefetchScalarGridSpec(
            num_scalar_prefetch=1, grid=(grid,), in_specs=in_specs, out_specs=out_specs
        ),
        out_shape=out_shape,
        compiler_params=pltpu.CompilerParams(vmem_limit_bytes=VMEM_LIMIT),
        cost_estimate=pl.CostEstimate(
            flops=flops // COST, bytes_accessed=moved // COST, transcendentals=0
        ),
    )(turns, *operands)


def rows_block(columns, block=BLOCK):
    return pl.BlockSpec((block, columns), lambda i, t: (i, 0))


def halves_kernel(count, t_ref, *refs):
    for i in range(count):
        into, term, out = refs[i], refs[count + i], refs[2 * count + i]
        out[...] = (into[...].astype(F32) + term[...].astype(F32)).astype(BF)


def add_halves(turns, items):
    count = len(items)
    depth, width = items[0][2].shape
    parts = 2
    into = [pl.BlockSpec((depth, width // parts), lambda i, t, h=h: (h, i)) for _, h, _ in items]
    term = pl.BlockSpec((depth, width // parts), lambda i, t: (0, i))
    return pl.pallas_call(
        functools.partial(halves_kernel, count),
        name="halves_kernel",
        grid_spec=pltpu.PrefetchScalarGridSpec(
            num_scalar_prefetch=1, grid=(parts,), in_specs=into + [term] * count, out_specs=into
        ),
        out_shape=[like(v.shape) for v, _, _ in items],
        input_output_aliases={1 + i: i for i in range(count)},
        compiler_params=pltpu.CompilerParams(vmem_limit_bytes=VMEM_LIMIT),
        cost_estimate=pl.CostEstimate(
            flops=0, bytes_accessed=6 * depth * width * count // COST, transcendentals=0
        ),
    )(turns, *[v for v, _, _ in items], *[v for _, _, v in items])


def wholes_kernel(t_ref, *refs):
    refs[-1][...] = sum(ref[...].astype(F32) for ref in refs[:-1]).astype(BF)


def add_wholes(turns, terms):
    depth, width = terms[0].shape
    block = rows_block(width, depth // 4)
    shape = like((depth, width))
    return call(wholes_kernel, turns, 4, [block] * len(terms), [block], [shape], terms)[0]


def turn_kernel(t_ref, x_ref, g_ref, v_ref, xo_ref, go_ref, vo_ref, s_ref):
    xo_ref[...] = x_ref[...]
    go_ref[...] = g_ref[...]
    vo_ref[...] = v_ref[...]
    s_ref[...] = jnp.sum(g_ref[...].astype(F32), 0, keepdims=True)


def turn_in(turns, x, g, vectors):
    rows = turns.shape[0]
    part = x.shape[1] // rows

    def specs(array, turned):
        index = (lambda k, t: (0, t[k])) if turned else (lambda k, t: (0, k))
        return pl.BlockSpec((array.shape[0], part), index)

    total_shape = like((1, x.shape[1]), F32)
    return call(
        turn_kernel,
        turns,
        rows,
        [specs(v, True) for v in (x, g, vectors)],
        [specs(v, False) for v in (x, g, vectors)] + [specs(total_shape, True)],
        [like(v.shape, v.dtype) for v in (x, g, vectors)] + [total_shape],
        [x, g, vectors],
    )


def split_kernel(t_ref, w_ref, u_ref, d_ref):
    u_ref[0] = w_ref[:, 0, :]
    d_ref[0] = w_ref[:, 1, :]


def split_mlp(turns, weights, blks):
    depth, _, hidden = weights.shape
    part = hidden // blks
    block = pl.BlockSpec((1, depth, part), lambda b, t: (b, 0, 0))
    return call(
        split_kernel,
        turns,
        blks,
        [pl.BlockSpec((depth, 2, part), lambda b, t: (0, 0, b))],
        [block] * 2,
        [like((blks, depth, part))] * 2,
        [weights],
    )


def join_kernel(t_ref, u_ref, d_ref, o_ref):
    o_ref[:, 0, :] = u_ref[0].astype(F32)
    o_ref[:, 1, :] = d_ref[0].astype(F32)


def join_mlp(turns, up, down):
    blks, depth, part = up.shape
    block = pl.BlockSpec((1, depth, part), lambda b, t: (b, 0, 0))
    return call(
        join_kernel,
        turns,
        blks,
        [block] * 2,
        [pl.BlockSpec((depth, 2, part), lambda b, t: (0, 0, b))],
        [like((depth, 2, blks * part), F32)],
        [up, down],
    )[0]


def split_attn_kernel(t_ref, q_ref, k_ref, v_ref, o_ref, qkv_ref, out_ref):
    for i, ref in enumerate((q_ref, k_ref, v_ref)):
        qkv_ref[0, :, i * HD : (i + 1) * HD] = ref[...]
    out_ref[...] = o_ref[...]


def split_attn(turns, weights, plan, width):
    depth = weights.shape[0]
    heads = width // HD
    part = width // plan.blks

    def head(i):
        def index(b, t):
            h = b % plan.group // plan.share * plan.per_row + b // plan.group
            return 0, i * heads + h

        return pl.BlockSpec((depth, HD), index)

    return call(
        split_attn_kernel,
        turns,
        plan.blks,
        [head(i) for i in range(3)] + [pl.BlockSpec((depth, part), lambda b, t: (0, 3 * plan.blks + b))],
        [
            pl.BlockSpec((1, depth, 3 * HD), lambda b, t: (b, 0, 0)),
            pl.BlockSpec((depth, part), lambda b, t: (0, b)),
        ],
        [like((plan.blks, depth, 3 * HD)), like((depth, width))],
        [weights] * 4,
    )


def join_attn_kernel(plan, t_ref, qkv_ref, out_ref, o_ref):
    step = pl.program_id(0)
    heads = o_ref.shape[1] // HD

    @pl.when(step < 3)
    def _():
        at = pl.ds(pl.multiple_of(step * HD, HD), HD)
        for h in range(heads):
            first = h % plan.per_row * plan.group + h // plan.per_row * plan.share
            o_ref[:, h * HD : (h + 1) * HD] = sum(
                qkv_ref[first + i, :, at].astype(F32) for i in range(plan.share)
            )

    @pl.when(step == 3)
    def _():
        o_ref[...] = out_ref[...]


def join_attn(turns, qkv, out, plan):
    depth, width = out.shape
    return call(
        functools.partial(join_attn_kernel, plan),
        turns,
        4,
        [whole(qkv), whole(out)],
        [pl.BlockSpec((depth, width), lambda j, t: (0, j))],
        [like((depth, 4 * width), F32)],
        [qkv, out],
    )[0]


def pick_kernel(count, t_ref, *refs):
    pieces, outs = refs[:count], refs[count:]
    share = t_ref.shape[0] // len(outs)
    for n, out in enumerate(outs):
        for i in range(share):
            for k, piece in enumerate(pieces):

                @pl.when(t_ref[n * share + i] == k)
                def _(i=i, out=out, piece=piece):
                    out[...] = piece[...] if i == 0 else out[...] + piece[...]


def pick(table, pieces, count):
    return call(
        functools.partial(pick_kernel, len(pieces)),
        table,
        1,
        [whole(p) for p in pieces],
        [whole(pieces[0])] * count,
        [like(pieces[0].shape)] * count,
        pieces,
    )


def place_kernel(t_ref, *refs):
    *pieces, out_ref = refs
    for k, piece in enumerate(pieces):
        depth = piece.shape[0]
        out_ref[pl.ds(pl.multiple_of(t_ref[k] * depth, depth), depth)] = piece[...]


def place(table, pieces):
    depth, width = pieces[0].shape
    shape = like((len(pieces) * depth, width))
    return call(place_kernel, table, 1, [whole(p) for p in pieces], [whole(shape)], [shape], pieces)[0]


def norm_kernel(t_ref, x_ref, v_ref, a1_ref, a2_ref):
    field = x_ref[...].astype(F32)
    centred = field - jnp.mean(field, -1, keepdims=True)
    standard = centred * lax.rsqrt(jnp.mean(centred * centred, -1, keepdims=True) + EPSILON)
    a1_ref[...] = (standard * v_ref[0:1] + v_ref[1:2]).astype(BF)
    a2_ref[...] = (standard * v_ref[2:3] + v_ref[3:4]).astype(BF)


def norms(turns, x, vectors):
    count, width = x.shape
    return call(
        norm_kernel,
        turns,
        count // BLOCK,
        [rows_block(width), whole(vectors)],
        [rows_block(width)] * 2,
        [like(x.shape)] * 2,
        [x, vectors],
        20 * count * width,
    )


def times_pieces(left, pieces):
    out, start = None, 0
    for piece in pieces:
        depth = piece.shape[0]
        term = dot(left[:, start : start + depth], piece[...], 1, 0)
        out = term if out is None else out + term
        start += depth
    return out


def up_kernel(t_ref, a_ref, b_ref, *refs):
    pieces, (h_ref, s_ref) = refs[:-2], refs[-2:]
    pre = times_pieces(a_ref[...], pieces) + b_ref[...]
    cdf = 0.5 * (1.0 + lax.erf(pre * math.sqrt(0.5)))
    h_ref[...] = (pre * cdf).astype(BF)
    s_ref[...] = cdf + pre * (jnp.exp(-0.5 * pre * pre) * (1.0 / math.sqrt(2.0 * math.pi)))


def feed_up(turns, normed, bias, pieces):
    count, width = normed.shape
    hidden = bias.shape[0]
    return call(
        up_kernel,
        turns,
        count // BLOCK,
        [rows_block(width), pl.BlockSpec((1, hidden), lambda i, t: (0, 0))]
        + [whole(p) for p in pieces],
        [rows_block(hidden)] * 2,
        [like((count, hidden)), like((count, hidden), F32)],
        [normed, bias.reshape(1, hidden)] + pieces,
        2 * count * width * hidden,
    )


def slope_kernel(t_ref, g_ref, s_ref, *refs):
    pieces, (p_ref, sum_ref) = refs[:-2], refs[-2:]

    @pl.when(pl.program_id(0) == 0)
    def _():
        sum_ref[...] = jnp.zeros_like(sum_ref)

    grad = (times_pieces(g_ref[...], pieces) * s_ref[...]).astype(BF)
    p_ref[...] = grad
    sum_ref[...] += jnp.sum(grad.astype(F32), 0, keepdims=True)


def feed_slope(turns, grad, slope, pieces):
    count, width = grad.shape
    hidden = slope.shape[1]
    return call(
        slope_kernel,
        turns,
        count // BLOCK,
        [rows_block(width), rows_block(hidden)] + [whole(p) for p in pieces],
        [rows_block(hidden), pl.BlockSpec((1, hidden), lambda i, t: (0, 0))],
        [like((count, hidden)), like((1, hidden), F32)],
        [grad, slope] + pieces,
        2 * count * width * hidden,
    )


def lane_sum(field):
    return sum(field[:, i : i + LANES] for i in range(0, field.shape[1], LANES))


def weight_kernel(rows, layout, with_sums, t_ref, l_ref, r_ref, *refs):
    step = pl.program_id(0)
    depth = l_ref.shape[1]
    if with_sums:
        sum_ref, pieces, refs = refs[0], refs[1 : 1 + len(layout)], refs[1 + len(layout) :]
        parts_ref = refs[-1]
    grad = dot(l_ref[...], r_ref[...], 0, 0)
    for k in range(rows):

        @pl.when(step == k)
        def _(k=k):
            for i, (start, size) in enumerate(layout):
                if start // depth != k:
                    continue
                at = slice(start - k * depth, start - k * depth + size)
                refs[i][...] = grad[at].astype(BF)
                if with_sums:
                    piece = pieces[i][...].astype(F32)
                    parts_ref[0, at] = lane_sum(piece * grad[at])
                    parts_ref[1, at] = lane_sum(piece * sum_ref[...])


def weight_grad(turns, left, right, sums=None, pieces=()):
    rows = turns.shape[0]
    count, width = left.shape
    columns = right.shape[1]
    depth = width // rows
    layout = parts_of(rows, depth)
    out_shape = [like((size, columns)) for _, size in layout]
    out_specs = [whole(v) for v in out_shape]
    operands = [left, right]
    if pieces:
        operands += [sums] + pieces
        out_shape.append(like((2, width, LANES), F32))
        out_specs.append(pl.BlockSpec((2, depth, LANES), lambda k, t: (0, t[k], 0)))
    out = call(
        functools.partial(weight_kernel, rows, layout, bool(pieces)),
        turns,
        rows,
        [pl.BlockSpec((count, depth), lambda k, t: (0, k))] + [whole(v) for v in operands[1:]],
        out_specs,
        out_shape,
        operands,
        2 * count * width * columns,
    )
    if pieces:
        return out[:-1], out[-1]
    return out


def out_kernel(rows, t_ref, o_ref, g_ref, *refs):
    *outs, grad_ref = refs
    depth = outs[0].shape[0]
    grad_ref[...] = dot(o_ref[...], g_ref[...], 0, 0)
    for j, out in enumerate(outs):
        at = pl.multiple_of(t_ref[rows + j] * depth, depth)
        out[...] = grad_ref[pl.ds(at, depth)].astype(BF)


def out_grad(turns, places, attended, grad):
    rows, group = turns.shape[0], places.shape[0]
    count, width = grad.shape
    part = width // rows
    depth = HD // group
    return pl.pallas_call(
        functools.partial(out_kernel, rows),
        name="out_kernel",
        grid_spec=pltpu.PrefetchScalarGridSpec(
            num_scalar_prefetch=1,
            grid=(rows,),
            in_specs=[whole(attended), pl.BlockSpec((count, part), lambda k, t: (0, k))],
            out_specs=[pl.BlockSpec((depth, part), lambda k, t: (0, t[k]))] * group,
            scratch_shapes=[pltpu.VMEM((HD, part), F32)],
        ),
        out_shape=[like((depth, width))] * group,
        compiler_params=pltpu.CompilerParams(vmem_limit_bytes=VMEM_LIMIT),
        cost_estimate=pl.CostEstimate(
            flops=2 * count * width * HD // COST,
            bytes_accessed=2 * (count * (width + HD) + width * HD) // COST,
            transcendentals=0,
        ),
    )(jnp.concatenate([turns, places]), attended, grad)


def turned_columns(t_ref, w_ref, start, size, depth):
    at = t_ref[start // depth] * depth + start % depth
    return w_ref[:, pl.ds(pl.multiple_of(at, LANES), size)]


def sum_kernel(layout, depth, t_ref, h_ref, o_ref, w_ref, *refs):
    pieces, y_ref = refs[:-1], refs[-1]
    for piece, (start, size) in zip(pieces, layout):
        term = dot(h_ref[...], piece[...], 1, 1)
        term += dot(o_ref[...], turned_columns(t_ref, w_ref, start, size, depth), 1, 0)
        y_ref[:, start : start + size] = term.astype(BF)


def out_sum(turns, hidden, pieces, attended, out_w):
    rows = turns.shape[0]
    count = hidden.shape[0]
    width = out_w.shape[1]
    return call(
        functools.partial(sum_kernel, parts_of(rows, width // rows), width // rows),
        turns,
        count // BLOCK,
        [rows_block(hidden.shape[1]), rows_block(HD), whole(out_w)] + [whole(p) for p in pieces],
        [rows_block(width)],
        [like((count, width))],
        [hidden, attended, out_w] + pieces,
        2 * count * width * (hidden.shape[1] + HD),
    )[0]


def back_kernel(layout, t_ref, p_ref, q_ref, v_ref, *refs):
    pieces, c_ref = refs[:-1], refs[-1]
    count = len(layout)
    for up, qkv, (start, size) in zip(pieces[:count], pieces[count:], layout):
        cols = slice(start, start + size)
        term = dot(p_ref[...], up[...], 1, 1) * v_ref[2:3, cols]
        term += dot(q_ref[...], qkv[...], 1, 1) * v_ref[0:1, cols]
        c_ref[:, cols] = term.astype(BF)


def norm_back(turns, pre_grad, up_pieces, qkv_grad, qkv_pieces, vectors):
    rows = turns.shape[0]
    count = pre_grad.shape[0]
    width = vectors.shape[1]
    columns = pre_grad.shape[1] + qkv_grad.shape[1]
    return call(
        functools.partial(back_kernel, parts_of(rows, width // rows)),
        turns,
        count // BLOCK,
        [rows_block(pre_grad.shape[1]), rows_block(qkv_grad.shape[1]), whole(vectors)]
        + [whole(p) for p in up_pieces + qkv_pieces],
        [rows_block(width)],
        [like((count, width))],
        [pre_grad, qkv_grad, vectors] + up_pieces + qkv_pieces,
        2 * count * width * columns,
    )[0]


def turned(field, cosine, minus, plus):
    head = field[:, :LANES]
    half = ROT // 2
    head = (
        head * cosine
        + pltpu.roll(head, LANES - half, 1) * minus
        + pltpu.roll(head, half, 1) * plus
    )
    return jnp.concatenate([head, field[:, LANES:]], 1)


def allowed_pairs(length, dq_ref, dk_ref):
    spot = lax.broadcasted_iota(jnp.int32, (length, length), 0)
    other = lax.broadcasted_iota(jnp.int32, (length, length), 1)
    return (dq_ref[0] == dk_ref[0]) & (other <= spot)


def forward_kernel(t_ref, a_ref, b_ref, c_ref, m_ref, p_ref, dq_ref, dk_ref, *refs):
    pieces, (qkv_ref, o_ref, lse_ref) = refs[:-3], refs[-3:]
    qkv = times_pieces(a_ref[...], pieces) + b_ref[...]
    tables = c_ref[0], m_ref[0], p_ref[0]
    queries = (turned(qkv[:, :HD], *tables) * HD ** (-0.5)).astype(BF)
    keys = turned(qkv[:, HD : 2 * HD], *tables).astype(BF)
    values = qkv[:, 2 * HD :].astype(BF)
    for i, field in enumerate((queries, keys, values)):
        qkv_ref[:, i * HD : (i + 1) * HD] = field
    allowed = allowed_pairs(a_ref.shape[0], dq_ref, dk_ref)
    scores = jnp.where(allowed, dot(queries, keys, 1, 1), MASKED)
    largest = jnp.max(scores, -1, keepdims=True)
    weights = jnp.where(allowed, jnp.exp(scores - largest), 0.0)
    mass = jnp.sum(weights, -1, keepdims=True)
    o_ref[...] = dot((weights / mass).astype(BF), values, 1, 0).astype(BF)
    lse_ref[...] = largest + jnp.log(mass)


def backward_kernel(
    parts, t_ref, g_ref, w_ref, qkv_ref, o_ref, lse_ref, c_ref, m_ref, p_ref, dq_ref, dk_ref,
    grad_ref, sum_ref,
):
    queries, keys, values = (qkv_ref[:, i * HD : (i + 1) * HD] for i in range(3))
    tables = c_ref[0], -m_ref[0], -p_ref[0]
    depth = w_ref.shape[1] // parts
    heads_grad = None
    for k in range(parts):
        cols = slice(k * depth, (k + 1) * depth)
        term = dot(g_ref[:, cols], turned_columns(t_ref, w_ref, k * depth, depth, depth), 1, 1)
        heads_grad = term if heads_grad is None else heads_grad + term
    heads_grad = heads_grad.astype(BF)
    allowed = allowed_pairs(g_ref.shape[0], dq_ref, dk_ref)
    scores = jnp.where(allowed, dot(queries, keys, 1, 1), MASKED)
    weights = jnp.where(allowed, jnp.exp(scores - lse_ref[...]), 0.0)
    deltas = jnp.sum(heads_grad.astype(F32) * o_ref[...].astype(F32), -1, keepdims=True)
    score_grad = (weights * (dot(heads_grad, values, 1, 1) - deltas)).astype(BF)
    query_grad = dot(score_grad, keys, 1, 0) * HD ** (-0.5)
    key_grad = dot(score_grad, queries, 0, 0)
    value_grad = dot(weights.astype(BF), heads_grad, 0, 0)
    fields = turned(query_grad, *tables), turned(key_grad, *tables), value_grad

    @pl.when(pl.program_id(0) == 0)
    def _():
        sum_ref[...] = jnp.zeros_like(sum_ref)

    for i, field in enumerate(fields):
        field = field.astype(BF)
        cols = slice(i * HD, (i + 1) * HD)
        grad_ref[:, cols] = field
        sum_ref[:, cols] += jnp.sum(field.astype(F32), 0, keepdims=True)


def pair_specs(length):
    table = pl.BlockSpec((1, length, LANES), lambda r, t: (r, 0, 0))
    return [table] * 3 + [
        pl.BlockSpec((1, length, 1), lambda r, t: (r, 0, 0)),
        pl.BlockSpec((1, 1, length), lambda r, t: (r, 0, 0)),
    ]


def head_forward(turns, normed, bias, pairs, pieces, length):
    count, width = normed.shape
    columns = 3 * HD
    return call(
        forward_kernel,
        turns,
        count // length,
        [rows_block(width, length), pl.BlockSpec((1, columns), lambda r, t: (0, 0))]
        + pair_specs(length)
        + [whole(p) for p in pieces],
        [rows_block(columns, length), rows_block(HD, length), rows_block(1, length)],
        [like((count, columns)), like((count, HD)), like((count, 1), F32)],
        [normed, bias.reshape(1, columns)] + pairs + pieces,
        2 * count * (width * columns + 2 * length * HD),
    )


def head_backward(turns, grad, out_w, qkv, attended, lse, pairs, length):
    count, width = grad.shape
    columns = 3 * HD
    return call(
        functools.partial(backward_kernel, turns.shape[0]),
        turns,
        count // length,
        [
            rows_block(width, length),
            whole(out_w),
            rows_block(columns, length),
            rows_block(HD, length),
            rows_block(1, length),
        ]
        + pair_specs(length),
        [rows_block(columns, length), pl.BlockSpec((1, columns), lambda r, t: (0, 0))],
        [like((count, columns)), like((1, columns), F32)],
        [grad, out_w, qkv, attended, lse] + pairs,
        2 * count * (width * HD + 5 * length * HD),
    )


def finish_kernel(rows, with_norm, t_ref, x_ref, s_ref, o_ref, out_ref):
    depth = x_ref.shape[1] // rows
    term = s_ref[...].astype(F32)
    if with_norm:
        centred = x_ref[...].astype(F32)
        centred = centred - jnp.mean(centred, -1, keepdims=True)
        rstd = lax.rsqrt(jnp.mean(centred * centred, -1, keepdims=True) + EPSILON)
        centred = centred * rstd
        term = term - jnp.mean(term, -1, keepdims=True) - centred * jnp.mean(
            term * centred, -1, keepdims=True
        )
        field = o_ref[...].astype(F32) + rstd * term
    else:
        field = x_ref[...].astype(F32) + term + o_ref[4:5]
    for k in range(rows):
        at = pl.multiple_of(t_ref[k] * depth, LANES)
        out_ref[:, pl.ds(at, depth)] = field[:, k * depth : (k + 1) * depth].astype(BF)


def finish(turns, x, term, other, with_norm):
    return call(
        functools.partial(finish_kernel, turns.shape[0], with_norm),
        turns,
        1,
        [whole(v) for v in (x, term, other)],
        [whole(x)],
        [like(x.shape)],
        [x, term, other],
    )[0]


def shards(
    plan,
    tokens,
    attn_weights,
    mlp_weights,
    ln1_gain,
    ln1_bias,
    ln2_gain,
    ln2_bias,
    qkv_bias,
    dense_bias,
    up_bias,
    down_bias,
    doc_lengths,
    cotangent,
):
    row_count, shard_len, width = tokens.shape
    depth = attn_weights.shape[0]
    heads = width // HD
    rows, blks = plan.rows, plan.blks
    own_hidden = mlp_weights.shape[-1] // blks
    me = lax.axis_index("blk")
    length = shard_len * blks
    count = row_count * length
    head_of = me % plan.group // plan.share * plan.per_row + me // plan.group
    part = me % plan.share
    own_rows = row_count // plan.share
    row = lax.axis_index("row")
    turns = row ^ jnp.arange(rows, dtype=jnp.int32)
    places = me % plan.group ^ jnp.arange(plan.group, dtype=jnp.int32)

    def exchange(field):
        return lax.all_to_all(field, "blk", 0, 0)

    def collect(field):
        return exchange(field.reshape(blks, -1, field.shape[-1]))

    def gather_blocks(field):
        field = field.reshape(row_count, shard_len, width)
        return lax.all_gather(field, "blk", axis=1, tiled=True).reshape(count, width)

    def sum_blocks(field):
        field = field.reshape(row_count, length, width)
        field = lax.psum_scatter(field, "blk", scatter_dimension=1, tiled=True)
        return field.reshape(row_count * shard_len, width)

    zeros = jnp.zeros((3, width), F32)
    vectors = jnp.stack([ln1_gain, ln1_bias, ln2_gain, ln2_bias, dense_bias + down_bias])
    x_own, g_own, vectors, g_sum = turn_in(
        turns,
        tokens.reshape(row_count * shard_len, width),
        cotangent.reshape(row_count * shard_len, width),
        jnp.concatenate([vectors, zeros]),
    )
    qkv_send, out_own = split_attn(turns, attn_weights, plan, width)
    qkv_mine = exchange(qkv_send)
    out_send = pick(
        row ^ places // plan.share,
        [out_own] + [swap(out_own, "row", rows, k) for k in range(1, rows)],
        plan.group,
    )
    up_send, down_send = split_mlp(turns, after(mlp_weights, qkv_send), blks)
    qkv_mine, up_send, *out_send = lax.optimization_barrier((qkv_mine, up_send, *out_send))
    up_mine = exchange(up_send)
    qkv_gather = Gather(qkv_mine.reshape(-1, 3 * HD), plan)
    out_got = [out_send[0]] + [swap_group(out_send[j], plan, j) for j in range(1, plan.group)]
    joined = (up_mine, *out_got[1:], *qkv_gather.first())
    up_mine = after(*joined)
    x_all = gather_blocks(after(x_own, *joined))
    down_mine = exchange(after(down_send, *joined))
    out_w = place(places, out_got)
    up_gather = Gather(up_mine.reshape(-1, own_hidden), plan)
    qkv_pieces = qkv_gather.finish(up_mine)
    joined = (down_mine, qkv_pieces[-2], qkv_pieces[-1], *up_gather.first())
    g_all = gather_blocks(after(g_own, *joined))
    down_gather = Gather(after(*joined).reshape(-1, own_hidden), plan)
    up_pieces = up_gather.finish(down_mine)
    normed1, normed2 = norms(turns, after(x_all, *joined), vectors)

    lengths = lax.dynamic_slice_in_dim(doc_lengths, part * own_rows, own_rows, 0)
    doc_ends = jnp.cumsum(lengths, axis=-1)
    starts = doc_ends - lengths
    spots = jnp.arange(length, dtype=jnp.int32)
    doc_ids = jnp.sum((spots[None, :, None] >= doc_ends[:, None, :]).astype(jnp.int32), -1)
    picked = doc_ids[:, :, None] == jnp.arange(lengths.shape[-1], dtype=jnp.int32)
    positions = spots - jnp.sum(jnp.where(picked, starts[:, None, :], 0), -1)
    lane = jnp.arange(LANES)
    inverse = 10000.0 ** (-2.0 * (lane % (ROT // 2)).astype(F32) / ROT)
    angles = positions.astype(F32)[..., None] * inverse
    sine = jnp.sin(angles)
    pairs = [
        jnp.where(lane < ROT, jnp.cos(angles), 1.0),
        jnp.where(lane < ROT // 2, -sine, 0.0),
        jnp.where((lane >= ROT // 2) & (lane < ROT), sine, 0.0),
        doc_ids[:, :, None],
        doc_ids[:, None, :],
    ]

    def own(field):
        if plan.share == 1:
            return field
        return lax.dynamic_slice_in_dim(field, part * own_rows * length, own_rows * length, 0)

    def spread(field):
        if plan.share == 1:
            return field
        blank = jnp.zeros((count, field.shape[1]), field.dtype)
        return lax.dynamic_update_slice_in_dim(blank, field, part * own_rows * length, 0)

    up_b = lax.dynamic_slice_in_dim(up_bias, me * own_hidden, own_hidden)
    qkv_b = lax.dynamic_index_in_dim(qkv_bias.reshape(3, heads, HD), head_of, 1, keepdims=False)
    own_normed1 = own(normed1)
    qkv, attended, lse = head_forward(
        turns, own_normed1, qkv_b.reshape(-1), pairs, qkv_pieces, length
    )
    joined = (attended, up_pieces[-2], up_pieces[-1], *down_gather.first())
    hidden, slope = feed_up(turns, after(normed2, *joined), up_b, up_pieces)
    down_pieces = down_gather.finish(*joined)
    out_term = out_sum(turns, hidden, down_pieces, spread(attended), out_w)
    out_total = sum_blocks(out_term)

    g_all = after(g_all, out_term)
    down_g = weight_grad(turns, g_all, hidden)
    down_scatter = Scatter(down_g, plan)
    pre_grad, up_sum = feed_slope(turns, after(g_all, down_g[0]), slope, down_pieces)
    down_second = down_scatter.second(turns, pre_grad)
    up_g, up_parts = weight_grad(
        turns, after(normed2, *down_second), pre_grad, up_sum, up_pieces
    )
    up_scatter = Scatter(up_g, plan)
    own_grad = own(after(g_all, up_g[0]))
    qkv_grad, qkv_sum = head_backward(
        turns, own_grad, out_w, qkv, attended, lse, pairs, length
    )
    down_total = down_scatter.finish(turns, qkv_grad)
    down_back = collect(down_total)
    qkv_g, qkv_parts = weight_grad(
        turns, after(own_normed1, down_total, out_total), qkv_grad, qkv_sum, qkv_pieces
    )
    qkv_scatter = Scatter(qkv_g, plan)
    up_second = up_scatter.second(turns, qkv_g[0])
    norm_term = norm_back(
        turns,
        after(pre_grad, *up_second),
        up_pieces,
        spread(qkv_grad),
        qkv_pieces,
        vectors,
    )
    norm_total = sum_blocks(norm_term)
    qkv_second = qkv_scatter.second(turns, norm_term)
    up_total = up_scatter.finish(turns, norm_term)
    out_g = out_grad(turns, places, after(attended, down_back, *qkv_second), own_grad)
    out_got = [out_g[0]] + [swap_group(out_g[j], plan, j) for j in range(1, plan.group)]
    up_back = collect(after(up_total, down_back))
    qkv_total = qkv_scatter.finish(turns, *out_got[1:])
    qkv_back = collect(after(qkv_total, up_back))
    holders = turns[:, None] * plan.share + jnp.arange(plan.share, dtype=jnp.int32)
    out_send = pick((me % plan.group ^ holders).reshape(-1), out_got, rows)
    out_back = out_send[0].astype(F32) + sum(
        swap(out_send[k], "row", rows, k).astype(F32) for k in range(1, rows)
    )

    terms = [jnp.sum(after(v, up_total), -1) for v in (qkv_parts, up_parts)]
    terms += [g_sum, qkv_sum, up_sum]
    terms = [v.reshape(-1) for v in terms]
    used = sum(v.size for v in terms)
    terms.append(jnp.zeros((-used % (8 * LANES),), F32))
    sums = jnp.concatenate(terms)
    sums = sums + sum(swap(sums, "row", rows, k) for k in range(1, rows))
    sums = jnp.stack([sums] + [swap(sums, "blk", blks, k) for k in range(1, blks)])
    sums = sums[me ^ jnp.arange(blks, dtype=jnp.int32)]
    gain1, bias1, gain2, bias2, g_total = jnp.split(
        jnp.sum(sums[:, : 5 * width], 0), 5
    )
    sums = sums[:, 5 * width : used]
    qkv_bias_grad = sums[:, : 3 * HD].reshape(plan.per_row, rows, plan.share, 3, HD)
    qkv_bias_grad = jnp.sum(qkv_bias_grad, 2).transpose(2, 1, 0, 3).reshape(-1)
    up_bias_grad = sums[:, 3 * HD :].reshape(-1)

    layer_out = finish(turns, x_own, out_total, vectors, False)
    tokens_grad = finish(turns, x_own, norm_total, g_own, True)
    return (
        layer_out.reshape(tokens.shape),
        tokens_grad.reshape(tokens.shape),
        join_attn(turns, qkv_back, out_back, plan),
        join_mlp(turns, up_back, down_back),
        (gain1 - ln1_bias * bias1) / ln1_gain,
        bias1,
        (gain2 - ln2_bias * bias2) / ln2_gain,
        bias2,
        qkv_bias_grad,
        g_total,
        up_bias_grad,
        g_total,
    )


def solution(mesh):
    rows, blks = mesh.shape["row"], mesh.shape["blk"]
    vector = P()
    tokens = P("row", "blk", None)
    attn = P(("row", "blk"), None)
    mlp = P(("row", "blk"), None, None)

    def run(*arrays):
        plan = Plan(rows, blks, arrays[0].shape[-1] // HD)
        return jax.shard_map(
            functools.partial(shards, plan),
            mesh=mesh,
            in_specs=(tokens, attn, mlp) + (vector,) * 8 + (P("row", None), tokens),
            out_specs=(tokens, tokens, attn, mlp) + (vector,) * 8,
            check_vma=False,
        )(*arrays)

    return run
```

```python
import functools
import math

import jax
import jax.numpy as jnp
import numpy as np
from jax import lax
from jax.experimental import pallas as pl
from jax.experimental.pallas import tpu as pltpu
from jax.sharding import PartitionSpec as P

HD = 256
ROT = 64
LANES = 128
BLOCK = 256
EPSILON = 1e-05
MASKED = -1e30
BF = jnp.bfloat16
F32 = jnp.float32
COST = 100
VMEM_LIMIT = 56 * 2**20
SMALL = 16 * 2**20


class Plan:
    def __init__(self, rows, blks, heads):
        self.rows = rows
        self.blks = blks
        self.share = blks // heads
        self.per_row = heads // rows
        self.group = blks // self.per_row
        self.groups = [
            list(range(i * self.group, (i + 1) * self.group)) for i in range(self.per_row)
        ]


def after(field, *others):
    return lax.optimization_barrier((field,) + others)[0] if others else field


def swap(field, axis, size, bit):
    return lax.ppermute(field, axis, [(i, i ^ bit) for i in range(size)])


def bits_of(size):
    return [1 << i for i in range(size.bit_length() - 1)]


def swap_group(field, plan, bits):
    return lax.ppermute(field, "blk", [(i, i ^ bits) for i in range(plan.blks)])


def near(k):
    return k & (k - 1) == 0


def orders(plan):
    bits = bits_of(plan.rows)
    return bits, bits[::-1]


def half_of(field, h):
    middle = field.shape[0] // 2
    return field[h * middle : (h + 1) * middle]


def parts_of(rows, depth):
    out = []
    for k in range(rows):
        if near(k):
            out.append((k * depth, depth))
        else:
            out += [(k * depth, depth // 2), (k * depth + depth // 2, depth // 2)]
    return out


class Gather:
    def __init__(self, own, plan):
        self.plan = plan
        self.whole = {0: own}
        for bit in bits_of(plan.rows):
            self.whole[bit] = swap(own, "row", plan.rows, bit)

    def first(self):
        return [v for k, v in self.whole.items() if k]

    def finish(self, *others):
        plan = self.plan
        halves = []
        for h, order in enumerate(orders(plan)):
            got = {0: None}
            for bit in order:
                for k in list(got):
                    if k == 0:
                        got[bit] = half_of(after(self.whole[bit], *others), h)
                    else:
                        got[k ^ bit] = swap(got[k], "row", plan.rows, bit)
            halves.append(got)
        out = []
        for k in range(plan.rows):
            out += [self.whole[k]] if near(k) else [half[k] for half in halves]
        return out


class Scatter:
    def __init__(self, pieces, plan):
        self.plan = plan
        pieces = iter(pieces)
        self.whole, far = {}, [{}, {}]
        for k in range(plan.rows):
            if near(k):
                self.whole[k] = next(pieces)
            else:
                far[0][k], far[1][k] = next(pieces), next(pieces)
        self.got = []
        for h, order in enumerate(orders(plan)):
            held = far[h]
            for bit in order:
                for k in [k for k in held if k & bit]:
                    term = swap(held.pop(k), "row", plan.rows, bit)
                    if near(k ^ bit):
                        self.got.append((k ^ bit, h, term))
                    else:
                        held[k ^ bit] = (held[k ^ bit].astype(F32) + term.astype(F32)).astype(BF)

    def first(self):
        return [term for _, _, term in self.got]

    def second(self, turns, *others):
        got = [(k, h, after(term, *others)) for k, h, term in self.got]
        while got:
            first = {}
            for item in got:
                first.setdefault(item[0], item)
            got = [item for item in got if all(item is not v for v in first.values())]
            sums = add_halves(turns, [(self.whole[k], h, term) for k, h, term in first.values()])
            self.whole.update(zip(first, sums))
        return [v for k, v in self.whole.items() if k]

    def finish(self, turns, *others):
        terms = [after(self.whole[0], *others)]
        for bit in bits_of(self.plan.rows):
            terms.append(swap(self.whole[bit], "row", self.plan.rows, bit))
        return add_wholes(turns, terms)


def dot(left, right, left_dim, right_dim):
    return lax.dot_general(
        left, right, (((left_dim,), (right_dim,)), ((), ())), preferred_element_type=F32
    )


def whole(array):
    return pl.BlockSpec(array.shape, lambda *i: (0,) * len(array.shape))


def like(shape, kind=BF):
    return jax.ShapeDtypeStruct(shape, kind)


def call(body, turns, grid, in_specs, out_specs, out_shape, operands, flops=0, limit=None):
    moved = sum(v.size * v.dtype.itemsize for v in operands)
    moved += sum(math.prod(v.shape) * jnp.dtype(v.dtype).itemsize for v in out_shape)
    return pl.pallas_call(
        body,
        name=getattr(body, "func", body).__name__,
        grid_spec=pltpu.PrefetchScalarGridSpec(
            num_scalar_prefetch=1, grid=(grid,), in_specs=in_specs, out_specs=out_specs
        ),
        out_shape=out_shape,
        compiler_params=pltpu.CompilerParams(vmem_limit_bytes=limit or VMEM_LIMIT),
        cost_estimate=pl.CostEstimate(
            flops=flops // COST, bytes_accessed=moved // COST, transcendentals=0
        ),
    )(turns, *operands)


def rows_block(columns, block=BLOCK):
    return pl.BlockSpec((block, columns), lambda i, t: (i, 0))


def halves_kernel(count, t_ref, *refs):
    for i in range(count):
        into, term, out = refs[i], refs[count + i], refs[2 * count + i]
        out[...] = (into[...].astype(F32) + term[...].astype(F32)).astype(BF)


def add_halves(turns, items):
    count = len(items)
    depth, width = items[0][2].shape
    parts = 2
    into = [pl.BlockSpec((depth, width // parts), lambda i, t, h=h: (h, i)) for _, h, _ in items]
    term = pl.BlockSpec((depth, width // parts), lambda i, t: (0, i))
    return pl.pallas_call(
        functools.partial(halves_kernel, count),
        name="halves_kernel",
        grid_spec=pltpu.PrefetchScalarGridSpec(
            num_scalar_prefetch=1, grid=(parts,), in_specs=into + [term] * count, out_specs=into
        ),
        out_shape=[like(v.shape) for v, _, _ in items],
        input_output_aliases={1 + i: i for i in range(count)},
        compiler_params=pltpu.CompilerParams(vmem_limit_bytes=SMALL),
        cost_estimate=pl.CostEstimate(
            flops=0, bytes_accessed=6 * depth * width * count // COST, transcendentals=0
        ),
    )(turns, *[v for v, _, _ in items], *[v for _, _, v in items])


def wholes_kernel(t_ref, *refs):
    refs[-1][...] = sum(ref[...].astype(F32) for ref in refs[:-1]).astype(BF)


def add_wholes(turns, terms):
    depth, width = terms[0].shape
    block = rows_block(width, depth // 4)
    shape = like((depth, width))
    return call(
        wholes_kernel, turns, 4, [block] * len(terms), [block], [shape], terms, limit=SMALL
    )[0]


def turn_kernel(t_ref, x_ref, g_ref, v_ref, xo_ref, go_ref, vo_ref, s_ref):
    xo_ref[...] = x_ref[...]
    go_ref[...] = g_ref[...]
    vo_ref[...] = v_ref[...]
    s_ref[...] = jnp.sum(g_ref[...].astype(F32), 0, keepdims=True)


def turn_in(turns, x, g, vectors):
    rows = turns.shape[0]
    part = x.shape[1] // rows

    def specs(array, turned):
        index = (lambda k, t: (0, t[k])) if turned else (lambda k, t: (0, k))
        return pl.BlockSpec((array.shape[0], part), index)

    total_shape = like((1, x.shape[1]), F32)
    return call(
        turn_kernel,
        turns,
        rows,
        [specs(v, True) for v in (x, g, vectors)],
        [specs(v, False) for v in (x, g, vectors)] + [specs(total_shape, True)],
        [like(v.shape, v.dtype) for v in (x, g, vectors)] + [total_shape],
        [x, g, vectors],
    )


def split_kernel(t_ref, w_ref, u_ref, d_ref):
    u_ref[0] = w_ref[:, 0, :]
    d_ref[0] = w_ref[:, 1, :]


def split_mlp(turns, weights, blks):
    depth, _, hidden = weights.shape
    part = hidden // blks
    block = pl.BlockSpec((1, depth, part), lambda b, t: (b, 0, 0))
    return call(
        split_kernel,
        turns,
        blks,
        [pl.BlockSpec((depth, 2, part), lambda b, t: (0, 0, b))],
        [block] * 2,
        [like((blks, depth, part))] * 2,
        [weights],
    )


def join_kernel(t_ref, u_ref, d_ref, o_ref):
    o_ref[:, 0, :] = u_ref[0].astype(F32)
    o_ref[:, 1, :] = d_ref[0].astype(F32)


def join_mlp(turns, up, down):
    blks, depth, part = up.shape
    block = pl.BlockSpec((1, depth, part), lambda b, t: (b, 0, 0))
    return call(
        join_kernel,
        turns,
        blks,
        [block] * 2,
        [pl.BlockSpec((depth, 2, part), lambda b, t: (0, 0, b))],
        [like((depth, 2, blks * part), F32)],
        [up, down],
    )[0]


def split_attn_kernel(plan, width, t_ref, w_ref, qkv_ref, out_ref):
    b = pl.program_id(0)
    head = b % plan.group // plan.share * plan.per_row + b // plan.group
    for i in range(3):
        at = pl.multiple_of(i * width + head * HD, HD)
        qkv_ref[0, :, i * HD : (i + 1) * HD] = w_ref[:, pl.ds(at, HD)]

    @pl.when(b == 0)
    def _():
        out_ref[...] = w_ref[:, 3 * width :]


def split_attn(turns, weights, plan, width):
    depth = weights.shape[0]
    return call(
        functools.partial(split_attn_kernel, plan, width),
        turns,
        plan.blks,
        [whole(weights)],
        [
            pl.BlockSpec((1, depth, 3 * HD), lambda b, t: (b, 0, 0)),
            pl.BlockSpec((depth, width), lambda b, t: (0, 0)),
        ],
        [like((plan.blks, depth, 3 * HD)), like((depth, width))],
        [weights],
        limit=SMALL,
    )


def join_attn_kernel(plan, t_ref, qkv_ref, out_ref, o_ref):
    step = pl.program_id(0)
    heads = o_ref.shape[1] // HD

    @pl.when(step < 3)
    def _():
        at = pl.ds(pl.multiple_of(step * HD, HD), HD)
        for h in range(heads):
            first = h % plan.per_row * plan.group + h // plan.per_row * plan.share
            o_ref[:, h * HD : (h + 1) * HD] = sum(
                qkv_ref[first + i, :, at].astype(F32) for i in range(plan.share)
            )

    @pl.when(step == 3)
    def _():
        o_ref[...] = out_ref[...]


def join_attn(turns, qkv, out, plan):
    depth, width = out.shape
    return call(
        functools.partial(join_attn_kernel, plan),
        turns,
        4,
        [whole(qkv), whole(out)],
        [pl.BlockSpec((depth, width), lambda j, t: (0, j))],
        [like((depth, 4 * width), F32)],
        [qkv, out],
    )[0]


def pick_kernel(count, t_ref, *refs):
    pieces, outs = refs[:count], refs[count:]
    share = t_ref.shape[0] // len(outs)
    for n, out in enumerate(outs):
        for i in range(share):
            for k, piece in enumerate(pieces):

                @pl.when(t_ref[n * share + i] == k)
                def _(i=i, out=out, piece=piece):
                    out[...] = piece[...] if i == 0 else out[...] + piece[...]


def pick(table, pieces, count):
    return call(
        functools.partial(pick_kernel, len(pieces)),
        table,
        1,
        [whole(p) for p in pieces],
        [whole(pieces[0])] * count,
        [like(pieces[0].shape)] * count,
        pieces,
    )


def place_kernel(t_ref, *refs):
    *pieces, out_ref = refs
    for k, piece in enumerate(pieces):
        depth = piece.shape[0]
        out_ref[pl.ds(pl.multiple_of(t_ref[k] * depth, depth), depth)] = piece[...]


def place(table, pieces):
    depth, width = pieces[0].shape
    shape = like((len(pieces) * depth, width))
    return call(place_kernel, table, 1, [whole(p) for p in pieces], [whole(shape)], [shape], pieces)[0]


def norm_kernel(t_ref, x_ref, v_ref, a1_ref, a2_ref):
    field = x_ref[...].astype(F32)
    centred = field - jnp.mean(field, -1, keepdims=True)
    standard = centred * lax.rsqrt(jnp.mean(centred * centred, -1, keepdims=True) + EPSILON)
    a1_ref[...] = (standard * v_ref[0:1] + v_ref[1:2]).astype(BF)
    a2_ref[...] = (standard * v_ref[2:3] + v_ref[3:4]).astype(BF)


def norms(turns, x, vectors):
    count, width = x.shape
    return call(
        norm_kernel,
        turns,
        count // BLOCK,
        [rows_block(width), whole(vectors)],
        [rows_block(width)] * 2,
        [like(x.shape)] * 2,
        [x, vectors],
        20 * count * width,
    )


def times_pieces(left, pieces):
    out, start = None, 0
    for piece in pieces:
        depth = piece.shape[0]
        term = dot(left[:, start : start + depth], piece[...], 1, 0)
        out = term if out is None else out + term
        start += depth
    return out


def up_kernel(t_ref, a_ref, b_ref, *refs):
    pieces, (h_ref, s_ref) = refs[:-2], refs[-2:]
    pre = times_pieces(a_ref[...], pieces) + b_ref[...]
    cdf = 0.5 * (1.0 + lax.erf(pre * math.sqrt(0.5)))
    h_ref[...] = (pre * cdf).astype(BF)
    s_ref[...] = cdf + pre * (jnp.exp(-0.5 * pre * pre) * (1.0 / math.sqrt(2.0 * math.pi)))


def feed_up(turns, normed, bias, pieces):
    count, width = normed.shape
    hidden = bias.shape[0]
    return call(
        up_kernel,
        turns,
        count // BLOCK,
        [rows_block(width), pl.BlockSpec((1, hidden), lambda i, t: (0, 0))]
        + [whole(p) for p in pieces],
        [rows_block(hidden)] * 2,
        [like((count, hidden)), like((count, hidden), F32)],
        [normed, bias.reshape(1, hidden)] + pieces,
        2 * count * width * hidden,
    )


def slope_kernel(t_ref, g_ref, s_ref, *refs):
    pieces, (p_ref, sum_ref) = refs[:-2], refs[-2:]

    @pl.when(pl.program_id(0) == 0)
    def _():
        sum_ref[...] = jnp.zeros_like(sum_ref)

    grad = (times_pieces(g_ref[...], pieces) * s_ref[...]).astype(BF)
    p_ref[...] = grad
    sum_ref[...] += jnp.sum(grad.astype(F32), 0, keepdims=True)


def feed_slope(turns, grad, slope, pieces):
    count, width = grad.shape
    hidden = slope.shape[1]
    return call(
        slope_kernel,
        turns,
        count // BLOCK,
        [rows_block(width), rows_block(hidden)] + [whole(p) for p in pieces],
        [rows_block(hidden), pl.BlockSpec((1, hidden), lambda i, t: (0, 0))],
        [like((count, hidden)), like((1, hidden), F32)],
        [grad, slope] + pieces,
        2 * count * width * hidden,
    )


def lane_sum(field):
    return sum(field[:, i : i + LANES] for i in range(0, field.shape[1], LANES))


def weight_kernel(rows, layout, with_sums, t_ref, l_ref, r_ref, *refs):
    step = pl.program_id(0)
    depth = l_ref.shape[1]
    if with_sums:
        sum_ref, pieces, refs = refs[0], refs[1 : 1 + len(layout)], refs[1 + len(layout) :]
        parts_ref = refs[-1]
    grad = dot(l_ref[...], r_ref[...], 0, 0)
    for k in range(rows):

        @pl.when(step == k)
        def _(k=k):
            for i, (start, size) in enumerate(layout):
                if start // depth != k:
                    continue
                at = slice(start - k * depth, start - k * depth + size)
                refs[i][...] = grad[at].astype(BF)
                if with_sums:
                    piece = pieces[i][...].astype(F32)
                    parts_ref[0, at] = lane_sum(piece * grad[at])
                    parts_ref[1, at] = lane_sum(piece * sum_ref[...])


def weight_grad(turns, left, right, sums=None, pieces=()):
    rows = turns.shape[0]
    count, width = left.shape
    columns = right.shape[1]
    depth = width // rows
    layout = parts_of(rows, depth)
    out_shape = [like((size, columns)) for _, size in layout]
    out_specs = [whole(v) for v in out_shape]
    operands = [left, right]
    if pieces:
        operands += [sums] + pieces
        out_shape.append(like((2, width, LANES), F32))
        out_specs.append(pl.BlockSpec((2, depth, LANES), lambda k, t: (0, t[k], 0)))
    out = call(
        functools.partial(weight_kernel, rows, layout, bool(pieces)),
        turns,
        rows,
        [pl.BlockSpec((count, depth), lambda k, t: (0, k))] + [whole(v) for v in operands[1:]],
        out_specs,
        out_shape,
        operands,
        2 * count * width * columns,
    )
    if pieces:
        return out[:-1], out[-1]
    return out


def out_kernel(rows, t_ref, o_ref, g_ref, *refs):
    *outs, grad_ref = refs
    depth = outs[0].shape[0]
    grad_ref[...] = dot(o_ref[...], g_ref[...], 0, 0)
    for j, out in enumerate(outs):
        at = pl.multiple_of(t_ref[rows + j] * depth, depth)
        out[...] = grad_ref[pl.ds(at, depth)].astype(BF)


def out_grad(turns, places, attended, grad):
    rows, group = turns.shape[0], places.shape[0]
    count, width = grad.shape
    part = width // rows
    depth = HD // group
    return pl.pallas_call(
        functools.partial(out_kernel, rows),
        name="out_kernel",
        grid_spec=pltpu.PrefetchScalarGridSpec(
            num_scalar_prefetch=1,
            grid=(rows,),
            in_specs=[whole(attended), pl.BlockSpec((count, part), lambda k, t: (0, k))],
            out_specs=[pl.BlockSpec((depth, part), lambda k, t: (0, t[k]))] * group,
            scratch_shapes=[pltpu.VMEM((HD, part), F32)],
        ),
        out_shape=[like((depth, width))] * group,
        compiler_params=pltpu.CompilerParams(vmem_limit_bytes=VMEM_LIMIT),
        cost_estimate=pl.CostEstimate(
            flops=2 * count * width * HD // COST,
            bytes_accessed=2 * (count * (width + HD) + width * HD) // COST,
            transcendentals=0,
        ),
    )(jnp.concatenate([turns, places]), attended, grad)


def turned_columns(t_ref, w_ref, start, size, depth):
    at = t_ref[start // depth] * depth + start % depth
    return w_ref[:, pl.ds(pl.multiple_of(at, LANES), size)]


def sum_kernel(layout, depth, t_ref, h_ref, o_ref, w_ref, *refs):
    pieces, y_ref = refs[:-1], refs[-1]
    for piece, (start, size) in zip(pieces, layout):
        term = dot(h_ref[...], piece[...], 1, 1)
        term += dot(o_ref[...], turned_columns(t_ref, w_ref, start, size, depth), 1, 0)
        y_ref[:, start : start + size] = term.astype(BF)


def out_sum(turns, hidden, pieces, attended, out_w):
    rows = turns.shape[0]
    count = hidden.shape[0]
    width = out_w.shape[1]
    return call(
        functools.partial(sum_kernel, parts_of(rows, width // rows), width // rows),
        turns,
        count // BLOCK,
        [rows_block(hidden.shape[1]), rows_block(HD), whole(out_w)] + [whole(p) for p in pieces],
        [rows_block(width)],
        [like((count, width))],
        [hidden, attended, out_w] + pieces,
        2 * count * width * (hidden.shape[1] + HD),
    )[0]


def back_kernel(layout, t_ref, p_ref, q_ref, v_ref, *refs):
    pieces, c_ref = refs[:-1], refs[-1]
    count = len(layout)
    for up, qkv, (start, size) in zip(pieces[:count], pieces[count:], layout):
        cols = slice(start, start + size)
        term = dot(p_ref[...], up[...], 1, 1) * v_ref[2:3, cols]
        term += dot(q_ref[...], qkv[...], 1, 1) * v_ref[0:1, cols]
        c_ref[:, cols] = term.astype(BF)


def norm_back(turns, pre_grad, up_pieces, qkv_grad, qkv_pieces, vectors):
    rows = turns.shape[0]
    count = pre_grad.shape[0]
    width = vectors.shape[1]
    columns = pre_grad.shape[1] + qkv_grad.shape[1]
    return call(
        functools.partial(back_kernel, parts_of(rows, width // rows)),
        turns,
        count // BLOCK,
        [rows_block(pre_grad.shape[1]), rows_block(qkv_grad.shape[1]), whole(vectors)]
        + [whole(p) for p in up_pieces + qkv_pieces],
        [rows_block(width)],
        [like((count, width))],
        [pre_grad, qkv_grad, vectors] + up_pieces + qkv_pieces,
        2 * count * width * columns,
    )[0]


def turned(field, cosine, minus, plus):
    head = field[:, :LANES]
    half = ROT // 2
    head = (
        head * cosine
        + pltpu.roll(head, LANES - half, 1) * minus
        + pltpu.roll(head, half, 1) * plus
    )
    return jnp.concatenate([head, field[:, LANES:]], 1)


def allowed_pairs(length, dq_ref, dk_ref):
    spot = lax.broadcasted_iota(jnp.int32, (length, length), 0)
    other = lax.broadcasted_iota(jnp.int32, (length, length), 1)
    return (dq_ref[0] == dk_ref[0]) & (other <= spot)


def forward_kernel(t_ref, a_ref, b_ref, c_ref, m_ref, p_ref, dq_ref, dk_ref, *refs):
    pieces, (qkv_ref, o_ref, lse_ref) = refs[:-3], refs[-3:]
    qkv = times_pieces(a_ref[...], pieces) + b_ref[...]
    tables = c_ref[0], m_ref[0], p_ref[0]
    queries = (turned(qkv[:, :HD], *tables) * HD ** (-0.5)).astype(BF)
    keys = turned(qkv[:, HD : 2 * HD], *tables).astype(BF)
    values = qkv[:, 2 * HD :].astype(BF)
    for i, field in enumerate((queries, keys, values)):
        qkv_ref[:, i * HD : (i + 1) * HD] = field
    allowed = allowed_pairs(a_ref.shape[0], dq_ref, dk_ref)
    scores = jnp.where(allowed, dot(queries, keys, 1, 1), MASKED)
    largest = jnp.max(scores, -1, keepdims=True)
    weights = jnp.where(allowed, jnp.exp(scores - largest), 0.0)
    mass = jnp.sum(weights, -1, keepdims=True)
    o_ref[...] = dot((weights / mass).astype(BF), values, 1, 0).astype(BF)
    lse_ref[...] = largest + jnp.log(mass)


def backward_kernel(
    parts, t_ref, g_ref, w_ref, qkv_ref, o_ref, lse_ref, c_ref, m_ref, p_ref, dq_ref, dk_ref,
    grad_ref, sum_ref,
):
    queries, keys, values = (qkv_ref[:, i * HD : (i + 1) * HD] for i in range(3))
    tables = c_ref[0], -m_ref[0], -p_ref[0]
    depth = w_ref.shape[1] // parts
    heads_grad = None
    for k in range(parts):
        cols = slice(k * depth, (k + 1) * depth)
        term = dot(g_ref[:, cols], turned_columns(t_ref, w_ref, k * depth, depth, depth), 1, 1)
        heads_grad = term if heads_grad is None else heads_grad + term
    heads_grad = heads_grad.astype(BF)
    allowed = allowed_pairs(g_ref.shape[0], dq_ref, dk_ref)
    scores = jnp.where(allowed, dot(queries, keys, 1, 1), MASKED)
    weights = jnp.where(allowed, jnp.exp(scores - lse_ref[...]), 0.0)
    deltas = jnp.sum(heads_grad.astype(F32) * o_ref[...].astype(F32), -1, keepdims=True)
    score_grad = (weights * (dot(heads_grad, values, 1, 1) - deltas)).astype(BF)
    query_grad = dot(score_grad, keys, 1, 0) * HD ** (-0.5)
    key_grad = dot(score_grad, queries, 0, 0)
    value_grad = dot(weights.astype(BF), heads_grad, 0, 0)
    fields = turned(query_grad, *tables), turned(key_grad, *tables), value_grad

    @pl.when(pl.program_id(0) == 0)
    def _():
        sum_ref[...] = jnp.zeros_like(sum_ref)

    for i, field in enumerate(fields):
        field = field.astype(BF)
        cols = slice(i * HD, (i + 1) * HD)
        grad_ref[:, cols] = field
        sum_ref[:, cols] += jnp.sum(field.astype(F32), 0, keepdims=True)


def pair_specs(length):
    table = pl.BlockSpec((1, length, LANES), lambda r, t: (r, 0, 0))
    return [table] * 3 + [
        pl.BlockSpec((1, length, 1), lambda r, t: (r, 0, 0)),
        pl.BlockSpec((1, 1, length), lambda r, t: (r, 0, 0)),
    ]


def head_forward(turns, normed, bias, pairs, pieces, length):
    count, width = normed.shape
    columns = 3 * HD
    return call(
        forward_kernel,
        turns,
        count // length,
        [rows_block(width, length), pl.BlockSpec((1, columns), lambda r, t: (0, 0))]
        + pair_specs(length)
        + [whole(p) for p in pieces],
        [rows_block(columns, length), rows_block(HD, length), rows_block(1, length)],
        [like((count, columns)), like((count, HD)), like((count, 1), F32)],
        [normed, bias.reshape(1, columns)] + pairs + pieces,
        2 * count * (width * columns + 2 * length * HD),
    )


def head_backward(turns, grad, out_w, qkv, attended, lse, pairs, length):
    count, width = grad.shape
    columns = 3 * HD
    return call(
        functools.partial(backward_kernel, turns.shape[0]),
        turns,
        count // length,
        [
            rows_block(width, length),
            whole(out_w),
            rows_block(columns, length),
            rows_block(HD, length),
            rows_block(1, length),
        ]
        + pair_specs(length),
        [rows_block(columns, length), pl.BlockSpec((1, columns), lambda r, t: (0, 0))],
        [like((count, columns)), like((1, columns), F32)],
        [grad, out_w, qkv, attended, lse] + pairs,
        2 * count * (width * HD + 5 * length * HD),
    )


def finish_kernel(rows, with_norm, t_ref, x_ref, s_ref, o_ref, out_ref):
    depth = x_ref.shape[1] // rows
    term = s_ref[...].astype(F32)
    if with_norm:
        centred = x_ref[...].astype(F32)
        centred = centred - jnp.mean(centred, -1, keepdims=True)
        rstd = lax.rsqrt(jnp.mean(centred * centred, -1, keepdims=True) + EPSILON)
        centred = centred * rstd
        term = term - jnp.mean(term, -1, keepdims=True) - centred * jnp.mean(
            term * centred, -1, keepdims=True
        )
        field = o_ref[...].astype(F32) + rstd * term
    else:
        field = x_ref[...].astype(F32) + term + o_ref[4:5]
    for k in range(rows):
        at = pl.multiple_of(t_ref[k] * depth, LANES)
        out_ref[:, pl.ds(at, depth)] = field[:, k * depth : (k + 1) * depth].astype(BF)


def finish(turns, x, term, other, with_norm):
    return call(
        functools.partial(finish_kernel, turns.shape[0], with_norm),
        turns,
        1,
        [whole(v) for v in (x, term, other)],
        [whole(x)],
        [like(x.shape)],
        [x, term, other],
    )[0]


def shards(
    plan,
    tokens,
    attn_weights,
    mlp_weights,
    ln1_gain,
    ln1_bias,
    ln2_gain,
    ln2_bias,
    qkv_bias,
    dense_bias,
    up_bias,
    down_bias,
    doc_lengths,
    cotangent,
):
    row_count, shard_len, width = tokens.shape
    depth = attn_weights.shape[0]
    heads = width // HD
    rows, blks = plan.rows, plan.blks
    own_hidden = mlp_weights.shape[-1] // blks
    me = lax.axis_index("blk")
    length = shard_len * blks
    count = row_count * length
    head_of = me % plan.group // plan.share * plan.per_row + me // plan.group
    part = me % plan.share
    own_rows = row_count // plan.share
    row = lax.axis_index("row")
    turns = row ^ jnp.arange(rows, dtype=jnp.int32)
    places = me % plan.group ^ jnp.arange(plan.group, dtype=jnp.int32)

    def exchange(field):
        return lax.all_to_all(field, "blk", 0, 0)

    def collect(field):
        return exchange(field.reshape(blks, -1, field.shape[-1]))

    def gather_blocks(field):
        field = field.reshape(row_count, shard_len, width)
        return lax.all_gather(field, "blk", axis=1, tiled=True).reshape(count, width)

    def sum_blocks(field):
        field = field.reshape(row_count, length, width)
        field = lax.psum_scatter(field, "blk", scatter_dimension=1, tiled=True)
        return field.reshape(row_count * shard_len, width)

    zeros = jnp.zeros((3, width), F32)
    vectors = jnp.stack([ln1_gain, ln1_bias, ln2_gain, ln2_bias, dense_bias + down_bias])
    x_own, g_own, vectors, g_sum = turn_in(
        turns,
        tokens.reshape(row_count * shard_len, width),
        cotangent.reshape(row_count * shard_len, width),
        jnp.concatenate([vectors, zeros]),
    )
    qkv_send, out_own = split_attn(turns, attn_weights, plan, width)
    qkv_mine = exchange(qkv_send)
    out_send = pick(
        row ^ places // plan.share,
        [out_own] + [swap(out_own, "row", rows, k) for k in range(1, rows)],
        plan.group,
    )
    up_send, down_send = split_mlp(turns, after(mlp_weights, qkv_send), blks)
    qkv_mine, up_send, *out_send = lax.optimization_barrier((qkv_mine, up_send, *out_send))
    up_mine = exchange(up_send)
    qkv_gather = Gather(qkv_mine.reshape(-1, 3 * HD), plan)
    out_got = [out_send[0]] + [swap_group(out_send[j], plan, j) for j in range(1, plan.group)]
    joined = (up_mine, *out_got[1:], *qkv_gather.first())
    up_mine = after(*joined)
    x_all = gather_blocks(after(x_own, *joined))
    down_mine = exchange(after(down_send, *joined))
    out_w = place(places, out_got)
    up_gather = Gather(up_mine.reshape(-1, own_hidden), plan)
    qkv_pieces = qkv_gather.finish(up_mine)
    joined = (down_mine, qkv_pieces[-2], qkv_pieces[-1], *up_gather.first())
    g_all = gather_blocks(after(g_own, *joined))
    down_gather = Gather(after(*joined).reshape(-1, own_hidden), plan)
    up_pieces = up_gather.finish(down_mine)
    normed1, normed2 = norms(turns, after(x_all, *joined), vectors)

    lengths = lax.dynamic_slice_in_dim(doc_lengths, part * own_rows, own_rows, 0)
    doc_ends = jnp.cumsum(lengths, axis=-1)
    starts = doc_ends - lengths
    spots = jnp.arange(length, dtype=jnp.int32)
    doc_ids = jnp.sum((spots[None, :, None] >= doc_ends[:, None, :]).astype(jnp.int32), -1)
    picked = doc_ids[:, :, None] == jnp.arange(lengths.shape[-1], dtype=jnp.int32)
    positions = spots - jnp.sum(jnp.where(picked, starts[:, None, :], 0), -1)
    lane = jnp.arange(LANES)
    inverse = 10000.0 ** (-2.0 * (lane % (ROT // 2)).astype(F32) / ROT)
    angles = positions.astype(F32)[..., None] * inverse
    sine = jnp.sin(angles)
    pairs = [
        jnp.where(lane < ROT, jnp.cos(angles), 1.0),
        jnp.where(lane < ROT // 2, -sine, 0.0),
        jnp.where((lane >= ROT // 2) & (lane < ROT), sine, 0.0),
        doc_ids[:, :, None],
        doc_ids[:, None, :],
    ]

    def own(field):
        if plan.share == 1:
            return field
        return lax.dynamic_slice_in_dim(field, part * own_rows * length, own_rows * length, 0)

    def spread(field):
        if plan.share == 1:
            return field
        blank = jnp.zeros((count, field.shape[1]), field.dtype)
        return lax.dynamic_update_slice_in_dim(blank, field, part * own_rows * length, 0)

    up_b = lax.dynamic_slice_in_dim(up_bias, me * own_hidden, own_hidden)
    qkv_b = lax.dynamic_index_in_dim(qkv_bias.reshape(3, heads, HD), head_of, 1, keepdims=False)
    own_normed1 = own(normed1)
    qkv, attended, lse = head_forward(
        turns, own_normed1, qkv_b.reshape(-1), pairs, qkv_pieces, length
    )
    joined = (attended, up_pieces[-2], up_pieces[-1], *down_gather.first())
    hidden, slope = feed_up(turns, after(normed2, *joined), up_b, up_pieces)
    down_pieces = down_gather.finish(*joined)
    out_term = out_sum(turns, hidden, down_pieces, spread(attended), out_w)
    out_total = sum_blocks(out_term)

    g_all = after(g_all, out_term)
    down_g = weight_grad(turns, g_all, hidden)
    down_scatter = Scatter(down_g, plan)
    pre_grad, up_sum = feed_slope(turns, after(g_all, down_g[0]), slope, down_pieces)
    own_grad = own(after(g_all, *down_scatter.second(turns, pre_grad)))
    qkv_grad, qkv_sum = head_backward(
        turns, own_grad, out_w, qkv, attended, lse, pairs, length
    )
    norm_term = norm_back(
        turns, pre_grad, up_pieces, spread(qkv_grad), qkv_pieces, vectors
    )
    norm_total = sum_blocks(norm_term)
    down_total = down_scatter.finish(turns, norm_term)
    down_back = collect(down_total)
    up_g, up_parts = weight_grad(
        turns, after(normed2, down_total, out_total), pre_grad, up_sum, up_pieces
    )
    up_scatter = Scatter(up_g, plan)
    up_second = up_scatter.second(turns)
    out_g = out_grad(turns, places, after(attended, up_g[0]), own_grad)
    out_got = [out_g[0]] + [swap_group(out_g[j], plan, j) for j in range(1, plan.group)]
    qkv_g, qkv_parts = weight_grad(
        turns,
        after(own_normed1, down_back, *up_second, *out_got[1:]),
        qkv_grad,
        qkv_sum,
        qkv_pieces,
    )
    qkv_scatter = Scatter(qkv_g, plan)
    qkv_second = qkv_scatter.second(turns)
    up_total = up_scatter.finish(turns, *qkv_second)
    up_back = collect(up_total)
    holders = turns[:, None] * plan.share + jnp.arange(plan.share, dtype=jnp.int32)
    out_send = pick((me % plan.group ^ holders).reshape(-1), out_got, rows)
    out_back = out_send[0].astype(F32) + sum(
        swap(after(out_send[k], up_total), "row", rows, k).astype(F32) for k in range(1, rows)
    )

    terms = [jnp.sum(after(v, up_total), -1) for v in (qkv_parts, up_parts)]
    terms += [g_sum, qkv_sum, up_sum]
    terms = [v.reshape(-1) for v in terms]
    used = sum(v.size for v in terms)
    terms.append(jnp.zeros((-used % (8 * LANES),), F32))
    sums = jnp.concatenate(terms)
    sums = sums + sum(swap(sums, "row", rows, k) for k in range(1, rows))

    qkv_total = qkv_scatter.finish(turns, out_back, sums, norm_total, up_back)
    qkv_back = collect(qkv_total)
    sums = after(sums, qkv_total)
    sums = jnp.stack([sums] + [swap(sums, "blk", blks, k) for k in range(1, blks)])
    sums = sums[me ^ jnp.arange(blks, dtype=jnp.int32)]
    gain1, bias1, gain2, bias2, g_total = jnp.split(
        jnp.sum(sums[:, : 5 * width], 0), 5
    )
    sums = sums[:, 5 * width : used]
    qkv_bias_grad = sums[:, : 3 * HD].reshape(plan.per_row, rows, plan.share, 3, HD)
    qkv_bias_grad = jnp.sum(qkv_bias_grad, 2).transpose(2, 1, 0, 3).reshape(-1)
    up_bias_grad = sums[:, 3 * HD :].reshape(-1)

    layer_out = finish(turns, x_own, out_total, vectors, False)
    tokens_grad = finish(turns, x_own, norm_total, g_own, True)
    return (
        layer_out.reshape(tokens.shape),
        tokens_grad.reshape(tokens.shape),
        join_attn(turns, qkv_back, out_back, plan),
        join_mlp(turns, up_back, down_back),
        (gain1 - ln1_bias * bias1) / ln1_gain,
        bias1,
        (gain2 - ln2_bias * bias2) / ln2_gain,
        bias2,
        qkv_bias_grad,
        g_total,
        up_bias_grad,
        g_total,
    )


def solution(mesh):
    rows, blks = mesh.shape["row"], mesh.shape["blk"]
    vector = P()
    tokens = P("row", "blk", None)
    attn = P(("row", "blk"), None)
    mlp = P(("row", "blk"), None, None)

    def run(*arrays):
        plan = Plan(rows, blks, arrays[0].shape[-1] // HD)
        return jax.shard_map(
            functools.partial(shards, plan),
            mesh=mesh,
            in_specs=(tokens, attn, mlp) + (vector,) * 8 + (P("row", None), tokens),
            out_specs=(tokens, tokens, attn, mlp) + (vector,) * 8,
            check_vma=False,
        )(*arrays)

    return run
```

```python
import functools
import math

import jax
import jax.numpy as jnp
import numpy as np
from jax import lax
from jax.experimental import pallas as pl
from jax.experimental.pallas import tpu as pltpu
from jax.sharding import PartitionSpec as P

HD = 256
ROT = 64
LANES = 128
BLOCK = 256
EPSILON = 1e-05
MASKED = -1e30
BF = jnp.bfloat16
F32 = jnp.float32
COST = 100
VMEM_LIMIT = 56 * 2**20
SMALL = 16 * 2**20


class Plan:
    def __init__(self, rows, blks, heads):
        self.rows = rows
        self.blks = blks
        self.share = blks // heads
        self.per_row = heads // rows
        self.group = blks // self.per_row
        self.groups = [
            list(range(i * self.group, (i + 1) * self.group)) for i in range(self.per_row)
        ]


def after(field, *others):
    return lax.optimization_barrier((field,) + others)[0] if others else field


def swap(field, axis, size, bit):
    return lax.ppermute(field, axis, [(i, i ^ bit) for i in range(size)])


def swap_group(field, plan, bits):
    return lax.ppermute(field, "blk", [(i, i ^ bits) for i in range(plan.blks)])


def gather_row(own, plan):
    return [own] + [swap(own, "row", plan.rows, k) for k in range(1, plan.rows)]


def scatter_row(pieces, plan):
    return [pieces[0]] + [swap(pieces[k], "row", plan.rows, k) for k in range(1, plan.rows)]


def dot(left, right, left_dim, right_dim):
    return lax.dot_general(
        left, right, (((left_dim,), (right_dim,)), ((), ())), preferred_element_type=F32
    )


def whole(array):
    return pl.BlockSpec(array.shape, lambda *i: (0,) * len(array.shape))


def like(shape, kind=BF):
    return jax.ShapeDtypeStruct(shape, kind)


def call(body, turns, grid, in_specs, out_specs, out_shape, operands, flops=0, limit=None):
    moved = sum(v.size * v.dtype.itemsize for v in operands)
    moved += sum(math.prod(v.shape) * jnp.dtype(v.dtype).itemsize for v in out_shape)
    return pl.pallas_call(
        body,
        name=getattr(body, "func", body).__name__,
        grid_spec=pltpu.PrefetchScalarGridSpec(
            num_scalar_prefetch=1, grid=(grid,), in_specs=in_specs, out_specs=out_specs
        ),
        out_shape=out_shape,
        compiler_params=pltpu.CompilerParams(vmem_limit_bytes=limit or VMEM_LIMIT),
        cost_estimate=pl.CostEstimate(
            flops=flops // COST, bytes_accessed=moved // COST, transcendentals=0
        ),
    )(turns, *operands)


def rows_block(columns, block=BLOCK):
    return pl.BlockSpec((block, columns), lambda i, t: (i, 0))


def add_kernel(t_ref, *refs):
    refs[-1][...] = sum(ref[...].astype(F32) for ref in refs[:-1]).astype(BF)


def add_pieces(turns, terms):
    depth, width = terms[0].shape
    block = rows_block(width, depth // 4)
    shape = like((depth, width))
    return call(
        add_kernel, turns, 4, [block] * len(terms), [block], [shape], terms, limit=SMALL
    )[0]


def turn_kernel(t_ref, x_ref, g_ref, v_ref, xo_ref, go_ref, vo_ref, s_ref):
    xo_ref[...] = x_ref[...]
    go_ref[...] = g_ref[...]
    vo_ref[...] = v_ref[...]
    s_ref[...] = jnp.sum(g_ref[...].astype(F32), 0, keepdims=True)


def turn_in(turns, x, g, vectors):
    rows = turns.shape[0]
    part = x.shape[1] // rows

    def specs(array, turned):
        index = (lambda k, t: (0, t[k])) if turned else (lambda k, t: (0, k))
        return pl.BlockSpec((array.shape[0], part), index)

    total_shape = like((1, x.shape[1]), F32)
    return call(
        turn_kernel,
        turns,
        rows,
        [specs(v, True) for v in (x, g, vectors)],
        [specs(v, False) for v in (x, g, vectors)] + [specs(total_shape, True)],
        [like(v.shape, v.dtype) for v in (x, g, vectors)] + [total_shape],
        [x, g, vectors],
    )


def split_kernel(t_ref, w_ref, u_ref, d_ref):
    u_ref[0] = w_ref[:, 0, :]
    d_ref[0] = w_ref[:, 1, :]


def split_mlp(turns, weights, blks):
    depth, _, hidden = weights.shape
    part = hidden // blks
    block = pl.BlockSpec((1, depth, part), lambda b, t: (b, 0, 0))
    return call(
        split_kernel,
        turns,
        blks,
        [pl.BlockSpec((depth, 2, part), lambda b, t: (0, 0, b))],
        [block] * 2,
        [like((blks, depth, part))] * 2,
        [weights],
    )


def join_kernel(t_ref, u_ref, d_ref, o_ref):
    o_ref[:, 0, :] = u_ref[0].astype(F32)
    o_ref[:, 1, :] = d_ref[0].astype(F32)


def join_mlp(turns, up, down):
    blks, depth, part = up.shape
    block = pl.BlockSpec((1, depth, part), lambda b, t: (b, 0, 0))
    return call(
        join_kernel,
        turns,
        blks,
        [block] * 2,
        [pl.BlockSpec((depth, 2, part), lambda b, t: (0, 0, b))],
        [like((depth, 2, blks * part), F32)],
        [up, down],
    )[0]


def split_attn_kernel(plan, width, t_ref, w_ref, qkv_ref, out_ref):
    b = pl.program_id(0)
    head = b % plan.group // plan.share * plan.per_row + b // plan.group
    for i in range(3):
        at = pl.multiple_of(i * width + head * HD, HD)
        qkv_ref[0, :, i * HD : (i + 1) * HD] = w_ref[:, pl.ds(at, HD)]

    @pl.when(b == 0)
    def _():
        out_ref[...] = w_ref[:, 3 * width :]


def split_attn(turns, weights, plan, width):
    depth = weights.shape[0]
    return call(
        functools.partial(split_attn_kernel, plan, width),
        turns,
        plan.blks,
        [whole(weights)],
        [
            pl.BlockSpec((1, depth, 3 * HD), lambda b, t: (b, 0, 0)),
            pl.BlockSpec((depth, width), lambda b, t: (0, 0)),
        ],
        [like((plan.blks, depth, 3 * HD)), like((depth, width))],
        [weights],
        limit=SMALL,
    )


def join_attn_kernel(plan, t_ref, qkv_ref, out_ref, o_ref):
    step = pl.program_id(0)
    heads = o_ref.shape[1] // HD

    @pl.when(step < 3)
    def _():
        at = pl.ds(pl.multiple_of(step * HD, HD), HD)
        for h in range(heads):
            first = h % plan.per_row * plan.group + h // plan.per_row * plan.share
            o_ref[:, h * HD : (h + 1) * HD] = sum(
                qkv_ref[first + i, :, at].astype(F32) for i in range(plan.share)
            )

    @pl.when(step == 3)
    def _():
        o_ref[...] = out_ref[...]


def join_attn(turns, qkv, out, plan):
    depth, width = out.shape
    return call(
        functools.partial(join_attn_kernel, plan),
        turns,
        4,
        [whole(qkv), whole(out)],
        [pl.BlockSpec((depth, width), lambda j, t: (0, j))],
        [like((depth, 4 * width), F32)],
        [qkv, out],
    )[0]


def pick_kernel(count, t_ref, *refs):
    pieces, outs = refs[:count], refs[count:]
    share = t_ref.shape[0] // len(outs)
    for n, out in enumerate(outs):
        for i in range(share):
            for k, piece in enumerate(pieces):

                @pl.when(t_ref[n * share + i] == k)
                def _(i=i, out=out, piece=piece):
                    out[...] = piece[...] if i == 0 else out[...] + piece[...]


def pick(table, pieces, count):
    return call(
        functools.partial(pick_kernel, len(pieces)),
        table,
        1,
        [whole(p) for p in pieces],
        [whole(pieces[0])] * count,
        [like(pieces[0].shape)] * count,
        pieces,
    )


def place_kernel(t_ref, *refs):
    *pieces, out_ref = refs
    for k, piece in enumerate(pieces):
        depth = piece.shape[0]
        out_ref[pl.ds(pl.multiple_of(t_ref[k] * depth, depth), depth)] = piece[...]


def place(table, pieces):
    depth, width = pieces[0].shape
    shape = like((len(pieces) * depth, width))
    return call(place_kernel, table, 1, [whole(p) for p in pieces], [whole(shape)], [shape], pieces)[0]


def norm_kernel(t_ref, x_ref, v_ref, a1_ref, a2_ref):
    field = x_ref[...].astype(F32)
    centred = field - jnp.mean(field, -1, keepdims=True)
    standard = centred * lax.rsqrt(jnp.mean(centred * centred, -1, keepdims=True) + EPSILON)
    a1_ref[...] = (standard * v_ref[0:1] + v_ref[1:2]).astype(BF)
    a2_ref[...] = (standard * v_ref[2:3] + v_ref[3:4]).astype(BF)


def norms(turns, x, vectors):
    count, width = x.shape
    return call(
        norm_kernel,
        turns,
        count // BLOCK,
        [rows_block(width), whole(vectors)],
        [rows_block(width)] * 2,
        [like(x.shape)] * 2,
        [x, vectors],
        20 * count * width,
    )


def times_pieces(left, pieces):
    out, start = None, 0
    for piece in pieces:
        depth = piece.shape[0]
        term = dot(left[:, start : start + depth], piece[...], 1, 0)
        out = term if out is None else out + term
        start += depth
    return out


def up_kernel(t_ref, a_ref, b_ref, *refs):
    pieces, (h_ref, s_ref) = refs[:-2], refs[-2:]
    pre = times_pieces(a_ref[...], pieces) + b_ref[...]
    cdf = 0.5 * (1.0 + lax.erf(pre * math.sqrt(0.5)))
    h_ref[...] = (pre * cdf).astype(BF)
    s_ref[...] = cdf + pre * (jnp.exp(-0.5 * pre * pre) * (1.0 / math.sqrt(2.0 * math.pi)))


def feed_up(turns, normed, bias, pieces):
    count, width = normed.shape
    hidden = bias.shape[0]
    return call(
        up_kernel,
        turns,
        count // BLOCK,
        [rows_block(width), pl.BlockSpec((1, hidden), lambda i, t: (0, 0))]
        + [whole(p) for p in pieces],
        [rows_block(hidden)] * 2,
        [like((count, hidden)), like((count, hidden), F32)],
        [normed, bias.reshape(1, hidden)] + pieces,
        2 * count * width * hidden,
    )


def slope_kernel(t_ref, g_ref, s_ref, *refs):
    pieces, (p_ref, sum_ref) = refs[:-2], refs[-2:]

    @pl.when(pl.program_id(0) == 0)
    def _():
        sum_ref[...] = jnp.zeros_like(sum_ref)

    grad = (times_pieces(g_ref[...], pieces) * s_ref[...]).astype(BF)
    p_ref[...] = grad
    sum_ref[...] += jnp.sum(grad.astype(F32), 0, keepdims=True)


def feed_slope(turns, grad, slope, pieces):
    count, width = grad.shape
    hidden = slope.shape[1]
    return call(
        slope_kernel,
        turns,
        count // BLOCK,
        [rows_block(width), rows_block(hidden)] + [whole(p) for p in pieces],
        [rows_block(hidden), pl.BlockSpec((1, hidden), lambda i, t: (0, 0))],
        [like((count, hidden)), like((1, hidden), F32)],
        [grad, slope] + pieces,
        2 * count * width * hidden,
    )


def lane_sum(field):
    return sum(field[:, i : i + LANES] for i in range(0, field.shape[1], LANES))


def weight_kernel(rows, with_sums, t_ref, l_ref, r_ref, *refs):
    step = pl.program_id(0)
    if with_sums:
        sum_ref, pieces, refs = refs[0], refs[1 : 1 + rows], refs[1 + rows :]
        parts_ref = refs[-1]
    grad = dot(l_ref[...], r_ref[...], 0, 0)
    for k in range(rows):

        @pl.when(step == k)
        def _(k=k):
            refs[k][...] = grad.astype(BF)
            if with_sums:
                piece = pieces[k][...].astype(F32)
                parts_ref[0] = lane_sum(piece * grad)
                parts_ref[1] = lane_sum(piece * sum_ref[...])


def weight_grad(turns, left, right, sums=None, pieces=()):
    rows = turns.shape[0]
    count, width = left.shape
    columns = right.shape[1]
    depth = width // rows
    out_shape = [like((depth, columns))] * rows
    out_specs = [whole(v) for v in out_shape]
    operands = [left, right]
    if pieces:
        operands += [sums] + pieces
        out_shape.append(like((2, width, LANES), F32))
        out_specs.append(pl.BlockSpec((2, depth, LANES), lambda k, t: (0, t[k], 0)))
    out = call(
        functools.partial(weight_kernel, rows, bool(pieces)),
        turns,
        rows,
        [pl.BlockSpec((count, depth), lambda k, t: (0, k))] + [whole(v) for v in operands[1:]],
        out_specs,
        out_shape,
        operands,
        2 * count * width * columns,
    )
    if pieces:
        return out[:-1], out[-1]
    return out


def out_kernel(rows, t_ref, o_ref, g_ref, *refs):
    *outs, grad_ref = refs
    depth = outs[0].shape[0]
    grad_ref[...] = dot(o_ref[...], g_ref[...], 0, 0)
    for j, out in enumerate(outs):
        at = pl.multiple_of(t_ref[rows + j] * depth, depth)
        out[...] = grad_ref[pl.ds(at, depth)].astype(BF)


def out_grad(turns, places, attended, grad):
    rows, group = turns.shape[0], places.shape[0]
    count, width = grad.shape
    part = width // rows
    depth = HD // group
    return pl.pallas_call(
        functools.partial(out_kernel, rows),
        name="out_kernel",
        grid_spec=pltpu.PrefetchScalarGridSpec(
            num_scalar_prefetch=1,
            grid=(rows,),
            in_specs=[whole(attended), pl.BlockSpec((count, part), lambda k, t: (0, k))],
            out_specs=[pl.BlockSpec((depth, part), lambda k, t: (0, t[k]))] * group,
            scratch_shapes=[pltpu.VMEM((HD, part), F32)],
        ),
        out_shape=[like((depth, width))] * group,
        compiler_params=pltpu.CompilerParams(vmem_limit_bytes=VMEM_LIMIT),
        cost_estimate=pl.CostEstimate(
            flops=2 * count * width * HD // COST,
            bytes_accessed=2 * (count * (width + HD) + width * HD) // COST,
            transcendentals=0,
        ),
    )(jnp.concatenate([turns, places]), attended, grad)


def turned_columns(t_ref, w_ref, k, depth):
    return w_ref[:, pl.ds(pl.multiple_of(t_ref[k] * depth, LANES), depth)]


def sum_kernel(t_ref, h_ref, o_ref, w_ref, *refs):
    pieces, y_ref = refs[:-1], refs[-1]
    for k, piece in enumerate(pieces):
        depth = piece.shape[0]
        term = dot(h_ref[...], piece[...], 1, 1)
        term += dot(o_ref[...], turned_columns(t_ref, w_ref, k, depth), 1, 0)
        y_ref[:, k * depth : (k + 1) * depth] = term.astype(BF)


def out_sum(turns, hidden, pieces, attended, out_w):
    count = hidden.shape[0]
    width = out_w.shape[1]
    return call(
        sum_kernel,
        turns,
        count // BLOCK,
        [rows_block(hidden.shape[1]), rows_block(HD), whole(out_w)] + [whole(p) for p in pieces],
        [rows_block(width)],
        [like((count, width))],
        [hidden, attended, out_w] + pieces,
        2 * count * width * (hidden.shape[1] + HD),
    )[0]


def back_kernel(t_ref, p_ref, q_ref, v_ref, *refs):
    pieces, c_ref = refs[:-1], refs[-1]
    count = len(pieces) // 2
    for k, (up, qkv) in enumerate(zip(pieces[:count], pieces[count:])):
        depth = up.shape[0]
        cols = slice(k * depth, (k + 1) * depth)
        term = dot(p_ref[...], up[...], 1, 1) * v_ref[2:3, cols]
        term += dot(q_ref[...], qkv[...], 1, 1) * v_ref[0:1, cols]
        c_ref[:, cols] = term.astype(BF)


def norm_back(turns, pre_grad, up_pieces, qkv_grad, qkv_pieces, vectors):
    count = pre_grad.shape[0]
    width = vectors.shape[1]
    columns = pre_grad.shape[1] + qkv_grad.shape[1]
    return call(
        back_kernel,
        turns,
        count // BLOCK,
        [rows_block(pre_grad.shape[1]), rows_block(qkv_grad.shape[1]), whole(vectors)]
        + [whole(p) for p in up_pieces + qkv_pieces],
        [rows_block(width)],
        [like((count, width))],
        [pre_grad, qkv_grad, vectors] + up_pieces + qkv_pieces,
        2 * count * width * columns,
    )[0]


def turned(field, cosine, minus, plus):
    head = field[:, :LANES]
    half = ROT // 2
    head = (
        head * cosine
        + pltpu.roll(head, LANES - half, 1) * minus
        + pltpu.roll(head, half, 1) * plus
    )
    return jnp.concatenate([head, field[:, LANES:]], 1)


def allowed_pairs(length, dq_ref, dk_ref):
    spot = lax.broadcasted_iota(jnp.int32, (length, length), 0)
    other = lax.broadcasted_iota(jnp.int32, (length, length), 1)
    return (dq_ref[0] == dk_ref[0]) & (other <= spot)


def forward_kernel(t_ref, a_ref, b_ref, c_ref, m_ref, p_ref, dq_ref, dk_ref, *refs):
    pieces, (qkv_ref, o_ref, lse_ref) = refs[:-3], refs[-3:]
    qkv = times_pieces(a_ref[...], pieces) + b_ref[...]
    tables = c_ref[0], m_ref[0], p_ref[0]
    queries = (turned(qkv[:, :HD], *tables) * HD ** (-0.5)).astype(BF)
    keys = turned(qkv[:, HD : 2 * HD], *tables).astype(BF)
    values = qkv[:, 2 * HD :].astype(BF)
    for i, field in enumerate((queries, keys, values)):
        qkv_ref[:, i * HD : (i + 1) * HD] = field
    allowed = allowed_pairs(a_ref.shape[0], dq_ref, dk_ref)
    scores = jnp.where(allowed, dot(queries, keys, 1, 1), MASKED)
    largest = jnp.max(scores, -1, keepdims=True)
    weights = jnp.where(allowed, jnp.exp(scores - largest), 0.0)
    mass = jnp.sum(weights, -1, keepdims=True)
    o_ref[...] = dot((weights / mass).astype(BF), values, 1, 0).astype(BF)
    lse_ref[...] = largest + jnp.log(mass)


def backward_kernel(
    parts, t_ref, g_ref, w_ref, qkv_ref, o_ref, lse_ref, c_ref, m_ref, p_ref, dq_ref, dk_ref,
    grad_ref, sum_ref,
):
    queries, keys, values = (qkv_ref[:, i * HD : (i + 1) * HD] for i in range(3))
    tables = c_ref[0], -m_ref[0], -p_ref[0]
    depth = w_ref.shape[1] // parts
    heads_grad = None
    for k in range(parts):
        cols = slice(k * depth, (k + 1) * depth)
        term = dot(g_ref[:, cols], turned_columns(t_ref, w_ref, k, depth), 1, 1)
        heads_grad = term if heads_grad is None else heads_grad + term
    heads_grad = heads_grad.astype(BF)
    allowed = allowed_pairs(g_ref.shape[0], dq_ref, dk_ref)
    scores = jnp.where(allowed, dot(queries, keys, 1, 1), MASKED)
    weights = jnp.where(allowed, jnp.exp(scores - lse_ref[...]), 0.0)
    deltas = jnp.sum(heads_grad.astype(F32) * o_ref[...].astype(F32), -1, keepdims=True)
    score_grad = (weights * (dot(heads_grad, values, 1, 1) - deltas)).astype(BF)
    query_grad = dot(score_grad, keys, 1, 0) * HD ** (-0.5)
    key_grad = dot(score_grad, queries, 0, 0)
    value_grad = dot(weights.astype(BF), heads_grad, 0, 0)
    fields = turned(query_grad, *tables), turned(key_grad, *tables), value_grad

    @pl.when(pl.program_id(0) == 0)
    def _():
        sum_ref[...] = jnp.zeros_like(sum_ref)

    for i, field in enumerate(fields):
        field = field.astype(BF)
        cols = slice(i * HD, (i + 1) * HD)
        grad_ref[:, cols] = field
        sum_ref[:, cols] += jnp.sum(field.astype(F32), 0, keepdims=True)


def pair_specs(length):
    table = pl.BlockSpec((1, length, LANES), lambda r, t: (r, 0, 0))
    return [table] * 3 + [
        pl.BlockSpec((1, length, 1), lambda r, t: (r, 0, 0)),
        pl.BlockSpec((1, 1, length), lambda r, t: (r, 0, 0)),
    ]


def head_forward(turns, normed, bias, pairs, pieces, length):
    count, width = normed.shape
    columns = 3 * HD
    return call(
        forward_kernel,
        turns,
        count // length,
        [rows_block(width, length), pl.BlockSpec((1, columns), lambda r, t: (0, 0))]
        + pair_specs(length)
        + [whole(p) for p in pieces],
        [rows_block(columns, length), rows_block(HD, length), rows_block(1, length)],
        [like((count, columns)), like((count, HD)), like((count, 1), F32)],
        [normed, bias.reshape(1, columns)] + pairs + pieces,
        2 * count * (width * columns + 2 * length * HD),
    )


def head_backward(turns, grad, out_w, qkv, attended, lse, pairs, length):
    count, width = grad.shape
    columns = 3 * HD
    return call(
        functools.partial(backward_kernel, turns.shape[0]),
        turns,
        count // length,
        [
            rows_block(width, length),
            whole(out_w),
            rows_block(columns, length),
            rows_block(HD, length),
            rows_block(1, length),
        ]
        + pair_specs(length),
        [rows_block(columns, length), pl.BlockSpec((1, columns), lambda r, t: (0, 0))],
        [like((count, columns)), like((1, columns), F32)],
        [grad, out_w, qkv, attended, lse] + pairs,
        2 * count * (width * HD + 5 * length * HD),
    )


def finish_kernel(rows, with_norm, t_ref, x_ref, s_ref, o_ref, out_ref):
    depth = x_ref.shape[1] // rows
    term = s_ref[...].astype(F32)
    if with_norm:
        centred = x_ref[...].astype(F32)
        centred = centred - jnp.mean(centred, -1, keepdims=True)
        rstd = lax.rsqrt(jnp.mean(centred * centred, -1, keepdims=True) + EPSILON)
        centred = centred * rstd
        term = term - jnp.mean(term, -1, keepdims=True) - centred * jnp.mean(
            term * centred, -1, keepdims=True
        )
        field = o_ref[...].astype(F32) + rstd * term
    else:
        field = x_ref[...].astype(F32) + term + o_ref[4:5]
    for k in range(rows):
        at = pl.multiple_of(t_ref[k] * depth, LANES)
        out_ref[:, pl.ds(at, depth)] = field[:, k * depth : (k + 1) * depth].astype(BF)


def finish(turns, x, term, other, with_norm):
    return call(
        functools.partial(finish_kernel, turns.shape[0], with_norm),
        turns,
        1,
        [whole(v) for v in (x, term, other)],
        [whole(x)],
        [like(x.shape)],
        [x, term, other],
    )[0]


def shards(
    plan,
    tokens,
    attn_weights,
    mlp_weights,
    ln1_gain,
    ln1_bias,
    ln2_gain,
    ln2_bias,
    qkv_bias,
    dense_bias,
    up_bias,
    down_bias,
    doc_lengths,
    cotangent,
):
    row_count, shard_len, width = tokens.shape
    depth = attn_weights.shape[0]
    heads = width // HD
    rows, blks = plan.rows, plan.blks
    own_hidden = mlp_weights.shape[-1] // blks
    me = lax.axis_index("blk")
    length = shard_len * blks
    count = row_count * length
    head_of = me % plan.group // plan.share * plan.per_row + me // plan.group
    part = me % plan.share
    own_rows = row_count // plan.share
    row = lax.axis_index("row")
    turns = row ^ jnp.arange(rows, dtype=jnp.int32)
    places = me % plan.group ^ jnp.arange(plan.group, dtype=jnp.int32)

    def exchange(field):
        return lax.all_to_all(field, "blk", 0, 0)

    def collect(field):
        return exchange(field.reshape(blks, -1, field.shape[-1]))

    def gather_blocks(field):
        field = field.reshape(row_count, shard_len, width)
        return lax.all_gather(field, "blk", axis=1, tiled=True).reshape(count, width)

    def sum_blocks(field):
        field = field.reshape(row_count, length, width)
        field = lax.psum_scatter(field, "blk", scatter_dimension=1, tiled=True)
        return field.reshape(row_count * shard_len, width)

    zeros = jnp.zeros((3, width), F32)
    vectors = jnp.stack([ln1_gain, ln1_bias, ln2_gain, ln2_bias, dense_bias + down_bias])
    x_own, g_own, vectors, g_sum = turn_in(
        turns,
        tokens.reshape(row_count * shard_len, width),
        cotangent.reshape(row_count * shard_len, width),
        jnp.concatenate([vectors, zeros]),
    )
    qkv_send, out_own = split_attn(turns, attn_weights, plan, width)
    qkv_mine = exchange(qkv_send)
    out_send = pick(
        row ^ places // plan.share,
        [out_own] + [swap(out_own, "row", rows, k) for k in range(1, rows)],
        plan.group,
    )
    up_send, down_send = split_mlp(turns, after(mlp_weights, qkv_send), blks)
    qkv_mine, up_send, *out_send = lax.optimization_barrier((qkv_mine, up_send, *out_send))
    up_mine = exchange(up_send)
    qkv_pieces = gather_row(qkv_mine.reshape(-1, 3 * HD), plan)
    out_got = [out_send[0]] + [swap_group(out_send[j], plan, j) for j in range(1, plan.group)]
    up_mine, x_own, down_send, *qkv_pieces = lax.optimization_barrier(
        (up_mine, x_own, down_send, *qkv_pieces, *out_got)
    )[: 3 + rows]
    x_all = gather_blocks(x_own)
    down_mine = exchange(down_send)
    up_pieces = gather_row(up_mine.reshape(-1, own_hidden), plan)
    out_w = place(places, out_got)
    down_mine, g_own, x_all, *up_pieces = lax.optimization_barrier(
        (down_mine, g_own, x_all, *up_pieces)
    )
    g_all = gather_blocks(g_own)
    down_pieces = gather_row(down_mine.reshape(-1, own_hidden), plan)
    normed1, normed2 = norms(turns, x_all, vectors)

    lengths = lax.dynamic_slice_in_dim(doc_lengths, part * own_rows, own_rows, 0)
    doc_ends = jnp.cumsum(lengths, axis=-1)
    starts = doc_ends - lengths
    spots = jnp.arange(length, dtype=jnp.int32)
    doc_ids = jnp.sum((spots[None, :, None] >= doc_ends[:, None, :]).astype(jnp.int32), -1)
    picked = doc_ids[:, :, None] == jnp.arange(lengths.shape[-1], dtype=jnp.int32)
    positions = spots - jnp.sum(jnp.where(picked, starts[:, None, :], 0), -1)
    lane = jnp.arange(LANES)
    inverse = 10000.0 ** (-2.0 * (lane % (ROT // 2)).astype(F32) / ROT)
    angles = positions.astype(F32)[..., None] * inverse
    sine = jnp.sin(angles)
    pairs = [
        jnp.where(lane < ROT, jnp.cos(angles), 1.0),
        jnp.where(lane < ROT // 2, -sine, 0.0),
        jnp.where((lane >= ROT // 2) & (lane < ROT), sine, 0.0),
        doc_ids[:, :, None],
        doc_ids[:, None, :],
    ]

    def own(field):
        if plan.share == 1:
            return field
        return lax.dynamic_slice_in_dim(field, part * own_rows * length, own_rows * length, 0)

    def spread(field):
        if plan.share == 1:
            return field
        blank = jnp.zeros((count, field.shape[1]), field.dtype)
        return lax.dynamic_update_slice_in_dim(blank, field, part * own_rows * length, 0)

    up_b = lax.dynamic_slice_in_dim(up_bias, me * own_hidden, own_hidden)
    qkv_b = lax.dynamic_index_in_dim(qkv_bias.reshape(3, heads, HD), head_of, 1, keepdims=False)
    own_normed1 = own(normed1)
    qkv, attended, lse = head_forward(
        turns, own_normed1, qkv_b.reshape(-1), pairs, qkv_pieces, length
    )
    hidden, slope = feed_up(turns, after(normed2, attended), up_b, up_pieces)
    out_term = out_sum(turns, hidden, down_pieces, spread(attended), out_w)
    out_total = sum_blocks(out_term)

    g_all = after(g_all, out_term)
    down_g = weight_grad(turns, g_all, hidden)
    down_got = scatter_row(down_g, plan)
    pre_grad, up_sum = feed_slope(turns, after(g_all, down_g[0]), slope, down_pieces)
    own_grad = own(after(g_all, pre_grad))
    qkv_grad, qkv_sum = head_backward(
        turns, own_grad, out_w, qkv, attended, lse, pairs, length
    )
    norm_term = norm_back(
        turns, pre_grad, up_pieces, spread(qkv_grad), qkv_pieces, vectors
    )
    norm_total = sum_blocks(norm_term)
    down_total = add_pieces(turns, [after(down_got[0], norm_term)] + down_got[1:])
    down_back = collect(down_total)
    up_g, up_parts = weight_grad(
        turns, after(normed2, down_total, out_total), pre_grad, up_sum, up_pieces
    )
    up_got = scatter_row(up_g, plan)
    qkv_g, qkv_parts = weight_grad(
        turns, after(own_normed1, up_g[0]), qkv_grad, qkv_sum, qkv_pieces
    )
    qkv_got = scatter_row(qkv_g, plan)
    out_g = out_grad(turns, places, after(attended, qkv_g[0], down_back), own_grad)
    out_got = [out_g[0]] + [swap_group(out_g[j], plan, j) for j in range(1, plan.group)]
    up_total = add_pieces(turns, [after(up_got[0], *out_got)] + up_got[1:])
    up_back = collect(up_total)
    holders = turns[:, None] * plan.share + jnp.arange(plan.share, dtype=jnp.int32)
    out_send = pick((me % plan.group ^ holders).reshape(-1), out_got, rows)
    out_back = out_send[0].astype(F32) + sum(
        swap(after(out_send[k], up_total), "row", rows, k).astype(F32) for k in range(1, rows)
    )

    terms = [jnp.sum(after(v, up_total), -1) for v in (qkv_parts, up_parts)]
    terms += [g_sum, qkv_sum, up_sum]
    terms = [v.reshape(-1) for v in terms]
    used = sum(v.size for v in terms)
    terms.append(jnp.zeros((-used % (8 * LANES),), F32))
    sums = jnp.concatenate(terms)
    sums = sums + sum(swap(sums, "row", rows, k) for k in range(1, rows))

    qkv_total = add_pieces(turns, [after(qkv_got[0], out_back, sums, up_back)] + qkv_got[1:])
    qkv_back = collect(qkv_total)
    sums = after(sums, qkv_total)
    sums = jnp.stack([sums] + [swap(sums, "blk", blks, k) for k in range(1, blks)])
    sums = sums[me ^ jnp.arange(blks, dtype=jnp.int32)]
    gain1, bias1, gain2, bias2, g_total = jnp.split(
        jnp.sum(sums[:, : 5 * width], 0), 5
    )
    sums = sums[:, 5 * width : used]
    qkv_bias_grad = sums[:, : 3 * HD].reshape(plan.per_row, rows, plan.share, 3, HD)
    qkv_bias_grad = jnp.sum(qkv_bias_grad, 2).transpose(2, 1, 0, 3).reshape(-1)
    up_bias_grad = sums[:, 3 * HD :].reshape(-1)

    layer_out = finish(turns, x_own, out_total, vectors, False)
    tokens_grad = finish(turns, x_own, norm_total, g_own, True)
    return (
        layer_out.reshape(tokens.shape),
        tokens_grad.reshape(tokens.shape),
        join_attn(turns, qkv_back, out_back, plan),
        join_mlp(turns, up_back, down_back),
        (gain1 - ln1_bias * bias1) / ln1_gain,
        bias1,
        (gain2 - ln2_bias * bias2) / ln2_gain,
        bias2,
        qkv_bias_grad,
        g_total,
        up_bias_grad,
        g_total,
    )


def solution(mesh):
    rows, blks = mesh.shape["row"], mesh.shape["blk"]
    vector = P()
    tokens = P("row", "blk", None)
    attn = P(("row", "blk"), None)
    mlp = P(("row", "blk"), None, None)

    def run(*arrays):
        plan = Plan(rows, blks, arrays[0].shape[-1] // HD)
        return jax.shard_map(
            functools.partial(shards, plan),
            mesh=mesh,
            in_specs=(tokens, attn, mlp) + (vector,) * 8 + (P("row", None), tokens),
            out_specs=(tokens, tokens, attn, mlp) + (vector,) * 8,
            check_vma=False,
        )(*arrays)

    return run
```

```python
import functools
import math

import jax
import jax.numpy as jnp
import numpy as np
from jax import lax
from jax.experimental import pallas as pl
from jax.experimental.pallas import tpu as pltpu
from jax.sharding import PartitionSpec as P

HD = 256
ROT = 64
LANES = 128
BLOCK = 256
EPSILON = 1e-05
MASKED = -1e30
BF = jnp.bfloat16
F32 = jnp.float32
COST = 100
VMEM_LIMIT = 56 * 2**20
SMALL = 16 * 2**20


class Plan:
    def __init__(self, rows, blks, heads):
        self.rows = rows
        self.blks = blks
        self.share = blks // heads
        self.per_row = heads // rows
        self.group = blks // self.per_row
        self.groups = [
            list(range(i * self.group, (i + 1) * self.group)) for i in range(self.per_row)
        ]


def after(field, *others):
    return lax.optimization_barrier((field,) + others)[0] if others else field


def swap(field, axis, size, bit):
    return lax.ppermute(field, axis, [(i, i ^ bit) for i in range(size)])


def swap_group(field, plan, bits):
    return lax.ppermute(field, "blk", [(i, i ^ bits) for i in range(plan.blks)])


def gather_row(own, plan):
    return [own] + [swap(own, "row", plan.rows, k) for k in range(1, plan.rows)]


def scatter_row(pieces, plan):
    return [pieces[0]] + [swap(pieces[k], "row", plan.rows, k) for k in range(1, plan.rows)]


def dot(left, right, left_dim, right_dim):
    return lax.dot_general(
        left, right, (((left_dim,), (right_dim,)), ((), ())), preferred_element_type=F32
    )


def whole(array):
    return pl.BlockSpec(array.shape, lambda *i: (0,) * len(array.shape))


def like(shape, kind=BF):
    return jax.ShapeDtypeStruct(shape, kind)


def call(body, turns, grid, in_specs, out_specs, out_shape, operands, flops=0, limit=None):
    moved = sum(v.size * v.dtype.itemsize for v in operands)
    moved += sum(math.prod(v.shape) * jnp.dtype(v.dtype).itemsize for v in out_shape)
    return pl.pallas_call(
        body,
        name=getattr(body, "func", body).__name__,
        grid_spec=pltpu.PrefetchScalarGridSpec(
            num_scalar_prefetch=1, grid=(grid,), in_specs=in_specs, out_specs=out_specs
        ),
        out_shape=out_shape,
        compiler_params=pltpu.CompilerParams(vmem_limit_bytes=limit or VMEM_LIMIT),
        cost_estimate=pl.CostEstimate(
            flops=flops // COST, bytes_accessed=moved // COST, transcendentals=0
        ),
    )(turns, *operands)


def rows_block(columns, block=BLOCK):
    return pl.BlockSpec((block, columns), lambda i, t: (i, 0))


def add_kernel(t_ref, *refs):
    refs[-1][...] = sum(ref[...].astype(F32) for ref in refs[:-1]).astype(BF)


def add_pieces(turns, terms):
    depth, width = terms[0].shape
    block = rows_block(width, depth // 4)
    shape = like((depth, width))
    return call(
        add_kernel, turns, 4, [block] * len(terms), [block], [shape], terms, limit=SMALL
    )[0]


def turn_kernel(t_ref, x_ref, g_ref, v_ref, xo_ref, go_ref, vo_ref, s_ref):
    xo_ref[...] = x_ref[...]
    go_ref[...] = g_ref[...]
    vo_ref[...] = v_ref[...]
    s_ref[...] = jnp.sum(g_ref[...].astype(F32), 0, keepdims=True)


def turn_in(turns, x, g, vectors):
    rows = turns.shape[0]
    part = x.shape[1] // rows

    def specs(array, turned):
        index = (lambda k, t: (0, t[k])) if turned else (lambda k, t: (0, k))
        return pl.BlockSpec((array.shape[0], part), index)

    total_shape = like((1, x.shape[1]), F32)
    return call(
        turn_kernel,
        turns,
        rows,
        [specs(v, True) for v in (x, g, vectors)],
        [specs(v, False) for v in (x, g, vectors)] + [specs(total_shape, True)],
        [like(v.shape, v.dtype) for v in (x, g, vectors)] + [total_shape],
        [x, g, vectors],
    )


def split_kernel(t_ref, w_ref, u_ref, d_ref):
    u_ref[0] = w_ref[:, 0, :]
    d_ref[0] = w_ref[:, 1, :]


def split_mlp(turns, weights, blks):
    depth, _, hidden = weights.shape
    part = hidden // blks
    block = pl.BlockSpec((1, depth, part), lambda b, t: (b, 0, 0))
    return call(
        split_kernel,
        turns,
        blks,
        [pl.BlockSpec((depth, 2, part), lambda b, t: (0, 0, b))],
        [block] * 2,
        [like((blks, depth, part))] * 2,
        [weights],
    )


def join_kernel(t_ref, u_ref, d_ref, o_ref):
    o_ref[:, 0, :] = u_ref[0].astype(F32)
    o_ref[:, 1, :] = d_ref[0].astype(F32)


def join_mlp(turns, up, down):
    blks, depth, part = up.shape
    block = pl.BlockSpec((1, depth, part), lambda b, t: (b, 0, 0))
    return call(
        join_kernel,
        turns,
        blks,
        [block] * 2,
        [pl.BlockSpec((depth, 2, part), lambda b, t: (0, 0, b))],
        [like((depth, 2, blks * part), F32)],
        [up, down],
    )[0]


def split_attn_kernel(plan, width, t_ref, w_ref, qkv_ref, out_ref):
    b = pl.program_id(0)
    head = b % plan.group // plan.share * plan.per_row + b // plan.group
    for i in range(3):
        at = pl.multiple_of(i * width + head * HD, HD)
        qkv_ref[0, :, i * HD : (i + 1) * HD] = w_ref[:, pl.ds(at, HD)]

    @pl.when(b == 0)
    def _():
        out_ref[...] = w_ref[:, 3 * width :]


def split_attn(turns, weights, plan, width):
    depth = weights.shape[0]
    return call(
        functools.partial(split_attn_kernel, plan, width),
        turns,
        plan.blks,
        [whole(weights)],
        [
            pl.BlockSpec((1, depth, 3 * HD), lambda b, t: (b, 0, 0)),
            pl.BlockSpec((depth, width), lambda b, t: (0, 0)),
        ],
        [like((plan.blks, depth, 3 * HD)), like((depth, width))],
        [weights],
        limit=SMALL,
    )


def join_attn_kernel(plan, t_ref, qkv_ref, out_ref, o_ref):
    step = pl.program_id(0)
    heads = o_ref.shape[1] // HD

    @pl.when(step < 3)
    def _():
        at = pl.ds(pl.multiple_of(step * HD, HD), HD)
        for h in range(heads):
            first = h % plan.per_row * plan.group + h // plan.per_row * plan.share
            o_ref[:, h * HD : (h + 1) * HD] = sum(
                qkv_ref[first + i, :, at].astype(F32) for i in range(plan.share)
            )

    @pl.when(step == 3)
    def _():
        o_ref[...] = out_ref[...]


def join_attn(turns, qkv, out, plan):
    depth, width = out.shape
    return call(
        functools.partial(join_attn_kernel, plan),
        turns,
        4,
        [whole(qkv), whole(out)],
        [pl.BlockSpec((depth, width), lambda j, t: (0, j))],
        [like((depth, 4 * width), F32)],
        [qkv, out],
    )[0]


def pick_kernel(count, t_ref, *refs):
    pieces, outs = refs[:count], refs[count:]
    share = t_ref.shape[0] // len(outs)
    for n, out in enumerate(outs):
        for i in range(share):
            for k, piece in enumerate(pieces):

                @pl.when(t_ref[n * share + i] == k)
                def _(i=i, out=out, piece=piece):
                    out[...] = piece[...] if i == 0 else out[...] + piece[...]


def pick(table, pieces, count):
    return call(
        functools.partial(pick_kernel, len(pieces)),
        table,
        1,
        [whole(p) for p in pieces],
        [whole(pieces[0])] * count,
        [like(pieces[0].shape)] * count,
        pieces,
    )


def place_kernel(t_ref, *refs):
    *pieces, out_ref = refs
    for k, piece in enumerate(pieces):
        depth = piece.shape[0]
        out_ref[pl.ds(pl.multiple_of(t_ref[k] * depth, depth), depth)] = piece[...]


def place(table, pieces):
    depth, width = pieces[0].shape
    shape = like((len(pieces) * depth, width))
    return call(place_kernel, table, 1, [whole(p) for p in pieces], [whole(shape)], [shape], pieces)[0]


def norm_kernel(t_ref, x_ref, v_ref, a1_ref, a2_ref):
    field = x_ref[...].astype(F32)
    centred = field - jnp.mean(field, -1, keepdims=True)
    standard = centred * lax.rsqrt(jnp.mean(centred * centred, -1, keepdims=True) + EPSILON)
    a1_ref[...] = (standard * v_ref[0:1] + v_ref[1:2]).astype(BF)
    a2_ref[...] = (standard * v_ref[2:3] + v_ref[3:4]).astype(BF)


def norms(turns, x, vectors):
    count, width = x.shape
    return call(
        norm_kernel,
        turns,
        count // BLOCK,
        [rows_block(width), whole(vectors)],
        [rows_block(width)] * 2,
        [like(x.shape)] * 2,
        [x, vectors],
        20 * count * width,
    )


def times_pieces(left, pieces):
    out, start = None, 0
    for piece in pieces:
        depth = piece.shape[0]
        term = dot(left[:, start : start + depth], piece[...], 1, 0)
        out = term if out is None else out + term
        start += depth
    return out


def up_kernel(t_ref, a_ref, b_ref, *refs):
    pieces, (h_ref, s_ref) = refs[:-2], refs[-2:]
    pre = times_pieces(a_ref[...], pieces) + b_ref[...]
    cdf = 0.5 * (1.0 + lax.erf(pre * math.sqrt(0.5)))
    h_ref[...] = (pre * cdf).astype(BF)
    s_ref[...] = cdf + pre * (jnp.exp(-0.5 * pre * pre) * (1.0 / math.sqrt(2.0 * math.pi)))


def feed_up(turns, normed, bias, pieces):
    count, width = normed.shape
    hidden = bias.shape[0]
    return call(
        up_kernel,
        turns,
        count // BLOCK,
        [rows_block(width), pl.BlockSpec((1, hidden), lambda i, t: (0, 0))]
        + [whole(p) for p in pieces],
        [rows_block(hidden)] * 2,
        [like((count, hidden)), like((count, hidden), F32)],
        [normed, bias.reshape(1, hidden)] + pieces,
        2 * count * width * hidden,
    )


def slope_kernel(t_ref, g_ref, s_ref, *refs):
    pieces, (p_ref, sum_ref) = refs[:-2], refs[-2:]

    @pl.when(pl.program_id(0) == 0)
    def _():
        sum_ref[...] = jnp.zeros_like(sum_ref)

    grad = (times_pieces(g_ref[...], pieces) * s_ref[...]).astype(BF)
    p_ref[...] = grad
    sum_ref[...] += jnp.sum(grad.astype(F32), 0, keepdims=True)


def feed_slope(turns, grad, slope, pieces):
    count, width = grad.shape
    hidden = slope.shape[1]
    return call(
        slope_kernel,
        turns,
        count // BLOCK,
        [rows_block(width), rows_block(hidden)] + [whole(p) for p in pieces],
        [rows_block(hidden), pl.BlockSpec((1, hidden), lambda i, t: (0, 0))],
        [like((count, hidden)), like((1, hidden), F32)],
        [grad, slope] + pieces,
        2 * count * width * hidden,
    )


def lane_sum(field):
    return sum(field[:, i : i + LANES] for i in range(0, field.shape[1], LANES))


def weight_kernel(rows, with_sums, t_ref, l_ref, r_ref, *refs):
    step = pl.program_id(0)
    if with_sums:
        sum_ref, pieces, refs = refs[0], refs[1 : 1 + rows], refs[1 + rows :]
        parts_ref = refs[-1]
    grad = dot(l_ref[...], r_ref[...], 0, 0)
    for k in range(rows):

        @pl.when(step == k)
        def _(k=k):
            refs[k][...] = grad.astype(BF)
            if with_sums:
                piece = pieces[k][...].astype(F32)
                parts_ref[0] = lane_sum(piece * grad)
                parts_ref[1] = lane_sum(piece * sum_ref[...])


def weight_grad(turns, left, right, sums=None, pieces=()):
    rows = turns.shape[0]
    count, width = left.shape
    columns = right.shape[1]
    depth = width // rows
    out_shape = [like((depth, columns))] * rows
    out_specs = [whole(v) for v in out_shape]
    operands = [left, right]
    if pieces:
        operands += [sums] + pieces
        out_shape.append(like((2, width, LANES), F32))
        out_specs.append(pl.BlockSpec((2, depth, LANES), lambda k, t: (0, t[k], 0)))
    out = call(
        functools.partial(weight_kernel, rows, bool(pieces)),
        turns,
        rows,
        [pl.BlockSpec((count, depth), lambda k, t: (0, k))] + [whole(v) for v in operands[1:]],
        out_specs,
        out_shape,
        operands,
        2 * count * width * columns,
    )
    if pieces:
        return out[:-1], out[-1]
    return out


def out_kernel(rows, t_ref, o_ref, g_ref, *refs):
    *outs, grad_ref = refs
    depth = outs[0].shape[0]
    grad_ref[...] = dot(o_ref[...], g_ref[...], 0, 0)
    for j, out in enumerate(outs):
        at = pl.multiple_of(t_ref[rows + j] * depth, depth)
        out[...] = grad_ref[pl.ds(at, depth)].astype(BF)


def out_grad(turns, places, attended, grad):
    rows, group = turns.shape[0], places.shape[0]
    count, width = grad.shape
    part = width // rows
    depth = HD // group
    return pl.pallas_call(
        functools.partial(out_kernel, rows),
        name="out_kernel",
        grid_spec=pltpu.PrefetchScalarGridSpec(
            num_scalar_prefetch=1,
            grid=(rows,),
            in_specs=[whole(attended), pl.BlockSpec((count, part), lambda k, t: (0, k))],
            out_specs=[pl.BlockSpec((depth, part), lambda k, t: (0, t[k]))] * group,
            scratch_shapes=[pltpu.VMEM((HD, part), F32)],
        ),
        out_shape=[like((depth, width))] * group,
        compiler_params=pltpu.CompilerParams(vmem_limit_bytes=VMEM_LIMIT),
        cost_estimate=pl.CostEstimate(
            flops=2 * count * width * HD // COST,
            bytes_accessed=2 * (count * (width + HD) + width * HD) // COST,
            transcendentals=0,
        ),
    )(jnp.concatenate([turns, places]), attended, grad)


def turned_columns(t_ref, w_ref, k, depth):
    return w_ref[:, pl.ds(pl.multiple_of(t_ref[k] * depth, LANES), depth)]


def sum_kernel(t_ref, h_ref, o_ref, w_ref, *refs):
    pieces, y_ref = refs[:-1], refs[-1]
    for k, piece in enumerate(pieces):
        depth = piece.shape[0]
        term = dot(h_ref[...], piece[...], 1, 1)
        term += dot(o_ref[...], turned_columns(t_ref, w_ref, k, depth), 1, 0)
        y_ref[:, k * depth : (k + 1) * depth] = term.astype(BF)


def out_sum(turns, hidden, pieces, attended, out_w):
    count = hidden.shape[0]
    width = out_w.shape[1]
    return call(
        sum_kernel,
        turns,
        count // BLOCK,
        [rows_block(hidden.shape[1]), rows_block(HD), whole(out_w)] + [whole(p) for p in pieces],
        [rows_block(width)],
        [like((count, width))],
        [hidden, attended, out_w] + pieces,
        2 * count * width * (hidden.shape[1] + HD),
    )[0]


def back_kernel(t_ref, p_ref, q_ref, v_ref, *refs):
    pieces, c_ref = refs[:-1], refs[-1]
    count = len(pieces) // 2
    for k, (up, qkv) in enumerate(zip(pieces[:count], pieces[count:])):
        depth = up.shape[0]
        cols = slice(k * depth, (k + 1) * depth)
        term = dot(p_ref[...], up[...], 1, 1) * v_ref[2:3, cols]
        term += dot(q_ref[...], qkv[...], 1, 1) * v_ref[0:1, cols]
        c_ref[:, cols] = term.astype(BF)


def norm_back(turns, pre_grad, up_pieces, qkv_grad, qkv_pieces, vectors):
    count = pre_grad.shape[0]
    width = vectors.shape[1]
    columns = pre_grad.shape[1] + qkv_grad.shape[1]
    return call(
        back_kernel,
        turns,
        count // BLOCK,
        [rows_block(pre_grad.shape[1]), rows_block(qkv_grad.shape[1]), whole(vectors)]
        + [whole(p) for p in up_pieces + qkv_pieces],
        [rows_block(width)],
        [like((count, width))],
        [pre_grad, qkv_grad, vectors] + up_pieces + qkv_pieces,
        2 * count * width * columns,
    )[0]


def turned(field, cosine, minus, plus):
    head = field[:, :LANES]
    half = ROT // 2
    head = (
        head * cosine
        + pltpu.roll(head, LANES - half, 1) * minus
        + pltpu.roll(head, half, 1) * plus
    )
    return jnp.concatenate([head, field[:, LANES:]], 1)


def allowed_pairs(length, dq_ref, dk_ref):
    spot = lax.broadcasted_iota(jnp.int32, (length, length), 0)
    other = lax.broadcasted_iota(jnp.int32, (length, length), 1)
    return (dq_ref[0] == dk_ref[0]) & (other <= spot)


def forward_kernel(t_ref, a_ref, b_ref, c_ref, m_ref, p_ref, dq_ref, dk_ref, *refs):
    pieces, (qkv_ref, o_ref, lse_ref) = refs[:-3], refs[-3:]
    qkv = times_pieces(a_ref[...], pieces) + b_ref[...]
    tables = c_ref[0], m_ref[0], p_ref[0]
    queries = (turned(qkv[:, :HD], *tables) * HD ** (-0.5)).astype(BF)
    keys = turned(qkv[:, HD : 2 * HD], *tables).astype(BF)
    values = qkv[:, 2 * HD :].astype(BF)
    for i, field in enumerate((queries, keys, values)):
        qkv_ref[:, i * HD : (i + 1) * HD] = field
    allowed = allowed_pairs(a_ref.shape[0], dq_ref, dk_ref)
    scores = jnp.where(allowed, dot(queries, keys, 1, 1), MASKED)
    largest = jnp.max(scores, -1, keepdims=True)
    weights = jnp.where(allowed, jnp.exp(scores - largest), 0.0)
    mass = jnp.sum(weights, -1, keepdims=True)
    o_ref[...] = dot((weights / mass).astype(BF), values, 1, 0).astype(BF)
    lse_ref[...] = largest + jnp.log(mass)


def backward_kernel(
    parts, t_ref, g_ref, w_ref, qkv_ref, o_ref, lse_ref, c_ref, m_ref, p_ref, dq_ref, dk_ref,
    grad_ref, sum_ref,
):
    queries, keys, values = (qkv_ref[:, i * HD : (i + 1) * HD] for i in range(3))
    tables = c_ref[0], -m_ref[0], -p_ref[0]
    depth = w_ref.shape[1] // parts
    heads_grad = None
    for k in range(parts):
        cols = slice(k * depth, (k + 1) * depth)
        term = dot(g_ref[:, cols], turned_columns(t_ref, w_ref, k, depth), 1, 1)
        heads_grad = term if heads_grad is None else heads_grad + term
    heads_grad = heads_grad.astype(BF)
    allowed = allowed_pairs(g_ref.shape[0], dq_ref, dk_ref)
    scores = jnp.where(allowed, dot(queries, keys, 1, 1), MASKED)
    weights = jnp.where(allowed, jnp.exp(scores - lse_ref[...]), 0.0)
    deltas = jnp.sum(heads_grad.astype(F32) * o_ref[...].astype(F32), -1, keepdims=True)
    score_grad = (weights * (dot(heads_grad, values, 1, 1) - deltas)).astype(BF)
    query_grad = dot(score_grad, keys, 1, 0) * HD ** (-0.5)
    key_grad = dot(score_grad, queries, 0, 0)
    value_grad = dot(weights.astype(BF), heads_grad, 0, 0)
    fields = turned(query_grad, *tables), turned(key_grad, *tables), value_grad

    @pl.when(pl.program_id(0) == 0)
    def _():
        sum_ref[...] = jnp.zeros_like(sum_ref)

    for i, field in enumerate(fields):
        field = field.astype(BF)
        cols = slice(i * HD, (i + 1) * HD)
        grad_ref[:, cols] = field
        sum_ref[:, cols] += jnp.sum(field.astype(F32), 0, keepdims=True)


def pair_specs(length):
    table = pl.BlockSpec((1, length, LANES), lambda r, t: (r, 0, 0))
    return [table] * 3 + [
        pl.BlockSpec((1, length, 1), lambda r, t: (r, 0, 0)),
        pl.BlockSpec((1, 1, length), lambda r, t: (r, 0, 0)),
    ]


def head_forward(turns, normed, bias, pairs, pieces, length):
    count, width = normed.shape
    columns = 3 * HD
    return call(
        forward_kernel,
        turns,
        count // length,
        [rows_block(width, length), pl.BlockSpec((1, columns), lambda r, t: (0, 0))]
        + pair_specs(length)
        + [whole(p) for p in pieces],
        [rows_block(columns, length), rows_block(HD, length), rows_block(1, length)],
        [like((count, columns)), like((count, HD)), like((count, 1), F32)],
        [normed, bias.reshape(1, columns)] + pairs + pieces,
        2 * count * (width * columns + 2 * length * HD),
    )


def head_backward(turns, grad, out_w, qkv, attended, lse, pairs, length):
    count, width = grad.shape
    columns = 3 * HD
    return call(
        functools.partial(backward_kernel, turns.shape[0]),
        turns,
        count // length,
        [
            rows_block(width, length),
            whole(out_w),
            rows_block(columns, length),
            rows_block(HD, length),
            rows_block(1, length),
        ]
        + pair_specs(length),
        [rows_block(columns, length), pl.BlockSpec((1, columns), lambda r, t: (0, 0))],
        [like((count, columns)), like((1, columns), F32)],
        [grad, out_w, qkv, attended, lse] + pairs,
        2 * count * (width * HD + 5 * length * HD),
    )


def finish_kernel(rows, with_norm, t_ref, x_ref, s_ref, o_ref, out_ref):
    depth = x_ref.shape[1] // rows
    term = s_ref[...].astype(F32)
    if with_norm:
        centred = x_ref[...].astype(F32)
        centred = centred - jnp.mean(centred, -1, keepdims=True)
        rstd = lax.rsqrt(jnp.mean(centred * centred, -1, keepdims=True) + EPSILON)
        centred = centred * rstd
        term = term - jnp.mean(term, -1, keepdims=True) - centred * jnp.mean(
            term * centred, -1, keepdims=True
        )
        field = o_ref[...].astype(F32) + rstd * term
    else:
        field = x_ref[...].astype(F32) + term + o_ref[4:5]
    for k in range(rows):
        at = pl.multiple_of(t_ref[k] * depth, LANES)
        out_ref[:, pl.ds(at, depth)] = field[:, k * depth : (k + 1) * depth].astype(BF)


def finish(turns, x, term, other, with_norm):
    return call(
        functools.partial(finish_kernel, turns.shape[0], with_norm),
        turns,
        1,
        [whole(v) for v in (x, term, other)],
        [whole(x)],
        [like(x.shape)],
        [x, term, other],
    )[0]


def shards(
    plan,
    tokens,
    attn_weights,
    mlp_weights,
    ln1_gain,
    ln1_bias,
    ln2_gain,
    ln2_bias,
    qkv_bias,
    dense_bias,
    up_bias,
    down_bias,
    doc_lengths,
    cotangent,
):
    row_count, shard_len, width = tokens.shape
    depth = attn_weights.shape[0]
    heads = width // HD
    rows, blks = plan.rows, plan.blks
    own_hidden = mlp_weights.shape[-1] // blks
    me = lax.axis_index("blk")
    length = shard_len * blks
    count = row_count * length
    head_of = me % plan.group // plan.share * plan.per_row + me // plan.group
    part = me % plan.share
    own_rows = row_count // plan.share
    row = lax.axis_index("row")
    turns = row ^ jnp.arange(rows, dtype=jnp.int32)
    places = me % plan.group ^ jnp.arange(plan.group, dtype=jnp.int32)

    def exchange(field):
        return lax.all_to_all(field, "blk", 0, 0)

    def collect(field):
        return exchange(field.reshape(blks, -1, field.shape[-1]))

    def gather_blocks(field):
        field = field.reshape(row_count, shard_len, width)
        return lax.all_gather(field, "blk", axis=1, tiled=True).reshape(count, width)

    def sum_blocks(field):
        field = field.reshape(row_count, length, width)
        field = lax.psum_scatter(field, "blk", scatter_dimension=1, tiled=True)
        return field.reshape(row_count * shard_len, width)

    zeros = jnp.zeros((3, width), F32)
    vectors = jnp.stack([ln1_gain, ln1_bias, ln2_gain, ln2_bias, dense_bias + down_bias])
    x_own, g_own, vectors, g_sum = turn_in(
        turns,
        tokens.reshape(row_count * shard_len, width),
        cotangent.reshape(row_count * shard_len, width),
        jnp.concatenate([vectors, zeros]),
    )
    qkv_send, out_own = split_attn(turns, attn_weights, plan, width)
    qkv_mine = exchange(qkv_send)
    out_send = pick(
        row ^ places // plan.share,
        [out_own] + [swap(out_own, "row", rows, k) for k in range(1, rows)],
        plan.group,
    )
    up_send, down_send = split_mlp(turns, after(mlp_weights, qkv_send), blks)
    qkv_mine, up_send, *out_send = lax.optimization_barrier((qkv_mine, up_send, *out_send))
    up_mine = exchange(up_send)
    qkv_pieces = gather_row(qkv_mine.reshape(-1, 3 * HD), plan)
    out_got = [out_send[0]] + [swap_group(out_send[j], plan, j) for j in range(1, plan.group)]
    up_mine, x_own, down_send, *qkv_pieces = lax.optimization_barrier(
        (up_mine, x_own, down_send, *qkv_pieces, *out_got)
    )[: 3 + rows]
    x_all = gather_blocks(x_own)
    down_mine = exchange(down_send)
    up_pieces = gather_row(up_mine.reshape(-1, own_hidden), plan)
    out_w = place(places, out_got)
    down_mine, g_own, *up_pieces = lax.optimization_barrier((down_mine, g_own, *up_pieces))
    g_all = gather_blocks(g_own)
    down_pieces = gather_row(down_mine.reshape(-1, own_hidden), plan)
    normed1, normed2 = norms(turns, x_all, vectors)

    lengths = lax.dynamic_slice_in_dim(doc_lengths, part * own_rows, own_rows, 0)
    doc_ends = jnp.cumsum(lengths, axis=-1)
    starts = doc_ends - lengths
    spots = jnp.arange(length, dtype=jnp.int32)
    doc_ids = jnp.sum((spots[None, :, None] >= doc_ends[:, None, :]).astype(jnp.int32), -1)
    picked = doc_ids[:, :, None] == jnp.arange(lengths.shape[-1], dtype=jnp.int32)
    positions = spots - jnp.sum(jnp.where(picked, starts[:, None, :], 0), -1)
    lane = jnp.arange(LANES)
    inverse = 10000.0 ** (-2.0 * (lane % (ROT // 2)).astype(F32) / ROT)
    angles = positions.astype(F32)[..., None] * inverse
    sine = jnp.sin(angles)
    pairs = [
        jnp.where(lane < ROT, jnp.cos(angles), 1.0),
        jnp.where(lane < ROT // 2, -sine, 0.0),
        jnp.where((lane >= ROT // 2) & (lane < ROT), sine, 0.0),
        doc_ids[:, :, None],
        doc_ids[:, None, :],
    ]

    def own(field):
        if plan.share == 1:
            return field
        return lax.dynamic_slice_in_dim(field, part * own_rows * length, own_rows * length, 0)

    def spread(field):
        if plan.share == 1:
            return field
        blank = jnp.zeros((count, field.shape[1]), field.dtype)
        return lax.dynamic_update_slice_in_dim(blank, field, part * own_rows * length, 0)

    up_b = lax.dynamic_slice_in_dim(up_bias, me * own_hidden, own_hidden)
    qkv_b = lax.dynamic_index_in_dim(qkv_bias.reshape(3, heads, HD), head_of, 1, keepdims=False)
    own_normed1 = own(normed1)
    qkv, attended, lse = head_forward(
        turns, own_normed1, qkv_b.reshape(-1), pairs, qkv_pieces, length
    )
    hidden, slope = feed_up(turns, after(normed2, attended), up_b, up_pieces)
    out_term = out_sum(turns, hidden, down_pieces, spread(attended), out_w)
    out_total = sum_blocks(out_term)

    g_all = after(g_all, out_term)
    down_g = weight_grad(turns, g_all, hidden)
    down_got = scatter_row(down_g, plan)
    pre_grad, up_sum = feed_slope(turns, after(g_all, down_g[0]), slope, down_pieces)
    own_grad = own(after(g_all, pre_grad))
    qkv_grad, qkv_sum = head_backward(
        turns, own_grad, out_w, qkv, attended, lse, pairs, length
    )
    norm_term = norm_back(
        turns, pre_grad, up_pieces, spread(qkv_grad), qkv_pieces, vectors
    )
    down_total = add_pieces(turns, [after(down_got[0], norm_term)] + down_got[1:])
    norm_total = sum_blocks(after(norm_term, down_total))
    down_back = collect(down_total)
    up_g, up_parts = weight_grad(
        turns, after(normed2, down_total, out_total), pre_grad, up_sum, up_pieces
    )
    up_got = scatter_row(up_g, plan)
    qkv_g, qkv_parts = weight_grad(
        turns, after(own_normed1, up_g[0]), qkv_grad, qkv_sum, qkv_pieces
    )
    out_g = out_grad(turns, places, after(attended, qkv_g[0], down_back), own_grad)
    out_got = [out_g[0]] + [swap_group(out_g[j], plan, j) for j in range(1, plan.group)]
    up_total = add_pieces(turns, [after(up_got[0], *out_got)] + up_got[1:])
    up_back = collect(up_total)
    qkv_got = scatter_row([after(v, up_total) for v in qkv_g], plan)
    holders = turns[:, None] * plan.share + jnp.arange(plan.share, dtype=jnp.int32)
    out_send = pick((me % plan.group ^ holders).reshape(-1), out_got, rows)
    out_back = out_send[0].astype(F32) + sum(
        swap(after(out_send[k], up_total), "row", rows, k).astype(F32) for k in range(1, rows)
    )

    terms = [jnp.sum(after(v, up_total), -1) for v in (qkv_parts, up_parts)]
    terms += [g_sum, qkv_sum, up_sum]
    terms = [v.reshape(-1) for v in terms]
    used = sum(v.size for v in terms)
    terms.append(jnp.zeros((-used % (8 * LANES),), F32))
    sums = jnp.concatenate(terms)
    sums = sums + sum(swap(sums, "row", rows, k) for k in range(1, rows))

    qkv_total = add_pieces(turns, [after(qkv_got[0], out_back, sums, up_back)] + qkv_got[1:])
    qkv_back = collect(qkv_total)
    sums = after(sums, qkv_total)
    sums = jnp.stack([sums] + [swap(sums, "blk", blks, k) for k in range(1, blks)])
    sums = sums[me ^ jnp.arange(blks, dtype=jnp.int32)]
    gain1, bias1, gain2, bias2, g_total = jnp.split(
        jnp.sum(sums[:, : 5 * width], 0), 5
    )
    sums = sums[:, 5 * width : used]
    qkv_bias_grad = sums[:, : 3 * HD].reshape(plan.per_row, rows, plan.share, 3, HD)
    qkv_bias_grad = jnp.sum(qkv_bias_grad, 2).transpose(2, 1, 0, 3).reshape(-1)
    up_bias_grad = sums[:, 3 * HD :].reshape(-1)

    layer_out = finish(turns, x_own, out_total, vectors, False)
    tokens_grad = finish(turns, x_own, norm_total, g_own, True)
    return (
        layer_out.reshape(tokens.shape),
        tokens_grad.reshape(tokens.shape),
        join_attn(turns, qkv_back, out_back, plan),
        join_mlp(turns, up_back, down_back),
        (gain1 - ln1_bias * bias1) / ln1_gain,
        bias1,
        (gain2 - ln2_bias * bias2) / ln2_gain,
        bias2,
        qkv_bias_grad,
        g_total,
        up_bias_grad,
        g_total,
    )


def solution(mesh):
    rows, blks = mesh.shape["row"], mesh.shape["blk"]
    vector = P()
    tokens = P("row", "blk", None)
    attn = P(("row", "blk"), None)
    mlp = P(("row", "blk"), None, None)

    def run(*arrays):
        plan = Plan(rows, blks, arrays[0].shape[-1] // HD)
        return jax.shard_map(
            functools.partial(shards, plan),
            mesh=mesh,
            in_specs=(tokens, attn, mlp) + (vector,) * 8 + (P("row", None), tokens),
            out_specs=(tokens, tokens, attn, mlp) + (vector,) * 8,
            check_vma=False,
        )(*arrays)

    return run
```

```python
import functools
import math

import jax
import jax.numpy as jnp
import numpy as np
from jax import lax
from jax.experimental import pallas as pl
from jax.experimental.pallas import tpu as pltpu
from jax.sharding import PartitionSpec as P

HD = 256
ROT = 64
LANES = 128
BLOCK = 256
EPSILON = 1e-05
MASKED = -1e30
BF = jnp.bfloat16
F32 = jnp.float32
COST = 100
VMEM_LIMIT = 56 * 2**20
SMALL = 16 * 2**20


class Plan:
    def __init__(self, rows, blks, heads):
        self.rows = rows
        self.blks = blks
        self.share = blks // heads
        self.per_row = heads // rows
        self.group = blks // self.per_row
        self.groups = [
            list(range(i * self.group, (i + 1) * self.group)) for i in range(self.per_row)
        ]


def after(field, *others):
    return lax.optimization_barrier((field,) + others)[0] if others else field


def swap(field, axis, size, bit):
    return lax.ppermute(field, axis, [(i, i ^ bit) for i in range(size)])


def swap_group(field, plan, bits):
    return lax.ppermute(field, "blk", [(i, i ^ bits) for i in range(plan.blks)])


def gather_row(own, plan):
    return [own] + [swap(own, "row", plan.rows, k) for k in range(1, plan.rows)]


def scatter_row(pieces, plan):
    return [pieces[0]] + [swap(pieces[k], "row", plan.rows, k) for k in range(1, plan.rows)]


def dot(left, right, left_dim, right_dim):
    return lax.dot_general(
        left, right, (((left_dim,), (right_dim,)), ((), ())), preferred_element_type=F32
    )


def whole(array):
    return pl.BlockSpec(array.shape, lambda *i: (0,) * len(array.shape))


def like(shape, kind=BF):
    return jax.ShapeDtypeStruct(shape, kind)


def call(body, turns, grid, in_specs, out_specs, out_shape, operands, flops=0, limit=None):
    moved = sum(v.size * v.dtype.itemsize for v in operands)
    moved += sum(math.prod(v.shape) * jnp.dtype(v.dtype).itemsize for v in out_shape)
    return pl.pallas_call(
        body,
        name=getattr(body, "func", body).__name__,
        grid_spec=pltpu.PrefetchScalarGridSpec(
            num_scalar_prefetch=1, grid=(grid,), in_specs=in_specs, out_specs=out_specs
        ),
        out_shape=out_shape,
        compiler_params=pltpu.CompilerParams(vmem_limit_bytes=limit or VMEM_LIMIT),
        cost_estimate=pl.CostEstimate(
            flops=flops // COST, bytes_accessed=moved // COST, transcendentals=0
        ),
    )(turns, *operands)


def rows_block(columns, block=BLOCK):
    return pl.BlockSpec((block, columns), lambda i, t: (i, 0))


def add_kernel(t_ref, *refs):
    refs[-1][...] = sum(ref[...].astype(F32) for ref in refs[:-1]).astype(BF)


def add_pieces(turns, terms):
    depth, width = terms[0].shape
    block = rows_block(width, depth // 4)
    shape = like((depth, width))
    return call(
        add_kernel, turns, 4, [block] * len(terms), [block], [shape], terms, limit=SMALL
    )[0]


def turn_kernel(t_ref, x_ref, g_ref, v_ref, xo_ref, go_ref, vo_ref, s_ref):
    xo_ref[...] = x_ref[...]
    go_ref[...] = g_ref[...]
    vo_ref[...] = v_ref[...]
    s_ref[...] = jnp.sum(g_ref[...].astype(F32), 0, keepdims=True)


def turn_in(turns, x, g, vectors):
    rows = turns.shape[0]
    part = x.shape[1] // rows

    def specs(array, turned):
        index = (lambda k, t: (0, t[k])) if turned else (lambda k, t: (0, k))
        return pl.BlockSpec((array.shape[0], part), index)

    total_shape = like((1, x.shape[1]), F32)
    return call(
        turn_kernel,
        turns,
        rows,
        [specs(v, True) for v in (x, g, vectors)],
        [specs(v, False) for v in (x, g, vectors)] + [specs(total_shape, True)],
        [like(v.shape, v.dtype) for v in (x, g, vectors)] + [total_shape],
        [x, g, vectors],
    )


def split_kernel(t_ref, w_ref, u_ref, d_ref):
    u_ref[0] = w_ref[:, 0, :]
    d_ref[0] = w_ref[:, 1, :]


def split_mlp(turns, weights, blks):
    depth, _, hidden = weights.shape
    part = hidden // blks
    block = pl.BlockSpec((1, depth, part), lambda b, t: (b, 0, 0))
    return call(
        split_kernel,
        turns,
        blks,
        [pl.BlockSpec((depth, 2, part), lambda b, t: (0, 0, b))],
        [block] * 2,
        [like((blks, depth, part))] * 2,
        [weights],
    )


def join_kernel(t_ref, u_ref, d_ref, o_ref):
    o_ref[:, 0, :] = u_ref[0].astype(F32)
    o_ref[:, 1, :] = d_ref[0].astype(F32)


def join_mlp(turns, up, down):
    blks, depth, part = up.shape
    block = pl.BlockSpec((1, depth, part), lambda b, t: (b, 0, 0))
    return call(
        join_kernel,
        turns,
        blks,
        [block] * 2,
        [pl.BlockSpec((depth, 2, part), lambda b, t: (0, 0, b))],
        [like((depth, 2, blks * part), F32)],
        [up, down],
    )[0]


def split_attn_kernel(plan, width, t_ref, w_ref, qkv_ref, out_ref):
    b = pl.program_id(0)
    head = b % plan.group // plan.share * plan.per_row + b // plan.group
    for i in range(3):
        at = pl.multiple_of(i * width + head * HD, HD)
        qkv_ref[0, :, i * HD : (i + 1) * HD] = w_ref[:, pl.ds(at, HD)]

    @pl.when(b == 0)
    def _():
        out_ref[...] = w_ref[:, 3 * width :]


def split_attn(turns, weights, plan, width):
    depth = weights.shape[0]
    return call(
        functools.partial(split_attn_kernel, plan, width),
        turns,
        plan.blks,
        [whole(weights)],
        [
            pl.BlockSpec((1, depth, 3 * HD), lambda b, t: (b, 0, 0)),
            pl.BlockSpec((depth, width), lambda b, t: (0, 0)),
        ],
        [like((plan.blks, depth, 3 * HD)), like((depth, width))],
        [weights],
        limit=SMALL,
    )


def join_attn_kernel(plan, t_ref, qkv_ref, out_ref, o_ref):
    step = pl.program_id(0)
    heads = o_ref.shape[1] // HD

    @pl.when(step < 3)
    def _():
        at = pl.ds(pl.multiple_of(step * HD, HD), HD)
        for h in range(heads):
            first = h % plan.per_row * plan.group + h // plan.per_row * plan.share
            o_ref[:, h * HD : (h + 1) * HD] = sum(
                qkv_ref[first + i, :, at].astype(F32) for i in range(plan.share)
            )

    @pl.when(step == 3)
    def _():
        o_ref[...] = out_ref[...]


def join_attn(turns, qkv, out, plan):
    depth, width = out.shape
    return call(
        functools.partial(join_attn_kernel, plan),
        turns,
        4,
        [whole(qkv), whole(out)],
        [pl.BlockSpec((depth, width), lambda j, t: (0, j))],
        [like((depth, 4 * width), F32)],
        [qkv, out],
    )[0]


def pick_kernel(count, t_ref, *refs):
    pieces, outs = refs[:count], refs[count:]
    share = t_ref.shape[0] // len(outs)
    for n, out in enumerate(outs):
        for i in range(share):
            for k, piece in enumerate(pieces):

                @pl.when(t_ref[n * share + i] == k)
                def _(i=i, out=out, piece=piece):
                    out[...] = piece[...] if i == 0 else out[...] + piece[...]


def pick(table, pieces, count):
    return call(
        functools.partial(pick_kernel, len(pieces)),
        table,
        1,
        [whole(p) for p in pieces],
        [whole(pieces[0])] * count,
        [like(pieces[0].shape)] * count,
        pieces,
    )


def place_kernel(t_ref, *refs):
    *pieces, out_ref = refs
    for k, piece in enumerate(pieces):
        depth = piece.shape[0]
        out_ref[pl.ds(pl.multiple_of(t_ref[k] * depth, depth), depth)] = piece[...]


def place(table, pieces):
    depth, width = pieces[0].shape
    shape = like((len(pieces) * depth, width))
    return call(place_kernel, table, 1, [whole(p) for p in pieces], [whole(shape)], [shape], pieces)[0]


def norm_kernel(t_ref, x_ref, v_ref, a1_ref, a2_ref):
    field = x_ref[...].astype(F32)
    centred = field - jnp.mean(field, -1, keepdims=True)
    standard = centred * lax.rsqrt(jnp.mean(centred * centred, -1, keepdims=True) + EPSILON)
    a1_ref[...] = (standard * v_ref[0:1] + v_ref[1:2]).astype(BF)
    a2_ref[...] = (standard * v_ref[2:3] + v_ref[3:4]).astype(BF)


def norms(turns, x, vectors):
    count, width = x.shape
    return call(
        norm_kernel,
        turns,
        count // BLOCK,
        [rows_block(width), whole(vectors)],
        [rows_block(width)] * 2,
        [like(x.shape)] * 2,
        [x, vectors],
        20 * count * width,
    )


def times_pieces(left, pieces):
    out, start = None, 0
    for piece in pieces:
        depth = piece.shape[0]
        term = dot(left[:, start : start + depth], piece[...], 1, 0)
        out = term if out is None else out + term
        start += depth
    return out


def up_kernel(t_ref, a_ref, b_ref, *refs):
    pieces, (h_ref, s_ref) = refs[:-2], refs[-2:]
    pre = times_pieces(a_ref[...], pieces) + b_ref[...]
    cdf = 0.5 * (1.0 + lax.erf(pre * math.sqrt(0.5)))
    h_ref[...] = (pre * cdf).astype(BF)
    s_ref[...] = cdf + pre * (jnp.exp(-0.5 * pre * pre) * (1.0 / math.sqrt(2.0 * math.pi)))


def feed_up(turns, normed, bias, pieces):
    count, width = normed.shape
    hidden = bias.shape[0]
    return call(
        up_kernel,
        turns,
        count // BLOCK,
        [rows_block(width), pl.BlockSpec((1, hidden), lambda i, t: (0, 0))]
        + [whole(p) for p in pieces],
        [rows_block(hidden)] * 2,
        [like((count, hidden)), like((count, hidden), F32)],
        [normed, bias.reshape(1, hidden)] + pieces,
        2 * count * width * hidden,
    )


def slope_kernel(t_ref, g_ref, s_ref, *refs):
    pieces, (p_ref, sum_ref) = refs[:-2], refs[-2:]

    @pl.when(pl.program_id(0) == 0)
    def _():
        sum_ref[...] = jnp.zeros_like(sum_ref)

    grad = (times_pieces(g_ref[...], pieces) * s_ref[...]).astype(BF)
    p_ref[...] = grad
    sum_ref[...] += jnp.sum(grad.astype(F32), 0, keepdims=True)


def feed_slope(turns, grad, slope, pieces):
    count, width = grad.shape
    hidden = slope.shape[1]
    return call(
        slope_kernel,
        turns,
        count // BLOCK,
        [rows_block(width), rows_block(hidden)] + [whole(p) for p in pieces],
        [rows_block(hidden), pl.BlockSpec((1, hidden), lambda i, t: (0, 0))],
        [like((count, hidden)), like((1, hidden), F32)],
        [grad, slope] + pieces,
        2 * count * width * hidden,
    )


def lane_sum(field):
    return sum(field[:, i : i + LANES] for i in range(0, field.shape[1], LANES))


def weight_kernel(rows, with_sums, t_ref, l_ref, r_ref, *refs):
    step = pl.program_id(0)
    if with_sums:
        sum_ref, pieces, refs = refs[0], refs[1 : 1 + rows], refs[1 + rows :]
        parts_ref = refs[-1]
    grad = dot(l_ref[...], r_ref[...], 0, 0)
    for k in range(rows):

        @pl.when(step == k)
        def _(k=k):
            refs[k][...] = grad.astype(BF)
            if with_sums:
                piece = pieces[k][...].astype(F32)
                parts_ref[0] = lane_sum(piece * grad)
                parts_ref[1] = lane_sum(piece * sum_ref[...])


def weight_grad(turns, left, right, sums=None, pieces=()):
    rows = turns.shape[0]
    count, width = left.shape
    columns = right.shape[1]
    depth = width // rows
    out_shape = [like((depth, columns))] * rows
    out_specs = [whole(v) for v in out_shape]
    operands = [left, right]
    if pieces:
        operands += [sums] + pieces
        out_shape.append(like((2, width, LANES), F32))
        out_specs.append(pl.BlockSpec((2, depth, LANES), lambda k, t: (0, t[k], 0)))
    out = call(
        functools.partial(weight_kernel, rows, bool(pieces)),
        turns,
        rows,
        [pl.BlockSpec((count, depth), lambda k, t: (0, k))] + [whole(v) for v in operands[1:]],
        out_specs,
        out_shape,
        operands,
        2 * count * width * columns,
    )
    if pieces:
        return out[:-1], out[-1]
    return out


def out_kernel(rows, t_ref, o_ref, g_ref, *refs):
    *outs, grad_ref = refs
    depth = outs[0].shape[0]
    grad_ref[...] = dot(o_ref[...], g_ref[...], 0, 0)
    for j, out in enumerate(outs):
        at = pl.multiple_of(t_ref[rows + j] * depth, depth)
        out[...] = grad_ref[pl.ds(at, depth)].astype(BF)


def out_grad(turns, places, attended, grad):
    rows, group = turns.shape[0], places.shape[0]
    count, width = grad.shape
    part = width // rows
    depth = HD // group
    return pl.pallas_call(
        functools.partial(out_kernel, rows),
        name="out_kernel",
        grid_spec=pltpu.PrefetchScalarGridSpec(
            num_scalar_prefetch=1,
            grid=(rows,),
            in_specs=[whole(attended), pl.BlockSpec((count, part), lambda k, t: (0, k))],
            out_specs=[pl.BlockSpec((depth, part), lambda k, t: (0, t[k]))] * group,
            scratch_shapes=[pltpu.VMEM((HD, part), F32)],
        ),
        out_shape=[like((depth, width))] * group,
        compiler_params=pltpu.CompilerParams(vmem_limit_bytes=VMEM_LIMIT),
        cost_estimate=pl.CostEstimate(
            flops=2 * count * width * HD // COST,
            bytes_accessed=2 * (count * (width + HD) + width * HD) // COST,
            transcendentals=0,
        ),
    )(jnp.concatenate([turns, places]), attended, grad)


def turned_columns(t_ref, w_ref, k, depth):
    return w_ref[:, pl.ds(pl.multiple_of(t_ref[k] * depth, LANES), depth)]


def sum_kernel(t_ref, h_ref, o_ref, w_ref, *refs):
    pieces, y_ref = refs[:-1], refs[-1]
    for k, piece in enumerate(pieces):
        depth = piece.shape[0]
        term = dot(h_ref[...], piece[...], 1, 1)
        term += dot(o_ref[...], turned_columns(t_ref, w_ref, k, depth), 1, 0)
        y_ref[:, k * depth : (k + 1) * depth] = term.astype(BF)


def out_sum(turns, hidden, pieces, attended, out_w):
    count = hidden.shape[0]
    width = out_w.shape[1]
    return call(
        sum_kernel,
        turns,
        count // BLOCK,
        [rows_block(hidden.shape[1]), rows_block(HD), whole(out_w)] + [whole(p) for p in pieces],
        [rows_block(width)],
        [like((count, width))],
        [hidden, attended, out_w] + pieces,
        2 * count * width * (hidden.shape[1] + HD),
    )[0]


def back_kernel(t_ref, p_ref, q_ref, v_ref, *refs):
    pieces, c_ref = refs[:-1], refs[-1]
    count = len(pieces) // 2
    for k, (up, qkv) in enumerate(zip(pieces[:count], pieces[count:])):
        depth = up.shape[0]
        cols = slice(k * depth, (k + 1) * depth)
        term = dot(p_ref[...], up[...], 1, 1) * v_ref[2:3, cols]
        term += dot(q_ref[...], qkv[...], 1, 1) * v_ref[0:1, cols]
        c_ref[:, cols] = term.astype(BF)


def norm_back(turns, pre_grad, up_pieces, qkv_grad, qkv_pieces, vectors):
    count = pre_grad.shape[0]
    width = vectors.shape[1]
    columns = pre_grad.shape[1] + qkv_grad.shape[1]
    return call(
        back_kernel,
        turns,
        count // BLOCK,
        [rows_block(pre_grad.shape[1]), rows_block(qkv_grad.shape[1]), whole(vectors)]
        + [whole(p) for p in up_pieces + qkv_pieces],
        [rows_block(width)],
        [like((count, width))],
        [pre_grad, qkv_grad, vectors] + up_pieces + qkv_pieces,
        2 * count * width * columns,
    )[0]


def turned(field, cosine, minus, plus):
    head = field[:, :LANES]
    half = ROT // 2
    head = (
        head * cosine
        + pltpu.roll(head, LANES - half, 1) * minus
        + pltpu.roll(head, half, 1) * plus
    )
    return jnp.concatenate([head, field[:, LANES:]], 1)


def allowed_pairs(length, dq_ref, dk_ref):
    spot = lax.broadcasted_iota(jnp.int32, (length, length), 0)
    other = lax.broadcasted_iota(jnp.int32, (length, length), 1)
    return (dq_ref[0] == dk_ref[0]) & (other <= spot)


def forward_kernel(t_ref, a_ref, b_ref, c_ref, m_ref, p_ref, dq_ref, dk_ref, *refs):
    pieces, (qkv_ref, o_ref, lse_ref) = refs[:-3], refs[-3:]
    qkv = times_pieces(a_ref[...], pieces) + b_ref[...]
    tables = c_ref[0], m_ref[0], p_ref[0]
    queries = (turned(qkv[:, :HD], *tables) * HD ** (-0.5)).astype(BF)
    keys = turned(qkv[:, HD : 2 * HD], *tables).astype(BF)
    values = qkv[:, 2 * HD :].astype(BF)
    for i, field in enumerate((queries, keys, values)):
        qkv_ref[:, i * HD : (i + 1) * HD] = field
    allowed = allowed_pairs(a_ref.shape[0], dq_ref, dk_ref)
    scores = jnp.where(allowed, dot(queries, keys, 1, 1), MASKED)
    largest = jnp.max(scores, -1, keepdims=True)
    weights = jnp.where(allowed, jnp.exp(scores - largest), 0.0)
    mass = jnp.sum(weights, -1, keepdims=True)
    o_ref[...] = dot((weights / mass).astype(BF), values, 1, 0).astype(BF)
    lse_ref[...] = largest + jnp.log(mass)


def backward_kernel(
    parts, t_ref, g_ref, w_ref, qkv_ref, o_ref, lse_ref, c_ref, m_ref, p_ref, dq_ref, dk_ref,
    grad_ref, sum_ref,
):
    queries, keys, values = (qkv_ref[:, i * HD : (i + 1) * HD] for i in range(3))
    tables = c_ref[0], -m_ref[0], -p_ref[0]
    depth = w_ref.shape[1] // parts
    heads_grad = None
    for k in range(parts):
        cols = slice(k * depth, (k + 1) * depth)
        term = dot(g_ref[:, cols], turned_columns(t_ref, w_ref, k, depth), 1, 1)
        heads_grad = term if heads_grad is None else heads_grad + term
    heads_grad = heads_grad.astype(BF)
    allowed = allowed_pairs(g_ref.shape[0], dq_ref, dk_ref)
    scores = jnp.where(allowed, dot(queries, keys, 1, 1), MASKED)
    weights = jnp.where(allowed, jnp.exp(scores - lse_ref[...]), 0.0)
    deltas = jnp.sum(heads_grad.astype(F32) * o_ref[...].astype(F32), -1, keepdims=True)
    score_grad = (weights * (dot(heads_grad, values, 1, 1) - deltas)).astype(BF)
    query_grad = dot(score_grad, keys, 1, 0) * HD ** (-0.5)
    key_grad = dot(score_grad, queries, 0, 0)
    value_grad = dot(weights.astype(BF), heads_grad, 0, 0)
    fields = turned(query_grad, *tables), turned(key_grad, *tables), value_grad

    @pl.when(pl.program_id(0) == 0)
    def _():
        sum_ref[...] = jnp.zeros_like(sum_ref)

    for i, field in enumerate(fields):
        field = field.astype(BF)
        cols = slice(i * HD, (i + 1) * HD)
        grad_ref[:, cols] = field
        sum_ref[:, cols] += jnp.sum(field.astype(F32), 0, keepdims=True)


def pair_specs(length):
    table = pl.BlockSpec((1, length, LANES), lambda r, t: (r, 0, 0))
    return [table] * 3 + [
        pl.BlockSpec((1, length, 1), lambda r, t: (r, 0, 0)),
        pl.BlockSpec((1, 1, length), lambda r, t: (r, 0, 0)),
    ]


def head_forward(turns, normed, bias, pairs, pieces, length):
    count, width = normed.shape
    columns = 3 * HD
    return call(
        forward_kernel,
        turns,
        count // length,
        [rows_block(width, length), pl.BlockSpec((1, columns), lambda r, t: (0, 0))]
        + pair_specs(length)
        + [whole(p) for p in pieces],
        [rows_block(columns, length), rows_block(HD, length), rows_block(1, length)],
        [like((count, columns)), like((count, HD)), like((count, 1), F32)],
        [normed, bias.reshape(1, columns)] + pairs + pieces,
        2 * count * (width * columns + 2 * length * HD),
    )


def head_backward(turns, grad, out_w, qkv, attended, lse, pairs, length):
    count, width = grad.shape
    columns = 3 * HD
    return call(
        functools.partial(backward_kernel, turns.shape[0]),
        turns,
        count // length,
        [
            rows_block(width, length),
            whole(out_w),
            rows_block(columns, length),
            rows_block(HD, length),
            rows_block(1, length),
        ]
        + pair_specs(length),
        [rows_block(columns, length), pl.BlockSpec((1, columns), lambda r, t: (0, 0))],
        [like((count, columns)), like((1, columns), F32)],
        [grad, out_w, qkv, attended, lse] + pairs,
        2 * count * (width * HD + 5 * length * HD),
    )


def finish_kernel(rows, with_norm, t_ref, x_ref, s_ref, o_ref, out_ref):
    depth = x_ref.shape[1] // rows
    term = s_ref[...].astype(F32)
    if with_norm:
        centred = x_ref[...].astype(F32)
        centred = centred - jnp.mean(centred, -1, keepdims=True)
        rstd = lax.rsqrt(jnp.mean(centred * centred, -1, keepdims=True) + EPSILON)
        centred = centred * rstd
        term = term - jnp.mean(term, -1, keepdims=True) - centred * jnp.mean(
            term * centred, -1, keepdims=True
        )
        field = o_ref[...].astype(F32) + rstd * term
    else:
        field = x_ref[...].astype(F32) + term + o_ref[4:5]
    for k in range(rows):
        at = pl.multiple_of(t_ref[k] * depth, LANES)
        out_ref[:, pl.ds(at, depth)] = field[:, k * depth : (k + 1) * depth].astype(BF)


def finish(turns, x, term, other, with_norm):
    return call(
        functools.partial(finish_kernel, turns.shape[0], with_norm),
        turns,
        1,
        [whole(v) for v in (x, term, other)],
        [whole(x)],
        [like(x.shape)],
        [x, term, other],
    )[0]


def shards(
    plan,
    tokens,
    attn_weights,
    mlp_weights,
    ln1_gain,
    ln1_bias,
    ln2_gain,
    ln2_bias,
    qkv_bias,
    dense_bias,
    up_bias,
    down_bias,
    doc_lengths,
    cotangent,
):
    row_count, shard_len, width = tokens.shape
    depth = attn_weights.shape[0]
    heads = width // HD
    rows, blks = plan.rows, plan.blks
    own_hidden = mlp_weights.shape[-1] // blks
    me = lax.axis_index("blk")
    length = shard_len * blks
    count = row_count * length
    head_of = me % plan.group // plan.share * plan.per_row + me // plan.group
    part = me % plan.share
    own_rows = row_count // plan.share
    row = lax.axis_index("row")
    turns = row ^ jnp.arange(rows, dtype=jnp.int32)
    places = me % plan.group ^ jnp.arange(plan.group, dtype=jnp.int32)

    def exchange(field):
        return lax.all_to_all(field, "blk", 0, 0)

    def collect(field):
        return exchange(field.reshape(blks, -1, field.shape[-1]))

    def gather_blocks(field):
        field = field.reshape(row_count, shard_len, width)
        return lax.all_gather(field, "blk", axis=1, tiled=True).reshape(count, width)

    def sum_blocks(field):
        field = field.reshape(row_count, length, width)
        field = lax.psum_scatter(field, "blk", scatter_dimension=1, tiled=True)
        return field.reshape(row_count * shard_len, width)

    zeros = jnp.zeros((3, width), F32)
    vectors = jnp.stack([ln1_gain, ln1_bias, ln2_gain, ln2_bias, dense_bias + down_bias])
    x_own, g_own, vectors, g_sum = turn_in(
        turns,
        tokens.reshape(row_count * shard_len, width),
        cotangent.reshape(row_count * shard_len, width),
        jnp.concatenate([vectors, zeros]),
    )
    qkv_send, out_own = split_attn(turns, attn_weights, plan, width)
    qkv_mine = exchange(qkv_send)
    out_send = pick(
        row ^ places // plan.share,
        [out_own] + [swap(out_own, "row", rows, k) for k in range(1, rows)],
        plan.group,
    )
    up_send, down_send = split_mlp(turns, after(mlp_weights, qkv_send), blks)
    qkv_mine, up_send, *out_send = lax.optimization_barrier((qkv_mine, up_send, *out_send))
    up_mine = exchange(up_send)
    qkv_pieces = gather_row(qkv_mine.reshape(-1, 3 * HD), plan)
    out_got = [out_send[0]] + [swap_group(out_send[j], plan, j) for j in range(1, plan.group)]
    up_mine, x_own, down_send, *qkv_pieces = lax.optimization_barrier(
        (up_mine, x_own, down_send, *qkv_pieces, *out_got)
    )[: 3 + rows]
    x_all = gather_blocks(x_own)
    down_mine = exchange(down_send)
    up_pieces = gather_row(up_mine.reshape(-1, own_hidden), plan)
    out_w = place(places, out_got)
    down_mine, g_own, *up_pieces = lax.optimization_barrier((down_mine, g_own, *up_pieces))
    g_all = gather_blocks(g_own)
    down_pieces = gather_row(down_mine.reshape(-1, own_hidden), plan)
    normed1, normed2 = norms(turns, x_all, vectors)

    lengths = lax.dynamic_slice_in_dim(doc_lengths, part * own_rows, own_rows, 0)
    doc_ends = jnp.cumsum(lengths, axis=-1)
    starts = doc_ends - lengths
    spots = jnp.arange(length, dtype=jnp.int32)
    doc_ids = jnp.sum((spots[None, :, None] >= doc_ends[:, None, :]).astype(jnp.int32), -1)
    picked = doc_ids[:, :, None] == jnp.arange(lengths.shape[-1], dtype=jnp.int32)
    positions = spots - jnp.sum(jnp.where(picked, starts[:, None, :], 0), -1)
    lane = jnp.arange(LANES)
    inverse = 10000.0 ** (-2.0 * (lane % (ROT // 2)).astype(F32) / ROT)
    angles = positions.astype(F32)[..., None] * inverse
    sine = jnp.sin(angles)
    pairs = [
        jnp.where(lane < ROT, jnp.cos(angles), 1.0),
        jnp.where(lane < ROT // 2, -sine, 0.0),
        jnp.where((lane >= ROT // 2) & (lane < ROT), sine, 0.0),
        doc_ids[:, :, None],
        doc_ids[:, None, :],
    ]

    def own(field):
        if plan.share == 1:
            return field
        return lax.dynamic_slice_in_dim(field, part * own_rows * length, own_rows * length, 0)

    def spread(field):
        if plan.share == 1:
            return field
        blank = jnp.zeros((count, field.shape[1]), field.dtype)
        return lax.dynamic_update_slice_in_dim(blank, field, part * own_rows * length, 0)

    up_b = lax.dynamic_slice_in_dim(up_bias, me * own_hidden, own_hidden)
    qkv_b = lax.dynamic_index_in_dim(qkv_bias.reshape(3, heads, HD), head_of, 1, keepdims=False)
    own_normed1 = own(normed1)
    qkv, attended, lse = head_forward(
        turns, own_normed1, qkv_b.reshape(-1), pairs, qkv_pieces, length
    )
    hidden, slope = feed_up(turns, after(normed2, attended), up_b, up_pieces)
    out_term = out_sum(turns, hidden, down_pieces, spread(attended), out_w)
    out_total = sum_blocks(out_term)

    g_all = after(g_all, out_term)
    down_g = weight_grad(turns, g_all, hidden)
    down_got = scatter_row(down_g, plan)
    own_grad = own(after(g_all, down_g[0]))
    out_g = out_grad(turns, places, attended, own_grad)
    out_got = [out_g[0]] + [swap_group(out_g[j], plan, j) for j in range(1, plan.group)]
    pre_grad, up_sum = feed_slope(turns, after(g_all, out_g[0]), slope, down_pieces)
    qkv_grad, qkv_sum = head_backward(
        turns, after(own_grad, pre_grad), out_w, qkv, attended, lse, pairs, length
    )
    norm_term = norm_back(
        turns, pre_grad, up_pieces, spread(qkv_grad), qkv_pieces, vectors
    )
    down_total = add_pieces(
        turns, [after(down_got[0], norm_term, *out_got[1:])] + down_got[1:]
    )
    norm_total = sum_blocks(after(norm_term, down_total))
    down_back = collect(down_total)
    holders = turns[:, None] * plan.share + jnp.arange(plan.share, dtype=jnp.int32)
    out_send = pick((me % plan.group ^ holders).reshape(-1), out_got, rows)
    out_back = out_send[0].astype(F32) + sum(
        swap(after(out_send[k], down_total), "row", rows, k).astype(F32) for k in range(1, rows)
    )
    qkv_g, qkv_parts = weight_grad(
        turns, after(own_normed1, down_total), qkv_grad, qkv_sum, qkv_pieces
    )
    qkv_got = scatter_row(qkv_g, plan)
    up_g, up_parts = weight_grad(
        turns, after(normed2, qkv_g[0], out_total), pre_grad, up_sum, up_pieces
    )
    up_got = scatter_row(up_g, plan)

    terms = [jnp.sum(v, -1) for v in (qkv_parts, up_parts)] + [g_sum, qkv_sum, up_sum]
    terms = [v.reshape(-1) for v in terms]
    used = sum(v.size for v in terms)
    terms.append(jnp.zeros((-used % (8 * LANES),), F32))
    sums = jnp.concatenate(terms)
    sums = sums + sum(swap(sums, "row", rows, k) for k in range(1, rows))

    qkv_total = add_pieces(turns, [after(qkv_got[0], up_g[0], down_back)] + qkv_got[1:])
    qkv_back = collect(qkv_total)
    up_total = add_pieces(turns, [after(up_got[0], qkv_back, out_back, sums)] + up_got[1:])
    up_back = collect(up_total)
    sums = after(sums, up_total)
    sums = jnp.stack([sums] + [swap(sums, "blk", blks, k) for k in range(1, blks)])
    sums = sums[me ^ jnp.arange(blks, dtype=jnp.int32)]
    gain1, bias1, gain2, bias2, g_total = jnp.split(
        jnp.sum(sums[:, : 5 * width], 0), 5
    )
    sums = sums[:, 5 * width : used]
    qkv_bias_grad = sums[:, : 3 * HD].reshape(plan.per_row, rows, plan.share, 3, HD)
    qkv_bias_grad = jnp.sum(qkv_bias_grad, 2).transpose(2, 1, 0, 3).reshape(-1)
    up_bias_grad = sums[:, 3 * HD :].reshape(-1)

    layer_out = finish(turns, x_own, out_total, vectors, False)
    tokens_grad = finish(turns, x_own, norm_total, g_own, True)
    return (
        layer_out.reshape(tokens.shape),
        tokens_grad.reshape(tokens.shape),
        join_attn(turns, qkv_back, out_back, plan),
        join_mlp(turns, up_back, down_back),
        (gain1 - ln1_bias * bias1) / ln1_gain,
        bias1,
        (gain2 - ln2_bias * bias2) / ln2_gain,
        bias2,
        qkv_bias_grad,
        g_total,
        up_bias_grad,
        g_total,
    )


def solution(mesh):
    rows, blks = mesh.shape["row"], mesh.shape["blk"]
    vector = P()
    tokens = P("row", "blk", None)
    attn = P(("row", "blk"), None)
    mlp = P(("row", "blk"), None, None)

    def run(*arrays):
        plan = Plan(rows, blks, arrays[0].shape[-1] // HD)
        return jax.shard_map(
            functools.partial(shards, plan),
            mesh=mesh,
            in_specs=(tokens, attn, mlp) + (vector,) * 8 + (P("row", None), tokens),
            out_specs=(tokens, tokens, attn, mlp) + (vector,) * 8,
            check_vma=False,
        )(*arrays)

    return run
```

```python
import functools
import math

import jax
import jax.numpy as jnp
import numpy as np
from jax import lax
from jax.experimental import pallas as pl
from jax.experimental.pallas import tpu as pltpu
from jax.sharding import PartitionSpec as P

HD = 256
ROT = 64
LANES = 128
BLOCK = 256
EPSILON = 1e-05
MASKED = -1e30
BF = jnp.bfloat16
F32 = jnp.float32
COST = 100
VMEM_LIMIT = 56 * 2**20
SMALL = 16 * 2**20


class Plan:
    def __init__(self, rows, blks, heads):
        self.rows = rows
        self.blks = blks
        self.share = blks // heads
        self.per_row = heads // rows
        self.group = blks // self.per_row
        self.groups = [
            list(range(i * self.group, (i + 1) * self.group)) for i in range(self.per_row)
        ]


def after(field, *others):
    return lax.optimization_barrier((field,) + others)[0] if others else field


def swap(field, axis, size, bit):
    return lax.ppermute(field, axis, [(i, i ^ bit) for i in range(size)])


def swap_group(field, plan, bits):
    return lax.ppermute(field, "blk", [(i, i ^ bits) for i in range(plan.blks)])


def gather_row(own, plan):
    return [own] + [swap(own, "row", plan.rows, k) for k in range(1, plan.rows)]


def near(k):
    return k > 0 and k & (k - 1) == 0


def scatter_row(pieces, plan, far=None):
    return [
        swap(v, "row", plan.rows, k)
        for k, v in enumerate(pieces)
        if k and (far is None or far is not near(k))
    ]


def dot(left, right, left_dim, right_dim):
    return lax.dot_general(
        left, right, (((left_dim,), (right_dim,)), ((), ())), preferred_element_type=F32
    )


def whole(array):
    return pl.BlockSpec(array.shape, lambda *i: (0,) * len(array.shape))


def like(shape, kind=BF):
    return jax.ShapeDtypeStruct(shape, kind)


def call(body, turns, grid, in_specs, out_specs, out_shape, operands, flops=0, limit=None):
    moved = sum(v.size * v.dtype.itemsize for v in operands)
    moved += sum(math.prod(v.shape) * jnp.dtype(v.dtype).itemsize for v in out_shape)
    return pl.pallas_call(
        body,
        name=getattr(body, "func", body).__name__,
        grid_spec=pltpu.PrefetchScalarGridSpec(
            num_scalar_prefetch=1, grid=(grid,), in_specs=in_specs, out_specs=out_specs
        ),
        out_shape=out_shape,
        compiler_params=pltpu.CompilerParams(vmem_limit_bytes=limit or VMEM_LIMIT),
        cost_estimate=pl.CostEstimate(
            flops=flops // COST, bytes_accessed=moved // COST, transcendentals=0
        ),
    )(turns, *operands)


def rows_block(columns, block=BLOCK):
    return pl.BlockSpec((block, columns), lambda i, t: (i, 0))


def add_kernel(t_ref, *refs):
    refs[-1][...] = sum(ref[...].astype(F32) for ref in refs[:-1]).astype(BF)


def add_pieces(turns, terms):
    depth, width = terms[0].shape
    block = rows_block(width, depth // 4)
    shape = like((depth, width))
    return call(
        add_kernel, turns, 4, [block] * len(terms), [block], [shape], terms, limit=SMALL
    )[0]


def turn_kernel(t_ref, x_ref, g_ref, v_ref, xo_ref, go_ref, vo_ref, s_ref):
    xo_ref[...] = x_ref[...]
    go_ref[...] = g_ref[...]
    vo_ref[...] = v_ref[...]
    s_ref[...] = jnp.sum(g_ref[...].astype(F32), 0, keepdims=True)


def turn_in(turns, x, g, vectors):
    rows = turns.shape[0]
    part = x.shape[1] // rows

    def specs(array, turned):
        index = (lambda k, t: (0, t[k])) if turned else (lambda k, t: (0, k))
        return pl.BlockSpec((array.shape[0], part), index)

    total_shape = like((1, x.shape[1]), F32)
    return call(
        turn_kernel,
        turns,
        rows,
        [specs(v, True) for v in (x, g, vectors)],
        [specs(v, False) for v in (x, g, vectors)] + [specs(total_shape, True)],
        [like(v.shape, v.dtype) for v in (x, g, vectors)] + [total_shape],
        [x, g, vectors],
    )


def split_kernel(t_ref, w_ref, u_ref, d_ref):
    u_ref[0] = w_ref[:, 0, :]
    d_ref[0] = w_ref[:, 1, :]


def split_mlp(turns, weights, blks):
    depth, _, hidden = weights.shape
    part = hidden // blks
    block = pl.BlockSpec((1, depth, part), lambda b, t: (b, 0, 0))
    return call(
        split_kernel,
        turns,
        blks,
        [pl.BlockSpec((depth, 2, part), lambda b, t: (0, 0, b))],
        [block] * 2,
        [like((blks, depth, part))] * 2,
        [weights],
    )


def join_kernel(t_ref, u_ref, d_ref, o_ref):
    o_ref[:, 0, :] = u_ref[0].astype(F32)
    o_ref[:, 1, :] = d_ref[0].astype(F32)


def join_mlp(turns, up, down):
    blks, depth, part = up.shape
    block = pl.BlockSpec((1, depth, part), lambda b, t: (b, 0, 0))
    return call(
        join_kernel,
        turns,
        blks,
        [block] * 2,
        [pl.BlockSpec((depth, 2, part), lambda b, t: (0, 0, b))],
        [like((depth, 2, blks * part), F32)],
        [up, down],
    )[0]


def split_attn_kernel(plan, width, t_ref, w_ref, qkv_ref, out_ref):
    b = pl.program_id(0)
    head = b % plan.group // plan.share * plan.per_row + b // plan.group
    for i in range(3):
        at = pl.multiple_of(i * width + head * HD, HD)
        qkv_ref[0, :, i * HD : (i + 1) * HD] = w_ref[:, pl.ds(at, HD)]

    @pl.when(b == 0)
    def _():
        out_ref[...] = w_ref[:, 3 * width :]


def split_attn(turns, weights, plan, width):
    depth = weights.shape[0]
    return call(
        functools.partial(split_attn_kernel, plan, width),
        turns,
        plan.blks,
        [whole(weights)],
        [
            pl.BlockSpec((1, depth, 3 * HD), lambda b, t: (b, 0, 0)),
            pl.BlockSpec((depth, width), lambda b, t: (0, 0)),
        ],
        [like((plan.blks, depth, 3 * HD)), like((depth, width))],
        [weights],
        limit=SMALL,
    )


def join_attn_kernel(plan, t_ref, qkv_ref, out_ref, o_ref):
    step = pl.program_id(0)
    heads = o_ref.shape[1] // HD

    @pl.when(step < 3)
    def _():
        at = pl.ds(pl.multiple_of(step * HD, HD), HD)
        for h in range(heads):
            first = h % plan.per_row * plan.group + h // plan.per_row * plan.share
            o_ref[:, h * HD : (h + 1) * HD] = sum(
                qkv_ref[first + i, :, at].astype(F32) for i in range(plan.share)
            )

    @pl.when(step == 3)
    def _():
        o_ref[...] = out_ref[...]


def join_attn(turns, qkv, out, plan):
    depth, width = out.shape
    return call(
        functools.partial(join_attn_kernel, plan),
        turns,
        4,
        [whole(qkv), whole(out)],
        [pl.BlockSpec((depth, width), lambda j, t: (0, j))],
        [like((depth, 4 * width), F32)],
        [qkv, out],
    )[0]


def pick_kernel(count, t_ref, *refs):
    pieces, outs = refs[:count], refs[count:]
    share = t_ref.shape[0] // len(outs)
    for n, out in enumerate(outs):
        for i in range(share):
            for k, piece in enumerate(pieces):

                @pl.when(t_ref[n * share + i] == k)
                def _(i=i, out=out, piece=piece):
                    out[...] = piece[...] if i == 0 else out[...] + piece[...]


def pick(table, pieces, count):
    return call(
        functools.partial(pick_kernel, len(pieces)),
        table,
        1,
        [whole(p) for p in pieces],
        [whole(pieces[0])] * count,
        [like(pieces[0].shape)] * count,
        pieces,
    )


def place_kernel(t_ref, *refs):
    *pieces, out_ref = refs
    for k, piece in enumerate(pieces):
        depth = piece.shape[0]
        out_ref[pl.ds(pl.multiple_of(t_ref[k] * depth, depth), depth)] = piece[...]


def place(table, pieces):
    depth, width = pieces[0].shape
    shape = like((len(pieces) * depth, width))
    return call(place_kernel, table, 1, [whole(p) for p in pieces], [whole(shape)], [shape], pieces)[0]


def norm_kernel(t_ref, x_ref, v_ref, a1_ref, a2_ref):
    field = x_ref[...].astype(F32)
    centred = field - jnp.mean(field, -1, keepdims=True)
    standard = centred * lax.rsqrt(jnp.mean(centred * centred, -1, keepdims=True) + EPSILON)
    a1_ref[...] = (standard * v_ref[0:1] + v_ref[1:2]).astype(BF)
    a2_ref[...] = (standard * v_ref[2:3] + v_ref[3:4]).astype(BF)


def norms(turns, x, vectors):
    count, width = x.shape
    return call(
        norm_kernel,
        turns,
        count // BLOCK,
        [rows_block(width), whole(vectors)],
        [rows_block(width)] * 2,
        [like(x.shape)] * 2,
        [x, vectors],
        20 * count * width,
    )


def times_pieces(left, pieces):
    out, start = None, 0
    for piece in pieces:
        depth = piece.shape[0]
        term = dot(left[:, start : start + depth], piece[...], 1, 0)
        out = term if out is None else out + term
        start += depth
    return out


def up_kernel(t_ref, a_ref, b_ref, *refs):
    pieces, (h_ref, s_ref) = refs[:-2], refs[-2:]
    pre = times_pieces(a_ref[...], pieces) + b_ref[...]
    cdf = 0.5 * (1.0 + lax.erf(pre * math.sqrt(0.5)))
    h_ref[...] = (pre * cdf).astype(BF)
    s_ref[...] = cdf + pre * (jnp.exp(-0.5 * pre * pre) * (1.0 / math.sqrt(2.0 * math.pi)))


def feed_up(turns, normed, bias, pieces):
    count, width = normed.shape
    hidden = bias.shape[0]
    return call(
        up_kernel,
        turns,
        count // BLOCK,
        [rows_block(width), pl.BlockSpec((1, hidden), lambda i, t: (0, 0))]
        + [whole(p) for p in pieces],
        [rows_block(hidden)] * 2,
        [like((count, hidden)), like((count, hidden), F32)],
        [normed, bias.reshape(1, hidden)] + pieces,
        2 * count * width * hidden,
    )


def slope_kernel(t_ref, g_ref, s_ref, *refs):
    pieces, (p_ref, sum_ref) = refs[:-2], refs[-2:]

    @pl.when(pl.program_id(0) == 0)
    def _():
        sum_ref[...] = jnp.zeros_like(sum_ref)

    grad = (times_pieces(g_ref[...], pieces) * s_ref[...]).astype(BF)
    p_ref[...] = grad
    sum_ref[...] += jnp.sum(grad.astype(F32), 0, keepdims=True)


def feed_slope(turns, grad, slope, pieces):
    count, width = grad.shape
    hidden = slope.shape[1]
    return call(
        slope_kernel,
        turns,
        count // BLOCK,
        [rows_block(width), rows_block(hidden)] + [whole(p) for p in pieces],
        [rows_block(hidden), pl.BlockSpec((1, hidden), lambda i, t: (0, 0))],
        [like((count, hidden)), like((1, hidden), F32)],
        [grad, slope] + pieces,
        2 * count * width * hidden,
    )


def lane_sum(field):
    return sum(field[:, i : i + LANES] for i in range(0, field.shape[1], LANES))


def weight_kernel(rows, with_sums, t_ref, l_ref, r_ref, *refs):
    step = pl.program_id(0)
    if with_sums:
        sum_ref, pieces, refs = refs[0], refs[1 : 1 + rows], refs[1 + rows :]
        parts_ref = refs[-1]
    grad = dot(l_ref[...], r_ref[...], 0, 0)
    for k in range(rows):

        @pl.when(step == k)
        def _(k=k):
            refs[k][...] = grad.astype(BF)
            if with_sums:
                piece = pieces[k][...].astype(F32)
                parts_ref[0] = lane_sum(piece * grad)
                parts_ref[1] = lane_sum(piece * sum_ref[...])


def weight_grad(turns, left, right, sums=None, pieces=()):
    rows = turns.shape[0]
    count, width = left.shape
    columns = right.shape[1]
    depth = width // rows
    out_shape = [like((depth, columns))] * rows
    out_specs = [whole(v) for v in out_shape]
    operands = [left, right]
    if pieces:
        operands += [sums] + pieces
        out_shape.append(like((2, width, LANES), F32))
        out_specs.append(pl.BlockSpec((2, depth, LANES), lambda k, t: (0, t[k], 0)))
    out = call(
        functools.partial(weight_kernel, rows, bool(pieces)),
        turns,
        rows,
        [pl.BlockSpec((count, depth), lambda k, t: (0, k))] + [whole(v) for v in operands[1:]],
        out_specs,
        out_shape,
        operands,
        2 * count * width * columns,
    )
    if pieces:
        return out[:-1], out[-1]
    return out


def out_kernel(rows, t_ref, o_ref, g_ref, *refs):
    *outs, grad_ref = refs
    depth = outs[0].shape[0]
    grad_ref[...] = dot(o_ref[...], g_ref[...], 0, 0)
    for j, out in enumerate(outs):
        at = pl.multiple_of(t_ref[rows + j] * depth, depth)
        out[...] = grad_ref[pl.ds(at, depth)].astype(BF)


def out_grad(turns, places, attended, grad):
    rows, group = turns.shape[0], places.shape[0]
    count, width = grad.shape
    part = width // rows
    depth = HD // group
    return pl.pallas_call(
        functools.partial(out_kernel, rows),
        name="out_kernel",
        grid_spec=pltpu.PrefetchScalarGridSpec(
            num_scalar_prefetch=1,
            grid=(rows,),
            in_specs=[whole(attended), pl.BlockSpec((count, part), lambda k, t: (0, k))],
            out_specs=[pl.BlockSpec((depth, part), lambda k, t: (0, t[k]))] * group,
            scratch_shapes=[pltpu.VMEM((HD, part), F32)],
        ),
        out_shape=[like((depth, width))] * group,
        compiler_params=pltpu.CompilerParams(vmem_limit_bytes=VMEM_LIMIT),
        cost_estimate=pl.CostEstimate(
            flops=2 * count * width * HD // COST,
            bytes_accessed=2 * (count * (width + HD) + width * HD) // COST,
            transcendentals=0,
        ),
    )(jnp.concatenate([turns, places]), attended, grad)


def turned_columns(t_ref, w_ref, k, depth):
    return w_ref[:, pl.ds(pl.multiple_of(t_ref[k] * depth, LANES), depth)]


def sum_kernel(t_ref, h_ref, o_ref, w_ref, *refs):
    pieces, y_ref = refs[:-1], refs[-1]
    for k, piece in enumerate(pieces):
        depth = piece.shape[0]
        term = dot(h_ref[...], piece[...], 1, 1)
        term += dot(o_ref[...], turned_columns(t_ref, w_ref, k, depth), 1, 0)
        y_ref[:, k * depth : (k + 1) * depth] = term.astype(BF)


def out_sum(turns, hidden, pieces, attended, out_w):
    count = hidden.shape[0]
    width = out_w.shape[1]
    return call(
        sum_kernel,
        turns,
        count // BLOCK,
        [rows_block(hidden.shape[1]), rows_block(HD), whole(out_w)] + [whole(p) for p in pieces],
        [rows_block(width)],
        [like((count, width))],
        [hidden, attended, out_w] + pieces,
        2 * count * width * (hidden.shape[1] + HD),
    )[0]


def back_kernel(t_ref, p_ref, q_ref, v_ref, *refs):
    pieces, c_ref = refs[:-1], refs[-1]
    count = len(pieces) // 2
    for k, (up, qkv) in enumerate(zip(pieces[:count], pieces[count:])):
        depth = up.shape[0]
        cols = slice(k * depth, (k + 1) * depth)
        term = dot(p_ref[...], up[...], 1, 1) * v_ref[2:3, cols]
        term += dot(q_ref[...], qkv[...], 1, 1) * v_ref[0:1, cols]
        c_ref[:, cols] = term.astype(BF)


def norm_back(turns, pre_grad, up_pieces, qkv_grad, qkv_pieces, vectors):
    count = pre_grad.shape[0]
    width = vectors.shape[1]
    columns = pre_grad.shape[1] + qkv_grad.shape[1]
    return call(
        back_kernel,
        turns,
        count // BLOCK,
        [rows_block(pre_grad.shape[1]), rows_block(qkv_grad.shape[1]), whole(vectors)]
        + [whole(p) for p in up_pieces + qkv_pieces],
        [rows_block(width)],
        [like((count, width))],
        [pre_grad, qkv_grad, vectors] + up_pieces + qkv_pieces,
        2 * count * width * columns,
    )[0]


def turned(field, cosine, minus, plus):
    head = field[:, :LANES]
    half = ROT // 2
    head = (
        head * cosine
        + pltpu.roll(head, LANES - half, 1) * minus
        + pltpu.roll(head, half, 1) * plus
    )
    return jnp.concatenate([head, field[:, LANES:]], 1)


def allowed_pairs(length, dq_ref, dk_ref):
    spot = lax.broadcasted_iota(jnp.int32, (length, length), 0)
    other = lax.broadcasted_iota(jnp.int32, (length, length), 1)
    return (dq_ref[0] == dk_ref[0]) & (other <= spot)


def forward_kernel(t_ref, a_ref, b_ref, c_ref, m_ref, p_ref, dq_ref, dk_ref, *refs):
    pieces, (qkv_ref, o_ref, lse_ref) = refs[:-3], refs[-3:]
    qkv = times_pieces(a_ref[...], pieces) + b_ref[...]
    tables = c_ref[0], m_ref[0], p_ref[0]
    queries = (turned(qkv[:, :HD], *tables) * HD ** (-0.5)).astype(BF)
    keys = turned(qkv[:, HD : 2 * HD], *tables).astype(BF)
    values = qkv[:, 2 * HD :].astype(BF)
    for i, field in enumerate((queries, keys, values)):
        qkv_ref[:, i * HD : (i + 1) * HD] = field
    allowed = allowed_pairs(a_ref.shape[0], dq_ref, dk_ref)
    scores = jnp.where(allowed, dot(queries, keys, 1, 1), MASKED)
    largest = jnp.max(scores, -1, keepdims=True)
    weights = jnp.where(allowed, jnp.exp(scores - largest), 0.0)
    mass = jnp.sum(weights, -1, keepdims=True)
    o_ref[...] = dot((weights / mass).astype(BF), values, 1, 0).astype(BF)
    lse_ref[...] = largest + jnp.log(mass)


def backward_kernel(
    parts, t_ref, g_ref, w_ref, qkv_ref, o_ref, lse_ref, c_ref, m_ref, p_ref, dq_ref, dk_ref,
    grad_ref, sum_ref,
):
    queries, keys, values = (qkv_ref[:, i * HD : (i + 1) * HD] for i in range(3))
    tables = c_ref[0], -m_ref[0], -p_ref[0]
    depth = w_ref.shape[1] // parts
    heads_grad = None
    for k in range(parts):
        cols = slice(k * depth, (k + 1) * depth)
        term = dot(g_ref[:, cols], turned_columns(t_ref, w_ref, k, depth), 1, 1)
        heads_grad = term if heads_grad is None else heads_grad + term
    heads_grad = heads_grad.astype(BF)
    allowed = allowed_pairs(g_ref.shape[0], dq_ref, dk_ref)
    scores = jnp.where(allowed, dot(queries, keys, 1, 1), MASKED)
    weights = jnp.where(allowed, jnp.exp(scores - lse_ref[...]), 0.0)
    deltas = jnp.sum(heads_grad.astype(F32) * o_ref[...].astype(F32), -1, keepdims=True)
    score_grad = (weights * (dot(heads_grad, values, 1, 1) - deltas)).astype(BF)
    query_grad = dot(score_grad, keys, 1, 0) * HD ** (-0.5)
    key_grad = dot(score_grad, queries, 0, 0)
    value_grad = dot(weights.astype(BF), heads_grad, 0, 0)
    fields = turned(query_grad, *tables), turned(key_grad, *tables), value_grad

    @pl.when(pl.program_id(0) == 0)
    def _():
        sum_ref[...] = jnp.zeros_like(sum_ref)

    for i, field in enumerate(fields):
        field = field.astype(BF)
        cols = slice(i * HD, (i + 1) * HD)
        grad_ref[:, cols] = field
        sum_ref[:, cols] += jnp.sum(field.astype(F32), 0, keepdims=True)


def pair_specs(length):
    table = pl.BlockSpec((1, length, LANES), lambda r, t: (r, 0, 0))
    return [table] * 3 + [
        pl.BlockSpec((1, length, 1), lambda r, t: (r, 0, 0)),
        pl.BlockSpec((1, 1, length), lambda r, t: (r, 0, 0)),
    ]


def head_forward(turns, normed, bias, pairs, pieces, length):
    count, width = normed.shape
    columns = 3 * HD
    return call(
        forward_kernel,
        turns,
        count // length,
        [rows_block(width, length), pl.BlockSpec((1, columns), lambda r, t: (0, 0))]
        + pair_specs(length)
        + [whole(p) for p in pieces],
        [rows_block(columns, length), rows_block(HD, length), rows_block(1, length)],
        [like((count, columns)), like((count, HD)), like((count, 1), F32)],
        [normed, bias.reshape(1, columns)] + pairs + pieces,
        2 * count * (width * columns + 2 * length * HD),
    )


def head_backward(turns, grad, out_w, qkv, attended, lse, pairs, length):
    count, width = grad.shape
    columns = 3 * HD
    return call(
        functools.partial(backward_kernel, turns.shape[0]),
        turns,
        count // length,
        [
            rows_block(width, length),
            whole(out_w),
            rows_block(columns, length),
            rows_block(HD, length),
            rows_block(1, length),
        ]
        + pair_specs(length),
        [rows_block(columns, length), pl.BlockSpec((1, columns), lambda r, t: (0, 0))],
        [like((count, columns)), like((1, columns), F32)],
        [grad, out_w, qkv, attended, lse] + pairs,
        2 * count * (width * HD + 5 * length * HD),
    )


def finish_kernel(rows, with_norm, t_ref, x_ref, s_ref, o_ref, out_ref):
    depth = x_ref.shape[1] // rows
    term = s_ref[...].astype(F32)
    if with_norm:
        centred = x_ref[...].astype(F32)
        centred = centred - jnp.mean(centred, -1, keepdims=True)
        rstd = lax.rsqrt(jnp.mean(centred * centred, -1, keepdims=True) + EPSILON)
        centred = centred * rstd
        term = term - jnp.mean(term, -1, keepdims=True) - centred * jnp.mean(
            term * centred, -1, keepdims=True
        )
        field = o_ref[...].astype(F32) + rstd * term
    else:
        field = x_ref[...].astype(F32) + term + o_ref[4:5]
    for k in range(rows):
        at = pl.multiple_of(t_ref[k] * depth, LANES)
        out_ref[:, pl.ds(at, depth)] = field[:, k * depth : (k + 1) * depth].astype(BF)


def finish(turns, x, term, other, with_norm):
    return call(
        functools.partial(finish_kernel, turns.shape[0], with_norm),
        turns,
        1,
        [whole(v) for v in (x, term, other)],
        [whole(x)],
        [like(x.shape)],
        [x, term, other],
    )[0]


def shards(
    plan,
    tokens,
    attn_weights,
    mlp_weights,
    ln1_gain,
    ln1_bias,
    ln2_gain,
    ln2_bias,
    qkv_bias,
    dense_bias,
    up_bias,
    down_bias,
    doc_lengths,
    cotangent,
):
    row_count, shard_len, width = tokens.shape
    depth = attn_weights.shape[0]
    heads = width // HD
    rows, blks = plan.rows, plan.blks
    own_hidden = mlp_weights.shape[-1] // blks
    me = lax.axis_index("blk")
    length = shard_len * blks
    count = row_count * length
    head_of = me % plan.group // plan.share * plan.per_row + me // plan.group
    part = me % plan.share
    own_rows = row_count // plan.share
    row = lax.axis_index("row")
    turns = row ^ jnp.arange(rows, dtype=jnp.int32)
    places = me % plan.group ^ jnp.arange(plan.group, dtype=jnp.int32)

    def exchange(field):
        return lax.all_to_all(field, "blk", 0, 0)

    def collect(field):
        return exchange(field.reshape(blks, -1, field.shape[-1]))

    def gather_blocks(field):
        field = field.reshape(row_count, shard_len, width)
        return lax.all_gather(field, "blk", axis=1, tiled=True).reshape(count, width)

    def sum_blocks(field):
        field = field.reshape(row_count, length, width)
        field = lax.psum_scatter(field, "blk", scatter_dimension=1, tiled=True)
        return field.reshape(row_count * shard_len, width)

    zeros = jnp.zeros((3, width), F32)
    vectors = jnp.stack([ln1_gain, ln1_bias, ln2_gain, ln2_bias, dense_bias + down_bias])
    x_own, g_own, vectors, g_sum = turn_in(
        turns,
        tokens.reshape(row_count * shard_len, width),
        cotangent.reshape(row_count * shard_len, width),
        jnp.concatenate([vectors, zeros]),
    )
    qkv_send, out_own = split_attn(turns, attn_weights, plan, width)
    qkv_mine = exchange(qkv_send)
    out_send = pick(
        row ^ places // plan.share,
        [out_own] + [swap(out_own, "row", rows, k) for k in range(1, rows)],
        plan.group,
    )
    up_send, down_send = split_mlp(turns, after(mlp_weights, qkv_send), blks)
    qkv_mine, up_send, *out_send = lax.optimization_barrier((qkv_mine, up_send, *out_send))
    up_mine = exchange(up_send)
    qkv_pieces = gather_row(qkv_mine.reshape(-1, 3 * HD), plan)
    out_got = [out_send[0]] + [swap_group(out_send[j], plan, j) for j in range(1, plan.group)]
    up_mine, x_own, down_send, *qkv_pieces = lax.optimization_barrier(
        (up_mine, x_own, down_send, *qkv_pieces, *out_got)
    )[: 3 + rows]
    x_all = gather_blocks(x_own)
    down_mine = exchange(down_send)
    up_pieces = gather_row(up_mine.reshape(-1, own_hidden), plan)
    out_w = place(places, out_got)
    down_mine, g_own, *up_pieces = lax.optimization_barrier((down_mine, g_own, *up_pieces))
    g_all = gather_blocks(g_own)
    down_pieces = gather_row(down_mine.reshape(-1, own_hidden), plan)
    normed1, normed2 = norms(turns, x_all, vectors)

    lengths = lax.dynamic_slice_in_dim(doc_lengths, part * own_rows, own_rows, 0)
    doc_ends = jnp.cumsum(lengths, axis=-1)
    starts = doc_ends - lengths
    spots = jnp.arange(length, dtype=jnp.int32)
    doc_ids = jnp.sum((spots[None, :, None] >= doc_ends[:, None, :]).astype(jnp.int32), -1)
    picked = doc_ids[:, :, None] == jnp.arange(lengths.shape[-1], dtype=jnp.int32)
    positions = spots - jnp.sum(jnp.where(picked, starts[:, None, :], 0), -1)
    lane = jnp.arange(LANES)
    inverse = 10000.0 ** (-2.0 * (lane % (ROT // 2)).astype(F32) / ROT)
    angles = positions.astype(F32)[..., None] * inverse
    sine = jnp.sin(angles)
    pairs = [
        jnp.where(lane < ROT, jnp.cos(angles), 1.0),
        jnp.where(lane < ROT // 2, -sine, 0.0),
        jnp.where((lane >= ROT // 2) & (lane < ROT), sine, 0.0),
        doc_ids[:, :, None],
        doc_ids[:, None, :],
    ]

    def own(field):
        if plan.share == 1:
            return field
        return lax.dynamic_slice_in_dim(field, part * own_rows * length, own_rows * length, 0)

    def spread(field):
        if plan.share == 1:
            return field
        blank = jnp.zeros((count, field.shape[1]), field.dtype)
        return lax.dynamic_update_slice_in_dim(blank, field, part * own_rows * length, 0)

    up_b = lax.dynamic_slice_in_dim(up_bias, me * own_hidden, own_hidden)
    qkv_b = lax.dynamic_index_in_dim(qkv_bias.reshape(3, heads, HD), head_of, 1, keepdims=False)
    own_normed1 = own(normed1)
    qkv, attended, lse = head_forward(
        turns, own_normed1, qkv_b.reshape(-1), pairs, qkv_pieces, length
    )
    hidden, slope = feed_up(turns, after(normed2, attended), up_b, up_pieces)
    out_term = out_sum(turns, hidden, down_pieces, spread(attended), out_w)
    out_total = sum_blocks(out_term)

    g_all = after(g_all, out_term)
    down_g = weight_grad(turns, g_all, hidden)
    down_got = scatter_row(down_g, plan)
    own_grad = own(after(g_all, down_g[0]))
    out_g = out_grad(turns, places, attended, own_grad)
    out_got = [out_g[0]] + [swap_group(out_g[j], plan, j) for j in range(1, plan.group)]
    pre_grad, up_sum = feed_slope(turns, after(g_all, out_g[0]), slope, down_pieces)
    qkv_grad, qkv_sum = head_backward(
        turns, after(own_grad, pre_grad), out_w, qkv, attended, lse, pairs, length
    )
    norm_term = norm_back(
        turns, pre_grad, up_pieces, spread(qkv_grad), qkv_pieces, vectors
    )
    down_total = add_pieces(
        turns, [after(down_g[0], norm_term, *out_got[1:])] + down_got
    )
    norm_total = sum_blocks(after(norm_term, down_total))
    down_back = collect(down_total)
    holders = turns[:, None] * plan.share + jnp.arange(plan.share, dtype=jnp.int32)
    out_send = pick((me % plan.group ^ holders).reshape(-1), out_got, rows)
    out_back = out_send[0].astype(F32) + sum(
        swap(after(out_send[k], down_total), "row", rows, k).astype(F32) for k in range(1, rows)
    )
    qkv_g, qkv_parts = weight_grad(
        turns, after(own_normed1, down_total), qkv_grad, qkv_sum, qkv_pieces
    )
    qkv_got = scatter_row(qkv_g, plan, False)
    up_g, up_parts = weight_grad(
        turns, after(normed2, qkv_g[0], out_back, out_total), pre_grad, up_sum, up_pieces
    )
    up_got = scatter_row([after(v, *qkv_got) for v in up_g], plan, False)
    qkv_got += scatter_row([after(v, up_g[0]) for v in qkv_g], plan, True)

    terms = [jnp.sum(v, -1) for v in (qkv_parts, up_parts)] + [g_sum, qkv_sum, up_sum]
    terms = [v.reshape(-1) for v in terms]
    used = sum(v.size for v in terms)
    terms.append(jnp.zeros((-used % (8 * LANES),), F32))
    sums = jnp.concatenate(terms)
    sums = sums + sum(swap(sums, "row", rows, k) for k in range(1, rows))

    qkv_total = add_pieces(turns, [after(qkv_g[0], down_back, *up_got)] + qkv_got)
    qkv_back = collect(qkv_total)
    up_got += scatter_row([after(v, qkv_total) for v in up_g], plan, True)
    up_total = add_pieces(turns, [after(up_g[0], qkv_back, sums)] + up_got)
    up_back = collect(up_total)
    sums = after(sums, up_total)
    sums = jnp.stack([sums] + [swap(sums, "blk", blks, k) for k in range(1, blks)])
    sums = sums[me ^ jnp.arange(blks, dtype=jnp.int32)]
    gain1, bias1, gain2, bias2, g_total = jnp.split(
        jnp.sum(sums[:, : 5 * width], 0), 5
    )
    sums = sums[:, 5 * width : used]
    qkv_bias_grad = sums[:, : 3 * HD].reshape(plan.per_row, rows, plan.share, 3, HD)
    qkv_bias_grad = jnp.sum(qkv_bias_grad, 2).transpose(2, 1, 0, 3).reshape(-1)
    up_bias_grad = sums[:, 3 * HD :].reshape(-1)

    layer_out = finish(turns, x_own, out_total, vectors, False)
    tokens_grad = finish(turns, x_own, norm_total, g_own, True)
    return (
        layer_out.reshape(tokens.shape),
        tokens_grad.reshape(tokens.shape),
        join_attn(turns, qkv_back, out_back, plan),
        join_mlp(turns, up_back, down_back),
        (gain1 - ln1_bias * bias1) / ln1_gain,
        bias1,
        (gain2 - ln2_bias * bias2) / ln2_gain,
        bias2,
        qkv_bias_grad,
        g_total,
        up_bias_grad,
        g_total,
    )


def solution(mesh):
    rows, blks = mesh.shape["row"], mesh.shape["blk"]
    vector = P()
    tokens = P("row", "blk", None)
    attn = P(("row", "blk"), None)
    mlp = P(("row", "blk"), None, None)

    def run(*arrays):
        plan = Plan(rows, blks, arrays[0].shape[-1] // HD)
        return jax.shard_map(
            functools.partial(shards, plan),
            mesh=mesh,
            in_specs=(tokens, attn, mlp) + (vector,) * 8 + (P("row", None), tokens),
            out_specs=(tokens, tokens, attn, mlp) + (vector,) * 8,
            check_vma=False,
        )(*arrays)

    return run
```

```python
import functools
import math

import jax
import jax.numpy as jnp
import numpy as np
from jax import lax
from jax.experimental import pallas as pl
from jax.experimental.pallas import tpu as pltpu
from jax.sharding import PartitionSpec as P

HD = 256
ROT = 64
LANES = 128
BLOCK = 256
EPSILON = 1e-05
MASKED = -1e30
BF = jnp.bfloat16
F32 = jnp.float32
COST = 100
VMEM_LIMIT = 56 * 2**20
SMALL = 16 * 2**20


class Plan:
    def __init__(self, rows, blks, heads):
        self.rows = rows
        self.blks = blks
        self.share = blks // heads
        self.per_row = heads // rows
        self.group = blks // self.per_row
        self.groups = [
            list(range(i * self.group, (i + 1) * self.group)) for i in range(self.per_row)
        ]


def after(field, *others):
    return lax.optimization_barrier((field,) + others)[0] if others else field


def swap(field, axis, size, bit):
    return lax.ppermute(field, axis, [(i, i ^ bit) for i in range(size)])


def swap_group(field, plan, bits):
    return lax.ppermute(field, "blk", [(i, i ^ bits) for i in range(plan.blks)])


def gather_row(own, plan):
    return [own] + [swap(own, "row", plan.rows, k) for k in range(1, plan.rows)]


def scatter_row(pieces, plan, far=None):
    return [
        swap(v, "row", plan.rows, k)
        for k, v in enumerate(pieces)
        if k and (far is None or far == (k & (k - 1) != 0))
    ]


def dot(left, right, left_dim, right_dim):
    return lax.dot_general(
        left, right, (((left_dim,), (right_dim,)), ((), ())), preferred_element_type=F32
    )


def whole(array):
    return pl.BlockSpec(array.shape, lambda *i: (0,) * len(array.shape))


def like(shape, kind=BF):
    return jax.ShapeDtypeStruct(shape, kind)


def call(body, turns, grid, in_specs, out_specs, out_shape, operands, flops=0, limit=None):
    moved = sum(v.size * v.dtype.itemsize for v in operands)
    moved += sum(math.prod(v.shape) * jnp.dtype(v.dtype).itemsize for v in out_shape)
    return pl.pallas_call(
        body,
        name=getattr(body, "func", body).__name__,
        grid_spec=pltpu.PrefetchScalarGridSpec(
            num_scalar_prefetch=1, grid=(grid,), in_specs=in_specs, out_specs=out_specs
        ),
        out_shape=out_shape,
        compiler_params=pltpu.CompilerParams(vmem_limit_bytes=limit or VMEM_LIMIT),
        cost_estimate=pl.CostEstimate(
            flops=flops // COST, bytes_accessed=moved // COST, transcendentals=0
        ),
    )(turns, *operands)


def rows_block(columns, block=BLOCK):
    return pl.BlockSpec((block, columns), lambda i, t: (i, 0))


def add_kernel(t_ref, *refs):
    refs[-1][...] = sum(ref[...].astype(F32) for ref in refs[:-1]).astype(BF)


def add_pieces(turns, terms):
    depth, width = terms[0].shape
    block = rows_block(width, depth // 4)
    shape = like((depth, width))
    return call(
        add_kernel, turns, 4, [block] * len(terms), [block], [shape], terms, limit=SMALL
    )[0]


def turn_kernel(t_ref, x_ref, g_ref, v_ref, xo_ref, go_ref, vo_ref, s_ref):
    xo_ref[...] = x_ref[...]
    go_ref[...] = g_ref[...]
    vo_ref[...] = v_ref[...]
    s_ref[...] = jnp.sum(g_ref[...].astype(F32), 0, keepdims=True)


def turn_in(turns, x, g, vectors):
    rows = turns.shape[0]
    part = x.shape[1] // rows

    def specs(array, turned):
        index = (lambda k, t: (0, t[k])) if turned else (lambda k, t: (0, k))
        return pl.BlockSpec((array.shape[0], part), index)

    total_shape = like((1, x.shape[1]), F32)
    return call(
        turn_kernel,
        turns,
        rows,
        [specs(v, True) for v in (x, g, vectors)],
        [specs(v, False) for v in (x, g, vectors)] + [specs(total_shape, True)],
        [like(v.shape, v.dtype) for v in (x, g, vectors)] + [total_shape],
        [x, g, vectors],
    )


def split_kernel(t_ref, w_ref, u_ref, d_ref):
    u_ref[0] = w_ref[:, 0, :]
    d_ref[0] = w_ref[:, 1, :]


def split_mlp(turns, weights, blks):
    depth, _, hidden = weights.shape
    part = hidden // blks
    block = pl.BlockSpec((1, depth, part), lambda b, t: (b, 0, 0))
    return call(
        split_kernel,
        turns,
        blks,
        [pl.BlockSpec((depth, 2, part), lambda b, t: (0, 0, b))],
        [block] * 2,
        [like((blks, depth, part))] * 2,
        [weights],
    )


def join_kernel(t_ref, u_ref, d_ref, o_ref):
    o_ref[:, 0, :] = u_ref[0].astype(F32)
    o_ref[:, 1, :] = d_ref[0].astype(F32)


def join_mlp(turns, up, down):
    blks, depth, part = up.shape
    block = pl.BlockSpec((1, depth, part), lambda b, t: (b, 0, 0))
    return call(
        join_kernel,
        turns,
        blks,
        [block] * 2,
        [pl.BlockSpec((depth, 2, part), lambda b, t: (0, 0, b))],
        [like((depth, 2, blks * part), F32)],
        [up, down],
    )[0]


def split_attn_kernel(plan, width, t_ref, w_ref, qkv_ref, out_ref):
    b = pl.program_id(0)
    head = b % plan.group // plan.share * plan.per_row + b // plan.group
    for i in range(3):
        at = pl.multiple_of(i * width + head * HD, HD)
        qkv_ref[0, :, i * HD : (i + 1) * HD] = w_ref[:, pl.ds(at, HD)]

    @pl.when(b == 0)
    def _():
        out_ref[...] = w_ref[:, 3 * width :]


def split_attn(turns, weights, plan, width):
    depth = weights.shape[0]
    return call(
        functools.partial(split_attn_kernel, plan, width),
        turns,
        plan.blks,
        [whole(weights)],
        [
            pl.BlockSpec((1, depth, 3 * HD), lambda b, t: (b, 0, 0)),
            pl.BlockSpec((depth, width), lambda b, t: (0, 0)),
        ],
        [like((plan.blks, depth, 3 * HD)), like((depth, width))],
        [weights],
        limit=SMALL,
    )


def join_attn_kernel(plan, t_ref, qkv_ref, out_ref, o_ref):
    step = pl.program_id(0)
    heads = o_ref.shape[1] // HD

    @pl.when(step < 3)
    def _():
        at = pl.ds(pl.multiple_of(step * HD, HD), HD)
        for h in range(heads):
            first = h % plan.per_row * plan.group + h // plan.per_row * plan.share
            o_ref[:, h * HD : (h + 1) * HD] = sum(
                qkv_ref[first + i, :, at].astype(F32) for i in range(plan.share)
            )

    @pl.when(step == 3)
    def _():
        o_ref[...] = out_ref[...]


def join_attn(turns, qkv, out, plan):
    depth, width = out.shape
    return call(
        functools.partial(join_attn_kernel, plan),
        turns,
        4,
        [whole(qkv), whole(out)],
        [pl.BlockSpec((depth, width), lambda j, t: (0, j))],
        [like((depth, 4 * width), F32)],
        [qkv, out],
    )[0]


def pick_kernel(count, t_ref, *refs):
    pieces, outs = refs[:count], refs[count:]
    share = t_ref.shape[0] // len(outs)
    for n, out in enumerate(outs):
        for i in range(share):
            for k, piece in enumerate(pieces):

                @pl.when(t_ref[n * share + i] == k)
                def _(i=i, out=out, piece=piece):
                    out[...] = piece[...] if i == 0 else out[...] + piece[...]


def pick(table, pieces, count):
    return call(
        functools.partial(pick_kernel, len(pieces)),
        table,
        1,
        [whole(p) for p in pieces],
        [whole(pieces[0])] * count,
        [like(pieces[0].shape)] * count,
        pieces,
    )


def place_kernel(t_ref, *refs):
    *pieces, out_ref = refs
    for k, piece in enumerate(pieces):
        depth = piece.shape[0]
        out_ref[pl.ds(pl.multiple_of(t_ref[k] * depth, depth), depth)] = piece[...]


def place(table, pieces):
    depth, width = pieces[0].shape
    shape = like((len(pieces) * depth, width))
    return call(place_kernel, table, 1, [whole(p) for p in pieces], [whole(shape)], [shape], pieces)[0]


def norm_kernel(t_ref, x_ref, v_ref, a1_ref, a2_ref):
    field = x_ref[...].astype(F32)
    centred = field - jnp.mean(field, -1, keepdims=True)
    standard = centred * lax.rsqrt(jnp.mean(centred * centred, -1, keepdims=True) + EPSILON)
    a1_ref[...] = (standard * v_ref[0:1] + v_ref[1:2]).astype(BF)
    a2_ref[...] = (standard * v_ref[2:3] + v_ref[3:4]).astype(BF)


def norms(turns, x, vectors):
    count, width = x.shape
    return call(
        norm_kernel,
        turns,
        count // BLOCK,
        [rows_block(width), whole(vectors)],
        [rows_block(width)] * 2,
        [like(x.shape)] * 2,
        [x, vectors],
        20 * count * width,
    )


def times_pieces(left, pieces):
    out, start = None, 0
    for piece in pieces:
        depth = piece.shape[0]
        term = dot(left[:, start : start + depth], piece[...], 1, 0)
        out = term if out is None else out + term
        start += depth
    return out


def up_kernel(t_ref, a_ref, b_ref, *refs):
    pieces, (h_ref, s_ref) = refs[:-2], refs[-2:]
    pre = times_pieces(a_ref[...], pieces) + b_ref[...]
    cdf = 0.5 * (1.0 + lax.erf(pre * math.sqrt(0.5)))
    h_ref[...] = (pre * cdf).astype(BF)
    s_ref[...] = cdf + pre * (jnp.exp(-0.5 * pre * pre) * (1.0 / math.sqrt(2.0 * math.pi)))


def feed_up(turns, normed, bias, pieces):
    count, width = normed.shape
    hidden = bias.shape[0]
    return call(
        up_kernel,
        turns,
        count // BLOCK,
        [rows_block(width), pl.BlockSpec((1, hidden), lambda i, t: (0, 0))]
        + [whole(p) for p in pieces],
        [rows_block(hidden)] * 2,
        [like((count, hidden)), like((count, hidden), F32)],
        [normed, bias.reshape(1, hidden)] + pieces,
        2 * count * width * hidden,
    )


def slope_kernel(t_ref, g_ref, s_ref, *refs):
    pieces, (p_ref, sum_ref) = refs[:-2], refs[-2:]

    @pl.when(pl.program_id(0) == 0)
    def _():
        sum_ref[...] = jnp.zeros_like(sum_ref)

    grad = (times_pieces(g_ref[...], pieces) * s_ref[...]).astype(BF)
    p_ref[...] = grad
    sum_ref[...] += jnp.sum(grad.astype(F32), 0, keepdims=True)


def feed_slope(turns, grad, slope, pieces):
    count, width = grad.shape
    hidden = slope.shape[1]
    return call(
        slope_kernel,
        turns,
        count // BLOCK,
        [rows_block(width), rows_block(hidden)] + [whole(p) for p in pieces],
        [rows_block(hidden), pl.BlockSpec((1, hidden), lambda i, t: (0, 0))],
        [like((count, hidden)), like((1, hidden), F32)],
        [grad, slope] + pieces,
        2 * count * width * hidden,
    )


def lane_sum(field):
    return sum(field[:, i : i + LANES] for i in range(0, field.shape[1], LANES))


def weight_kernel(rows, with_sums, t_ref, l_ref, r_ref, *refs):
    step = pl.program_id(0)
    if with_sums:
        sum_ref, pieces, refs = refs[0], refs[1 : 1 + rows], refs[1 + rows :]
        parts_ref = refs[-1]
    grad = dot(l_ref[...], r_ref[...], 0, 0)
    for k in range(rows):

        @pl.when(step == k)
        def _(k=k):
            refs[k][...] = grad.astype(BF)
            if with_sums:
                piece = pieces[k][...].astype(F32)
                parts_ref[0] = lane_sum(piece * grad)
                parts_ref[1] = lane_sum(piece * sum_ref[...])


def weight_grad(turns, left, right, sums=None, pieces=()):
    rows = turns.shape[0]
    count, width = left.shape
    columns = right.shape[1]
    depth = width // rows
    out_shape = [like((depth, columns))] * rows
    out_specs = [whole(v) for v in out_shape]
    operands = [left, right]
    if pieces:
        operands += [sums] + pieces
        out_shape.append(like((2, width, LANES), F32))
        out_specs.append(pl.BlockSpec((2, depth, LANES), lambda k, t: (0, t[k], 0)))
    out = call(
        functools.partial(weight_kernel, rows, bool(pieces)),
        turns,
        rows,
        [pl.BlockSpec((count, depth), lambda k, t: (0, k))] + [whole(v) for v in operands[1:]],
        out_specs,
        out_shape,
        operands,
        2 * count * width * columns,
    )
    if pieces:
        return out[:-1], out[-1]
    return out


def out_kernel(rows, t_ref, o_ref, g_ref, *refs):
    *outs, grad_ref = refs
    depth = outs[0].shape[0]
    grad_ref[...] = dot(o_ref[...], g_ref[...], 0, 0)
    for j, out in enumerate(outs):
        at = pl.multiple_of(t_ref[rows + j] * depth, depth)
        out[...] = grad_ref[pl.ds(at, depth)].astype(BF)


def out_grad(turns, places, attended, grad):
    rows, group = turns.shape[0], places.shape[0]
    count, width = grad.shape
    part = width // rows
    depth = HD // group
    return pl.pallas_call(
        functools.partial(out_kernel, rows),
        name="out_kernel",
        grid_spec=pltpu.PrefetchScalarGridSpec(
            num_scalar_prefetch=1,
            grid=(rows,),
            in_specs=[whole(attended), pl.BlockSpec((count, part), lambda k, t: (0, k))],
            out_specs=[pl.BlockSpec((depth, part), lambda k, t: (0, t[k]))] * group,
            scratch_shapes=[pltpu.VMEM((HD, part), F32)],
        ),
        out_shape=[like((depth, width))] * group,
        compiler_params=pltpu.CompilerParams(vmem_limit_bytes=VMEM_LIMIT),
        cost_estimate=pl.CostEstimate(
            flops=2 * count * width * HD // COST,
            bytes_accessed=2 * (count * (width + HD) + width * HD) // COST,
            transcendentals=0,
        ),
    )(jnp.concatenate([turns, places]), attended, grad)


def turned_columns(t_ref, w_ref, k, depth):
    return w_ref[:, pl.ds(pl.multiple_of(t_ref[k] * depth, LANES), depth)]


def sum_kernel(t_ref, h_ref, o_ref, w_ref, *refs):
    pieces, y_ref = refs[:-1], refs[-1]
    for k, piece in enumerate(pieces):
        depth = piece.shape[0]
        term = dot(h_ref[...], piece[...], 1, 1)
        term += dot(o_ref[...], turned_columns(t_ref, w_ref, k, depth), 1, 0)
        y_ref[:, k * depth : (k + 1) * depth] = term.astype(BF)


def out_sum(turns, hidden, pieces, attended, out_w):
    count = hidden.shape[0]
    width = out_w.shape[1]
    return call(
        sum_kernel,
        turns,
        count // BLOCK,
        [rows_block(hidden.shape[1]), rows_block(HD), whole(out_w)] + [whole(p) for p in pieces],
        [rows_block(width)],
        [like((count, width))],
        [hidden, attended, out_w] + pieces,
        2 * count * width * (hidden.shape[1] + HD),
    )[0]


def back_kernel(t_ref, p_ref, q_ref, v_ref, *refs):
    pieces, c_ref = refs[:-1], refs[-1]
    count = len(pieces) // 2
    for k, (up, qkv) in enumerate(zip(pieces[:count], pieces[count:])):
        depth = up.shape[0]
        cols = slice(k * depth, (k + 1) * depth)
        term = dot(p_ref[...], up[...], 1, 1) * v_ref[2:3, cols]
        term += dot(q_ref[...], qkv[...], 1, 1) * v_ref[0:1, cols]
        c_ref[:, cols] = term.astype(BF)


def norm_back(turns, pre_grad, up_pieces, qkv_grad, qkv_pieces, vectors):
    count = pre_grad.shape[0]
    width = vectors.shape[1]
    columns = pre_grad.shape[1] + qkv_grad.shape[1]
    return call(
        back_kernel,
        turns,
        count // BLOCK,
        [rows_block(pre_grad.shape[1]), rows_block(qkv_grad.shape[1]), whole(vectors)]
        + [whole(p) for p in up_pieces + qkv_pieces],
        [rows_block(width)],
        [like((count, width))],
        [pre_grad, qkv_grad, vectors] + up_pieces + qkv_pieces,
        2 * count * width * columns,
    )[0]


def turned(field, cosine, minus, plus):
    head = field[:, :LANES]
    half = ROT // 2
    head = (
        head * cosine
        + pltpu.roll(head, LANES - half, 1) * minus
        + pltpu.roll(head, half, 1) * plus
    )
    return jnp.concatenate([head, field[:, LANES:]], 1)


def allowed_pairs(length, dq_ref, dk_ref):
    spot = lax.broadcasted_iota(jnp.int32, (length, length), 0)
    other = lax.broadcasted_iota(jnp.int32, (length, length), 1)
    return (dq_ref[0] == dk_ref[0]) & (other <= spot)


def forward_kernel(t_ref, a_ref, b_ref, c_ref, m_ref, p_ref, dq_ref, dk_ref, *refs):
    pieces, (qkv_ref, o_ref, lse_ref) = refs[:-3], refs[-3:]
    qkv = times_pieces(a_ref[...], pieces) + b_ref[...]
    tables = c_ref[0], m_ref[0], p_ref[0]
    queries = (turned(qkv[:, :HD], *tables) * HD ** (-0.5)).astype(BF)
    keys = turned(qkv[:, HD : 2 * HD], *tables).astype(BF)
    values = qkv[:, 2 * HD :].astype(BF)
    for i, field in enumerate((queries, keys, values)):
        qkv_ref[:, i * HD : (i + 1) * HD] = field
    allowed = allowed_pairs(a_ref.shape[0], dq_ref, dk_ref)
    scores = jnp.where(allowed, dot(queries, keys, 1, 1), MASKED)
    largest = jnp.max(scores, -1, keepdims=True)
    weights = jnp.where(allowed, jnp.exp(scores - largest), 0.0)
    mass = jnp.sum(weights, -1, keepdims=True)
    o_ref[...] = dot((weights / mass).astype(BF), values, 1, 0).astype(BF)
    lse_ref[...] = largest + jnp.log(mass)


def backward_kernel(
    parts, t_ref, g_ref, w_ref, qkv_ref, o_ref, lse_ref, c_ref, m_ref, p_ref, dq_ref, dk_ref,
    grad_ref, sum_ref,
):
    queries, keys, values = (qkv_ref[:, i * HD : (i + 1) * HD] for i in range(3))
    tables = c_ref[0], -m_ref[0], -p_ref[0]
    depth = w_ref.shape[1] // parts
    heads_grad = None
    for k in range(parts):
        cols = slice(k * depth, (k + 1) * depth)
        term = dot(g_ref[:, cols], turned_columns(t_ref, w_ref, k, depth), 1, 1)
        heads_grad = term if heads_grad is None else heads_grad + term
    heads_grad = heads_grad.astype(BF)
    allowed = allowed_pairs(g_ref.shape[0], dq_ref, dk_ref)
    scores = jnp.where(allowed, dot(queries, keys, 1, 1), MASKED)
    weights = jnp.where(allowed, jnp.exp(scores - lse_ref[...]), 0.0)
    deltas = jnp.sum(heads_grad.astype(F32) * o_ref[...].astype(F32), -1, keepdims=True)
    score_grad = (weights * (dot(heads_grad, values, 1, 1) - deltas)).astype(BF)
    query_grad = dot(score_grad, keys, 1, 0) * HD ** (-0.5)
    key_grad = dot(score_grad, queries, 0, 0)
    value_grad = dot(weights.astype(BF), heads_grad, 0, 0)
    fields = turned(query_grad, *tables), turned(key_grad, *tables), value_grad

    @pl.when(pl.program_id(0) == 0)
    def _():
        sum_ref[...] = jnp.zeros_like(sum_ref)

    for i, field in enumerate(fields):
        field = field.astype(BF)
        cols = slice(i * HD, (i + 1) * HD)
        grad_ref[:, cols] = field
        sum_ref[:, cols] += jnp.sum(field.astype(F32), 0, keepdims=True)


def pair_specs(length):
    table = pl.BlockSpec((1, length, LANES), lambda r, t: (r, 0, 0))
    return [table] * 3 + [
        pl.BlockSpec((1, length, 1), lambda r, t: (r, 0, 0)),
        pl.BlockSpec((1, 1, length), lambda r, t: (r, 0, 0)),
    ]


def head_forward(turns, normed, bias, pairs, pieces, length):
    count, width = normed.shape
    columns = 3 * HD
    return call(
        forward_kernel,
        turns,
        count // length,
        [rows_block(width, length), pl.BlockSpec((1, columns), lambda r, t: (0, 0))]
        + pair_specs(length)
        + [whole(p) for p in pieces],
        [rows_block(columns, length), rows_block(HD, length), rows_block(1, length)],
        [like((count, columns)), like((count, HD)), like((count, 1), F32)],
        [normed, bias.reshape(1, columns)] + pairs + pieces,
        2 * count * (width * columns + 2 * length * HD),
    )


def head_backward(turns, grad, out_w, qkv, attended, lse, pairs, length):
    count, width = grad.shape
    columns = 3 * HD
    return call(
        functools.partial(backward_kernel, turns.shape[0]),
        turns,
        count // length,
        [
            rows_block(width, length),
            whole(out_w),
            rows_block(columns, length),
            rows_block(HD, length),
            rows_block(1, length),
        ]
        + pair_specs(length),
        [rows_block(columns, length), pl.BlockSpec((1, columns), lambda r, t: (0, 0))],
        [like((count, columns)), like((1, columns), F32)],
        [grad, out_w, qkv, attended, lse] + pairs,
        2 * count * (width * HD + 5 * length * HD),
    )


def finish_kernel(rows, with_norm, t_ref, x_ref, s_ref, o_ref, out_ref):
    depth = x_ref.shape[1] // rows
    term = s_ref[...].astype(F32)
    if with_norm:
        centred = x_ref[...].astype(F32)
        centred = centred - jnp.mean(centred, -1, keepdims=True)
        rstd = lax.rsqrt(jnp.mean(centred * centred, -1, keepdims=True) + EPSILON)
        centred = centred * rstd
        term = term - jnp.mean(term, -1, keepdims=True) - centred * jnp.mean(
            term * centred, -1, keepdims=True
        )
        field = o_ref[...].astype(F32) + rstd * term
    else:
        field = x_ref[...].astype(F32) + term + o_ref[4:5]
    for k in range(rows):
        at = pl.multiple_of(t_ref[k] * depth, LANES)
        out_ref[:, pl.ds(at, depth)] = field[:, k * depth : (k + 1) * depth].astype(BF)


def finish(turns, x, term, other, with_norm):
    return call(
        functools.partial(finish_kernel, turns.shape[0], with_norm),
        turns,
        1,
        [whole(v) for v in (x, term, other)],
        [whole(x)],
        [like(x.shape)],
        [x, term, other],
    )[0]


def shards(
    plan,
    tokens,
    attn_weights,
    mlp_weights,
    ln1_gain,
    ln1_bias,
    ln2_gain,
    ln2_bias,
    qkv_bias,
    dense_bias,
    up_bias,
    down_bias,
    doc_lengths,
    cotangent,
):
    row_count, shard_len, width = tokens.shape
    depth = attn_weights.shape[0]
    heads = width // HD
    rows, blks = plan.rows, plan.blks
    own_hidden = mlp_weights.shape[-1] // blks
    me = lax.axis_index("blk")
    length = shard_len * blks
    count = row_count * length
    head_of = me % plan.group // plan.share * plan.per_row + me // plan.group
    part = me % plan.share
    own_rows = row_count // plan.share
    row = lax.axis_index("row")
    turns = row ^ jnp.arange(rows, dtype=jnp.int32)
    places = me % plan.group ^ jnp.arange(plan.group, dtype=jnp.int32)

    def exchange(field):
        return lax.all_to_all(field, "blk", 0, 0)

    def collect(field):
        return exchange(field.reshape(blks, -1, field.shape[-1]))

    def gather_blocks(field):
        field = field.reshape(row_count, shard_len, width)
        return lax.all_gather(field, "blk", axis=1, tiled=True).reshape(count, width)

    def sum_blocks(field):
        field = field.reshape(row_count, length, width)
        field = lax.psum_scatter(field, "blk", scatter_dimension=1, tiled=True)
        return field.reshape(row_count * shard_len, width)

    zeros = jnp.zeros((3, width), F32)
    vectors = jnp.stack([ln1_gain, ln1_bias, ln2_gain, ln2_bias, dense_bias + down_bias])
    x_own, g_own, vectors, g_sum = turn_in(
        turns,
        tokens.reshape(row_count * shard_len, width),
        cotangent.reshape(row_count * shard_len, width),
        jnp.concatenate([vectors, zeros]),
    )
    qkv_send, out_own = split_attn(turns, attn_weights, plan, width)
    qkv_mine = exchange(qkv_send)
    out_send = pick(
        row ^ places // plan.share,
        [out_own] + [swap(out_own, "row", rows, k) for k in range(1, rows)],
        plan.group,
    )
    up_send, down_send = split_mlp(turns, after(mlp_weights, qkv_send), blks)
    qkv_mine, up_send, *out_send = lax.optimization_barrier((qkv_mine, up_send, *out_send))
    up_mine = exchange(up_send)
    qkv_pieces = gather_row(qkv_mine.reshape(-1, 3 * HD), plan)
    out_got = [out_send[0]] + [swap_group(out_send[j], plan, j) for j in range(1, plan.group)]
    up_mine, x_own, down_send, *qkv_pieces = lax.optimization_barrier(
        (up_mine, x_own, down_send, *qkv_pieces, *out_got)
    )[: 3 + rows]
    x_all = gather_blocks(x_own)
    down_mine = exchange(down_send)
    up_pieces = gather_row(up_mine.reshape(-1, own_hidden), plan)
    out_w = place(places, out_got)
    down_mine, g_own, *up_pieces = lax.optimization_barrier((down_mine, g_own, *up_pieces))
    g_all = gather_blocks(g_own)
    down_pieces = gather_row(down_mine.reshape(-1, own_hidden), plan)
    normed1, normed2 = norms(turns, x_all, vectors)

    lengths = lax.dynamic_slice_in_dim(doc_lengths, part * own_rows, own_rows, 0)
    doc_ends = jnp.cumsum(lengths, axis=-1)
    starts = doc_ends - lengths
    spots = jnp.arange(length, dtype=jnp.int32)
    doc_ids = jnp.sum((spots[None, :, None] >= doc_ends[:, None, :]).astype(jnp.int32), -1)
    picked = doc_ids[:, :, None] == jnp.arange(lengths.shape[-1], dtype=jnp.int32)
    positions = spots - jnp.sum(jnp.where(picked, starts[:, None, :], 0), -1)
    lane = jnp.arange(LANES)
    inverse = 10000.0 ** (-2.0 * (lane % (ROT // 2)).astype(F32) / ROT)
    angles = positions.astype(F32)[..., None] * inverse
    sine = jnp.sin(angles)
    pairs = [
        jnp.where(lane < ROT, jnp.cos(angles), 1.0),
        jnp.where(lane < ROT // 2, -sine, 0.0),
        jnp.where((lane >= ROT // 2) & (lane < ROT), sine, 0.0),
        doc_ids[:, :, None],
        doc_ids[:, None, :],
    ]

    def own(field):
        if plan.share == 1:
            return field
        return lax.dynamic_slice_in_dim(field, part * own_rows * length, own_rows * length, 0)

    def spread(field):
        if plan.share == 1:
            return field
        blank = jnp.zeros((count, field.shape[1]), field.dtype)
        return lax.dynamic_update_slice_in_dim(blank, field, part * own_rows * length, 0)

    up_b = lax.dynamic_slice_in_dim(up_bias, me * own_hidden, own_hidden)
    qkv_b = lax.dynamic_index_in_dim(qkv_bias.reshape(3, heads, HD), head_of, 1, keepdims=False)
    own_normed1 = own(normed1)
    qkv, attended, lse = head_forward(
        turns, own_normed1, qkv_b.reshape(-1), pairs, qkv_pieces, length
    )
    hidden, slope = feed_up(turns, after(normed2, attended), up_b, up_pieces)
    out_term = out_sum(turns, hidden, down_pieces, spread(attended), out_w)
    out_total = sum_blocks(out_term)

    g_all = after(g_all, out_term)
    down_g = weight_grad(turns, g_all, hidden)
    down_got = scatter_row(down_g, plan)
    own_grad = own(after(g_all, down_g[0]))
    out_g = out_grad(turns, places, attended, own_grad)
    out_got = [out_g[0]] + [swap_group(out_g[j], plan, j) for j in range(1, plan.group)]
    pre_grad, up_sum = feed_slope(turns, after(g_all, out_g[0]), slope, down_pieces)
    up_g, up_parts = weight_grad(turns, normed2, pre_grad, up_sum, up_pieces)
    qkv_grad, qkv_sum = head_backward(
        turns, after(own_grad, up_g[0]), out_w, qkv, attended, lse, pairs, length
    )
    down_total = add_pieces(turns, [after(down_g[0], qkv_grad, *out_got)] + down_got)
    down_back = collect(down_total)
    up_near = scatter_row([after(v, down_total) for v in up_g], plan, False)
    qkv_g, qkv_parts = weight_grad(
        turns, after(own_normed1, down_total), qkv_grad, qkv_sum, qkv_pieces
    )
    norm_term = norm_back(
        turns,
        after(pre_grad, qkv_g[0], out_total, *up_near),
        up_pieces,
        spread(qkv_grad),
        qkv_pieces,
        vectors,
    )
    up_got = up_near + scatter_row([after(v, *up_near) for v in up_g], plan, True)

    terms = [jnp.sum(v, -1) for v in (qkv_parts, up_parts)] + [g_sum, qkv_sum, up_sum]
    terms = [v.reshape(-1) for v in terms]
    used = sum(v.size for v in terms)
    terms.append(jnp.zeros((-used % (8 * LANES),), F32))
    sums = jnp.concatenate(terms)
    sums = sums + sum(swap(sums, "row", rows, k) for k in range(1, rows))

    up_total = add_pieces(turns, [after(up_g[0], norm_term, down_back, sums)] + up_got)
    norm_total = sum_blocks(after(norm_term, up_total))
    up_back = collect(up_total)
    qkv_got = scatter_row([after(v, up_total) for v in qkv_g], plan)
    sums = after(sums, up_total)
    sums = jnp.stack([sums, swap(sums, "blk", blks, 1)])
    qkv_total = add_pieces(turns, [after(qkv_g[0], up_back, sums)] + qkv_got)
    qkv_back = collect(qkv_total)
    holders = turns[:, None] * plan.share + jnp.arange(plan.share, dtype=jnp.int32)
    out_send = pick((me % plan.group ^ holders).reshape(-1), out_got, rows)
    out_back = out_send[0].astype(F32) + sum(
        swap(after(out_send[k], qkv_total), "row", rows, k).astype(F32) for k in range(1, rows)
    )
    sums = after(sums, qkv_total)
    sums = jnp.concatenate([sums] + [swap(sums, "blk", blks, k) for k in range(2, blks, 2)])
    sums = sums[me ^ jnp.arange(blks, dtype=jnp.int32)]
    gain1, bias1, gain2, bias2, g_total = jnp.split(
        jnp.sum(sums[:, : 5 * width], 0), 5
    )
    sums = sums[:, 5 * width : used]
    qkv_bias_grad = sums[:, : 3 * HD].reshape(plan.per_row, rows, plan.share, 3, HD)
    qkv_bias_grad = jnp.sum(qkv_bias_grad, 2).transpose(2, 1, 0, 3).reshape(-1)
    up_bias_grad = sums[:, 3 * HD :].reshape(-1)

    layer_out = finish(turns, x_own, out_total, vectors, False)
    tokens_grad = finish(turns, x_own, norm_total, g_own, True)
    return (
        layer_out.reshape(tokens.shape),
        tokens_grad.reshape(tokens.shape),
        join_attn(turns, qkv_back, out_back, plan),
        join_mlp(turns, up_back, down_back),
        (gain1 - ln1_bias * bias1) / ln1_gain,
        bias1,
        (gain2 - ln2_bias * bias2) / ln2_gain,
        bias2,
        qkv_bias_grad,
        g_total,
        up_bias_grad,
        g_total,
    )


def solution(mesh):
    rows, blks = mesh.shape["row"], mesh.shape["blk"]
    vector = P()
    tokens = P("row", "blk", None)
    attn = P(("row", "blk"), None)
    mlp = P(("row", "blk"), None, None)

    def run(*arrays):
        plan = Plan(rows, blks, arrays[0].shape[-1] // HD)
        return jax.shard_map(
            functools.partial(shards, plan),
            mesh=mesh,
            in_specs=(tokens, attn, mlp) + (vector,) * 8 + (P("row", None), tokens),
            out_specs=(tokens, tokens, attn, mlp) + (vector,) * 8,
            check_vma=False,
        )(*arrays)

    return run
```

```python
import functools
import math

import jax
import jax.numpy as jnp
import numpy as np
from jax import lax
from jax.experimental import pallas as pl
from jax.experimental.pallas import tpu as pltpu
from jax.sharding import PartitionSpec as P

HD = 256
ROT = 64
LANES = 128
BLOCK = 256
EPSILON = 1e-05
MASKED = -1e30
BF = jnp.bfloat16
F32 = jnp.float32
COST = 100
VMEM_LIMIT = 56 * 2**20
SMALL = 16 * 2**20


class Plan:
    def __init__(self, rows, blks, heads):
        self.rows = rows
        self.blks = blks
        self.share = blks // heads
        self.per_row = heads // rows
        self.group = blks // self.per_row
        self.groups = [
            list(range(i * self.group, (i + 1) * self.group)) for i in range(self.per_row)
        ]


def after(field, *others):
    return lax.optimization_barrier((field,) + others)[0] if others else field


def swap(field, axis, size, bit):
    return lax.ppermute(field, axis, [(i, i ^ bit) for i in range(size)])


def swap_group(field, plan, bits):
    return lax.ppermute(field, "blk", [(i, i ^ bits) for i in range(plan.blks)])


def gather_row(own, plan):
    return [own] + [swap(own, "row", plan.rows, k) for k in range(1, plan.rows)]


def scatter_row(pieces, plan, far=None):
    return [
        swap(v, "row", plan.rows, k)
        for k, v in enumerate(pieces)
        if k and (far is None or far == (k & (k - 1) != 0))
    ]


def dot(left, right, left_dim, right_dim):
    return lax.dot_general(
        left, right, (((left_dim,), (right_dim,)), ((), ())), preferred_element_type=F32
    )


def whole(array):
    return pl.BlockSpec(array.shape, lambda *i: (0,) * len(array.shape))


def like(shape, kind=BF):
    return jax.ShapeDtypeStruct(shape, kind)


def call(body, turns, grid, in_specs, out_specs, out_shape, operands, flops=0, limit=None):
    moved = sum(v.size * v.dtype.itemsize for v in operands)
    moved += sum(math.prod(v.shape) * jnp.dtype(v.dtype).itemsize for v in out_shape)
    return pl.pallas_call(
        body,
        name=getattr(body, "func", body).__name__,
        grid_spec=pltpu.PrefetchScalarGridSpec(
            num_scalar_prefetch=1, grid=(grid,), in_specs=in_specs, out_specs=out_specs
        ),
        out_shape=out_shape,
        compiler_params=pltpu.CompilerParams(vmem_limit_bytes=limit or VMEM_LIMIT),
        cost_estimate=pl.CostEstimate(
            flops=flops // COST, bytes_accessed=moved // COST, transcendentals=0
        ),
    )(turns, *operands)


def rows_block(columns, block=BLOCK):
    return pl.BlockSpec((block, columns), lambda i, t: (i, 0))


def add_kernel(t_ref, *refs):
    refs[-1][...] = sum(ref[...].astype(F32) for ref in refs[:-1]).astype(BF)


def add_pieces(turns, terms):
    depth, width = terms[0].shape
    block = rows_block(width, depth // 4)
    shape = like((depth, width))
    return call(
        add_kernel, turns, 4, [block] * len(terms), [block], [shape], terms, limit=SMALL
    )[0]


def turn_kernel(t_ref, x_ref, g_ref, v_ref, xo_ref, go_ref, vo_ref, s_ref):
    xo_ref[...] = x_ref[...]
    go_ref[...] = g_ref[...]
    vo_ref[...] = v_ref[...]
    s_ref[...] = jnp.sum(g_ref[...].astype(F32), 0, keepdims=True)


def turn_in(turns, x, g, vectors):
    rows = turns.shape[0]
    part = x.shape[1] // rows

    def specs(array, turned):
        index = (lambda k, t: (0, t[k])) if turned else (lambda k, t: (0, k))
        return pl.BlockSpec((array.shape[0], part), index)

    total_shape = like((1, x.shape[1]), F32)
    return call(
        turn_kernel,
        turns,
        rows,
        [specs(v, True) for v in (x, g, vectors)],
        [specs(v, False) for v in (x, g, vectors)] + [specs(total_shape, True)],
        [like(v.shape, v.dtype) for v in (x, g, vectors)] + [total_shape],
        [x, g, vectors],
    )


def split_kernel(t_ref, w_ref, u_ref, d_ref):
    u_ref[0] = w_ref[:, 0, :]
    d_ref[0] = w_ref[:, 1, :]


def split_mlp(turns, weights, blks):
    depth, _, hidden = weights.shape
    part = hidden // blks
    block = pl.BlockSpec((1, depth, part), lambda b, t: (b, 0, 0))
    return call(
        split_kernel,
        turns,
        blks,
        [pl.BlockSpec((depth, 2, part), lambda b, t: (0, 0, b))],
        [block] * 2,
        [like((blks, depth, part))] * 2,
        [weights],
    )


def join_kernel(t_ref, u_ref, d_ref, o_ref):
    o_ref[:, 0, :] = u_ref[0].astype(F32)
    o_ref[:, 1, :] = d_ref[0].astype(F32)


def join_mlp(turns, up, down):
    blks, depth, part = up.shape
    block = pl.BlockSpec((1, depth, part), lambda b, t: (b, 0, 0))
    return call(
        join_kernel,
        turns,
        blks,
        [block] * 2,
        [pl.BlockSpec((depth, 2, part), lambda b, t: (0, 0, b))],
        [like((depth, 2, blks * part), F32)],
        [up, down],
    )[0]


def split_attn_kernel(plan, width, t_ref, w_ref, qkv_ref, out_ref):
    b = pl.program_id(0)
    head = b % plan.group // plan.share * plan.per_row + b // plan.group
    for i in range(3):
        at = pl.multiple_of(i * width + head * HD, HD)
        qkv_ref[0, :, i * HD : (i + 1) * HD] = w_ref[:, pl.ds(at, HD)]

    @pl.when(b == 0)
    def _():
        out_ref[...] = w_ref[:, 3 * width :]


def split_attn(turns, weights, plan, width):
    depth = weights.shape[0]
    return call(
        functools.partial(split_attn_kernel, plan, width),
        turns,
        plan.blks,
        [whole(weights)],
        [
            pl.BlockSpec((1, depth, 3 * HD), lambda b, t: (b, 0, 0)),
            pl.BlockSpec((depth, width), lambda b, t: (0, 0)),
        ],
        [like((plan.blks, depth, 3 * HD)), like((depth, width))],
        [weights],
        limit=SMALL,
    )


def join_attn_kernel(plan, t_ref, qkv_ref, out_ref, o_ref):
    step = pl.program_id(0)
    heads = o_ref.shape[1] // HD

    @pl.when(step < 3)
    def _():
        at = pl.ds(pl.multiple_of(step * HD, HD), HD)
        for h in range(heads):
            first = h % plan.per_row * plan.group + h // plan.per_row * plan.share
            o_ref[:, h * HD : (h + 1) * HD] = sum(
                qkv_ref[first + i, :, at].astype(F32) for i in range(plan.share)
            )

    @pl.when(step == 3)
    def _():
        o_ref[...] = out_ref[...]


def join_attn(turns, qkv, out, plan):
    depth, width = out.shape
    return call(
        functools.partial(join_attn_kernel, plan),
        turns,
        4,
        [whole(qkv), whole(out)],
        [pl.BlockSpec((depth, width), lambda j, t: (0, j))],
        [like((depth, 4 * width), F32)],
        [qkv, out],
    )[0]


def pick_kernel(count, t_ref, *refs):
    pieces, outs = refs[:count], refs[count:]
    share = t_ref.shape[0] // len(outs)
    for n, out in enumerate(outs):
        for i in range(share):
            for k, piece in enumerate(pieces):

                @pl.when(t_ref[n * share + i] == k)
                def _(i=i, out=out, piece=piece):
                    out[...] = piece[...] if i == 0 else out[...] + piece[...]


def pick(table, pieces, count):
    return call(
        functools.partial(pick_kernel, len(pieces)),
        table,
        1,
        [whole(p) for p in pieces],
        [whole(pieces[0])] * count,
        [like(pieces[0].shape)] * count,
        pieces,
    )


def place_kernel(t_ref, *refs):
    *pieces, out_ref = refs
    for k, piece in enumerate(pieces):
        depth = piece.shape[0]
        out_ref[pl.ds(pl.multiple_of(t_ref[k] * depth, depth), depth)] = piece[...]


def place(table, pieces):
    depth, width = pieces[0].shape
    shape = like((len(pieces) * depth, width))
    return call(place_kernel, table, 1, [whole(p) for p in pieces], [whole(shape)], [shape], pieces)[0]


def norm_kernel(t_ref, x_ref, v_ref, a1_ref, a2_ref):
    field = x_ref[...].astype(F32)
    centred = field - jnp.mean(field, -1, keepdims=True)
    standard = centred * lax.rsqrt(jnp.mean(centred * centred, -1, keepdims=True) + EPSILON)
    a1_ref[...] = (standard * v_ref[0:1] + v_ref[1:2]).astype(BF)
    a2_ref[...] = (standard * v_ref[2:3] + v_ref[3:4]).astype(BF)


def norms(turns, x, vectors):
    count, width = x.shape
    return call(
        norm_kernel,
        turns,
        count // BLOCK,
        [rows_block(width), whole(vectors)],
        [rows_block(width)] * 2,
        [like(x.shape)] * 2,
        [x, vectors],
        20 * count * width,
    )


def times_pieces(left, pieces):
    out, start = None, 0
    for piece in pieces:
        depth = piece.shape[0]
        term = dot(left[:, start : start + depth], piece[...], 1, 0)
        out = term if out is None else out + term
        start += depth
    return out


def up_kernel(t_ref, a_ref, b_ref, *refs):
    pieces, (h_ref, s_ref) = refs[:-2], refs[-2:]
    pre = times_pieces(a_ref[...], pieces) + b_ref[...]
    cdf = 0.5 * (1.0 + lax.erf(pre * math.sqrt(0.5)))
    h_ref[...] = (pre * cdf).astype(BF)
    s_ref[...] = cdf + pre * (jnp.exp(-0.5 * pre * pre) * (1.0 / math.sqrt(2.0 * math.pi)))


def feed_up(turns, normed, bias, pieces):
    count, width = normed.shape
    hidden = bias.shape[0]
    return call(
        up_kernel,
        turns,
        count // BLOCK,
        [rows_block(width), pl.BlockSpec((1, hidden), lambda i, t: (0, 0))]
        + [whole(p) for p in pieces],
        [rows_block(hidden)] * 2,
        [like((count, hidden)), like((count, hidden), F32)],
        [normed, bias.reshape(1, hidden)] + pieces,
        2 * count * width * hidden,
    )


def slope_kernel(t_ref, g_ref, s_ref, *refs):
    pieces, (p_ref, sum_ref) = refs[:-2], refs[-2:]

    @pl.when(pl.program_id(0) == 0)
    def _():
        sum_ref[...] = jnp.zeros_like(sum_ref)

    grad = (times_pieces(g_ref[...], pieces) * s_ref[...]).astype(BF)
    p_ref[...] = grad
    sum_ref[...] += jnp.sum(grad.astype(F32), 0, keepdims=True)


def feed_slope(turns, grad, slope, pieces):
    count, width = grad.shape
    hidden = slope.shape[1]
    return call(
        slope_kernel,
        turns,
        count // BLOCK,
        [rows_block(width), rows_block(hidden)] + [whole(p) for p in pieces],
        [rows_block(hidden), pl.BlockSpec((1, hidden), lambda i, t: (0, 0))],
        [like((count, hidden)), like((1, hidden), F32)],
        [grad, slope] + pieces,
        2 * count * width * hidden,
    )


def lane_sum(field):
    return sum(field[:, i : i + LANES] for i in range(0, field.shape[1], LANES))


def weight_kernel(rows, with_sums, t_ref, l_ref, r_ref, *refs):
    step = pl.program_id(0)
    if with_sums:
        sum_ref, pieces, refs = refs[0], refs[1 : 1 + rows], refs[1 + rows :]
        parts_ref = refs[-1]
    grad = dot(l_ref[...], r_ref[...], 0, 0)
    for k in range(rows):

        @pl.when(step == k)
        def _(k=k):
            refs[k][...] = grad.astype(BF)
            if with_sums:
                piece = pieces[k][...].astype(F32)
                parts_ref[0] = lane_sum(piece * grad)
                parts_ref[1] = lane_sum(piece * sum_ref[...])


def weight_grad(turns, left, right, sums=None, pieces=()):
    rows = turns.shape[0]
    count, width = left.shape
    columns = right.shape[1]
    depth = width // rows
    out_shape = [like((depth, columns))] * rows
    out_specs = [whole(v) for v in out_shape]
    operands = [left, right]
    if pieces:
        operands += [sums] + pieces
        out_shape.append(like((2, width, LANES), F32))
        out_specs.append(pl.BlockSpec((2, depth, LANES), lambda k, t: (0, t[k], 0)))
    out = call(
        functools.partial(weight_kernel, rows, bool(pieces)),
        turns,
        rows,
        [pl.BlockSpec((count, depth), lambda k, t: (0, k))] + [whole(v) for v in operands[1:]],
        out_specs,
        out_shape,
        operands,
        2 * count * width * columns,
    )
    if pieces:
        return out[:-1], out[-1]
    return out


def out_kernel(rows, t_ref, o_ref, g_ref, *refs):
    *outs, grad_ref = refs
    depth = outs[0].shape[0]
    grad_ref[...] = dot(o_ref[...], g_ref[...], 0, 0)
    for j, out in enumerate(outs):
        at = pl.multiple_of(t_ref[rows + j] * depth, depth)
        out[...] = grad_ref[pl.ds(at, depth)].astype(BF)


def out_grad(turns, places, attended, grad):
    rows, group = turns.shape[0], places.shape[0]
    count, width = grad.shape
    part = width // rows
    depth = HD // group
    return pl.pallas_call(
        functools.partial(out_kernel, rows),
        name="out_kernel",
        grid_spec=pltpu.PrefetchScalarGridSpec(
            num_scalar_prefetch=1,
            grid=(rows,),
            in_specs=[whole(attended), pl.BlockSpec((count, part), lambda k, t: (0, k))],
            out_specs=[pl.BlockSpec((depth, part), lambda k, t: (0, t[k]))] * group,
            scratch_shapes=[pltpu.VMEM((HD, part), F32)],
        ),
        out_shape=[like((depth, width))] * group,
        compiler_params=pltpu.CompilerParams(vmem_limit_bytes=VMEM_LIMIT),
        cost_estimate=pl.CostEstimate(
            flops=2 * count * width * HD // COST,
            bytes_accessed=2 * (count * (width + HD) + width * HD) // COST,
            transcendentals=0,
        ),
    )(jnp.concatenate([turns, places]), attended, grad)


def turned_columns(t_ref, w_ref, k, depth):
    return w_ref[:, pl.ds(pl.multiple_of(t_ref[k] * depth, LANES), depth)]


def sum_kernel(t_ref, h_ref, o_ref, w_ref, *refs):
    pieces, y_ref = refs[:-1], refs[-1]
    for k, piece in enumerate(pieces):
        depth = piece.shape[0]
        term = dot(h_ref[...], piece[...], 1, 1)
        term += dot(o_ref[...], turned_columns(t_ref, w_ref, k, depth), 1, 0)
        y_ref[:, k * depth : (k + 1) * depth] = term.astype(BF)


def out_sum(turns, hidden, pieces, attended, out_w):
    count = hidden.shape[0]
    width = out_w.shape[1]
    return call(
        sum_kernel,
        turns,
        count // BLOCK,
        [rows_block(hidden.shape[1]), rows_block(HD), whole(out_w)] + [whole(p) for p in pieces],
        [rows_block(width)],
        [like((count, width))],
        [hidden, attended, out_w] + pieces,
        2 * count * width * (hidden.shape[1] + HD),
    )[0]


def back_kernel(t_ref, p_ref, q_ref, v_ref, *refs):
    pieces, c_ref = refs[:-1], refs[-1]
    count = len(pieces) // 2
    for k, (up, qkv) in enumerate(zip(pieces[:count], pieces[count:])):
        depth = up.shape[0]
        cols = slice(k * depth, (k + 1) * depth)
        term = dot(p_ref[...], up[...], 1, 1) * v_ref[2:3, cols]
        term += dot(q_ref[...], qkv[...], 1, 1) * v_ref[0:1, cols]
        c_ref[:, cols] = term.astype(BF)


def norm_back(turns, pre_grad, up_pieces, qkv_grad, qkv_pieces, vectors):
    count = pre_grad.shape[0]
    width = vectors.shape[1]
    columns = pre_grad.shape[1] + qkv_grad.shape[1]
    return call(
        back_kernel,
        turns,
        count // BLOCK,
        [rows_block(pre_grad.shape[1]), rows_block(qkv_grad.shape[1]), whole(vectors)]
        + [whole(p) for p in up_pieces + qkv_pieces],
        [rows_block(width)],
        [like((count, width))],
        [pre_grad, qkv_grad, vectors] + up_pieces + qkv_pieces,
        2 * count * width * columns,
    )[0]


def turned(field, cosine, minus, plus):
    head = field[:, :LANES]
    half = ROT // 2
    head = (
        head * cosine
        + pltpu.roll(head, LANES - half, 1) * minus
        + pltpu.roll(head, half, 1) * plus
    )
    return jnp.concatenate([head, field[:, LANES:]], 1)


def allowed_pairs(length, dq_ref, dk_ref):
    spot = lax.broadcasted_iota(jnp.int32, (length, length), 0)
    other = lax.broadcasted_iota(jnp.int32, (length, length), 1)
    return (dq_ref[0] == dk_ref[0]) & (other <= spot)


def forward_kernel(t_ref, a_ref, b_ref, c_ref, m_ref, p_ref, dq_ref, dk_ref, *refs):
    pieces, (qkv_ref, o_ref, lse_ref) = refs[:-3], refs[-3:]
    qkv = times_pieces(a_ref[...], pieces) + b_ref[...]
    tables = c_ref[0], m_ref[0], p_ref[0]
    queries = (turned(qkv[:, :HD], *tables) * HD ** (-0.5)).astype(BF)
    keys = turned(qkv[:, HD : 2 * HD], *tables).astype(BF)
    values = qkv[:, 2 * HD :].astype(BF)
    for i, field in enumerate((queries, keys, values)):
        qkv_ref[:, i * HD : (i + 1) * HD] = field
    allowed = allowed_pairs(a_ref.shape[0], dq_ref, dk_ref)
    scores = jnp.where(allowed, dot(queries, keys, 1, 1), MASKED)
    largest = jnp.max(scores, -1, keepdims=True)
    weights = jnp.where(allowed, jnp.exp(scores - largest), 0.0)
    mass = jnp.sum(weights, -1, keepdims=True)
    o_ref[...] = dot((weights / mass).astype(BF), values, 1, 0).astype(BF)
    lse_ref[...] = largest + jnp.log(mass)


def backward_kernel(
    parts, t_ref, g_ref, w_ref, qkv_ref, o_ref, lse_ref, c_ref, m_ref, p_ref, dq_ref, dk_ref,
    grad_ref, sum_ref,
):
    queries, keys, values = (qkv_ref[:, i * HD : (i + 1) * HD] for i in range(3))
    tables = c_ref[0], -m_ref[0], -p_ref[0]
    depth = w_ref.shape[1] // parts
    heads_grad = None
    for k in range(parts):
        cols = slice(k * depth, (k + 1) * depth)
        term = dot(g_ref[:, cols], turned_columns(t_ref, w_ref, k, depth), 1, 1)
        heads_grad = term if heads_grad is None else heads_grad + term
    heads_grad = heads_grad.astype(BF)
    allowed = allowed_pairs(g_ref.shape[0], dq_ref, dk_ref)
    scores = jnp.where(allowed, dot(queries, keys, 1, 1), MASKED)
    weights = jnp.where(allowed, jnp.exp(scores - lse_ref[...]), 0.0)
    deltas = jnp.sum(heads_grad.astype(F32) * o_ref[...].astype(F32), -1, keepdims=True)
    score_grad = (weights * (dot(heads_grad, values, 1, 1) - deltas)).astype(BF)
    query_grad = dot(score_grad, keys, 1, 0) * HD ** (-0.5)
    key_grad = dot(score_grad, queries, 0, 0)
    value_grad = dot(weights.astype(BF), heads_grad, 0, 0)
    fields = turned(query_grad, *tables), turned(key_grad, *tables), value_grad

    @pl.when(pl.program_id(0) == 0)
    def _():
        sum_ref[...] = jnp.zeros_like(sum_ref)

    for i, field in enumerate(fields):
        field = field.astype(BF)
        cols = slice(i * HD, (i + 1) * HD)
        grad_ref[:, cols] = field
        sum_ref[:, cols] += jnp.sum(field.astype(F32), 0, keepdims=True)


def pair_specs(length):
    table = pl.BlockSpec((1, length, LANES), lambda r, t: (r, 0, 0))
    return [table] * 3 + [
        pl.BlockSpec((1, length, 1), lambda r, t: (r, 0, 0)),
        pl.BlockSpec((1, 1, length), lambda r, t: (r, 0, 0)),
    ]


def head_forward(turns, normed, bias, pairs, pieces, length):
    count, width = normed.shape
    columns = 3 * HD
    return call(
        forward_kernel,
        turns,
        count // length,
        [rows_block(width, length), pl.BlockSpec((1, columns), lambda r, t: (0, 0))]
        + pair_specs(length)
        + [whole(p) for p in pieces],
        [rows_block(columns, length), rows_block(HD, length), rows_block(1, length)],
        [like((count, columns)), like((count, HD)), like((count, 1), F32)],
        [normed, bias.reshape(1, columns)] + pairs + pieces,
        2 * count * (width * columns + 2 * length * HD),
    )


def head_backward(turns, grad, out_w, qkv, attended, lse, pairs, length):
    count, width = grad.shape
    columns = 3 * HD
    return call(
        functools.partial(backward_kernel, turns.shape[0]),
        turns,
        count // length,
        [
            rows_block(width, length),
            whole(out_w),
            rows_block(columns, length),
            rows_block(HD, length),
            rows_block(1, length),
        ]
        + pair_specs(length),
        [rows_block(columns, length), pl.BlockSpec((1, columns), lambda r, t: (0, 0))],
        [like((count, columns)), like((1, columns), F32)],
        [grad, out_w, qkv, attended, lse] + pairs,
        2 * count * (width * HD + 5 * length * HD),
    )


def finish_kernel(rows, with_norm, t_ref, x_ref, s_ref, o_ref, out_ref):
    depth = x_ref.shape[1] // rows
    term = s_ref[...].astype(F32)
    if with_norm:
        centred = x_ref[...].astype(F32)
        centred = centred - jnp.mean(centred, -1, keepdims=True)
        rstd = lax.rsqrt(jnp.mean(centred * centred, -1, keepdims=True) + EPSILON)
        centred = centred * rstd
        term = term - jnp.mean(term, -1, keepdims=True) - centred * jnp.mean(
            term * centred, -1, keepdims=True
        )
        field = o_ref[...].astype(F32) + rstd * term
    else:
        field = x_ref[...].astype(F32) + term + o_ref[4:5]
    for k in range(rows):
        at = pl.multiple_of(t_ref[k] * depth, LANES)
        out_ref[:, pl.ds(at, depth)] = field[:, k * depth : (k + 1) * depth].astype(BF)


def finish(turns, x, term, other, with_norm):
    return call(
        functools.partial(finish_kernel, turns.shape[0], with_norm),
        turns,
        1,
        [whole(v) for v in (x, term, other)],
        [whole(x)],
        [like(x.shape)],
        [x, term, other],
    )[0]


def shards(
    plan,
    tokens,
    attn_weights,
    mlp_weights,
    ln1_gain,
    ln1_bias,
    ln2_gain,
    ln2_bias,
    qkv_bias,
    dense_bias,
    up_bias,
    down_bias,
    doc_lengths,
    cotangent,
):
    row_count, shard_len, width = tokens.shape
    depth = attn_weights.shape[0]
    heads = width // HD
    rows, blks = plan.rows, plan.blks
    own_hidden = mlp_weights.shape[-1] // blks
    me = lax.axis_index("blk")
    length = shard_len * blks
    count = row_count * length
    head_of = me % plan.group // plan.share * plan.per_row + me // plan.group
    part = me % plan.share
    own_rows = row_count // plan.share
    row = lax.axis_index("row")
    turns = row ^ jnp.arange(rows, dtype=jnp.int32)
    places = me % plan.group ^ jnp.arange(plan.group, dtype=jnp.int32)

    def exchange(field):
        return lax.all_to_all(field, "blk", 0, 0)

    def collect(field):
        return exchange(field.reshape(blks, -1, field.shape[-1]))

    def gather_blocks(field):
        field = field.reshape(row_count, shard_len, width)
        return lax.all_gather(field, "blk", axis=1, tiled=True).reshape(count, width)

    def sum_blocks(field):
        field = field.reshape(row_count, length, width)
        field = lax.psum_scatter(field, "blk", scatter_dimension=1, tiled=True)
        return field.reshape(row_count * shard_len, width)

    zeros = jnp.zeros((3, width), F32)
    vectors = jnp.stack([ln1_gain, ln1_bias, ln2_gain, ln2_bias, dense_bias + down_bias])
    x_own, g_own, vectors, g_sum = turn_in(
        turns,
        tokens.reshape(row_count * shard_len, width),
        cotangent.reshape(row_count * shard_len, width),
        jnp.concatenate([vectors, zeros]),
    )
    qkv_send, out_own = split_attn(turns, attn_weights, plan, width)
    qkv_mine = exchange(qkv_send)
    out_send = pick(
        row ^ places // plan.share,
        [out_own] + [swap(out_own, "row", rows, k) for k in range(1, rows)],
        plan.group,
    )
    up_send, down_send = split_mlp(turns, after(mlp_weights, qkv_send), blks)
    qkv_mine, up_send, *out_send = lax.optimization_barrier((qkv_mine, up_send, *out_send))
    up_mine = exchange(up_send)
    qkv_pieces = gather_row(qkv_mine.reshape(-1, 3 * HD), plan)
    out_got = [out_send[0]] + [swap_group(out_send[j], plan, j) for j in range(1, plan.group)]
    up_mine, x_own, down_send, *qkv_pieces = lax.optimization_barrier(
        (up_mine, x_own, down_send, *qkv_pieces, *out_got)
    )[: 3 + rows]
    x_all = gather_blocks(x_own)
    down_mine = exchange(down_send)
    up_pieces = gather_row(up_mine.reshape(-1, own_hidden), plan)
    out_w = place(places, out_got)
    down_mine, g_own, *up_pieces = lax.optimization_barrier((down_mine, g_own, *up_pieces))
    g_all = gather_blocks(g_own)
    down_pieces = gather_row(down_mine.reshape(-1, own_hidden), plan)
    normed1, normed2 = norms(turns, x_all, vectors)

    lengths = lax.dynamic_slice_in_dim(doc_lengths, part * own_rows, own_rows, 0)
    doc_ends = jnp.cumsum(lengths, axis=-1)
    starts = doc_ends - lengths
    spots = jnp.arange(length, dtype=jnp.int32)
    doc_ids = jnp.sum((spots[None, :, None] >= doc_ends[:, None, :]).astype(jnp.int32), -1)
    picked = doc_ids[:, :, None] == jnp.arange(lengths.shape[-1], dtype=jnp.int32)
    positions = spots - jnp.sum(jnp.where(picked, starts[:, None, :], 0), -1)
    lane = jnp.arange(LANES)
    inverse = 10000.0 ** (-2.0 * (lane % (ROT // 2)).astype(F32) / ROT)
    angles = positions.astype(F32)[..., None] * inverse
    sine = jnp.sin(angles)
    pairs = [
        jnp.where(lane < ROT, jnp.cos(angles), 1.0),
        jnp.where(lane < ROT // 2, -sine, 0.0),
        jnp.where((lane >= ROT // 2) & (lane < ROT), sine, 0.0),
        doc_ids[:, :, None],
        doc_ids[:, None, :],
    ]

    def own(field):
        if plan.share == 1:
            return field
        return lax.dynamic_slice_in_dim(field, part * own_rows * length, own_rows * length, 0)

    def spread(field):
        if plan.share == 1:
            return field
        blank = jnp.zeros((count, field.shape[1]), field.dtype)
        return lax.dynamic_update_slice_in_dim(blank, field, part * own_rows * length, 0)

    up_b = lax.dynamic_slice_in_dim(up_bias, me * own_hidden, own_hidden)
    qkv_b = lax.dynamic_index_in_dim(qkv_bias.reshape(3, heads, HD), head_of, 1, keepdims=False)
    own_normed1 = own(normed1)
    qkv, attended, lse = head_forward(
        turns, own_normed1, qkv_b.reshape(-1), pairs, qkv_pieces, length
    )
    hidden, slope = feed_up(turns, after(normed2, attended), up_b, up_pieces)
    out_term = out_sum(turns, hidden, down_pieces, spread(attended), out_w)
    out_total = sum_blocks(out_term)

    g_all = after(g_all, out_term)
    down_g = weight_grad(turns, g_all, hidden)
    down_got = scatter_row(down_g, plan)
    own_grad = own(after(g_all, down_g[0]))
    out_g = out_grad(turns, places, attended, own_grad)
    out_got = [out_g[0]] + [swap_group(out_g[j], plan, j) for j in range(1, plan.group)]
    pre_grad, up_sum = feed_slope(turns, after(g_all, out_g[0]), slope, down_pieces)
    up_g, up_parts = weight_grad(turns, normed2, pre_grad, up_sum, up_pieces)
    qkv_grad, qkv_sum = head_backward(
        turns, after(own_grad, up_g[0]), out_w, qkv, attended, lse, pairs, length
    )
    down_total = add_pieces(turns, [after(down_g[0], qkv_grad, *out_got)] + down_got)
    down_back = collect(down_total)
    up_near = scatter_row([after(v, down_total) for v in up_g], plan, False)
    qkv_g, qkv_parts = weight_grad(
        turns, after(own_normed1, down_total), qkv_grad, qkv_sum, qkv_pieces
    )
    norm_term = norm_back(
        turns,
        after(pre_grad, qkv_g[0], out_total, *up_near),
        up_pieces,
        spread(qkv_grad),
        qkv_pieces,
        vectors,
    )
    up_got = up_near + scatter_row([after(v, *up_near) for v in up_g], plan, True)

    terms = [jnp.sum(after(v, norm_term), -1) for v in (qkv_parts, up_parts)]
    terms += [g_sum, qkv_sum, up_sum]
    terms = [v.reshape(-1) for v in terms]
    used = sum(v.size for v in terms)
    terms.append(jnp.zeros((-used % (8 * LANES),), F32))
    sums = jnp.concatenate(terms)
    sums = sums + sum(swap(sums, "row", rows, k) for k in range(1, rows))

    up_total = add_pieces(turns, [after(up_g[0], norm_term, down_back)] + up_got)
    norm_total = sum_blocks(norm_term)
    up_back = collect(up_total)
    qkv_got = scatter_row([after(v, up_total) for v in qkv_g], plan)
    sums = after(sums, up_total)
    sums = jnp.stack([sums, swap(sums, "blk", blks, 1)])
    holders = turns[:, None] * plan.share + jnp.arange(plan.share, dtype=jnp.int32)
    out_send = pick((me % plan.group ^ holders).reshape(-1), out_got, rows)
    layer_out = finish(turns, x_own, out_total, vectors, False)
    qkv_total = add_pieces(
        turns, [after(qkv_g[0], up_back, sums, out_send[0], layer_out)] + qkv_got
    )
    qkv_back = collect(qkv_total)
    out_back = out_send[0].astype(F32) + sum(
        swap(after(out_send[k], qkv_total), "row", rows, k).astype(F32) for k in range(1, rows)
    )
    sums = after(sums, qkv_total)
    sums = jnp.concatenate([sums] + [swap(sums, "blk", blks, k) for k in range(2, blks, 2)])
    sums = sums[me ^ jnp.arange(blks, dtype=jnp.int32)]
    gain1, bias1, gain2, bias2, g_total = jnp.split(
        jnp.sum(sums[:, : 5 * width], 0), 5
    )
    sums = sums[:, 5 * width : used]
    qkv_bias_grad = sums[:, : 3 * HD].reshape(plan.per_row, rows, plan.share, 3, HD)
    qkv_bias_grad = jnp.sum(qkv_bias_grad, 2).transpose(2, 1, 0, 3).reshape(-1)
    up_bias_grad = sums[:, 3 * HD :].reshape(-1)

    tokens_grad = finish(turns, x_own, norm_total, g_own, True)
    return (
        layer_out.reshape(tokens.shape),
        tokens_grad.reshape(tokens.shape),
        join_attn(turns, qkv_back, out_back, plan),
        join_mlp(turns, up_back, down_back),
        (gain1 - ln1_bias * bias1) / ln1_gain,
        bias1,
        (gain2 - ln2_bias * bias2) / ln2_gain,
        bias2,
        qkv_bias_grad,
        g_total,
        up_bias_grad,
        g_total,
    )


def solution(mesh):
    rows, blks = mesh.shape["row"], mesh.shape["blk"]
    vector = P()
    tokens = P("row", "blk", None)
    attn = P(("row", "blk"), None)
    mlp = P(("row", "blk"), None, None)

    def run(*arrays):
        plan = Plan(rows, blks, arrays[0].shape[-1] // HD)
        return jax.shard_map(
            functools.partial(shards, plan),
            mesh=mesh,
            in_specs=(tokens, attn, mlp) + (vector,) * 8 + (P("row", None), tokens),
            out_specs=(tokens, tokens, attn, mlp) + (vector,) * 8,
            check_vma=False,
        )(*arrays)

    return run
```

```python
import functools
import math

import jax
import jax.numpy as jnp
import numpy as np
from jax import lax
from jax.experimental import pallas as pl
from jax.experimental.pallas import tpu as pltpu
from jax.sharding import PartitionSpec as P

HD = 256
ROT = 64
LANES = 128
BLOCK = 256
EPSILON = 1e-05
MASKED = -1e30
BF = jnp.bfloat16
F32 = jnp.float32
COST = 100
VMEM_LIMIT = 56 * 2**20
SMALL = 16 * 2**20


class Plan:
    def __init__(self, rows, blks, heads):
        self.rows = rows
        self.blks = blks
        self.share = blks // heads
        self.per_row = heads // rows
        self.group = blks // self.per_row
        self.groups = [
            list(range(i * self.group, (i + 1) * self.group)) for i in range(self.per_row)
        ]


def after(field, *others):
    return lax.optimization_barrier((field,) + others)[0] if others else field


def swap(field, axis, size, bit):
    return lax.ppermute(field, axis, [(i, i ^ bit) for i in range(size)])


def swap_group(field, plan, bits):
    return lax.ppermute(field, "blk", [(i, i ^ bits) for i in range(plan.blks)])


def gather_row(own, plan):
    return [own] + [swap(own, "row", plan.rows, k) for k in range(1, plan.rows)]


def scatter_row(pieces, plan, far=None):
    return [
        swap(v, "row", plan.rows, k)
        for k, v in enumerate(pieces)
        if k and (far is None or far == (k & (k - 1) != 0))
    ]


def dot(left, right, left_dim, right_dim):
    return lax.dot_general(
        left, right, (((left_dim,), (right_dim,)), ((), ())), preferred_element_type=F32
    )


def whole(array):
    return pl.BlockSpec(array.shape, lambda *i: (0,) * len(array.shape))


def like(shape, kind=BF):
    return jax.ShapeDtypeStruct(shape, kind)


def call(body, turns, grid, in_specs, out_specs, out_shape, operands, flops=0, limit=None):
    moved = sum(v.size * v.dtype.itemsize for v in operands)
    moved += sum(math.prod(v.shape) * jnp.dtype(v.dtype).itemsize for v in out_shape)
    return pl.pallas_call(
        body,
        name=getattr(body, "func", body).__name__,
        grid_spec=pltpu.PrefetchScalarGridSpec(
            num_scalar_prefetch=1, grid=(grid,), in_specs=in_specs, out_specs=out_specs
        ),
        out_shape=out_shape,
        compiler_params=pltpu.CompilerParams(vmem_limit_bytes=limit or VMEM_LIMIT),
        cost_estimate=pl.CostEstimate(
            flops=flops // COST, bytes_accessed=moved // COST, transcendentals=0
        ),
    )(turns, *operands)


def rows_block(columns, block=BLOCK):
    return pl.BlockSpec((block, columns), lambda i, t: (i, 0))


def add_kernel(t_ref, *refs):
    refs[-1][...] = sum(ref[...].astype(F32) for ref in refs[:-1]).astype(BF)


def add_pieces(turns, terms):
    depth, width = terms[0].shape
    block = rows_block(width, depth // 4)
    shape = like((depth, width))
    return call(
        add_kernel, turns, 4, [block] * len(terms), [block], [shape], terms, limit=SMALL
    )[0]


def turn_kernel(t_ref, x_ref, g_ref, v_ref, xo_ref, go_ref, vo_ref, s_ref):
    xo_ref[...] = x_ref[...]
    go_ref[...] = g_ref[...]
    vo_ref[...] = v_ref[...]
    s_ref[...] = jnp.sum(g_ref[...].astype(F32), 0, keepdims=True)


def turn_in(turns, x, g, vectors):
    rows = turns.shape[0]
    part = x.shape[1] // rows

    def specs(array, turned):
        index = (lambda k, t: (0, t[k])) if turned else (lambda k, t: (0, k))
        return pl.BlockSpec((array.shape[0], part), index)

    total_shape = like((1, x.shape[1]), F32)
    return call(
        turn_kernel,
        turns,
        rows,
        [specs(v, True) for v in (x, g, vectors)],
        [specs(v, False) for v in (x, g, vectors)] + [specs(total_shape, True)],
        [like(v.shape, v.dtype) for v in (x, g, vectors)] + [total_shape],
        [x, g, vectors],
    )


def split_kernel(t_ref, w_ref, u_ref, d_ref):
    u_ref[0] = w_ref[:, 0, :]
    d_ref[0] = w_ref[:, 1, :]


def split_mlp(turns, weights, blks):
    depth, _, hidden = weights.shape
    part = hidden // blks
    block = pl.BlockSpec((1, depth, part), lambda b, t: (b, 0, 0))
    return call(
        split_kernel,
        turns,
        blks,
        [pl.BlockSpec((depth, 2, part), lambda b, t: (0, 0, b))],
        [block] * 2,
        [like((blks, depth, part))] * 2,
        [weights],
    )


def join_kernel(t_ref, u_ref, d_ref, o_ref):
    o_ref[:, 0, :] = u_ref[0].astype(F32)
    o_ref[:, 1, :] = d_ref[0].astype(F32)


def join_mlp(turns, up, down):
    blks, depth, part = up.shape
    block = pl.BlockSpec((1, depth, part), lambda b, t: (b, 0, 0))
    return call(
        join_kernel,
        turns,
        blks,
        [block] * 2,
        [pl.BlockSpec((depth, 2, part), lambda b, t: (0, 0, b))],
        [like((depth, 2, blks * part), F32)],
        [up, down],
    )[0]


def split_attn_kernel(plan, width, t_ref, w_ref, qkv_ref, out_ref):
    b = pl.program_id(0)
    head = b % plan.group // plan.share * plan.per_row + b // plan.group
    for i in range(3):
        at = pl.multiple_of(i * width + head * HD, HD)
        qkv_ref[0, :, i * HD : (i + 1) * HD] = w_ref[:, pl.ds(at, HD)]

    @pl.when(b == 0)
    def _():
        out_ref[...] = w_ref[:, 3 * width :]


def split_attn(turns, weights, plan, width):
    depth = weights.shape[0]
    return call(
        functools.partial(split_attn_kernel, plan, width),
        turns,
        plan.blks,
        [whole(weights)],
        [
            pl.BlockSpec((1, depth, 3 * HD), lambda b, t: (b, 0, 0)),
            pl.BlockSpec((depth, width), lambda b, t: (0, 0)),
        ],
        [like((plan.blks, depth, 3 * HD)), like((depth, width))],
        [weights],
        limit=SMALL,
    )


def join_attn_kernel(plan, t_ref, qkv_ref, out_ref, o_ref):
    step = pl.program_id(0)
    heads = o_ref.shape[1] // HD

    @pl.when(step < 3)
    def _():
        at = pl.ds(pl.multiple_of(step * HD, HD), HD)
        for h in range(heads):
            first = h % plan.per_row * plan.group + h // plan.per_row * plan.share
            o_ref[:, h * HD : (h + 1) * HD] = sum(
                qkv_ref[first + i, :, at].astype(F32) for i in range(plan.share)
            )

    @pl.when(step == 3)
    def _():
        o_ref[...] = out_ref[...]


def join_attn(turns, qkv, out, plan):
    depth, width = out.shape
    return call(
        functools.partial(join_attn_kernel, plan),
        turns,
        4,
        [whole(qkv), whole(out)],
        [pl.BlockSpec((depth, width), lambda j, t: (0, j))],
        [like((depth, 4 * width), F32)],
        [qkv, out],
    )[0]


def pick_kernel(count, t_ref, *refs):
    pieces, outs = refs[:count], refs[count:]
    share = t_ref.shape[0] // len(outs)
    for n, out in enumerate(outs):
        for i in range(share):
            for k, piece in enumerate(pieces):

                @pl.when(t_ref[n * share + i] == k)
                def _(i=i, out=out, piece=piece):
                    out[...] = piece[...] if i == 0 else out[...] + piece[...]


def pick(table, pieces, count):
    return call(
        functools.partial(pick_kernel, len(pieces)),
        table,
        1,
        [whole(p) for p in pieces],
        [whole(pieces[0])] * count,
        [like(pieces[0].shape)] * count,
        pieces,
    )


def place_kernel(t_ref, *refs):
    *pieces, out_ref = refs
    for k, piece in enumerate(pieces):
        depth = piece.shape[0]
        out_ref[pl.ds(pl.multiple_of(t_ref[k] * depth, depth), depth)] = piece[...]


def place(table, pieces):
    depth, width = pieces[0].shape
    shape = like((len(pieces) * depth, width))
    return call(place_kernel, table, 1, [whole(p) for p in pieces], [whole(shape)], [shape], pieces)[0]


def norm_kernel(t_ref, x_ref, v_ref, a1_ref, a2_ref):
    field = x_ref[...].astype(F32)
    centred = field - jnp.mean(field, -1, keepdims=True)
    standard = centred * lax.rsqrt(jnp.mean(centred * centred, -1, keepdims=True) + EPSILON)
    a1_ref[...] = (standard * v_ref[0:1] + v_ref[1:2]).astype(BF)
    a2_ref[...] = (standard * v_ref[2:3] + v_ref[3:4]).astype(BF)


def norms(turns, x, vectors):
    count, width = x.shape
    return call(
        norm_kernel,
        turns,
        count // BLOCK,
        [rows_block(width), whole(vectors)],
        [rows_block(width)] * 2,
        [like(x.shape)] * 2,
        [x, vectors],
        20 * count * width,
    )


def times_pieces(left, pieces):
    out, start = None, 0
    for piece in pieces:
        depth = piece.shape[0]
        term = dot(left[:, start : start + depth], piece[...], 1, 0)
        out = term if out is None else out + term
        start += depth
    return out


def up_kernel(t_ref, a_ref, b_ref, *refs):
    pieces, (h_ref, s_ref) = refs[:-2], refs[-2:]
    pre = times_pieces(a_ref[...], pieces) + b_ref[...]
    cdf = 0.5 * (1.0 + lax.erf(pre * math.sqrt(0.5)))
    h_ref[...] = (pre * cdf).astype(BF)
    s_ref[...] = cdf + pre * (jnp.exp(-0.5 * pre * pre) * (1.0 / math.sqrt(2.0 * math.pi)))


def feed_up(turns, normed, bias, pieces):
    count, width = normed.shape
    hidden = bias.shape[0]
    return call(
        up_kernel,
        turns,
        count // BLOCK,
        [rows_block(width), pl.BlockSpec((1, hidden), lambda i, t: (0, 0))]
        + [whole(p) for p in pieces],
        [rows_block(hidden)] * 2,
        [like((count, hidden)), like((count, hidden), F32)],
        [normed, bias.reshape(1, hidden)] + pieces,
        2 * count * width * hidden,
    )


def slope_kernel(t_ref, g_ref, s_ref, *refs):
    pieces, (p_ref, sum_ref) = refs[:-2], refs[-2:]

    @pl.when(pl.program_id(0) == 0)
    def _():
        sum_ref[...] = jnp.zeros_like(sum_ref)

    grad = (times_pieces(g_ref[...], pieces) * s_ref[...]).astype(BF)
    p_ref[...] = grad
    sum_ref[...] += jnp.sum(grad.astype(F32), 0, keepdims=True)


def feed_slope(turns, grad, slope, pieces):
    count, width = grad.shape
    hidden = slope.shape[1]
    return call(
        slope_kernel,
        turns,
        count // BLOCK,
        [rows_block(width), rows_block(hidden)] + [whole(p) for p in pieces],
        [rows_block(hidden), pl.BlockSpec((1, hidden), lambda i, t: (0, 0))],
        [like((count, hidden)), like((1, hidden), F32)],
        [grad, slope] + pieces,
        2 * count * width * hidden,
    )


def lane_sum(field):
    return sum(field[:, i : i + LANES] for i in range(0, field.shape[1], LANES))


def weight_kernel(rows, with_sums, t_ref, l_ref, r_ref, *refs):
    step = pl.program_id(0)
    if with_sums:
        sum_ref, pieces, refs = refs[0], refs[1 : 1 + rows], refs[1 + rows :]
        parts_ref = refs[-1]
    grad = dot(l_ref[...], r_ref[...], 0, 0)
    for k in range(rows):

        @pl.when(step == k)
        def _(k=k):
            refs[k][...] = grad.astype(BF)
            if with_sums:
                piece = pieces[k][...].astype(F32)
                parts_ref[0] = lane_sum(piece * grad)
                parts_ref[1] = lane_sum(piece * sum_ref[...])


def weight_grad(turns, left, right, sums=None, pieces=()):
    rows = turns.shape[0]
    count, width = left.shape
    columns = right.shape[1]
    depth = width // rows
    out_shape = [like((depth, columns))] * rows
    out_specs = [whole(v) for v in out_shape]
    operands = [left, right]
    if pieces:
        operands += [sums] + pieces
        out_shape.append(like((2, width, LANES), F32))
        out_specs.append(pl.BlockSpec((2, depth, LANES), lambda k, t: (0, t[k], 0)))
    out = call(
        functools.partial(weight_kernel, rows, bool(pieces)),
        turns,
        rows,
        [pl.BlockSpec((count, depth), lambda k, t: (0, k))] + [whole(v) for v in operands[1:]],
        out_specs,
        out_shape,
        operands,
        2 * count * width * columns,
    )
    if pieces:
        return out[:-1], out[-1]
    return out


def out_kernel(rows, t_ref, o_ref, g_ref, *refs):
    *outs, grad_ref = refs
    depth = outs[0].shape[0]
    grad_ref[...] = dot(o_ref[...], g_ref[...], 0, 0)
    for j, out in enumerate(outs):
        at = pl.multiple_of(t_ref[rows + j] * depth, depth)
        out[...] = grad_ref[pl.ds(at, depth)].astype(BF)


def out_grad(turns, places, attended, grad):
    rows, group = turns.shape[0], places.shape[0]
    count, width = grad.shape
    part = width // rows
    depth = HD // group
    return pl.pallas_call(
        functools.partial(out_kernel, rows),
        name="out_kernel",
        grid_spec=pltpu.PrefetchScalarGridSpec(
            num_scalar_prefetch=1,
            grid=(rows,),
            in_specs=[whole(attended), pl.BlockSpec((count, part), lambda k, t: (0, k))],
            out_specs=[pl.BlockSpec((depth, part), lambda k, t: (0, t[k]))] * group,
            scratch_shapes=[pltpu.VMEM((HD, part), F32)],
        ),
        out_shape=[like((depth, width))] * group,
        compiler_params=pltpu.CompilerParams(vmem_limit_bytes=VMEM_LIMIT),
        cost_estimate=pl.CostEstimate(
            flops=2 * count * width * HD // COST,
            bytes_accessed=2 * (count * (width + HD) + width * HD) // COST,
            transcendentals=0,
        ),
    )(jnp.concatenate([turns, places]), attended, grad)


def turned_columns(t_ref, w_ref, k, depth):
    return w_ref[:, pl.ds(pl.multiple_of(t_ref[k] * depth, LANES), depth)]


def sum_kernel(t_ref, h_ref, o_ref, w_ref, *refs):
    pieces, y_ref = refs[:-1], refs[-1]
    for k, piece in enumerate(pieces):
        depth = piece.shape[0]
        term = dot(h_ref[...], piece[...], 1, 1)
        term += dot(o_ref[...], turned_columns(t_ref, w_ref, k, depth), 1, 0)
        y_ref[:, k * depth : (k + 1) * depth] = term.astype(BF)


def out_sum(turns, hidden, pieces, attended, out_w):
    count = hidden.shape[0]
    width = out_w.shape[1]
    return call(
        sum_kernel,
        turns,
        count // BLOCK,
        [rows_block(hidden.shape[1]), rows_block(HD), whole(out_w)] + [whole(p) for p in pieces],
        [rows_block(width)],
        [like((count, width))],
        [hidden, attended, out_w] + pieces,
        2 * count * width * (hidden.shape[1] + HD),
    )[0]


def back_kernel(t_ref, p_ref, q_ref, v_ref, *refs):
    pieces, c_ref = refs[:-1], refs[-1]
    count = len(pieces) // 2
    for k, (up, qkv) in enumerate(zip(pieces[:count], pieces[count:])):
        depth = up.shape[0]
        cols = slice(k * depth, (k + 1) * depth)
        term = dot(p_ref[...], up[...], 1, 1) * v_ref[2:3, cols]
        term += dot(q_ref[...], qkv[...], 1, 1) * v_ref[0:1, cols]
        c_ref[:, cols] = term.astype(BF)


def norm_back(turns, pre_grad, up_pieces, qkv_grad, qkv_pieces, vectors):
    count = pre_grad.shape[0]
    width = vectors.shape[1]
    columns = pre_grad.shape[1] + qkv_grad.shape[1]
    return call(
        back_kernel,
        turns,
        count // BLOCK,
        [rows_block(pre_grad.shape[1]), rows_block(qkv_grad.shape[1]), whole(vectors)]
        + [whole(p) for p in up_pieces + qkv_pieces],
        [rows_block(width)],
        [like((count, width))],
        [pre_grad, qkv_grad, vectors] + up_pieces + qkv_pieces,
        2 * count * width * columns,
    )[0]


def turned(field, cosine, minus, plus):
    head = field[:, :LANES]
    half = ROT // 2
    head = (
        head * cosine
        + pltpu.roll(head, LANES - half, 1) * minus
        + pltpu.roll(head, half, 1) * plus
    )
    return jnp.concatenate([head, field[:, LANES:]], 1)


def allowed_pairs(length, dq_ref, dk_ref):
    spot = lax.broadcasted_iota(jnp.int32, (length, length), 0)
    other = lax.broadcasted_iota(jnp.int32, (length, length), 1)
    return (dq_ref[0] == dk_ref[0]) & (other <= spot)


def forward_kernel(t_ref, a_ref, b_ref, c_ref, m_ref, p_ref, dq_ref, dk_ref, *refs):
    pieces, (qkv_ref, o_ref, lse_ref) = refs[:-3], refs[-3:]
    qkv = times_pieces(a_ref[...], pieces) + b_ref[...]
    tables = c_ref[0], m_ref[0], p_ref[0]
    queries = (turned(qkv[:, :HD], *tables) * HD ** (-0.5)).astype(BF)
    keys = turned(qkv[:, HD : 2 * HD], *tables).astype(BF)
    values = qkv[:, 2 * HD :].astype(BF)
    for i, field in enumerate((queries, keys, values)):
        qkv_ref[:, i * HD : (i + 1) * HD] = field
    allowed = allowed_pairs(a_ref.shape[0], dq_ref, dk_ref)
    scores = jnp.where(allowed, dot(queries, keys, 1, 1), MASKED)
    largest = jnp.max(scores, -1, keepdims=True)
    weights = jnp.where(allowed, jnp.exp(scores - largest), 0.0)
    mass = jnp.sum(weights, -1, keepdims=True)
    o_ref[...] = dot((weights / mass).astype(BF), values, 1, 0).astype(BF)
    lse_ref[...] = largest + jnp.log(mass)


def backward_kernel(
    parts, t_ref, g_ref, w_ref, qkv_ref, o_ref, lse_ref, c_ref, m_ref, p_ref, dq_ref, dk_ref,
    grad_ref, sum_ref,
):
    queries, keys, values = (qkv_ref[:, i * HD : (i + 1) * HD] for i in range(3))
    tables = c_ref[0], -m_ref[0], -p_ref[0]
    depth = w_ref.shape[1] // parts
    heads_grad = None
    for k in range(parts):
        cols = slice(k * depth, (k + 1) * depth)
        term = dot(g_ref[:, cols], turned_columns(t_ref, w_ref, k, depth), 1, 1)
        heads_grad = term if heads_grad is None else heads_grad + term
    heads_grad = heads_grad.astype(BF)
    allowed = allowed_pairs(g_ref.shape[0], dq_ref, dk_ref)
    scores = jnp.where(allowed, dot(queries, keys, 1, 1), MASKED)
    weights = jnp.where(allowed, jnp.exp(scores - lse_ref[...]), 0.0)
    deltas = jnp.sum(heads_grad.astype(F32) * o_ref[...].astype(F32), -1, keepdims=True)
    score_grad = (weights * (dot(heads_grad, values, 1, 1) - deltas)).astype(BF)
    query_grad = dot(score_grad, keys, 1, 0) * HD ** (-0.5)
    key_grad = dot(score_grad, queries, 0, 0)
    value_grad = dot(weights.astype(BF), heads_grad, 0, 0)
    fields = turned(query_grad, *tables), turned(key_grad, *tables), value_grad

    @pl.when(pl.program_id(0) == 0)
    def _():
        sum_ref[...] = jnp.zeros_like(sum_ref)

    for i, field in enumerate(fields):
        field = field.astype(BF)
        cols = slice(i * HD, (i + 1) * HD)
        grad_ref[:, cols] = field
        sum_ref[:, cols] += jnp.sum(field.astype(F32), 0, keepdims=True)


def pair_specs(length):
    table = pl.BlockSpec((1, length, LANES), lambda r, t: (r, 0, 0))
    return [table] * 3 + [
        pl.BlockSpec((1, length, 1), lambda r, t: (r, 0, 0)),
        pl.BlockSpec((1, 1, length), lambda r, t: (r, 0, 0)),
    ]


def head_forward(turns, normed, bias, pairs, pieces, length):
    count, width = normed.shape
    columns = 3 * HD
    return call(
        forward_kernel,
        turns,
        count // length,
        [rows_block(width, length), pl.BlockSpec((1, columns), lambda r, t: (0, 0))]
        + pair_specs(length)
        + [whole(p) for p in pieces],
        [rows_block(columns, length), rows_block(HD, length), rows_block(1, length)],
        [like((count, columns)), like((count, HD)), like((count, 1), F32)],
        [normed, bias.reshape(1, columns)] + pairs + pieces,
        2 * count * (width * columns + 2 * length * HD),
    )


def head_backward(turns, grad, out_w, qkv, attended, lse, pairs, length):
    count, width = grad.shape
    columns = 3 * HD
    return call(
        functools.partial(backward_kernel, turns.shape[0]),
        turns,
        count // length,
        [
            rows_block(width, length),
            whole(out_w),
            rows_block(columns, length),
            rows_block(HD, length),
            rows_block(1, length),
        ]
        + pair_specs(length),
        [rows_block(columns, length), pl.BlockSpec((1, columns), lambda r, t: (0, 0))],
        [like((count, columns)), like((1, columns), F32)],
        [grad, out_w, qkv, attended, lse] + pairs,
        2 * count * (width * HD + 5 * length * HD),
    )


def finish_kernel(rows, with_norm, t_ref, x_ref, s_ref, o_ref, out_ref):
    depth = x_ref.shape[1] // rows
    term = s_ref[...].astype(F32)
    if with_norm:
        centred = x_ref[...].astype(F32)
        centred = centred - jnp.mean(centred, -1, keepdims=True)
        rstd = lax.rsqrt(jnp.mean(centred * centred, -1, keepdims=True) + EPSILON)
        centred = centred * rstd
        term = term - jnp.mean(term, -1, keepdims=True) - centred * jnp.mean(
            term * centred, -1, keepdims=True
        )
        field = o_ref[...].astype(F32) + rstd * term
    else:
        field = x_ref[...].astype(F32) + term + o_ref[4:5]
    for k in range(rows):
        at = pl.multiple_of(t_ref[k] * depth, LANES)
        out_ref[:, pl.ds(at, depth)] = field[:, k * depth : (k + 1) * depth].astype(BF)


def finish(turns, x, term, other, with_norm):
    return call(
        functools.partial(finish_kernel, turns.shape[0], with_norm),
        turns,
        1,
        [whole(v) for v in (x, term, other)],
        [whole(x)],
        [like(x.shape)],
        [x, term, other],
    )[0]


def shards(
    plan,
    tokens,
    attn_weights,
    mlp_weights,
    ln1_gain,
    ln1_bias,
    ln2_gain,
    ln2_bias,
    qkv_bias,
    dense_bias,
    up_bias,
    down_bias,
    doc_lengths,
    cotangent,
):
    row_count, shard_len, width = tokens.shape
    depth = attn_weights.shape[0]
    heads = width // HD
    rows, blks = plan.rows, plan.blks
    own_hidden = mlp_weights.shape[-1] // blks
    me = lax.axis_index("blk")
    length = shard_len * blks
    count = row_count * length
    head_of = me % plan.group // plan.share * plan.per_row + me // plan.group
    part = me % plan.share
    own_rows = row_count // plan.share
    row = lax.axis_index("row")
    turns = row ^ jnp.arange(rows, dtype=jnp.int32)
    places = me % plan.group ^ jnp.arange(plan.group, dtype=jnp.int32)

    def exchange(field):
        return lax.all_to_all(field, "blk", 0, 0)

    def collect(field):
        return exchange(field.reshape(blks, -1, field.shape[-1]))

    def gather_blocks(field):
        field = field.reshape(row_count, shard_len, width)
        return lax.all_gather(field, "blk", axis=1, tiled=True).reshape(count, width)

    def sum_blocks(field):
        field = field.reshape(row_count, length, width)
        field = lax.psum_scatter(field, "blk", scatter_dimension=1, tiled=True)
        return field.reshape(row_count * shard_len, width)

    zeros = jnp.zeros((3, width), F32)
    vectors = jnp.stack([ln1_gain, ln1_bias, ln2_gain, ln2_bias, dense_bias + down_bias])
    x_own, g_own, vectors, g_sum = turn_in(
        turns,
        tokens.reshape(row_count * shard_len, width),
        cotangent.reshape(row_count * shard_len, width),
        jnp.concatenate([vectors, zeros]),
    )
    qkv_send, out_own = split_attn(turns, attn_weights, plan, width)
    qkv_mine = exchange(qkv_send)
    out_send = pick(
        row ^ places // plan.share,
        [out_own] + [swap(out_own, "row", rows, k) for k in range(1, rows)],
        plan.group,
    )
    up_send, down_send = split_mlp(turns, after(mlp_weights, qkv_send), blks)
    qkv_mine, up_send, *out_send = lax.optimization_barrier((qkv_mine, up_send, *out_send))
    up_mine = exchange(up_send)
    qkv_pieces = gather_row(qkv_mine.reshape(-1, 3 * HD), plan)
    out_got = [out_send[0]] + [swap_group(out_send[j], plan, j) for j in range(1, plan.group)]
    up_mine, x_own, down_send, *qkv_pieces = lax.optimization_barrier(
        (up_mine, x_own, down_send, *qkv_pieces, *out_got)
    )[: 3 + rows]
    x_all = gather_blocks(x_own)
    down_mine = exchange(down_send)
    up_pieces = gather_row(up_mine.reshape(-1, own_hidden), plan)
    out_w = place(places, out_got)
    down_mine, g_own, *up_pieces = lax.optimization_barrier((down_mine, g_own, *up_pieces))
    g_all = gather_blocks(g_own)
    down_pieces = gather_row(down_mine.reshape(-1, own_hidden), plan)
    normed1, normed2 = norms(turns, x_all, vectors)

    lengths = lax.dynamic_slice_in_dim(doc_lengths, part * own_rows, own_rows, 0)
    doc_ends = jnp.cumsum(lengths, axis=-1)
    starts = doc_ends - lengths
    spots = jnp.arange(length, dtype=jnp.int32)
    doc_ids = jnp.sum((spots[None, :, None] >= doc_ends[:, None, :]).astype(jnp.int32), -1)
    picked = doc_ids[:, :, None] == jnp.arange(lengths.shape[-1], dtype=jnp.int32)
    positions = spots - jnp.sum(jnp.where(picked, starts[:, None, :], 0), -1)
    lane = jnp.arange(LANES)
    inverse = 10000.0 ** (-2.0 * (lane % (ROT // 2)).astype(F32) / ROT)
    angles = positions.astype(F32)[..., None] * inverse
    sine = jnp.sin(angles)
    pairs = [
        jnp.where(lane < ROT, jnp.cos(angles), 1.0),
        jnp.where(lane < ROT // 2, -sine, 0.0),
        jnp.where((lane >= ROT // 2) & (lane < ROT), sine, 0.0),
        doc_ids[:, :, None],
        doc_ids[:, None, :],
    ]

    def own(field):
        if plan.share == 1:
            return field
        return lax.dynamic_slice_in_dim(field, part * own_rows * length, own_rows * length, 0)

    def spread(field):
        if plan.share == 1:
            return field
        blank = jnp.zeros((count, field.shape[1]), field.dtype)
        return lax.dynamic_update_slice_in_dim(blank, field, part * own_rows * length, 0)

    up_b = lax.dynamic_slice_in_dim(up_bias, me * own_hidden, own_hidden)
    qkv_b = lax.dynamic_index_in_dim(qkv_bias.reshape(3, heads, HD), head_of, 1, keepdims=False)
    own_normed1 = own(normed1)
    qkv, attended, lse = head_forward(
        turns, own_normed1, qkv_b.reshape(-1), pairs, qkv_pieces, length
    )
    hidden, slope = feed_up(turns, after(normed2, attended), up_b, up_pieces)
    out_term = out_sum(turns, hidden, down_pieces, spread(attended), out_w)
    out_total = sum_blocks(out_term)

    g_all = after(g_all, out_term)
    down_g = weight_grad(turns, g_all, hidden)
    down_got = scatter_row(down_g, plan)
    own_grad = own(after(g_all, down_g[0]))
    out_g = out_grad(turns, places, attended, own_grad)
    out_got = [out_g[0]] + [swap_group(out_g[j], plan, j) for j in range(1, plan.group)]
    pre_grad, up_sum = feed_slope(turns, after(g_all, out_g[0]), slope, down_pieces)
    up_g, up_parts = weight_grad(turns, normed2, pre_grad, up_sum, up_pieces)
    qkv_grad, qkv_sum = head_backward(
        turns, after(own_grad, up_g[0]), out_w, qkv, attended, lse, pairs, length
    )
    down_total = add_pieces(turns, [after(down_g[0], qkv_grad, *out_got)] + down_got)
    down_back = collect(down_total)
    up_near = scatter_row([after(v, down_total) for v in up_g], plan, False)
    qkv_g, qkv_parts = weight_grad(
        turns, after(own_normed1, down_total), qkv_grad, qkv_sum, qkv_pieces
    )
    holders = turns[:, None] * plan.share + jnp.arange(plan.share, dtype=jnp.int32)
    out_send = pick((me % plan.group ^ holders).reshape(-1), out_got, rows)
    layer_out = finish(turns, x_own, out_total, vectors, False)
    norm_term = norm_back(
        turns,
        after(pre_grad, qkv_g[0], down_back, out_send[0], layer_out, *up_near),
        up_pieces,
        spread(qkv_grad),
        qkv_pieces,
        vectors,
    )
    up_got = up_near + scatter_row([after(v, qkv_g[0], *up_near) for v in up_g], plan, True)

    terms = [jnp.sum(after(v, norm_term), -1) for v in (qkv_parts, up_parts)]
    terms += [g_sum, qkv_sum, up_sum]
    terms = [v.reshape(-1) for v in terms]
    used = sum(v.size for v in terms)
    terms.append(jnp.zeros((-used % (8 * LANES),), F32))
    sums = jnp.concatenate(terms)
    sums = sums + sum(swap(sums, "row", rows, k) for k in range(1, rows))

    up_total = add_pieces(
        turns, [after(up_g[0], norm_term)] + up_got
    )
    norm_total = sum_blocks(after(norm_term, up_total))
    up_back = collect(up_total)
    qkv_got = scatter_row([after(v, up_total) for v in qkv_g], plan)
    sums = after(sums, up_total)
    sums = jnp.stack([sums, swap(sums, "blk", blks, 1)])
    qkv_total = add_pieces(turns, [after(qkv_g[0], up_back, sums)] + qkv_got)
    qkv_back = collect(qkv_total)
    out_back = out_send[0].astype(F32) + sum(
        swap(after(out_send[k], qkv_total), "row", rows, k).astype(F32) for k in range(1, rows)
    )
    sums = after(sums, qkv_total)
    sums = jnp.concatenate([sums] + [swap(sums, "blk", blks, k) for k in range(2, blks, 2)])
    sums = sums[me ^ jnp.arange(blks, dtype=jnp.int32)]
    gain1, bias1, gain2, bias2, g_total = jnp.split(
        jnp.sum(sums[:, : 5 * width], 0), 5
    )
    sums = sums[:, 5 * width : used]
    qkv_bias_grad = sums[:, : 3 * HD].reshape(plan.per_row, rows, plan.share, 3, HD)
    qkv_bias_grad = jnp.sum(qkv_bias_grad, 2).transpose(2, 1, 0, 3).reshape(-1)
    up_bias_grad = sums[:, 3 * HD :].reshape(-1)

    tokens_grad = finish(turns, x_own, norm_total, g_own, True)
    return (
        layer_out.reshape(tokens.shape),
        tokens_grad.reshape(tokens.shape),
        join_attn(turns, qkv_back, out_back, plan),
        join_mlp(turns, up_back, down_back),
        (gain1 - ln1_bias * bias1) / ln1_gain,
        bias1,
        (gain2 - ln2_bias * bias2) / ln2_gain,
        bias2,
        qkv_bias_grad,
        g_total,
        up_bias_grad,
        g_total,
    )


def solution(mesh):
    rows, blks = mesh.shape["row"], mesh.shape["blk"]
    vector = P()
    tokens = P("row", "blk", None)
    attn = P(("row", "blk"), None)
    mlp = P(("row", "blk"), None, None)

    def run(*arrays):
        plan = Plan(rows, blks, arrays[0].shape[-1] // HD)
        return jax.shard_map(
            functools.partial(shards, plan),
            mesh=mesh,
            in_specs=(tokens, attn, mlp) + (vector,) * 8 + (P("row", None), tokens),
            out_specs=(tokens, tokens, attn, mlp) + (vector,) * 8,
            check_vma=False,
        )(*arrays)

    return run
```

```python
import functools
import math

import jax
import jax.numpy as jnp
import numpy as np
from jax import lax
from jax.experimental import pallas as pl
from jax.experimental.pallas import tpu as pltpu
from jax.sharding import PartitionSpec as P

HD = 256
ROT = 64
LANES = 128
BLOCK = 256
EPSILON = 1e-05
MASKED = -1e30
BF = jnp.bfloat16
F32 = jnp.float32
COST = 100
VMEM_LIMIT = 56 * 2**20
SMALL = 16 * 2**20


class Plan:
    def __init__(self, rows, blks, heads):
        self.rows = rows
        self.blks = blks
        self.share = blks // heads
        self.per_row = heads // rows
        self.group = blks // self.per_row
        self.groups = [
            list(range(i * self.group, (i + 1) * self.group)) for i in range(self.per_row)
        ]


def after(field, *others):
    return lax.optimization_barrier((field,) + others)[0] if others else field


def swap(field, axis, size, bit):
    return lax.ppermute(field, axis, [(i, i ^ bit) for i in range(size)])


def swap_group(field, plan, bits):
    return lax.ppermute(field, "blk", [(i, i ^ bits) for i in range(plan.blks)])


def gather_row(own, plan):
    return [own] + [swap(own, "row", plan.rows, k) for k in range(1, plan.rows)]


def scatter_row(pieces, plan, far=None):
    return [
        swap(v, "row", plan.rows, k)
        for k, v in enumerate(pieces)
        if k and (far is None or far == (k & (k - 1) != 0))
    ]


def dot(left, right, left_dim, right_dim):
    return lax.dot_general(
        left, right, (((left_dim,), (right_dim,)), ((), ())), preferred_element_type=F32
    )


def whole(array):
    return pl.BlockSpec(array.shape, lambda *i: (0,) * len(array.shape))


def like(shape, kind=BF):
    return jax.ShapeDtypeStruct(shape, kind)


def call(body, turns, grid, in_specs, out_specs, out_shape, operands, flops=0, limit=None):
    moved = sum(v.size * v.dtype.itemsize for v in operands)
    moved += sum(math.prod(v.shape) * jnp.dtype(v.dtype).itemsize for v in out_shape)
    return pl.pallas_call(
        body,
        name=getattr(body, "func", body).__name__,
        grid_spec=pltpu.PrefetchScalarGridSpec(
            num_scalar_prefetch=1, grid=(grid,), in_specs=in_specs, out_specs=out_specs
        ),
        out_shape=out_shape,
        compiler_params=pltpu.CompilerParams(vmem_limit_bytes=limit or VMEM_LIMIT),
        cost_estimate=pl.CostEstimate(
            flops=flops // COST, bytes_accessed=moved // COST, transcendentals=0
        ),
    )(turns, *operands)


def rows_block(columns, block=BLOCK):
    return pl.BlockSpec((block, columns), lambda i, t: (i, 0))


def add_kernel(t_ref, *refs):
    refs[-1][...] = sum(ref[...].astype(F32) for ref in refs[:-1]).astype(BF)


def add_pieces(turns, terms):
    depth, width = terms[0].shape
    block = rows_block(width, depth // 4)
    shape = like((depth, width))
    return call(
        add_kernel, turns, 4, [block] * len(terms), [block], [shape], terms, limit=SMALL
    )[0]


def turn_kernel(t_ref, x_ref, g_ref, v_ref, xo_ref, go_ref, vo_ref, s_ref):
    xo_ref[...] = x_ref[...]
    go_ref[...] = g_ref[...]
    vo_ref[...] = v_ref[...]
    s_ref[...] = jnp.sum(g_ref[...].astype(F32), 0, keepdims=True)


def turn_in(turns, x, g, vectors):
    rows = turns.shape[0]
    part = x.shape[1] // rows

    def specs(array, turned):
        index = (lambda k, t: (0, t[k])) if turned else (lambda k, t: (0, k))
        return pl.BlockSpec((array.shape[0], part), index)

    total_shape = like((1, x.shape[1]), F32)
    return call(
        turn_kernel,
        turns,
        rows,
        [specs(v, True) for v in (x, g, vectors)],
        [specs(v, False) for v in (x, g, vectors)] + [specs(total_shape, True)],
        [like(v.shape, v.dtype) for v in (x, g, vectors)] + [total_shape],
        [x, g, vectors],
    )


def split_kernel(t_ref, w_ref, u_ref, d_ref):
    u_ref[0] = w_ref[:, 0, :]
    d_ref[0] = w_ref[:, 1, :]


def split_mlp(turns, weights, blks):
    depth, _, hidden = weights.shape
    part = hidden // blks
    block = pl.BlockSpec((1, depth, part), lambda b, t: (b, 0, 0))
    return call(
        split_kernel,
        turns,
        blks,
        [pl.BlockSpec((depth, 2, part), lambda b, t: (0, 0, b))],
        [block] * 2,
        [like((blks, depth, part))] * 2,
        [weights],
    )


def join_kernel(t_ref, u_ref, d_ref, o_ref):
    o_ref[:, 0, :] = u_ref[0].astype(F32)
    o_ref[:, 1, :] = d_ref[0].astype(F32)


def join_mlp(turns, up, down):
    blks, depth, part = up.shape
    block = pl.BlockSpec((1, depth, part), lambda b, t: (b, 0, 0))
    return call(
        join_kernel,
        turns,
        blks,
        [block] * 2,
        [pl.BlockSpec((depth, 2, part), lambda b, t: (0, 0, b))],
        [like((depth, 2, blks * part), F32)],
        [up, down],
    )[0]


def split_attn_kernel(plan, width, t_ref, w_ref, qkv_ref, out_ref):
    b = pl.program_id(0)
    head = b % plan.group // plan.share * plan.per_row + b // plan.group
    for i in range(3):
        at = pl.multiple_of(i * width + head * HD, HD)
        qkv_ref[0, :, i * HD : (i + 1) * HD] = w_ref[:, pl.ds(at, HD)]

    @pl.when(b == 0)
    def _():
        out_ref[...] = w_ref[:, 3 * width :]


def split_attn(turns, weights, plan, width):
    depth = weights.shape[0]
    return call(
        functools.partial(split_attn_kernel, plan, width),
        turns,
        plan.blks,
        [whole(weights)],
        [
            pl.BlockSpec((1, depth, 3 * HD), lambda b, t: (b, 0, 0)),
            pl.BlockSpec((depth, width), lambda b, t: (0, 0)),
        ],
        [like((plan.blks, depth, 3 * HD)), like((depth, width))],
        [weights],
        limit=SMALL,
    )


def join_attn_kernel(plan, t_ref, qkv_ref, out_ref, o_ref):
    step = pl.program_id(0)
    heads = o_ref.shape[1] // HD

    @pl.when(step < 3)
    def _():
        at = pl.ds(pl.multiple_of(step * HD, HD), HD)
        for h in range(heads):
            first = h % plan.per_row * plan.group + h // plan.per_row * plan.share
            o_ref[:, h * HD : (h + 1) * HD] = sum(
                qkv_ref[first + i, :, at].astype(F32) for i in range(plan.share)
            )

    @pl.when(step == 3)
    def _():
        o_ref[...] = out_ref[...]


def join_attn(turns, qkv, out, plan):
    depth, width = out.shape
    return call(
        functools.partial(join_attn_kernel, plan),
        turns,
        4,
        [whole(qkv), whole(out)],
        [pl.BlockSpec((depth, width), lambda j, t: (0, j))],
        [like((depth, 4 * width), F32)],
        [qkv, out],
    )[0]


def pick_kernel(count, t_ref, *refs):
    pieces, outs = refs[:count], refs[count:]
    share = t_ref.shape[0] // len(outs)
    for n, out in enumerate(outs):
        for i in range(share):
            for k, piece in enumerate(pieces):

                @pl.when(t_ref[n * share + i] == k)
                def _(i=i, out=out, piece=piece):
                    out[...] = piece[...] if i == 0 else out[...] + piece[...]


def pick(table, pieces, count):
    return call(
        functools.partial(pick_kernel, len(pieces)),
        table,
        1,
        [whole(p) for p in pieces],
        [whole(pieces[0])] * count,
        [like(pieces[0].shape)] * count,
        pieces,
    )


def place_kernel(t_ref, *refs):
    *pieces, out_ref = refs
    for k, piece in enumerate(pieces):
        depth = piece.shape[0]
        out_ref[pl.ds(pl.multiple_of(t_ref[k] * depth, depth), depth)] = piece[...]


def place(table, pieces):
    depth, width = pieces[0].shape
    shape = like((len(pieces) * depth, width))
    return call(place_kernel, table, 1, [whole(p) for p in pieces], [whole(shape)], [shape], pieces)[0]


def norm_kernel(t_ref, x_ref, v_ref, a1_ref, a2_ref):
    field = x_ref[...].astype(F32)
    centred = field - jnp.mean(field, -1, keepdims=True)
    standard = centred * lax.rsqrt(jnp.mean(centred * centred, -1, keepdims=True) + EPSILON)
    a1_ref[...] = (standard * v_ref[0:1] + v_ref[1:2]).astype(BF)
    a2_ref[...] = (standard * v_ref[2:3] + v_ref[3:4]).astype(BF)


def norms(turns, x, vectors):
    count, width = x.shape
    return call(
        norm_kernel,
        turns,
        count // BLOCK,
        [rows_block(width), whole(vectors)],
        [rows_block(width)] * 2,
        [like(x.shape)] * 2,
        [x, vectors],
        20 * count * width,
    )


def times_pieces(left, pieces):
    out, start = None, 0
    for piece in pieces:
        depth = piece.shape[0]
        term = dot(left[:, start : start + depth], piece[...], 1, 0)
        out = term if out is None else out + term
        start += depth
    return out


def up_kernel(t_ref, a_ref, b_ref, *refs):
    pieces, (h_ref, s_ref) = refs[:-2], refs[-2:]
    pre = times_pieces(a_ref[...], pieces) + b_ref[...]
    cdf = 0.5 * (1.0 + lax.erf(pre * math.sqrt(0.5)))
    h_ref[...] = (pre * cdf).astype(BF)
    s_ref[...] = cdf + pre * (jnp.exp(-0.5 * pre * pre) * (1.0 / math.sqrt(2.0 * math.pi)))


def feed_up(turns, normed, bias, pieces):
    count, width = normed.shape
    hidden = bias.shape[0]
    return call(
        up_kernel,
        turns,
        count // BLOCK,
        [rows_block(width), pl.BlockSpec((1, hidden), lambda i, t: (0, 0))]
        + [whole(p) for p in pieces],
        [rows_block(hidden)] * 2,
        [like((count, hidden)), like((count, hidden), F32)],
        [normed, bias.reshape(1, hidden)] + pieces,
        2 * count * width * hidden,
    )


def slope_kernel(t_ref, g_ref, s_ref, *refs):
    pieces, (p_ref, sum_ref) = refs[:-2], refs[-2:]

    @pl.when(pl.program_id(0) == 0)
    def _():
        sum_ref[...] = jnp.zeros_like(sum_ref)

    grad = (times_pieces(g_ref[...], pieces) * s_ref[...]).astype(BF)
    p_ref[...] = grad
    sum_ref[...] += jnp.sum(grad.astype(F32), 0, keepdims=True)


def feed_slope(turns, grad, slope, pieces):
    count, width = grad.shape
    hidden = slope.shape[1]
    return call(
        slope_kernel,
        turns,
        count // BLOCK,
        [rows_block(width), rows_block(hidden)] + [whole(p) for p in pieces],
        [rows_block(hidden), pl.BlockSpec((1, hidden), lambda i, t: (0, 0))],
        [like((count, hidden)), like((1, hidden), F32)],
        [grad, slope] + pieces,
        2 * count * width * hidden,
    )


def lane_sum(field):
    return sum(field[:, i : i + LANES] for i in range(0, field.shape[1], LANES))


def weight_kernel(rows, with_sums, t_ref, l_ref, r_ref, *refs):
    step = pl.program_id(0)
    if with_sums:
        sum_ref, pieces, refs = refs[0], refs[1 : 1 + rows], refs[1 + rows :]
        parts_ref = refs[-1]
    grad = dot(l_ref[...], r_ref[...], 0, 0)
    for k in range(rows):

        @pl.when(step == k)
        def _(k=k):
            refs[k][...] = grad.astype(BF)
            if with_sums:
                piece = pieces[k][...].astype(F32)
                parts_ref[0] = lane_sum(piece * grad)
                parts_ref[1] = lane_sum(piece * sum_ref[...])


def weight_grad(turns, left, right, sums=None, pieces=()):
    rows = turns.shape[0]
    count, width = left.shape
    columns = right.shape[1]
    depth = width // rows
    out_shape = [like((depth, columns))] * rows
    out_specs = [whole(v) for v in out_shape]
    operands = [left, right]
    if pieces:
        operands += [sums] + pieces
        out_shape.append(like((2, width, LANES), F32))
        out_specs.append(pl.BlockSpec((2, depth, LANES), lambda k, t: (0, t[k], 0)))
    out = call(
        functools.partial(weight_kernel, rows, bool(pieces)),
        turns,
        rows,
        [pl.BlockSpec((count, depth), lambda k, t: (0, k))] + [whole(v) for v in operands[1:]],
        out_specs,
        out_shape,
        operands,
        2 * count * width * columns,
    )
    if pieces:
        return out[:-1], out[-1]
    return out


def out_kernel(rows, t_ref, o_ref, g_ref, *refs):
    *outs, grad_ref = refs
    depth = outs[0].shape[0]
    grad_ref[...] = dot(o_ref[...], g_ref[...], 0, 0)
    for j, out in enumerate(outs):
        at = pl.multiple_of(t_ref[rows + j] * depth, depth)
        out[...] = grad_ref[pl.ds(at, depth)].astype(BF)


def out_grad(turns, places, attended, grad):
    rows, group = turns.shape[0], places.shape[0]
    count, width = grad.shape
    part = width // rows
    depth = HD // group
    return pl.pallas_call(
        functools.partial(out_kernel, rows),
        name="out_kernel",
        grid_spec=pltpu.PrefetchScalarGridSpec(
            num_scalar_prefetch=1,
            grid=(rows,),
            in_specs=[whole(attended), pl.BlockSpec((count, part), lambda k, t: (0, k))],
            out_specs=[pl.BlockSpec((depth, part), lambda k, t: (0, t[k]))] * group,
            scratch_shapes=[pltpu.VMEM((HD, part), F32)],
        ),
        out_shape=[like((depth, width))] * group,
        compiler_params=pltpu.CompilerParams(vmem_limit_bytes=VMEM_LIMIT),
        cost_estimate=pl.CostEstimate(
            flops=2 * count * width * HD // COST,
            bytes_accessed=2 * (count * (width + HD) + width * HD) // COST,
            transcendentals=0,
        ),
    )(jnp.concatenate([turns, places]), attended, grad)


def turned_columns(t_ref, w_ref, k, depth):
    return w_ref[:, pl.ds(pl.multiple_of(t_ref[k] * depth, LANES), depth)]


def sum_kernel(t_ref, h_ref, o_ref, w_ref, *refs):
    pieces, y_ref = refs[:-1], refs[-1]
    for k, piece in enumerate(pieces):
        depth = piece.shape[0]
        term = dot(h_ref[...], piece[...], 1, 1)
        term += dot(o_ref[...], turned_columns(t_ref, w_ref, k, depth), 1, 0)
        y_ref[:, k * depth : (k + 1) * depth] = term.astype(BF)


def out_sum(turns, hidden, pieces, attended, out_w):
    count = hidden.shape[0]
    width = out_w.shape[1]
    return call(
        sum_kernel,
        turns,
        count // BLOCK,
        [rows_block(hidden.shape[1]), rows_block(HD), whole(out_w)] + [whole(p) for p in pieces],
        [rows_block(width)],
        [like((count, width))],
        [hidden, attended, out_w] + pieces,
        2 * count * width * (hidden.shape[1] + HD),
    )[0]


def back_kernel(t_ref, p_ref, q_ref, v_ref, *refs):
    pieces, c_ref = refs[:-1], refs[-1]
    count = len(pieces) // 2
    for k, (up, qkv) in enumerate(zip(pieces[:count], pieces[count:])):
        depth = up.shape[0]
        cols = slice(k * depth, (k + 1) * depth)
        term = dot(p_ref[...], up[...], 1, 1) * v_ref[2:3, cols]
        term += dot(q_ref[...], qkv[...], 1, 1) * v_ref[0:1, cols]
        c_ref[:, cols] = term.astype(BF)


def norm_back(turns, pre_grad, up_pieces, qkv_grad, qkv_pieces, vectors):
    count = pre_grad.shape[0]
    width = vectors.shape[1]
    columns = pre_grad.shape[1] + qkv_grad.shape[1]
    return call(
        back_kernel,
        turns,
        count // BLOCK,
        [rows_block(pre_grad.shape[1]), rows_block(qkv_grad.shape[1]), whole(vectors)]
        + [whole(p) for p in up_pieces + qkv_pieces],
        [rows_block(width)],
        [like((count, width))],
        [pre_grad, qkv_grad, vectors] + up_pieces + qkv_pieces,
        2 * count * width * columns,
    )[0]


def turned(field, cosine, minus, plus):
    head = field[:, :LANES]
    half = ROT // 2
    head = (
        head * cosine
        + pltpu.roll(head, LANES - half, 1) * minus
        + pltpu.roll(head, half, 1) * plus
    )
    return jnp.concatenate([head, field[:, LANES:]], 1)


def allowed_pairs(length, dq_ref, dk_ref):
    spot = lax.broadcasted_iota(jnp.int32, (length, length), 0)
    other = lax.broadcasted_iota(jnp.int32, (length, length), 1)
    return (dq_ref[0] == dk_ref[0]) & (other <= spot)


def forward_kernel(t_ref, a_ref, b_ref, c_ref, m_ref, p_ref, dq_ref, dk_ref, *refs):
    pieces, (qkv_ref, o_ref, lse_ref) = refs[:-3], refs[-3:]
    qkv = times_pieces(a_ref[...], pieces) + b_ref[...]
    tables = c_ref[0], m_ref[0], p_ref[0]
    queries = (turned(qkv[:, :HD], *tables) * HD ** (-0.5)).astype(BF)
    keys = turned(qkv[:, HD : 2 * HD], *tables).astype(BF)
    values = qkv[:, 2 * HD :].astype(BF)
    for i, field in enumerate((queries, keys, values)):
        qkv_ref[:, i * HD : (i + 1) * HD] = field
    allowed = allowed_pairs(a_ref.shape[0], dq_ref, dk_ref)
    scores = jnp.where(allowed, dot(queries, keys, 1, 1), MASKED)
    largest = jnp.max(scores, -1, keepdims=True)
    weights = jnp.where(allowed, jnp.exp(scores - largest), 0.0)
    mass = jnp.sum(weights, -1, keepdims=True)
    o_ref[...] = dot((weights / mass).astype(BF), values, 1, 0).astype(BF)
    lse_ref[...] = largest + jnp.log(mass)


def backward_kernel(
    parts, t_ref, g_ref, w_ref, qkv_ref, o_ref, lse_ref, c_ref, m_ref, p_ref, dq_ref, dk_ref,
    grad_ref, sum_ref,
):
    queries, keys, values = (qkv_ref[:, i * HD : (i + 1) * HD] for i in range(3))
    tables = c_ref[0], -m_ref[0], -p_ref[0]
    depth = w_ref.shape[1] // parts
    heads_grad = None
    for k in range(parts):
        cols = slice(k * depth, (k + 1) * depth)
        term = dot(g_ref[:, cols], turned_columns(t_ref, w_ref, k, depth), 1, 1)
        heads_grad = term if heads_grad is None else heads_grad + term
    heads_grad = heads_grad.astype(BF)
    allowed = allowed_pairs(g_ref.shape[0], dq_ref, dk_ref)
    scores = jnp.where(allowed, dot(queries, keys, 1, 1), MASKED)
    weights = jnp.where(allowed, jnp.exp(scores - lse_ref[...]), 0.0)
    deltas = jnp.sum(heads_grad.astype(F32) * o_ref[...].astype(F32), -1, keepdims=True)
    score_grad = (weights * (dot(heads_grad, values, 1, 1) - deltas)).astype(BF)
    query_grad = dot(score_grad, keys, 1, 0) * HD ** (-0.5)
    key_grad = dot(score_grad, queries, 0, 0)
    value_grad = dot(weights.astype(BF), heads_grad, 0, 0)
    fields = turned(query_grad, *tables), turned(key_grad, *tables), value_grad

    @pl.when(pl.program_id(0) == 0)
    def _():
        sum_ref[...] = jnp.zeros_like(sum_ref)

    for i, field in enumerate(fields):
        field = field.astype(BF)
        cols = slice(i * HD, (i + 1) * HD)
        grad_ref[:, cols] = field
        sum_ref[:, cols] += jnp.sum(field.astype(F32), 0, keepdims=True)


def pair_specs(length):
    table = pl.BlockSpec((1, length, LANES), lambda r, t: (r, 0, 0))
    return [table] * 3 + [
        pl.BlockSpec((1, length, 1), lambda r, t: (r, 0, 0)),
        pl.BlockSpec((1, 1, length), lambda r, t: (r, 0, 0)),
    ]


def head_forward(turns, normed, bias, pairs, pieces, length):
    count, width = normed.shape
    columns = 3 * HD
    return call(
        forward_kernel,
        turns,
        count // length,
        [rows_block(width, length), pl.BlockSpec((1, columns), lambda r, t: (0, 0))]
        + pair_specs(length)
        + [whole(p) for p in pieces],
        [rows_block(columns, length), rows_block(HD, length), rows_block(1, length)],
        [like((count, columns)), like((count, HD)), like((count, 1), F32)],
        [normed, bias.reshape(1, columns)] + pairs + pieces,
        2 * count * (width * columns + 2 * length * HD),
    )


def head_backward(turns, grad, out_w, qkv, attended, lse, pairs, length):
    count, width = grad.shape
    columns = 3 * HD
    return call(
        functools.partial(backward_kernel, turns.shape[0]),
        turns,
        count // length,
        [
            rows_block(width, length),
            whole(out_w),
            rows_block(columns, length),
            rows_block(HD, length),
            rows_block(1, length),
        ]
        + pair_specs(length),
        [rows_block(columns, length), pl.BlockSpec((1, columns), lambda r, t: (0, 0))],
        [like((count, columns)), like((1, columns), F32)],
        [grad, out_w, qkv, attended, lse] + pairs,
        2 * count * (width * HD + 5 * length * HD),
    )


def finish_kernel(rows, with_norm, t_ref, x_ref, s_ref, o_ref, out_ref):
    depth = x_ref.shape[1] // rows
    term = s_ref[...].astype(F32)
    if with_norm:
        centred = x_ref[...].astype(F32)
        centred = centred - jnp.mean(centred, -1, keepdims=True)
        rstd = lax.rsqrt(jnp.mean(centred * centred, -1, keepdims=True) + EPSILON)
        centred = centred * rstd
        term = term - jnp.mean(term, -1, keepdims=True) - centred * jnp.mean(
            term * centred, -1, keepdims=True
        )
        field = o_ref[...].astype(F32) + rstd * term
    else:
        field = x_ref[...].astype(F32) + term + o_ref[4:5]
    for k in range(rows):
        at = pl.multiple_of(t_ref[k] * depth, LANES)
        out_ref[:, pl.ds(at, depth)] = field[:, k * depth : (k + 1) * depth].astype(BF)


def finish(turns, x, term, other, with_norm):
    return call(
        functools.partial(finish_kernel, turns.shape[0], with_norm),
        turns,
        1,
        [whole(v) for v in (x, term, other)],
        [whole(x)],
        [like(x.shape)],
        [x, term, other],
    )[0]


def shards(
    plan,
    tokens,
    attn_weights,
    mlp_weights,
    ln1_gain,
    ln1_bias,
    ln2_gain,
    ln2_bias,
    qkv_bias,
    dense_bias,
    up_bias,
    down_bias,
    doc_lengths,
    cotangent,
):
    row_count, shard_len, width = tokens.shape
    depth = attn_weights.shape[0]
    heads = width // HD
    rows, blks = plan.rows, plan.blks
    own_hidden = mlp_weights.shape[-1] // blks
    me = lax.axis_index("blk")
    length = shard_len * blks
    count = row_count * length
    head_of = me % plan.group // plan.share * plan.per_row + me // plan.group
    part = me % plan.share
    own_rows = row_count // plan.share
    row = lax.axis_index("row")
    turns = row ^ jnp.arange(rows, dtype=jnp.int32)
    places = me % plan.group ^ jnp.arange(plan.group, dtype=jnp.int32)

    def exchange(field):
        return lax.all_to_all(field, "blk", 0, 0)

    def collect(field):
        return exchange(field.reshape(blks, -1, field.shape[-1]))

    def gather_blocks(field):
        field = field.reshape(row_count, shard_len, width)
        return lax.all_gather(field, "blk", axis=1, tiled=True).reshape(count, width)

    def sum_blocks(field):
        field = field.reshape(row_count, length, width)
        field = lax.psum_scatter(field, "blk", scatter_dimension=1, tiled=True)
        return field.reshape(row_count * shard_len, width)

    zeros = jnp.zeros((3, width), F32)
    vectors = jnp.stack([ln1_gain, ln1_bias, ln2_gain, ln2_bias, dense_bias + down_bias])
    x_own, g_own, vectors, g_sum = turn_in(
        turns,
        tokens.reshape(row_count * shard_len, width),
        cotangent.reshape(row_count * shard_len, width),
        jnp.concatenate([vectors, zeros]),
    )
    qkv_send, out_own = split_attn(turns, attn_weights, plan, width)
    qkv_mine = exchange(qkv_send)
    out_send = pick(
        row ^ places // plan.share,
        [out_own] + [swap(out_own, "row", rows, k) for k in range(1, rows)],
        plan.group,
    )
    up_send, down_send = split_mlp(turns, after(mlp_weights, qkv_send), blks)
    qkv_mine, up_send, *out_send = lax.optimization_barrier((qkv_mine, up_send, *out_send))
    up_mine = exchange(up_send)
    qkv_pieces = gather_row(qkv_mine.reshape(-1, 3 * HD), plan)
    out_got = [out_send[0]] + [swap_group(out_send[j], plan, j) for j in range(1, plan.group)]
    up_mine, x_own, down_send, *qkv_pieces = lax.optimization_barrier(
        (up_mine, x_own, down_send, *qkv_pieces, *out_got)
    )[: 3 + rows]
    x_all = gather_blocks(x_own)
    down_mine = exchange(down_send)
    up_pieces = gather_row(up_mine.reshape(-1, own_hidden), plan)
    out_w = place(places, out_got)
    down_mine, g_own, *up_pieces = lax.optimization_barrier((down_mine, g_own, *up_pieces))
    g_all = gather_blocks(g_own)
    down_pieces = gather_row(down_mine.reshape(-1, own_hidden), plan)
    normed1, normed2 = norms(turns, x_all, vectors)

    lengths = lax.dynamic_slice_in_dim(doc_lengths, part * own_rows, own_rows, 0)
    doc_ends = jnp.cumsum(lengths, axis=-1)
    starts = doc_ends - lengths
    spots = jnp.arange(length, dtype=jnp.int32)
    doc_ids = jnp.sum((spots[None, :, None] >= doc_ends[:, None, :]).astype(jnp.int32), -1)
    picked = doc_ids[:, :, None] == jnp.arange(lengths.shape[-1], dtype=jnp.int32)
    positions = spots - jnp.sum(jnp.where(picked, starts[:, None, :], 0), -1)
    lane = jnp.arange(LANES)
    inverse = 10000.0 ** (-2.0 * (lane % (ROT // 2)).astype(F32) / ROT)
    angles = positions.astype(F32)[..., None] * inverse
    sine = jnp.sin(angles)
    pairs = [
        jnp.where(lane < ROT, jnp.cos(angles), 1.0),
        jnp.where(lane < ROT // 2, -sine, 0.0),
        jnp.where((lane >= ROT // 2) & (lane < ROT), sine, 0.0),
        doc_ids[:, :, None],
        doc_ids[:, None, :],
    ]

    def own(field):
        if plan.share == 1:
            return field
        return lax.dynamic_slice_in_dim(field, part * own_rows * length, own_rows * length, 0)

    def spread(field):
        if plan.share == 1:
            return field
        blank = jnp.zeros((count, field.shape[1]), field.dtype)
        return lax.dynamic_update_slice_in_dim(blank, field, part * own_rows * length, 0)

    up_b = lax.dynamic_slice_in_dim(up_bias, me * own_hidden, own_hidden)
    qkv_b = lax.dynamic_index_in_dim(qkv_bias.reshape(3, heads, HD), head_of, 1, keepdims=False)
    own_normed1 = own(normed1)
    qkv, attended, lse = head_forward(
        turns, own_normed1, qkv_b.reshape(-1), pairs, qkv_pieces, length
    )
    hidden, slope = feed_up(turns, after(normed2, attended), up_b, up_pieces)
    out_term = out_sum(turns, hidden, down_pieces, spread(attended), out_w)
    out_total = sum_blocks(out_term)

    g_all = after(g_all, out_term)
    down_g = weight_grad(turns, g_all, hidden)
    down_got = scatter_row(down_g, plan)
    own_grad = own(after(g_all, down_g[0]))
    out_g = out_grad(turns, places, attended, own_grad)
    out_got = [out_g[0]] + [swap_group(out_g[j], plan, j) for j in range(1, plan.group)]
    pre_grad, up_sum = feed_slope(turns, after(g_all, out_g[0]), slope, down_pieces)
    up_g, up_parts = weight_grad(turns, normed2, pre_grad, up_sum, up_pieces)
    qkv_grad, qkv_sum = head_backward(
        turns, after(own_grad, up_g[0]), out_w, qkv, attended, lse, pairs, length
    )
    down_total = add_pieces(turns, [after(down_g[0], qkv_grad, *out_got)] + down_got)
    down_back = collect(down_total)
    up_near = scatter_row([after(v, down_total) for v in up_g], plan, False)
    norm_term = norm_back(
        turns,
        after(pre_grad, down_total),
        up_pieces,
        spread(qkv_grad),
        qkv_pieces,
        vectors,
    )
    holders = turns[:, None] * plan.share + jnp.arange(plan.share, dtype=jnp.int32)
    out_send = pick((me % plan.group ^ holders).reshape(-1), out_got, rows)
    layer_out = finish(turns, x_own, out_total, vectors, False)
    up_got = up_near + scatter_row([after(v, norm_term, *up_near) for v in up_g], plan, True)
    norm_total = sum_blocks(after(norm_term, down_back, *up_near))
    qkv_g, qkv_parts = weight_grad(
        turns,
        after(own_normed1, down_back, out_send[0], layer_out, *up_near),
        qkv_grad,
        qkv_sum,
        qkv_pieces,
    )

    up_total = add_pieces(turns, [after(up_g[0], qkv_g[0])] + up_got)
    up_back = collect(up_total)
    qkv_got = scatter_row([after(v, up_total) for v in qkv_g], plan)

    terms = [jnp.sum(v, -1) for v in (qkv_parts, up_parts)]
    terms += [g_sum, qkv_sum, up_sum]
    terms = [v.reshape(-1) for v in terms]
    used = sum(v.size for v in terms)
    terms.append(jnp.zeros((-used % (8 * LANES),), F32))
    sums = jnp.concatenate(terms)
    sums = sums + sum(swap(sums, "row", rows, k) for k in range(1, rows))
    sums = after(sums, up_total)
    sums = jnp.stack([sums, swap(sums, "blk", blks, 1)])

    qkv_total = add_pieces(turns, [after(qkv_g[0], up_back, sums)] + qkv_got)
    qkv_back = collect(qkv_total)
    out_back = out_send[0].astype(F32) + sum(
        swap(after(out_send[k], qkv_total), "row", rows, k).astype(F32) for k in range(1, rows)
    )
    sums = after(sums, qkv_total)
    sums = jnp.concatenate([sums] + [swap(sums, "blk", blks, k) for k in range(2, blks, 2)])
    sums = sums[me ^ jnp.arange(blks, dtype=jnp.int32)]
    gain1, bias1, gain2, bias2, g_total = jnp.split(
        jnp.sum(sums[:, : 5 * width], 0), 5
    )
    sums = sums[:, 5 * width : used]
    qkv_bias_grad = sums[:, : 3 * HD].reshape(plan.per_row, rows, plan.share, 3, HD)
    qkv_bias_grad = jnp.sum(qkv_bias_grad, 2).transpose(2, 1, 0, 3).reshape(-1)
    up_bias_grad = sums[:, 3 * HD :].reshape(-1)

    tokens_grad = finish(turns, x_own, norm_total, g_own, True)
    return (
        layer_out.reshape(tokens.shape),
        tokens_grad.reshape(tokens.shape),
        join_attn(turns, qkv_back, after(out_back, tokens_grad), plan),
        join_mlp(turns, up_back, down_back),
        (gain1 - ln1_bias * bias1) / ln1_gain,
        bias1,
        (gain2 - ln2_bias * bias2) / ln2_gain,
        bias2,
        qkv_bias_grad,
        g_total,
        up_bias_grad,
        g_total,
    )


def solution(mesh):
    rows, blks = mesh.shape["row"], mesh.shape["blk"]
    vector = P()
    tokens = P("row", "blk", None)
    attn = P(("row", "blk"), None)
    mlp = P(("row", "blk"), None, None)

    def run(*arrays):
        plan = Plan(rows, blks, arrays[0].shape[-1] // HD)
        return jax.shard_map(
            functools.partial(shards, plan),
            mesh=mesh,
            in_specs=(tokens, attn, mlp) + (vector,) * 8 + (P("row", None), tokens),
            out_specs=(tokens, tokens, attn, mlp) + (vector,) * 8,
            check_vma=False,
        )(*arrays)

    return run
```

```python
import functools
import math

import jax
import jax.numpy as jnp
import numpy as np
from jax import lax
from jax.experimental import pallas as pl
from jax.experimental.pallas import tpu as pltpu
from jax.sharding import PartitionSpec as P

HD = 256
ROT = 64
LANES = 128
BLOCK = 256
EPSILON = 1e-05
MASKED = -1e30
BF = jnp.bfloat16
F32 = jnp.float32
COST = 100
VMEM_LIMIT = 56 * 2**20
SMALL = 16 * 2**20


class Plan:
    def __init__(self, rows, blks, heads):
        self.rows = rows
        self.blks = blks
        self.share = blks // heads
        self.per_row = heads // rows
        self.group = blks // self.per_row
        self.groups = [
            list(range(i * self.group, (i + 1) * self.group)) for i in range(self.per_row)
        ]


def after(field, *others):
    return lax.optimization_barrier((field,) + others)[0] if others else field


def swap(field, axis, size, bit):
    return lax.ppermute(field, axis, [(i, i ^ bit) for i in range(size)])


def swap_group(field, plan, bits):
    return lax.ppermute(field, "blk", [(i, i ^ bits) for i in range(plan.blks)])


def gather_row(own, plan):
    return [own] + [swap(own, "row", plan.rows, k) for k in range(1, plan.rows)]


def scatter_row(pieces, plan, far=None):
    return [
        swap(v, "row", plan.rows, k)
        for k, v in enumerate(pieces)
        if k and (far is None or far == (k & (k - 1) != 0))
    ]


def dot(left, right, left_dim, right_dim):
    return lax.dot_general(
        left, right, (((left_dim,), (right_dim,)), ((), ())), preferred_element_type=F32
    )


def whole(array):
    return pl.BlockSpec(array.shape, lambda *i: (0,) * len(array.shape))


def like(shape, kind=BF):
    return jax.ShapeDtypeStruct(shape, kind)


def call(body, turns, grid, in_specs, out_specs, out_shape, operands, flops=0, limit=None):
    moved = sum(v.size * v.dtype.itemsize for v in operands)
    moved += sum(math.prod(v.shape) * jnp.dtype(v.dtype).itemsize for v in out_shape)
    return pl.pallas_call(
        body,
        name=getattr(body, "func", body).__name__,
        grid_spec=pltpu.PrefetchScalarGridSpec(
            num_scalar_prefetch=1, grid=(grid,), in_specs=in_specs, out_specs=out_specs
        ),
        out_shape=out_shape,
        compiler_params=pltpu.CompilerParams(vmem_limit_bytes=limit or VMEM_LIMIT),
        cost_estimate=pl.CostEstimate(
            flops=flops // COST, bytes_accessed=moved // COST, transcendentals=0
        ),
    )(turns, *operands)


def rows_block(columns, block=BLOCK):
    return pl.BlockSpec((block, columns), lambda i, t: (i, 0))


def add_kernel(t_ref, *refs):
    refs[-1][...] = sum(ref[...].astype(F32) for ref in refs[:-1]).astype(BF)


def add_pieces(turns, terms):
    depth, width = terms[0].shape
    block = rows_block(width, depth // 4)
    shape = like((depth, width))
    return call(
        add_kernel, turns, 4, [block] * len(terms), [block], [shape], terms, limit=SMALL
    )[0]


def turn_kernel(t_ref, x_ref, g_ref, v_ref, xo_ref, go_ref, vo_ref, s_ref):
    xo_ref[...] = x_ref[...]
    go_ref[...] = g_ref[...]
    vo_ref[...] = v_ref[...]
    s_ref[...] = jnp.sum(g_ref[...].astype(F32), 0, keepdims=True)


def turn_in(turns, x, g, vectors):
    rows = turns.shape[0]
    part = x.shape[1] // rows

    def specs(array, turned):
        index = (lambda k, t: (0, t[k])) if turned else (lambda k, t: (0, k))
        return pl.BlockSpec((array.shape[0], part), index)

    total_shape = like((1, x.shape[1]), F32)
    return call(
        turn_kernel,
        turns,
        rows,
        [specs(v, True) for v in (x, g, vectors)],
        [specs(v, False) for v in (x, g, vectors)] + [specs(total_shape, True)],
        [like(v.shape, v.dtype) for v in (x, g, vectors)] + [total_shape],
        [x, g, vectors],
    )


def split_kernel(t_ref, w_ref, u_ref, d_ref):
    u_ref[0] = w_ref[:, 0, :]
    d_ref[0] = w_ref[:, 1, :]


def split_mlp(turns, weights, blks):
    depth, _, hidden = weights.shape
    part = hidden // blks
    block = pl.BlockSpec((1, depth, part), lambda b, t: (b, 0, 0))
    return call(
        split_kernel,
        turns,
        blks,
        [pl.BlockSpec((depth, 2, part), lambda b, t: (0, 0, b))],
        [block] * 2,
        [like((blks, depth, part))] * 2,
        [weights],
    )


def join_kernel(t_ref, u_ref, d_ref, o_ref):
    o_ref[:, 0, :] = u_ref[0].astype(F32)
    o_ref[:, 1, :] = d_ref[0].astype(F32)


def join_mlp(turns, up, down):
    blks, depth, part = up.shape
    block = pl.BlockSpec((1, depth, part), lambda b, t: (b, 0, 0))
    return call(
        join_kernel,
        turns,
        blks,
        [block] * 2,
        [pl.BlockSpec((depth, 2, part), lambda b, t: (0, 0, b))],
        [like((depth, 2, blks * part), F32)],
        [up, down],
    )[0]


def split_attn_kernel(plan, width, t_ref, w_ref, qkv_ref, out_ref):
    b = pl.program_id(0)
    head = b % plan.group // plan.share * plan.per_row + b // plan.group
    for i in range(3):
        at = pl.multiple_of(i * width + head * HD, HD)
        qkv_ref[0, :, i * HD : (i + 1) * HD] = w_ref[:, pl.ds(at, HD)]

    @pl.when(b == 0)
    def _():
        out_ref[...] = w_ref[:, 3 * width :]


def split_attn(turns, weights, plan, width):
    depth = weights.shape[0]
    return call(
        functools.partial(split_attn_kernel, plan, width),
        turns,
        plan.blks,
        [whole(weights)],
        [
            pl.BlockSpec((1, depth, 3 * HD), lambda b, t: (b, 0, 0)),
            pl.BlockSpec((depth, width), lambda b, t: (0, 0)),
        ],
        [like((plan.blks, depth, 3 * HD)), like((depth, width))],
        [weights],
        limit=SMALL,
    )


def join_attn_kernel(plan, t_ref, qkv_ref, out_ref, o_ref):
    step = pl.program_id(0)
    heads = o_ref.shape[1] // HD

    @pl.when(step < 3)
    def _():
        at = pl.ds(pl.multiple_of(step * HD, HD), HD)
        for h in range(heads):
            first = h % plan.per_row * plan.group + h // plan.per_row * plan.share
            o_ref[:, h * HD : (h + 1) * HD] = sum(
                qkv_ref[first + i, :, at].astype(F32) for i in range(plan.share)
            )

    @pl.when(step == 3)
    def _():
        o_ref[...] = out_ref[...]


def join_attn(turns, qkv, out, plan):
    depth, width = out.shape
    return call(
        functools.partial(join_attn_kernel, plan),
        turns,
        4,
        [whole(qkv), whole(out)],
        [pl.BlockSpec((depth, width), lambda j, t: (0, j))],
        [like((depth, 4 * width), F32)],
        [qkv, out],
    )[0]


def pick_kernel(count, t_ref, *refs):
    pieces, outs = refs[:count], refs[count:]
    share = t_ref.shape[0] // len(outs)
    for n, out in enumerate(outs):
        for i in range(share):
            for k, piece in enumerate(pieces):

                @pl.when(t_ref[n * share + i] == k)
                def _(i=i, out=out, piece=piece):
                    out[...] = piece[...] if i == 0 else out[...] + piece[...]


def pick(table, pieces, count):
    return call(
        functools.partial(pick_kernel, len(pieces)),
        table,
        1,
        [whole(p) for p in pieces],
        [whole(pieces[0])] * count,
        [like(pieces[0].shape)] * count,
        pieces,
    )


def place_kernel(t_ref, *refs):
    *pieces, out_ref = refs
    for k, piece in enumerate(pieces):
        depth = piece.shape[0]
        out_ref[pl.ds(pl.multiple_of(t_ref[k] * depth, depth), depth)] = piece[...]


def place(table, pieces):
    depth, width = pieces[0].shape
    shape = like((len(pieces) * depth, width))
    return call(place_kernel, table, 1, [whole(p) for p in pieces], [whole(shape)], [shape], pieces)[0]


def norm_kernel(t_ref, x_ref, v_ref, a1_ref, a2_ref):
    field = x_ref[...].astype(F32)
    centred = field - jnp.mean(field, -1, keepdims=True)
    standard = centred * lax.rsqrt(jnp.mean(centred * centred, -1, keepdims=True) + EPSILON)
    a1_ref[...] = (standard * v_ref[0:1] + v_ref[1:2]).astype(BF)
    a2_ref[...] = (standard * v_ref[2:3] + v_ref[3:4]).astype(BF)


def norms(turns, x, vectors):
    count, width = x.shape
    return call(
        norm_kernel,
        turns,
        count // BLOCK,
        [rows_block(width), whole(vectors)],
        [rows_block(width)] * 2,
        [like(x.shape)] * 2,
        [x, vectors],
        20 * count * width,
    )


def times_pieces(left, pieces):
    out, start = None, 0
    for piece in pieces:
        depth = piece.shape[0]
        term = dot(left[:, start : start + depth], piece[...], 1, 0)
        out = term if out is None else out + term
        start += depth
    return out


def up_kernel(t_ref, a_ref, b_ref, *refs):
    pieces, (h_ref, s_ref) = refs[:-2], refs[-2:]
    pre = times_pieces(a_ref[...], pieces) + b_ref[...]
    cdf = 0.5 * (1.0 + lax.erf(pre * math.sqrt(0.5)))
    h_ref[...] = (pre * cdf).astype(BF)
    s_ref[...] = cdf + pre * (jnp.exp(-0.5 * pre * pre) * (1.0 / math.sqrt(2.0 * math.pi)))


def feed_up(turns, normed, bias, pieces):
    count, width = normed.shape
    hidden = bias.shape[0]
    return call(
        up_kernel,
        turns,
        count // BLOCK,
        [rows_block(width), pl.BlockSpec((1, hidden), lambda i, t: (0, 0))]
        + [whole(p) for p in pieces],
        [rows_block(hidden)] * 2,
        [like((count, hidden)), like((count, hidden), F32)],
        [normed, bias.reshape(1, hidden)] + pieces,
        2 * count * width * hidden,
    )


def slope_kernel(t_ref, g_ref, s_ref, *refs):
    pieces, (p_ref, sum_ref) = refs[:-2], refs[-2:]

    @pl.when(pl.program_id(0) == 0)
    def _():
        sum_ref[...] = jnp.zeros_like(sum_ref)

    grad = (times_pieces(g_ref[...], pieces) * s_ref[...]).astype(BF)
    p_ref[...] = grad
    sum_ref[...] += jnp.sum(grad.astype(F32), 0, keepdims=True)


def feed_slope(turns, grad, slope, pieces):
    count, width = grad.shape
    hidden = slope.shape[1]
    return call(
        slope_kernel,
        turns,
        count // BLOCK,
        [rows_block(width), rows_block(hidden)] + [whole(p) for p in pieces],
        [rows_block(hidden), pl.BlockSpec((1, hidden), lambda i, t: (0, 0))],
        [like((count, hidden)), like((1, hidden), F32)],
        [grad, slope] + pieces,
        2 * count * width * hidden,
    )


def lane_sum(field):
    return sum(field[:, i : i + LANES] for i in range(0, field.shape[1], LANES))


def weight_kernel(rows, with_sums, t_ref, l_ref, r_ref, *refs):
    step = pl.program_id(0)
    if with_sums:
        sum_ref, pieces, refs = refs[0], refs[1 : 1 + rows], refs[1 + rows :]
        parts_ref = refs[-1]
    grad = dot(l_ref[...], r_ref[...], 0, 0)
    for k in range(rows):

        @pl.when(step == k)
        def _(k=k):
            refs[k][...] = grad.astype(BF)
            if with_sums:
                piece = pieces[k][...].astype(F32)
                parts_ref[0] = lane_sum(piece * grad)
                parts_ref[1] = lane_sum(piece * sum_ref[...])


def weight_grad(turns, left, right, sums=None, pieces=()):
    rows = turns.shape[0]
    count, width = left.shape
    columns = right.shape[1]
    depth = width // rows
    out_shape = [like((depth, columns))] * rows
    out_specs = [whole(v) for v in out_shape]
    operands = [left, right]
    if pieces:
        operands += [sums] + pieces
        out_shape.append(like((2, width, LANES), F32))
        out_specs.append(pl.BlockSpec((2, depth, LANES), lambda k, t: (0, t[k], 0)))
    out = call(
        functools.partial(weight_kernel, rows, bool(pieces)),
        turns,
        rows,
        [pl.BlockSpec((count, depth), lambda k, t: (0, k))] + [whole(v) for v in operands[1:]],
        out_specs,
        out_shape,
        operands,
        2 * count * width * columns,
    )
    if pieces:
        return out[:-1], out[-1]
    return out


def out_kernel(rows, t_ref, o_ref, g_ref, *refs):
    *outs, grad_ref = refs
    depth = outs[0].shape[0]
    grad_ref[...] = dot(o_ref[...], g_ref[...], 0, 0)
    for j, out in enumerate(outs):
        at = pl.multiple_of(t_ref[rows + j] * depth, depth)
        out[...] = grad_ref[pl.ds(at, depth)].astype(BF)


def out_grad(turns, places, attended, grad):
    rows, group = turns.shape[0], places.shape[0]
    count, width = grad.shape
    part = width // rows
    depth = HD // group
    return pl.pallas_call(
        functools.partial(out_kernel, rows),
        name="out_kernel",
        grid_spec=pltpu.PrefetchScalarGridSpec(
            num_scalar_prefetch=1,
            grid=(rows,),
            in_specs=[whole(attended), pl.BlockSpec((count, part), lambda k, t: (0, k))],
            out_specs=[pl.BlockSpec((depth, part), lambda k, t: (0, t[k]))] * group,
            scratch_shapes=[pltpu.VMEM((HD, part), F32)],
        ),
        out_shape=[like((depth, width))] * group,
        compiler_params=pltpu.CompilerParams(vmem_limit_bytes=VMEM_LIMIT),
        cost_estimate=pl.CostEstimate(
            flops=2 * count * width * HD // COST,
            bytes_accessed=2 * (count * (width + HD) + width * HD) // COST,
            transcendentals=0,
        ),
    )(jnp.concatenate([turns, places]), attended, grad)


def turned_columns(t_ref, w_ref, k, depth):
    return w_ref[:, pl.ds(pl.multiple_of(t_ref[k] * depth, LANES), depth)]


def sum_kernel(t_ref, h_ref, o_ref, w_ref, *refs):
    pieces, y_ref = refs[:-1], refs[-1]
    for k, piece in enumerate(pieces):
        depth = piece.shape[0]
        term = dot(h_ref[...], piece[...], 1, 1)
        term += dot(o_ref[...], turned_columns(t_ref, w_ref, k, depth), 1, 0)
        y_ref[:, k * depth : (k + 1) * depth] = term.astype(BF)


def out_sum(turns, hidden, pieces, attended, out_w):
    count = hidden.shape[0]
    width = out_w.shape[1]
    return call(
        sum_kernel,
        turns,
        count // BLOCK,
        [rows_block(hidden.shape[1]), rows_block(HD), whole(out_w)] + [whole(p) for p in pieces],
        [rows_block(width)],
        [like((count, width))],
        [hidden, attended, out_w] + pieces,
        2 * count * width * (hidden.shape[1] + HD),
    )[0]


def back_kernel(t_ref, p_ref, q_ref, v_ref, *refs):
    pieces, c_ref = refs[:-1], refs[-1]
    count = len(pieces) // 2
    for k, (up, qkv) in enumerate(zip(pieces[:count], pieces[count:])):
        depth = up.shape[0]
        cols = slice(k * depth, (k + 1) * depth)
        term = dot(p_ref[...], up[...], 1, 1) * v_ref[2:3, cols]
        term += dot(q_ref[...], qkv[...], 1, 1) * v_ref[0:1, cols]
        c_ref[:, cols] = term.astype(BF)


def norm_back(turns, pre_grad, up_pieces, qkv_grad, qkv_pieces, vectors):
    count = pre_grad.shape[0]
    width = vectors.shape[1]
    columns = pre_grad.shape[1] + qkv_grad.shape[1]
    return call(
        back_kernel,
        turns,
        count // BLOCK,
        [rows_block(pre_grad.shape[1]), rows_block(qkv_grad.shape[1]), whole(vectors)]
        + [whole(p) for p in up_pieces + qkv_pieces],
        [rows_block(width)],
        [like((count, width))],
        [pre_grad, qkv_grad, vectors] + up_pieces + qkv_pieces,
        2 * count * width * columns,
    )[0]


def turned(field, cosine, minus, plus):
    head = field[:, :LANES]
    half = ROT // 2
    head = (
        head * cosine
        + pltpu.roll(head, LANES - half, 1) * minus
        + pltpu.roll(head, half, 1) * plus
    )
    return jnp.concatenate([head, field[:, LANES:]], 1)


def allowed_pairs(length, dq_ref, dk_ref):
    spot = lax.broadcasted_iota(jnp.int32, (length, length), 0)
    other = lax.broadcasted_iota(jnp.int32, (length, length), 1)
    return (dq_ref[0] == dk_ref[0]) & (other <= spot)


def forward_kernel(t_ref, a_ref, b_ref, c_ref, m_ref, p_ref, dq_ref, dk_ref, *refs):
    pieces, (qkv_ref, o_ref, lse_ref) = refs[:-3], refs[-3:]
    qkv = times_pieces(a_ref[...], pieces) + b_ref[...]
    tables = c_ref[0], m_ref[0], p_ref[0]
    queries = (turned(qkv[:, :HD], *tables) * HD ** (-0.5)).astype(BF)
    keys = turned(qkv[:, HD : 2 * HD], *tables).astype(BF)
    values = qkv[:, 2 * HD :].astype(BF)
    for i, field in enumerate((queries, keys, values)):
        qkv_ref[:, i * HD : (i + 1) * HD] = field
    allowed = allowed_pairs(a_ref.shape[0], dq_ref, dk_ref)
    scores = jnp.where(allowed, dot(queries, keys, 1, 1), MASKED)
    largest = jnp.max(scores, -1, keepdims=True)
    weights = jnp.where(allowed, jnp.exp(scores - largest), 0.0)
    mass = jnp.sum(weights, -1, keepdims=True)
    o_ref[...] = dot((weights / mass).astype(BF), values, 1, 0).astype(BF)
    lse_ref[...] = largest + jnp.log(mass)


def backward_kernel(
    parts, t_ref, g_ref, w_ref, qkv_ref, o_ref, lse_ref, c_ref, m_ref, p_ref, dq_ref, dk_ref,
    grad_ref, sum_ref,
):
    queries, keys, values = (qkv_ref[:, i * HD : (i + 1) * HD] for i in range(3))
    tables = c_ref[0], -m_ref[0], -p_ref[0]
    depth = w_ref.shape[1] // parts
    heads_grad = None
    for k in range(parts):
        cols = slice(k * depth, (k + 1) * depth)
        term = dot(g_ref[:, cols], turned_columns(t_ref, w_ref, k, depth), 1, 1)
        heads_grad = term if heads_grad is None else heads_grad + term
    heads_grad = heads_grad.astype(BF)
    allowed = allowed_pairs(g_ref.shape[0], dq_ref, dk_ref)
    scores = jnp.where(allowed, dot(queries, keys, 1, 1), MASKED)
    weights = jnp.where(allowed, jnp.exp(scores - lse_ref[...]), 0.0)
    deltas = jnp.sum(heads_grad.astype(F32) * o_ref[...].astype(F32), -1, keepdims=True)
    score_grad = (weights * (dot(heads_grad, values, 1, 1) - deltas)).astype(BF)
    query_grad = dot(score_grad, keys, 1, 0) * HD ** (-0.5)
    key_grad = dot(score_grad, queries, 0, 0)
    value_grad = dot(weights.astype(BF), heads_grad, 0, 0)
    fields = turned(query_grad, *tables), turned(key_grad, *tables), value_grad

    @pl.when(pl.program_id(0) == 0)
    def _():
        sum_ref[...] = jnp.zeros_like(sum_ref)

    for i, field in enumerate(fields):
        field = field.astype(BF)
        cols = slice(i * HD, (i + 1) * HD)
        grad_ref[:, cols] = field
        sum_ref[:, cols] += jnp.sum(field.astype(F32), 0, keepdims=True)


def pair_specs(length):
    table = pl.BlockSpec((1, length, LANES), lambda r, t: (r, 0, 0))
    return [table] * 3 + [
        pl.BlockSpec((1, length, 1), lambda r, t: (r, 0, 0)),
        pl.BlockSpec((1, 1, length), lambda r, t: (r, 0, 0)),
    ]


def head_forward(turns, normed, bias, pairs, pieces, length):
    count, width = normed.shape
    columns = 3 * HD
    return call(
        forward_kernel,
        turns,
        count // length,
        [rows_block(width, length), pl.BlockSpec((1, columns), lambda r, t: (0, 0))]
        + pair_specs(length)
        + [whole(p) for p in pieces],
        [rows_block(columns, length), rows_block(HD, length), rows_block(1, length)],
        [like((count, columns)), like((count, HD)), like((count, 1), F32)],
        [normed, bias.reshape(1, columns)] + pairs + pieces,
        2 * count * (width * columns + 2 * length * HD),
    )


def head_backward(turns, grad, out_w, qkv, attended, lse, pairs, length):
    count, width = grad.shape
    columns = 3 * HD
    return call(
        functools.partial(backward_kernel, turns.shape[0]),
        turns,
        count // length,
        [
            rows_block(width, length),
            whole(out_w),
            rows_block(columns, length),
            rows_block(HD, length),
            rows_block(1, length),
        ]
        + pair_specs(length),
        [rows_block(columns, length), pl.BlockSpec((1, columns), lambda r, t: (0, 0))],
        [like((count, columns)), like((1, columns), F32)],
        [grad, out_w, qkv, attended, lse] + pairs,
        2 * count * (width * HD + 5 * length * HD),
    )


def finish_kernel(rows, with_norm, t_ref, x_ref, s_ref, o_ref, out_ref):
    depth = x_ref.shape[1] // rows
    term = s_ref[...].astype(F32)
    if with_norm:
        centred = x_ref[...].astype(F32)
        centred = centred - jnp.mean(centred, -1, keepdims=True)
        rstd = lax.rsqrt(jnp.mean(centred * centred, -1, keepdims=True) + EPSILON)
        centred = centred * rstd
        term = term - jnp.mean(term, -1, keepdims=True) - centred * jnp.mean(
            term * centred, -1, keepdims=True
        )
        field = o_ref[...].astype(F32) + rstd * term
    else:
        field = x_ref[...].astype(F32) + term + o_ref[4:5]
    for k in range(rows):
        at = pl.multiple_of(t_ref[k] * depth, LANES)
        out_ref[:, pl.ds(at, depth)] = field[:, k * depth : (k + 1) * depth].astype(BF)


def finish(turns, x, term, other, with_norm):
    return call(
        functools.partial(finish_kernel, turns.shape[0], with_norm),
        turns,
        1,
        [whole(v) for v in (x, term, other)],
        [whole(x)],
        [like(x.shape)],
        [x, term, other],
    )[0]


def shards(
    plan,
    tokens,
    attn_weights,
    mlp_weights,
    ln1_gain,
    ln1_bias,
    ln2_gain,
    ln2_bias,
    qkv_bias,
    dense_bias,
    up_bias,
    down_bias,
    doc_lengths,
    cotangent,
):
    row_count, shard_len, width = tokens.shape
    depth = attn_weights.shape[0]
    heads = width // HD
    rows, blks = plan.rows, plan.blks
    own_hidden = mlp_weights.shape[-1] // blks
    me = lax.axis_index("blk")
    length = shard_len * blks
    count = row_count * length
    head_of = me % plan.group // plan.share * plan.per_row + me // plan.group
    part = me % plan.share
    own_rows = row_count // plan.share
    row = lax.axis_index("row")
    turns = row ^ jnp.arange(rows, dtype=jnp.int32)
    places = me % plan.group ^ jnp.arange(plan.group, dtype=jnp.int32)

    def exchange(field):
        return lax.all_to_all(field, "blk", 0, 0)

    def collect(field):
        return exchange(field.reshape(blks, -1, field.shape[-1]))

    def gather_blocks(field):
        field = field.reshape(row_count, shard_len, width)
        return lax.all_gather(field, "blk", axis=1, tiled=True).reshape(count, width)

    def sum_blocks(field):
        field = field.reshape(row_count, length, width)
        field = lax.psum_scatter(field, "blk", scatter_dimension=1, tiled=True)
        return field.reshape(row_count * shard_len, width)

    lengths = lax.dynamic_slice_in_dim(doc_lengths, part * own_rows, own_rows, 0)
    doc_ends = jnp.cumsum(lengths, axis=-1)
    starts = doc_ends - lengths
    spots = jnp.arange(length, dtype=jnp.int32)
    doc_ids = jnp.sum((spots[None, :, None] >= doc_ends[:, None, :]).astype(jnp.int32), -1)
    picked = doc_ids[:, :, None] == jnp.arange(lengths.shape[-1], dtype=jnp.int32)
    positions = spots - jnp.sum(jnp.where(picked, starts[:, None, :], 0), -1)
    lane = jnp.arange(LANES)
    inverse = 10000.0 ** (-2.0 * (lane % (ROT // 2)).astype(F32) / ROT)
    angles = positions.astype(F32)[..., None] * inverse
    sine = jnp.sin(angles)
    pairs = [
        jnp.where(lane < ROT, jnp.cos(angles), 1.0),
        jnp.where(lane < ROT // 2, -sine, 0.0),
        jnp.where((lane >= ROT // 2) & (lane < ROT), sine, 0.0),
        doc_ids[:, :, None],
        doc_ids[:, None, :],
    ]

    up_b = lax.dynamic_slice_in_dim(up_bias, me * own_hidden, own_hidden)
    qkv_b = lax.dynamic_index_in_dim(qkv_bias.reshape(3, heads, HD), head_of, 1, keepdims=False)
    qkv_b = qkv_b.reshape(-1)

    zeros = jnp.zeros((3, width), F32)
    vectors = jnp.stack([ln1_gain, ln1_bias, ln2_gain, ln2_bias, dense_bias + down_bias])
    x_own, g_own, vectors, g_sum = turn_in(
        turns,
        tokens.reshape(row_count * shard_len, width),
        cotangent.reshape(row_count * shard_len, width),
        jnp.concatenate([vectors, zeros]),
    )
    qkv_send, out_own = split_attn(turns, attn_weights, plan, width)
    qkv_mine = exchange(qkv_send)
    out_send = pick(
        row ^ places // plan.share,
        [out_own] + [swap(out_own, "row", rows, k) for k in range(1, rows)],
        plan.group,
    )
    up_send, down_send = split_mlp(turns, after(mlp_weights, qkv_send), blks)
    qkv_mine, up_send, *out_send = lax.optimization_barrier((qkv_mine, up_send, *out_send))
    up_mine = exchange(up_send)
    qkv_pieces = gather_row(qkv_mine.reshape(-1, 3 * HD), plan)
    out_got = [out_send[0]] + [swap_group(out_send[j], plan, j) for j in range(1, plan.group)]
    up_mine, x_own, down_send, *qkv_pieces = lax.optimization_barrier(
        (up_mine, x_own, down_send, *qkv_pieces, *out_got)
    )[: 3 + rows]
    x_all = gather_blocks(x_own)
    down_mine = exchange(down_send)
    up_pieces = gather_row(up_mine.reshape(-1, own_hidden), plan)
    out_w = place(places, out_got)
    down_mine, g_own, out_w, up_b, qkv_b, *pairs = lax.optimization_barrier(
        (down_mine, g_own, out_w, up_b, qkv_b, *pairs, *up_pieces)
    )
    pairs, up_pieces = pairs[: -len(up_pieces)], pairs[-len(up_pieces) :]
    g_all = gather_blocks(g_own)
    down_pieces = gather_row(down_mine.reshape(-1, own_hidden), plan)
    normed1, normed2 = norms(turns, x_all, vectors)

    def own(field):
        if plan.share == 1:
            return field
        return lax.dynamic_slice_in_dim(field, part * own_rows * length, own_rows * length, 0)

    def spread(field):
        if plan.share == 1:
            return field
        blank = jnp.zeros((count, field.shape[1]), field.dtype)
        return lax.dynamic_update_slice_in_dim(blank, field, part * own_rows * length, 0)

    own_normed1 = own(normed1)
    qkv, attended, lse = head_forward(
        turns, own_normed1, qkv_b, pairs, qkv_pieces, length
    )
    hidden, slope = feed_up(turns, after(normed2, attended), up_b, up_pieces)
    out_term = out_sum(turns, hidden, down_pieces, spread(attended), out_w)
    out_total = sum_blocks(out_term)

    g_all = after(g_all, out_term)
    down_g = weight_grad(turns, g_all, hidden)
    down_got = scatter_row(down_g, plan)
    own_grad = own(after(g_all, down_g[0]))
    out_g = out_grad(turns, places, attended, own_grad)
    out_got = [out_g[0]] + [swap_group(out_g[j], plan, j) for j in range(1, plan.group)]
    pre_grad, up_sum = feed_slope(turns, after(g_all, out_g[0]), slope, down_pieces)
    up_g, up_parts = weight_grad(turns, normed2, pre_grad, up_sum, up_pieces)
    qkv_grad, qkv_sum = head_backward(
        turns, after(own_grad, up_g[0]), out_w, qkv, attended, lse, pairs, length
    )
    down_total = add_pieces(turns, [after(down_g[0], qkv_grad, *out_got)] + down_got)
    down_back = collect(down_total)
    up_near = scatter_row([after(v, down_total) for v in up_g], plan, False)
    norm_term = norm_back(
        turns,
        after(pre_grad, down_total),
        up_pieces,
        spread(qkv_grad),
        qkv_pieces,
        vectors,
    )
    up_got = up_near + scatter_row([after(v, norm_term, *up_near) for v in up_g], plan, True)
    norm_total = sum_blocks(after(norm_term, down_back, *up_near))
    qkv_g, qkv_parts = weight_grad(
        turns,
        after(own_normed1, down_back, out_total, *up_near),
        qkv_grad,
        qkv_sum,
        qkv_pieces,
    )

    up_total = add_pieces(turns, [after(up_g[0], qkv_g[0])] + up_got)
    up_back = collect(up_total)
    qkv_got = scatter_row([after(v, up_total) for v in qkv_g], plan)

    terms = [jnp.sum(v, -1) for v in (qkv_parts, up_parts)]
    terms += [g_sum, qkv_sum, up_sum]
    terms = [v.reshape(-1) for v in terms]
    used = sum(v.size for v in terms)
    terms.append(jnp.zeros((-used % (8 * LANES),), F32))
    sums = jnp.concatenate(terms)
    sums = sums + sum(swap(sums, "row", rows, k) for k in range(1, rows))
    sums = after(sums, up_total)
    sums = jnp.stack([sums, swap(sums, "blk", blks, 1)])

    holders = turns[:, None] * plan.share + jnp.arange(plan.share, dtype=jnp.int32)
    holders = after((me % plan.group ^ holders).reshape(-1), sums)
    out_send = pick(holders, out_got, rows)
    layer_out = finish(turns, after(x_own, sums), out_total, vectors, False)

    joined = (up_back, layer_out, sums, out_send[0])
    qkv_total = add_pieces(turns, [after(qkv_g[0], *joined)] + qkv_got)
    qkv_back = collect(qkv_total)
    out_back = out_send[0].astype(F32) + sum(
        swap(after(out_send[k], qkv_total), "row", rows, k).astype(F32) for k in range(1, rows)
    )
    sums = after(sums, qkv_total)
    sums = jnp.concatenate([sums] + [swap(sums, "blk", blks, k) for k in range(2, blks, 2)])
    sums = sums[me ^ jnp.arange(blks, dtype=jnp.int32)]
    gain1, bias1, gain2, bias2, g_total = jnp.split(
        jnp.sum(sums[:, : 5 * width], 0), 5
    )
    sums = sums[:, 5 * width : used]
    qkv_bias_grad = sums[:, : 3 * HD].reshape(plan.per_row, rows, plan.share, 3, HD)
    qkv_bias_grad = jnp.sum(qkv_bias_grad, 2).transpose(2, 1, 0, 3).reshape(-1)
    up_bias_grad = sums[:, 3 * HD :].reshape(-1)

    tokens_grad = finish(turns, x_own, norm_total, g_own, True)
    return (
        layer_out.reshape(tokens.shape),
        tokens_grad.reshape(tokens.shape),
        join_attn(turns, qkv_back, after(out_back, tokens_grad), plan),
        join_mlp(turns, up_back, down_back),
        (gain1 - ln1_bias * bias1) / ln1_gain,
        bias1,
        (gain2 - ln2_bias * bias2) / ln2_gain,
        bias2,
        qkv_bias_grad,
        g_total,
        up_bias_grad,
        g_total,
    )


def solution(mesh):
    rows, blks = mesh.shape["row"], mesh.shape["blk"]
    vector = P()
    tokens = P("row", "blk", None)
    attn = P(("row", "blk"), None)
    mlp = P(("row", "blk"), None, None)

    def run(*arrays):
        plan = Plan(rows, blks, arrays[0].shape[-1] // HD)
        return jax.shard_map(
            functools.partial(shards, plan),
            mesh=mesh,
            in_specs=(tokens, attn, mlp) + (vector,) * 8 + (P("row", None), tokens),
            out_specs=(tokens, tokens, attn, mlp) + (vector,) * 8,
            check_vma=False,
        )(*arrays)

    return run
```

```python
import functools
import math

import jax
import jax.numpy as jnp
import numpy as np
from jax import lax
from jax.experimental import pallas as pl
from jax.experimental.pallas import tpu as pltpu
from jax.sharding import PartitionSpec as P

HD = 256
ROT = 64
LANES = 128
BLOCK = 256
EPSILON = 1e-05
MASKED = -1e30
BF = jnp.bfloat16
F32 = jnp.float32
COST = 100
VMEM_LIMIT = 56 * 2**20
SMALL = 16 * 2**20


class Plan:
    def __init__(self, rows, blks, heads):
        self.rows = rows
        self.blks = blks
        self.share = blks // heads
        self.per_row = heads // rows
        self.group = blks // self.per_row
        self.groups = [
            list(range(i * self.group, (i + 1) * self.group)) for i in range(self.per_row)
        ]


def after(field, *others):
    return lax.optimization_barrier((field,) + others)[0] if others else field


def swap(field, axis, size, bit):
    return lax.ppermute(field, axis, [(i, i ^ bit) for i in range(size)])


def swap_group(field, plan, bits):
    return lax.ppermute(field, "blk", [(i, i ^ bits) for i in range(plan.blks)])


def gather_row(own, plan):
    return [own] + [swap(own, "row", plan.rows, k) for k in range(1, plan.rows)]


def bits_of(size):
    return [1 << i for i in range(size.bit_length() - 1)]


def near(k):
    return k & (k - 1) == 0


def orders(plan):
    bits = bits_of(plan.rows)
    return bits, bits[::-1]


def half_of(field, h):
    middle = field.shape[0] // 2
    return field[h * middle : (h + 1) * middle]


class Gather:
    def __init__(self, own, plan):
        self.plan = plan
        self.whole = {0: own}
        for bit in bits_of(plan.rows):
            self.whole[bit] = swap(own, "row", plan.rows, bit)

    def first(self):
        return [v for k, v in self.whole.items() if k]

    def finish(self, *others):
        plan = self.plan
        halves = []
        for h, order in enumerate(orders(plan)):
            got = {0: None}
            for bit in order:
                for k in list(got):
                    if k == 0:
                        got[bit] = half_of(after(self.whole[bit], *others), h)
                    else:
                        got[k ^ bit] = swap(got[k], "row", plan.rows, bit)
            halves.append(got)
        out = []
        for k in range(plan.rows):
            out += [self.whole[k]] if near(k) else [half[k] for half in halves]
        return out


class Scatter:
    def __init__(self, pieces, plan):
        self.plan = plan
        self.whole, far = {}, [{}, {}]
        for k, piece in enumerate(pieces):
            if near(k):
                self.whole[k] = piece
            else:
                far[0][k], far[1][k] = half_of(piece, 0), half_of(piece, 1)
        self.got = []
        for h, order in enumerate(orders(plan)):
            held = far[h]
            for bit in order:
                for k in [k for k in held if k & bit]:
                    term = swap(held.pop(k), "row", plan.rows, bit)
                    if near(k ^ bit):
                        self.got.append((k ^ bit, h, term))
                    else:
                        held[k ^ bit] = (held[k ^ bit].astype(F32) + term.astype(F32)).astype(BF)

    def first(self):
        return [term for _, _, term in self.got]

    def second(self, turns, *others):
        got = [(k, h, after(term, *others)) for k, h, term in self.got]
        while got:
            first = {}
            for item in got:
                first.setdefault(item[0], item)
            got = [item for item in got if all(item is not v for v in first.values())]
            sums = add_halves(turns, [(self.whole[k], h, term) for k, h, term in first.values()])
            self.whole.update(zip(first, sums))
        return [v for k, v in self.whole.items() if k]

    def finish(self):
        return [swap(self.whole[bit], "row", self.plan.rows, bit) for bit in bits_of(self.plan.rows)]


def scatter_row(pieces, plan):
    return [swap(pieces[k], "row", plan.rows, k) for k in range(1, plan.rows)]


def dot(left, right, left_dim, right_dim):
    return lax.dot_general(
        left, right, (((left_dim,), (right_dim,)), ((), ())), preferred_element_type=F32
    )


def whole(array):
    return pl.BlockSpec(array.shape, lambda *i: (0,) * len(array.shape))


def like(shape, kind=BF):
    return jax.ShapeDtypeStruct(shape, kind)


def call(body, turns, grid, in_specs, out_specs, out_shape, operands, flops=0, limit=None):
    moved = sum(v.size * v.dtype.itemsize for v in operands)
    moved += sum(math.prod(v.shape) * jnp.dtype(v.dtype).itemsize for v in out_shape)
    return pl.pallas_call(
        body,
        name=getattr(body, "func", body).__name__,
        grid_spec=pltpu.PrefetchScalarGridSpec(
            num_scalar_prefetch=1, grid=(grid,), in_specs=in_specs, out_specs=out_specs
        ),
        out_shape=out_shape,
        compiler_params=pltpu.CompilerParams(vmem_limit_bytes=limit or VMEM_LIMIT),
        cost_estimate=pl.CostEstimate(
            flops=flops // COST, bytes_accessed=moved // COST, transcendentals=0
        ),
    )(turns, *operands)


def rows_block(columns, block=BLOCK):
    return pl.BlockSpec((block, columns), lambda i, t: (i, 0))


def halves_kernel(count, t_ref, *refs):
    for i in range(count):
        into, term, out = refs[i], refs[count + i], refs[2 * count + i]
        out[...] = (into[...].astype(F32) + term[...].astype(F32)).astype(BF)


def add_halves(turns, items):
    count = len(items)
    depth, width = items[0][2].shape
    parts = 2
    into = [pl.BlockSpec((depth, width // parts), lambda i, t, h=h: (h, i)) for _, h, _ in items]
    term = pl.BlockSpec((depth, width // parts), lambda i, t: (0, i))
    return pl.pallas_call(
        functools.partial(halves_kernel, count),
        name="halves_kernel",
        grid_spec=pltpu.PrefetchScalarGridSpec(
            num_scalar_prefetch=1, grid=(parts,), in_specs=into + [term] * count, out_specs=into
        ),
        out_shape=[like(v.shape) for v, _, _ in items],
        input_output_aliases={1 + i: i for i in range(count)},
        compiler_params=pltpu.CompilerParams(vmem_limit_bytes=SMALL),
        cost_estimate=pl.CostEstimate(
            flops=0, bytes_accessed=6 * depth * width * count // COST, transcendentals=0
        ),
    )(turns, *[v for v, _, _ in items], *[v for _, _, v in items])


def add_kernel(t_ref, *refs):
    refs[-1][...] = sum(ref[...].astype(F32) for ref in refs[:-1]).astype(BF)


def add_pieces(turns, terms):
    depth, width = terms[0].shape
    block = rows_block(width, depth // 4)
    shape = like((depth, width))
    return call(
        add_kernel, turns, 4, [block] * len(terms), [block], [shape], terms, limit=SMALL
    )[0]


def turn_kernel(t_ref, x_ref, g_ref, v_ref, xo_ref, go_ref, vo_ref, s_ref):
    xo_ref[...] = x_ref[...]
    go_ref[...] = g_ref[...]
    vo_ref[...] = v_ref[...]
    s_ref[...] = jnp.sum(g_ref[...].astype(F32), 0, keepdims=True)


def turn_in(turns, x, g, vectors):
    rows = turns.shape[0]
    part = x.shape[1] // rows

    def specs(array, turned):
        index = (lambda k, t: (0, t[k])) if turned else (lambda k, t: (0, k))
        return pl.BlockSpec((array.shape[0], part), index)

    total_shape = like((1, x.shape[1]), F32)
    return call(
        turn_kernel,
        turns,
        rows,
        [specs(v, True) for v in (x, g, vectors)],
        [specs(v, False) for v in (x, g, vectors)] + [specs(total_shape, True)],
        [like(v.shape, v.dtype) for v in (x, g, vectors)] + [total_shape],
        [x, g, vectors],
    )


def split_kernel(t_ref, w_ref, u_ref, d_ref):
    u_ref[0] = w_ref[:, 0, :]
    d_ref[0] = w_ref[:, 1, :]


def split_mlp(turns, weights, blks):
    depth, _, hidden = weights.shape
    part = hidden // blks
    block = pl.BlockSpec((1, depth, part), lambda b, t: (b, 0, 0))
    return call(
        split_kernel,
        turns,
        blks,
        [pl.BlockSpec((depth, 2, part), lambda b, t: (0, 0, b))],
        [block] * 2,
        [like((blks, depth, part))] * 2,
        [weights],
    )


def join_kernel(t_ref, u_ref, d_ref, o_ref):
    o_ref[:, 0, :] = u_ref[0].astype(F32)
    o_ref[:, 1, :] = d_ref[0].astype(F32)


def join_mlp(turns, up, down):
    blks, depth, part = up.shape
    block = pl.BlockSpec((1, depth, part), lambda b, t: (b, 0, 0))
    return call(
        join_kernel,
        turns,
        blks,
        [block] * 2,
        [pl.BlockSpec((depth, 2, part), lambda b, t: (0, 0, b))],
        [like((depth, 2, blks * part), F32)],
        [up, down],
    )[0]


def split_attn_kernel(plan, width, t_ref, w_ref, qkv_ref, out_ref):
    b = pl.program_id(0)
    head = b % plan.group // plan.share * plan.per_row + b // plan.group
    for i in range(3):
        at = pl.multiple_of(i * width + head * HD, HD)
        qkv_ref[0, :, i * HD : (i + 1) * HD] = w_ref[:, pl.ds(at, HD)]

    @pl.when(b == 0)
    def _():
        out_ref[...] = w_ref[:, 3 * width :]


def split_attn(turns, weights, plan, width):
    depth = weights.shape[0]
    return call(
        functools.partial(split_attn_kernel, plan, width),
        turns,
        plan.blks,
        [whole(weights)],
        [
            pl.BlockSpec((1, depth, 3 * HD), lambda b, t: (b, 0, 0)),
            pl.BlockSpec((depth, width), lambda b, t: (0, 0)),
        ],
        [like((plan.blks, depth, 3 * HD)), like((depth, width))],
        [weights],
        limit=SMALL,
    )


def join_attn_kernel(plan, t_ref, qkv_ref, out_ref, o_ref):
    step = pl.program_id(0)
    heads = o_ref.shape[1] // HD

    @pl.when(step < 3)
    def _():
        at = pl.ds(pl.multiple_of(step * HD, HD), HD)
        for h in range(heads):
            first = h % plan.per_row * plan.group + h // plan.per_row * plan.share
            o_ref[:, h * HD : (h + 1) * HD] = sum(
                qkv_ref[first + i, :, at].astype(F32) for i in range(plan.share)
            )

    @pl.when(step == 3)
    def _():
        o_ref[...] = out_ref[...]


def join_attn(turns, qkv, out, plan):
    depth, width = out.shape
    return call(
        functools.partial(join_attn_kernel, plan),
        turns,
        4,
        [whole(qkv), whole(out)],
        [pl.BlockSpec((depth, width), lambda j, t: (0, j))],
        [like((depth, 4 * width), F32)],
        [qkv, out],
    )[0]


def pick_kernel(count, t_ref, *refs):
    pieces, outs = refs[:count], refs[count:]
    share = t_ref.shape[0] // len(outs)
    for n, out in enumerate(outs):
        for i in range(share):
            for k, piece in enumerate(pieces):

                @pl.when(t_ref[n * share + i] == k)
                def _(i=i, out=out, piece=piece):
                    out[...] = piece[...] if i == 0 else out[...] + piece[...]


def pick(table, pieces, count):
    return call(
        functools.partial(pick_kernel, len(pieces)),
        table,
        1,
        [whole(p) for p in pieces],
        [whole(pieces[0])] * count,
        [like(pieces[0].shape)] * count,
        pieces,
    )


def place_kernel(t_ref, *refs):
    *pieces, out_ref = refs
    for k, piece in enumerate(pieces):
        depth = piece.shape[0]
        out_ref[pl.ds(pl.multiple_of(t_ref[k] * depth, depth), depth)] = piece[...]


def place(table, pieces):
    depth, width = pieces[0].shape
    shape = like((len(pieces) * depth, width))
    return call(place_kernel, table, 1, [whole(p) for p in pieces], [whole(shape)], [shape], pieces)[0]


def norm_kernel(t_ref, x_ref, v_ref, a1_ref, a2_ref):
    field = x_ref[...].astype(F32)
    centred = field - jnp.mean(field, -1, keepdims=True)
    standard = centred * lax.rsqrt(jnp.mean(centred * centred, -1, keepdims=True) + EPSILON)
    a1_ref[...] = (standard * v_ref[0:1] + v_ref[1:2]).astype(BF)
    a2_ref[...] = (standard * v_ref[2:3] + v_ref[3:4]).astype(BF)


def norms(turns, x, vectors):
    count, width = x.shape
    return call(
        norm_kernel,
        turns,
        count // BLOCK,
        [rows_block(width), whole(vectors)],
        [rows_block(width)] * 2,
        [like(x.shape)] * 2,
        [x, vectors],
        20 * count * width,
    )


def times_pieces(left, pieces):
    out, start = None, 0
    for piece in pieces:
        depth = piece.shape[0]
        term = dot(left[:, start : start + depth], piece[...], 1, 0)
        out = term if out is None else out + term
        start += depth
    return out


def up_kernel(t_ref, a_ref, b_ref, *refs):
    pieces, (h_ref, s_ref) = refs[:-2], refs[-2:]
    pre = times_pieces(a_ref[...], pieces) + b_ref[...]
    cdf = 0.5 * (1.0 + lax.erf(pre * math.sqrt(0.5)))
    h_ref[...] = (pre * cdf).astype(BF)
    s_ref[...] = cdf + pre * (jnp.exp(-0.5 * pre * pre) * (1.0 / math.sqrt(2.0 * math.pi)))


def feed_up(turns, normed, bias, pieces):
    count, width = normed.shape
    hidden = bias.shape[0]
    return call(
        up_kernel,
        turns,
        count // BLOCK,
        [rows_block(width), pl.BlockSpec((1, hidden), lambda i, t: (0, 0))]
        + [whole(p) for p in pieces],
        [rows_block(hidden)] * 2,
        [like((count, hidden)), like((count, hidden), F32)],
        [normed, bias.reshape(1, hidden)] + pieces,
        2 * count * width * hidden,
    )


def slope_kernel(t_ref, g_ref, s_ref, *refs):
    pieces, (p_ref, sum_ref) = refs[:-2], refs[-2:]

    @pl.when(pl.program_id(0) == 0)
    def _():
        sum_ref[...] = jnp.zeros_like(sum_ref)

    grad = (times_pieces(g_ref[...], pieces) * s_ref[...]).astype(BF)
    p_ref[...] = grad
    sum_ref[...] += jnp.sum(grad.astype(F32), 0, keepdims=True)


def feed_slope(turns, grad, slope, pieces):
    count, width = grad.shape
    hidden = slope.shape[1]
    return call(
        slope_kernel,
        turns,
        count // BLOCK,
        [rows_block(width), rows_block(hidden)] + [whole(p) for p in pieces],
        [rows_block(hidden), pl.BlockSpec((1, hidden), lambda i, t: (0, 0))],
        [like((count, hidden)), like((1, hidden), F32)],
        [grad, slope] + pieces,
        2 * count * width * hidden,
    )


def lane_sum(field):
    return sum(field[:, i : i + LANES] for i in range(0, field.shape[1], LANES))


def weight_kernel(rows, with_sums, t_ref, l_ref, r_ref, *refs):
    step = pl.program_id(0)
    if with_sums:
        sum_ref, pieces, refs = refs[0], refs[1 : 1 + rows], refs[1 + rows :]
        parts_ref = refs[-1]
    grad = dot(l_ref[...], r_ref[...], 0, 0)
    for k in range(rows):

        @pl.when(step == k)
        def _(k=k):
            refs[k][...] = grad.astype(BF)
            if with_sums:
                piece = pieces[k][...].astype(F32)
                parts_ref[0] = lane_sum(piece * grad)
                parts_ref[1] = lane_sum(piece * sum_ref[...])


def weight_grad(turns, left, right, sums=None, pieces=()):
    rows = turns.shape[0]
    count, width = left.shape
    columns = right.shape[1]
    depth = width // rows
    out_shape = [like((depth, columns))] * rows
    out_specs = [whole(v) for v in out_shape]
    operands = [left, right]
    if pieces:
        operands += [sums] + pieces
        out_shape.append(like((2, width, LANES), F32))
        out_specs.append(pl.BlockSpec((2, depth, LANES), lambda k, t: (0, t[k], 0)))
    out = call(
        functools.partial(weight_kernel, rows, bool(pieces)),
        turns,
        rows,
        [pl.BlockSpec((count, depth), lambda k, t: (0, k))] + [whole(v) for v in operands[1:]],
        out_specs,
        out_shape,
        operands,
        2 * count * width * columns,
    )
    if pieces:
        return out[:-1], out[-1]
    return out


def out_kernel(rows, t_ref, o_ref, g_ref, *refs):
    *outs, grad_ref = refs
    depth = outs[0].shape[0]
    grad_ref[...] = dot(o_ref[...], g_ref[...], 0, 0)
    for j, out in enumerate(outs):
        at = pl.multiple_of(t_ref[rows + j] * depth, depth)
        out[...] = grad_ref[pl.ds(at, depth)].astype(BF)


def out_grad(turns, places, attended, grad):
    rows, group = turns.shape[0], places.shape[0]
    count, width = grad.shape
    part = width // rows
    depth = HD // group
    return pl.pallas_call(
        functools.partial(out_kernel, rows),
        name="out_kernel",
        grid_spec=pltpu.PrefetchScalarGridSpec(
            num_scalar_prefetch=1,
            grid=(rows,),
            in_specs=[whole(attended), pl.BlockSpec((count, part), lambda k, t: (0, k))],
            out_specs=[pl.BlockSpec((depth, part), lambda k, t: (0, t[k]))] * group,
            scratch_shapes=[pltpu.VMEM((HD, part), F32)],
        ),
        out_shape=[like((depth, width))] * group,
        compiler_params=pltpu.CompilerParams(vmem_limit_bytes=VMEM_LIMIT),
        cost_estimate=pl.CostEstimate(
            flops=2 * count * width * HD // COST,
            bytes_accessed=2 * (count * (width + HD) + width * HD) // COST,
            transcendentals=0,
        ),
    )(jnp.concatenate([turns, places]), attended, grad)


def turned_columns(t_ref, w_ref, start, size, depth):
    at = t_ref[start // depth] * depth + start % depth
    return w_ref[:, pl.ds(pl.multiple_of(at, LANES), size)]


def sum_kernel(depth, t_ref, h_ref, o_ref, w_ref, *refs):
    pieces, y_ref = refs[:-1], refs[-1]
    start = 0
    for piece in pieces:
        size = piece.shape[0]
        term = dot(h_ref[...], piece[...], 1, 1)
        term += dot(o_ref[...], turned_columns(t_ref, w_ref, start, size, depth), 1, 0)
        y_ref[:, start : start + size] = term.astype(BF)
        start += size


def out_sum(turns, hidden, pieces, attended, out_w):
    count = hidden.shape[0]
    width = out_w.shape[1]
    return call(
        functools.partial(sum_kernel, width // turns.shape[0]),
        turns,
        count // BLOCK,
        [rows_block(hidden.shape[1]), rows_block(HD), whole(out_w)] + [whole(p) for p in pieces],
        [rows_block(width)],
        [like((count, width))],
        [hidden, attended, out_w] + pieces,
        2 * count * width * (hidden.shape[1] + HD),
    )[0]


def back_kernel(t_ref, p_ref, q_ref, v_ref, *refs):
    pieces, c_ref = refs[:-1], refs[-1]
    count = len(pieces) // 2
    for k, (up, qkv) in enumerate(zip(pieces[:count], pieces[count:])):
        depth = up.shape[0]
        cols = slice(k * depth, (k + 1) * depth)
        term = dot(p_ref[...], up[...], 1, 1) * v_ref[2:3, cols]
        term += dot(q_ref[...], qkv[...], 1, 1) * v_ref[0:1, cols]
        c_ref[:, cols] = term.astype(BF)


def norm_back(turns, pre_grad, up_pieces, qkv_grad, qkv_pieces, vectors):
    count = pre_grad.shape[0]
    width = vectors.shape[1]
    columns = pre_grad.shape[1] + qkv_grad.shape[1]
    return call(
        back_kernel,
        turns,
        count // BLOCK,
        [rows_block(pre_grad.shape[1]), rows_block(qkv_grad.shape[1]), whole(vectors)]
        + [whole(p) for p in up_pieces + qkv_pieces],
        [rows_block(width)],
        [like((count, width))],
        [pre_grad, qkv_grad, vectors] + up_pieces + qkv_pieces,
        2 * count * width * columns,
    )[0]


def turned(field, cosine, minus, plus):
    head = field[:, :LANES]
    half = ROT // 2
    head = (
        head * cosine
        + pltpu.roll(head, LANES - half, 1) * minus
        + pltpu.roll(head, half, 1) * plus
    )
    return jnp.concatenate([head, field[:, LANES:]], 1)


def allowed_pairs(length, dq_ref, dk_ref):
    spot = lax.broadcasted_iota(jnp.int32, (length, length), 0)
    other = lax.broadcasted_iota(jnp.int32, (length, length), 1)
    return (dq_ref[0] == dk_ref[0]) & (other <= spot)


def forward_kernel(t_ref, a_ref, b_ref, c_ref, m_ref, p_ref, dq_ref, dk_ref, *refs):
    pieces, (qkv_ref, o_ref, lse_ref) = refs[:-3], refs[-3:]
    qkv = times_pieces(a_ref[...], pieces) + b_ref[...]
    tables = c_ref[0], m_ref[0], p_ref[0]
    queries = (turned(qkv[:, :HD], *tables) * HD ** (-0.5)).astype(BF)
    keys = turned(qkv[:, HD : 2 * HD], *tables).astype(BF)
    values = qkv[:, 2 * HD :].astype(BF)
    for i, field in enumerate((queries, keys, values)):
        qkv_ref[:, i * HD : (i + 1) * HD] = field
    allowed = allowed_pairs(a_ref.shape[0], dq_ref, dk_ref)
    scores = jnp.where(allowed, dot(queries, keys, 1, 1), MASKED)
    largest = jnp.max(scores, -1, keepdims=True)
    weights = jnp.where(allowed, jnp.exp(scores - largest), 0.0)
    mass = jnp.sum(weights, -1, keepdims=True)
    o_ref[...] = dot((weights / mass).astype(BF), values, 1, 0).astype(BF)
    lse_ref[...] = largest + jnp.log(mass)


def backward_kernel(
    parts, t_ref, g_ref, w_ref, qkv_ref, o_ref, lse_ref, c_ref, m_ref, p_ref, dq_ref, dk_ref,
    grad_ref, sum_ref,
):
    queries, keys, values = (qkv_ref[:, i * HD : (i + 1) * HD] for i in range(3))
    tables = c_ref[0], -m_ref[0], -p_ref[0]
    depth = w_ref.shape[1] // parts
    heads_grad = None
    for k in range(parts):
        cols = slice(k * depth, (k + 1) * depth)
        term = dot(g_ref[:, cols], turned_columns(t_ref, w_ref, k * depth, depth, depth), 1, 1)
        heads_grad = term if heads_grad is None else heads_grad + term
    heads_grad = heads_grad.astype(BF)
    allowed = allowed_pairs(g_ref.shape[0], dq_ref, dk_ref)
    scores = jnp.where(allowed, dot(queries, keys, 1, 1), MASKED)
    weights = jnp.where(allowed, jnp.exp(scores - lse_ref[...]), 0.0)
    deltas = jnp.sum(heads_grad.astype(F32) * o_ref[...].astype(F32), -1, keepdims=True)
    score_grad = (weights * (dot(heads_grad, values, 1, 1) - deltas)).astype(BF)
    query_grad = dot(score_grad, keys, 1, 0) * HD ** (-0.5)
    key_grad = dot(score_grad, queries, 0, 0)
    value_grad = dot(weights.astype(BF), heads_grad, 0, 0)
    fields = turned(query_grad, *tables), turned(key_grad, *tables), value_grad

    @pl.when(pl.program_id(0) == 0)
    def _():
        sum_ref[...] = jnp.zeros_like(sum_ref)

    for i, field in enumerate(fields):
        field = field.astype(BF)
        cols = slice(i * HD, (i + 1) * HD)
        grad_ref[:, cols] = field
        sum_ref[:, cols] += jnp.sum(field.astype(F32), 0, keepdims=True)


def pair_specs(length):
    table = pl.BlockSpec((1, length, LANES), lambda r, t: (r, 0, 0))
    return [table] * 3 + [
        pl.BlockSpec((1, length, 1), lambda r, t: (r, 0, 0)),
        pl.BlockSpec((1, 1, length), lambda r, t: (r, 0, 0)),
    ]


def head_forward(turns, normed, bias, pairs, pieces, length):
    count, width = normed.shape
    columns = 3 * HD
    return call(
        forward_kernel,
        turns,
        count // length,
        [rows_block(width, length), pl.BlockSpec((1, columns), lambda r, t: (0, 0))]
        + pair_specs(length)
        + [whole(p) for p in pieces],
        [rows_block(columns, length), rows_block(HD, length), rows_block(1, length)],
        [like((count, columns)), like((count, HD)), like((count, 1), F32)],
        [normed, bias.reshape(1, columns)] + pairs + pieces,
        2 * count * (width * columns + 2 * length * HD),
    )


def head_backward(turns, grad, out_w, qkv, attended, lse, pairs, length):
    count, width = grad.shape
    columns = 3 * HD
    return call(
        functools.partial(backward_kernel, turns.shape[0]),
        turns,
        count // length,
        [
            rows_block(width, length),
            whole(out_w),
            rows_block(columns, length),
            rows_block(HD, length),
            rows_block(1, length),
        ]
        + pair_specs(length),
        [rows_block(columns, length), pl.BlockSpec((1, columns), lambda r, t: (0, 0))],
        [like((count, columns)), like((1, columns), F32)],
        [grad, out_w, qkv, attended, lse] + pairs,
        2 * count * (width * HD + 5 * length * HD),
    )


def finish_kernel(rows, with_norm, t_ref, x_ref, s_ref, o_ref, out_ref):
    depth = x_ref.shape[1] // rows
    term = s_ref[...].astype(F32)
    if with_norm:
        centred = x_ref[...].astype(F32)
        centred = centred - jnp.mean(centred, -1, keepdims=True)
        rstd = lax.rsqrt(jnp.mean(centred * centred, -1, keepdims=True) + EPSILON)
        centred = centred * rstd
        term = term - jnp.mean(term, -1, keepdims=True) - centred * jnp.mean(
            term * centred, -1, keepdims=True
        )
        field = o_ref[...].astype(F32) + rstd * term
    else:
        field = x_ref[...].astype(F32) + term + o_ref[4:5]
    for k in range(rows):
        at = pl.multiple_of(t_ref[k] * depth, LANES)
        out_ref[:, pl.ds(at, depth)] = field[:, k * depth : (k + 1) * depth].astype(BF)


def finish(turns, x, term, other, with_norm):
    return call(
        functools.partial(finish_kernel, turns.shape[0], with_norm),
        turns,
        1,
        [whole(v) for v in (x, term, other)],
        [whole(x)],
        [like(x.shape)],
        [x, term, other],
    )[0]


def shards(
    plan,
    tokens,
    attn_weights,
    mlp_weights,
    ln1_gain,
    ln1_bias,
    ln2_gain,
    ln2_bias,
    qkv_bias,
    dense_bias,
    up_bias,
    down_bias,
    doc_lengths,
    cotangent,
):
    row_count, shard_len, width = tokens.shape
    depth = attn_weights.shape[0]
    heads = width // HD
    rows, blks = plan.rows, plan.blks
    own_hidden = mlp_weights.shape[-1] // blks
    me = lax.axis_index("blk")
    length = shard_len * blks
    count = row_count * length
    head_of = me % plan.group // plan.share * plan.per_row + me // plan.group
    part = me % plan.share
    own_rows = row_count // plan.share
    row = lax.axis_index("row")
    turns = row ^ jnp.arange(rows, dtype=jnp.int32)
    places = me % plan.group ^ jnp.arange(plan.group, dtype=jnp.int32)

    def exchange(field):
        return lax.all_to_all(field, "blk", 0, 0)

    def collect(field):
        return exchange(field.reshape(blks, -1, field.shape[-1]))

    def gather_blocks(field):
        field = field.reshape(row_count, shard_len, width)
        return lax.all_gather(field, "blk", axis=1, tiled=True).reshape(count, width)

    def sum_blocks(field):
        field = field.reshape(row_count, length, width)
        field = lax.psum_scatter(field, "blk", scatter_dimension=1, tiled=True)
        return field.reshape(row_count * shard_len, width)

    lengths = lax.dynamic_slice_in_dim(doc_lengths, part * own_rows, own_rows, 0)
    doc_ends = jnp.cumsum(lengths, axis=-1)
    starts = doc_ends - lengths
    spots = jnp.arange(length, dtype=jnp.int32)
    doc_ids = jnp.sum((spots[None, :, None] >= doc_ends[:, None, :]).astype(jnp.int32), -1)
    picked = doc_ids[:, :, None] == jnp.arange(lengths.shape[-1], dtype=jnp.int32)
    positions = spots - jnp.sum(jnp.where(picked, starts[:, None, :], 0), -1)
    lane = jnp.arange(LANES)
    inverse = 10000.0 ** (-2.0 * (lane % (ROT // 2)).astype(F32) / ROT)
    angles = positions.astype(F32)[..., None] * inverse
    sine = jnp.sin(angles)
    pairs = [
        jnp.where(lane < ROT, jnp.cos(angles), 1.0),
        jnp.where(lane < ROT // 2, -sine, 0.0),
        jnp.where((lane >= ROT // 2) & (lane < ROT), sine, 0.0),
        doc_ids[:, :, None],
        doc_ids[:, None, :],
    ]

    up_b = lax.dynamic_slice_in_dim(up_bias, me * own_hidden, own_hidden)
    qkv_b = lax.dynamic_index_in_dim(qkv_bias.reshape(3, heads, HD), head_of, 1, keepdims=False)
    qkv_b = qkv_b.reshape(-1)

    zeros = jnp.zeros((3, width), F32)
    vectors = jnp.stack([ln1_gain, ln1_bias, ln2_gain, ln2_bias, dense_bias + down_bias])
    x_own, g_own, vectors, g_sum = turn_in(
        turns,
        tokens.reshape(row_count * shard_len, width),
        cotangent.reshape(row_count * shard_len, width),
        jnp.concatenate([vectors, zeros]),
    )
    qkv_send, out_own = split_attn(turns, attn_weights, plan, width)
    qkv_mine = exchange(qkv_send)
    out_send = pick(
        row ^ places // plan.share,
        [out_own] + [swap(out_own, "row", rows, k) for k in range(1, rows)],
        plan.group,
    )
    up_send, down_send = split_mlp(turns, after(mlp_weights, qkv_send), blks)
    qkv_mine, up_send, *out_send = lax.optimization_barrier((qkv_mine, up_send, *out_send))
    up_mine = exchange(up_send)
    qkv_pieces = gather_row(qkv_mine.reshape(-1, 3 * HD), plan)
    out_got = [out_send[0]] + [swap_group(out_send[j], plan, j) for j in range(1, plan.group)]
    up_mine, x_own, down_send, *qkv_pieces = lax.optimization_barrier(
        (up_mine, x_own, down_send, *qkv_pieces, *out_got)
    )[: 3 + rows]
    x_all = gather_blocks(x_own)
    down_mine = exchange(down_send)
    up_pieces = gather_row(up_mine.reshape(-1, own_hidden), plan)
    out_w = place(places, out_got)
    down_mine, g_own, out_w, up_b, qkv_b, *pairs = lax.optimization_barrier(
        (down_mine, g_own, out_w, up_b, qkv_b, *pairs, *up_pieces)
    )
    pairs, up_pieces = pairs[: -len(up_pieces)], pairs[-len(up_pieces) :]
    g_all = gather_blocks(g_own)
    down_gather = Gather(down_mine.reshape(-1, own_hidden), plan)
    normed1, normed2 = norms(turns, x_all, vectors)

    def own(field):
        if plan.share == 1:
            return field
        return lax.dynamic_slice_in_dim(field, part * own_rows * length, own_rows * length, 0)

    def spread(field):
        if plan.share == 1:
            return field
        blank = jnp.zeros((count, field.shape[1]), field.dtype)
        return lax.dynamic_update_slice_in_dim(blank, field, part * own_rows * length, 0)

    own_normed1 = own(normed1)
    qkv, attended, lse = head_forward(
        turns, own_normed1, qkv_b, pairs, qkv_pieces, length
    )
    down_first = down_gather.first()
    hidden, slope = feed_up(turns, after(normed2, attended, *down_first), up_b, up_pieces)
    down_pieces = down_gather.finish(attended, *down_first)
    out_term = out_sum(turns, hidden, down_pieces, spread(attended), out_w)
    out_total = sum_blocks(out_term)

    g_all = after(g_all, out_term)
    down_g = weight_grad(turns, g_all, hidden)
    down_got = scatter_row(down_g, plan)
    own_grad = own(after(g_all, down_g[0]))
    out_g = out_grad(turns, places, attended, own_grad)
    out_got = [out_g[0]] + [swap_group(out_g[j], plan, j) for j in range(1, plan.group)]
    pre_grad, up_sum = feed_slope(turns, after(g_all, out_g[0]), slope, down_pieces)
    up_g, up_parts = weight_grad(turns, normed2, pre_grad, up_sum, up_pieces)
    qkv_grad, qkv_sum = head_backward(
        turns, after(own_grad, up_g[0]), out_w, qkv, attended, lse, pairs, length
    )
    down_total = add_pieces(turns, [after(down_g[0], qkv_grad, *out_got)] + down_got)
    down_back = collect(down_total)
    up_scatter = Scatter([after(v, down_total) for v in up_g], plan)
    norm_term = norm_back(
        turns,
        after(pre_grad, down_total),
        up_pieces,
        spread(qkv_grad),
        qkv_pieces,
        vectors,
    )
    up_near = up_scatter.second(turns, norm_term)
    up_got = up_scatter.finish()
    norm_total = sum_blocks(after(norm_term, down_back, *up_near))
    qkv_g, qkv_parts = weight_grad(
        turns,
        after(own_normed1, down_back, out_total, *up_near),
        qkv_grad,
        qkv_sum,
        qkv_pieces,
    )

    up_total = add_pieces(turns, [after(up_g[0], qkv_g[0])] + up_got)
    up_back = collect(up_total)
    qkv_got = scatter_row([after(v, up_total) for v in qkv_g], plan)

    terms = [jnp.sum(v, -1) for v in (qkv_parts, up_parts)]
    terms += [g_sum, qkv_sum, up_sum]
    terms = [v.reshape(-1) for v in terms]
    used = sum(v.size for v in terms)
    terms.append(jnp.zeros((-used % (8 * LANES),), F32))
    sums = jnp.concatenate(terms)
    sums = sums + sum(swap(sums, "row", rows, k) for k in range(1, rows))
    sums = after(sums, up_total)
    sums = jnp.stack([sums, swap(sums, "blk", blks, 1)])

    holders = turns[:, None] * plan.share + jnp.arange(plan.share, dtype=jnp.int32)
    holders = after((me % plan.group ^ holders).reshape(-1), sums)
    out_send = pick(holders, out_got, rows)
    layer_out = finish(turns, after(x_own, sums), out_total, vectors, False)

    joined = (up_back, layer_out, sums, out_send[0])
    qkv_total = add_pieces(turns, [after(qkv_g[0], *joined)] + qkv_got)
    qkv_back = collect(qkv_total)
    out_back = out_send[0].astype(F32) + sum(
        swap(after(out_send[k], qkv_total), "row", rows, k).astype(F32) for k in range(1, rows)
    )
    sums = after(sums, qkv_total)
    sums = jnp.concatenate([sums] + [swap(sums, "blk", blks, k) for k in range(2, blks, 2)])
    sums = sums[me ^ jnp.arange(blks, dtype=jnp.int32)]
    gain1, bias1, gain2, bias2, g_total = jnp.split(
        jnp.sum(sums[:, : 5 * width], 0), 5
    )
    sums = sums[:, 5 * width : used]
    qkv_bias_grad = sums[:, : 3 * HD].reshape(plan.per_row, rows, plan.share, 3, HD)
    qkv_bias_grad = jnp.sum(qkv_bias_grad, 2).transpose(2, 1, 0, 3).reshape(-1)
    up_bias_grad = sums[:, 3 * HD :].reshape(-1)

    tokens_grad = finish(turns, x_own, norm_total, g_own, True)
    return (
        layer_out.reshape(tokens.shape),
        tokens_grad.reshape(tokens.shape),
        join_attn(turns, qkv_back, after(out_back, tokens_grad), plan),
        join_mlp(turns, up_back, down_back),
        (gain1 - ln1_bias * bias1) / ln1_gain,
        bias1,
        (gain2 - ln2_bias * bias2) / ln2_gain,
        bias2,
        qkv_bias_grad,
        g_total,
        up_bias_grad,
        g_total,
    )


def solution(mesh):
    rows, blks = mesh.shape["row"], mesh.shape["blk"]
    vector = P()
    tokens = P("row", "blk", None)
    attn = P(("row", "blk"), None)
    mlp = P(("row", "blk"), None, None)

    def run(*arrays):
        plan = Plan(rows, blks, arrays[0].shape[-1] // HD)
        return jax.shard_map(
            functools.partial(shards, plan),
            mesh=mesh,
            in_specs=(tokens, attn, mlp) + (vector,) * 8 + (P("row", None), tokens),
            out_specs=(tokens, tokens, attn, mlp) + (vector,) * 8,
            check_vma=False,
        )(*arrays)

    return run
```

```python
import functools
import math

import jax
import jax.numpy as jnp
import numpy as np
from jax import lax
from jax.experimental import pallas as pl
from jax.experimental.pallas import tpu as pltpu
from jax.sharding import PartitionSpec as P

HD = 256
ROT = 64
LANES = 128
BLOCK = 256
EPSILON = 1e-05
MASKED = -1e30
BF = jnp.bfloat16
F32 = jnp.float32
COST = 100
VMEM_LIMIT = 56 * 2**20
SMALL = 16 * 2**20


class Plan:
    def __init__(self, rows, blks, heads):
        self.rows = rows
        self.blks = blks
        self.share = blks // heads
        self.per_row = heads // rows
        self.group = blks // self.per_row
        self.groups = [
            list(range(i * self.group, (i + 1) * self.group)) for i in range(self.per_row)
        ]


def after(field, *others):
    return lax.optimization_barrier((field,) + others)[0] if others else field


def swap(field, axis, size, bit):
    return lax.ppermute(field, axis, [(i, i ^ bit) for i in range(size)])


def swap_group(field, plan, bits):
    return lax.ppermute(field, "blk", [(i, i ^ bits) for i in range(plan.blks)])


def gather_row(own, plan):
    return [own] + [swap(own, "row", plan.rows, k) for k in range(1, plan.rows)]


def bits_of(size):
    return [1 << i for i in range(size.bit_length() - 1)]


def near(k):
    return k & (k - 1) == 0


def orders(plan):
    bits = bits_of(plan.rows)
    return bits, bits[::-1]


def half_of(field, h):
    middle = field.shape[0] // 2
    return field[h * middle : (h + 1) * middle]


class Gather:
    def __init__(self, own, plan):
        self.plan = plan
        self.whole = {0: own}
        for bit in bits_of(plan.rows):
            self.whole[bit] = swap(own, "row", plan.rows, bit)

    def first(self):
        return [v for k, v in self.whole.items() if k]

    def finish(self, *others):
        plan = self.plan
        halves = []
        for h, order in enumerate(orders(plan)):
            got = {0: None}
            for bit in order:
                for k in list(got):
                    if k == 0:
                        got[bit] = half_of(after(self.whole[bit], *others), h)
                    else:
                        got[k ^ bit] = swap(got[k], "row", plan.rows, bit)
            halves.append(got)
        out = []
        for k in range(plan.rows):
            out += [self.whole[k]] if near(k) else [half[k] for half in halves]
        return out


class Scatter:
    def __init__(self, pieces, plan):
        self.plan = plan
        self.whole, far = {}, [{}, {}]
        for k, piece in enumerate(pieces):
            if near(k):
                self.whole[k] = piece
            else:
                far[0][k], far[1][k] = half_of(piece, 0), half_of(piece, 1)
        self.got = []
        for h, order in enumerate(orders(plan)):
            held = far[h]
            for bit in order:
                for k in [k for k in held if k & bit]:
                    term = swap(held.pop(k), "row", plan.rows, bit)
                    if near(k ^ bit):
                        self.got.append((k ^ bit, h, term))
                    else:
                        held[k ^ bit] = (held[k ^ bit].astype(F32) + term.astype(F32)).astype(BF)

    def first(self):
        return [term for _, _, term in self.got]

    def second(self, turns, *others):
        got = [(k, h, after(term, *others)) for k, h, term in self.got]
        while got:
            first = {}
            for item in got:
                first.setdefault(item[0], item)
            got = [item for item in got if all(item is not v for v in first.values())]
            sums = add_halves(turns, [(self.whole[k], h, term) for k, h, term in first.values()])
            self.whole.update(zip(first, sums))
        return [v for k, v in self.whole.items() if k]

    def finish(self):
        return [swap(self.whole[bit], "row", self.plan.rows, bit) for bit in bits_of(self.plan.rows)]


def scatter_row(pieces, plan):
    return [swap(pieces[k], "row", plan.rows, k) for k in range(1, plan.rows)]


def dot(left, right, left_dim, right_dim):
    return lax.dot_general(
        left, right, (((left_dim,), (right_dim,)), ((), ())), preferred_element_type=F32
    )


def whole(array):
    return pl.BlockSpec(array.shape, lambda *i: (0,) * len(array.shape))


def like(shape, kind=BF):
    return jax.ShapeDtypeStruct(shape, kind)


def call(body, turns, grid, in_specs, out_specs, out_shape, operands, flops=0, limit=None):
    moved = sum(v.size * v.dtype.itemsize for v in operands)
    moved += sum(math.prod(v.shape) * jnp.dtype(v.dtype).itemsize for v in out_shape)
    return pl.pallas_call(
        body,
        name=getattr(body, "func", body).__name__,
        grid_spec=pltpu.PrefetchScalarGridSpec(
            num_scalar_prefetch=1, grid=(grid,), in_specs=in_specs, out_specs=out_specs
        ),
        out_shape=out_shape,
        compiler_params=pltpu.CompilerParams(vmem_limit_bytes=limit or VMEM_LIMIT),
        cost_estimate=pl.CostEstimate(
            flops=flops // COST, bytes_accessed=moved // COST, transcendentals=0
        ),
    )(turns, *operands)


def rows_block(columns, block=BLOCK):
    return pl.BlockSpec((block, columns), lambda i, t: (i, 0))


def halves_kernel(count, t_ref, *refs):
    for i in range(count):
        into, term, out = refs[i], refs[count + i], refs[2 * count + i]
        out[...] = (into[...].astype(F32) + term[...].astype(F32)).astype(BF)


def add_halves(turns, items):
    count = len(items)
    depth, width = items[0][2].shape
    parts = 2
    into = [pl.BlockSpec((depth, width // parts), lambda i, t, h=h: (h, i)) for _, h, _ in items]
    term = pl.BlockSpec((depth, width // parts), lambda i, t: (0, i))
    return pl.pallas_call(
        functools.partial(halves_kernel, count),
        name="halves_kernel",
        grid_spec=pltpu.PrefetchScalarGridSpec(
            num_scalar_prefetch=1, grid=(parts,), in_specs=into + [term] * count, out_specs=into
        ),
        out_shape=[like(v.shape) for v, _, _ in items],
        input_output_aliases={1 + i: i for i in range(count)},
        compiler_params=pltpu.CompilerParams(vmem_limit_bytes=SMALL),
        cost_estimate=pl.CostEstimate(
            flops=0, bytes_accessed=6 * depth * width * count // COST, transcendentals=0
        ),
    )(turns, *[v for v, _, _ in items], *[v for _, _, v in items])


def add_kernel(t_ref, *refs):
    refs[-1][...] = sum(ref[...].astype(F32) for ref in refs[:-1]).astype(BF)


def add_pieces(turns, terms):
    depth, width = terms[0].shape
    block = rows_block(width, depth // 4)
    shape = like((depth, width))
    return call(
        add_kernel, turns, 4, [block] * len(terms), [block], [shape], terms, limit=SMALL
    )[0]


def turn_kernel(t_ref, x_ref, g_ref, v_ref, xo_ref, go_ref, vo_ref, s_ref):
    xo_ref[...] = x_ref[...]
    go_ref[...] = g_ref[...]
    vo_ref[...] = v_ref[...]
    s_ref[...] = jnp.sum(g_ref[...].astype(F32), 0, keepdims=True)


def turn_in(turns, x, g, vectors):
    rows = turns.shape[0]
    part = x.shape[1] // rows

    def specs(array, turned):
        index = (lambda k, t: (0, t[k])) if turned else (lambda k, t: (0, k))
        return pl.BlockSpec((array.shape[0], part), index)

    total_shape = like((1, x.shape[1]), F32)
    return call(
        turn_kernel,
        turns,
        rows,
        [specs(v, True) for v in (x, g, vectors)],
        [specs(v, False) for v in (x, g, vectors)] + [specs(total_shape, True)],
        [like(v.shape, v.dtype) for v in (x, g, vectors)] + [total_shape],
        [x, g, vectors],
    )


def split_kernel(t_ref, w_ref, u_ref, d_ref):
    u_ref[0] = w_ref[:, 0, :]
    d_ref[0] = w_ref[:, 1, :]


def split_mlp(turns, weights, blks):
    depth, _, hidden = weights.shape
    part = hidden // blks
    block = pl.BlockSpec((1, depth, part), lambda b, t: (b, 0, 0))
    return call(
        split_kernel,
        turns,
        blks,
        [pl.BlockSpec((depth, 2, part), lambda b, t: (0, 0, b))],
        [block] * 2,
        [like((blks, depth, part))] * 2,
        [weights],
    )


def join_kernel(t_ref, u_ref, d_ref, o_ref):
    o_ref[:, 0, :] = u_ref[0].astype(F32)
    o_ref[:, 1, :] = d_ref[0].astype(F32)


def join_mlp(turns, up, down):
    blks, depth, part = up.shape
    block = pl.BlockSpec((1, depth, part), lambda b, t: (b, 0, 0))
    return call(
        join_kernel,
        turns,
        blks,
        [block] * 2,
        [pl.BlockSpec((depth, 2, part), lambda b, t: (0, 0, b))],
        [like((depth, 2, blks * part), F32)],
        [up, down],
    )[0]


def split_attn_kernel(plan, width, t_ref, w_ref, qkv_ref, out_ref):
    b = pl.program_id(0)
    head = b % plan.group // plan.share * plan.per_row + b // plan.group
    for i in range(3):
        at = pl.multiple_of(i * width + head * HD, HD)
        qkv_ref[0, :, i * HD : (i + 1) * HD] = w_ref[:, pl.ds(at, HD)]

    @pl.when(b == 0)
    def _():
        out_ref[...] = w_ref[:, 3 * width :]


def split_attn(turns, weights, plan, width):
    depth = weights.shape[0]
    return call(
        functools.partial(split_attn_kernel, plan, width),
        turns,
        plan.blks,
        [whole(weights)],
        [
            pl.BlockSpec((1, depth, 3 * HD), lambda b, t: (b, 0, 0)),
            pl.BlockSpec((depth, width), lambda b, t: (0, 0)),
        ],
        [like((plan.blks, depth, 3 * HD)), like((depth, width))],
        [weights],
        limit=SMALL,
    )


def join_attn_kernel(plan, t_ref, qkv_ref, out_ref, o_ref):
    step = pl.program_id(0)
    heads = o_ref.shape[1] // HD

    @pl.when(step < 3)
    def _():
        at = pl.ds(pl.multiple_of(step * HD, HD), HD)
        for h in range(heads):
            first = h % plan.per_row * plan.group + h // plan.per_row * plan.share
            o_ref[:, h * HD : (h + 1) * HD] = sum(
                qkv_ref[first + i, :, at].astype(F32) for i in range(plan.share)
            )

    @pl.when(step == 3)
    def _():
        o_ref[...] = out_ref[...]


def join_attn(turns, qkv, out, plan):
    depth, width = out.shape
    return call(
        functools.partial(join_attn_kernel, plan),
        turns,
        4,
        [whole(qkv), whole(out)],
        [pl.BlockSpec((depth, width), lambda j, t: (0, j))],
        [like((depth, 4 * width), F32)],
        [qkv, out],
    )[0]


def pick_kernel(count, t_ref, *refs):
    pieces, outs = refs[:count], refs[count:]
    share = t_ref.shape[0] // len(outs)
    for n, out in enumerate(outs):
        for i in range(share):
            for k, piece in enumerate(pieces):

                @pl.when(t_ref[n * share + i] == k)
                def _(i=i, out=out, piece=piece):
                    out[...] = piece[...] if i == 0 else out[...] + piece[...]


def pick(table, pieces, count):
    return call(
        functools.partial(pick_kernel, len(pieces)),
        table,
        1,
        [whole(p) for p in pieces],
        [whole(pieces[0])] * count,
        [like(pieces[0].shape)] * count,
        pieces,
    )


def place_kernel(t_ref, *refs):
    *pieces, out_ref = refs
    for k, piece in enumerate(pieces):
        depth = piece.shape[0]
        out_ref[pl.ds(pl.multiple_of(t_ref[k] * depth, depth), depth)] = piece[...]


def place(table, pieces):
    depth, width = pieces[0].shape
    shape = like((len(pieces) * depth, width))
    return call(place_kernel, table, 1, [whole(p) for p in pieces], [whole(shape)], [shape], pieces)[0]


def norm_kernel(t_ref, x_ref, v_ref, a1_ref, a2_ref):
    field = x_ref[...].astype(F32)
    centred = field - jnp.mean(field, -1, keepdims=True)
    standard = centred * lax.rsqrt(jnp.mean(centred * centred, -1, keepdims=True) + EPSILON)
    a1_ref[...] = (standard * v_ref[0:1] + v_ref[1:2]).astype(BF)
    a2_ref[...] = (standard * v_ref[2:3] + v_ref[3:4]).astype(BF)


def norms(turns, x, vectors):
    count, width = x.shape
    return call(
        norm_kernel,
        turns,
        count // BLOCK,
        [rows_block(width), whole(vectors)],
        [rows_block(width)] * 2,
        [like(x.shape)] * 2,
        [x, vectors],
        20 * count * width,
    )


def times_pieces(left, pieces):
    out, start = None, 0
    for piece in pieces:
        depth = piece.shape[0]
        term = dot(left[:, start : start + depth], piece[...], 1, 0)
        out = term if out is None else out + term
        start += depth
    return out


def up_kernel(t_ref, a_ref, b_ref, *refs):
    pieces, (h_ref, s_ref) = refs[:-2], refs[-2:]
    pre = times_pieces(a_ref[...], pieces) + b_ref[...]
    cdf = 0.5 * (1.0 + lax.erf(pre * math.sqrt(0.5)))
    h_ref[...] = (pre * cdf).astype(BF)
    s_ref[...] = cdf + pre * (jnp.exp(-0.5 * pre * pre) * (1.0 / math.sqrt(2.0 * math.pi)))


def feed_up(turns, normed, bias, pieces):
    count, width = normed.shape
    hidden = bias.shape[0]
    return call(
        up_kernel,
        turns,
        count // BLOCK,
        [rows_block(width), pl.BlockSpec((1, hidden), lambda i, t: (0, 0))]
        + [whole(p) for p in pieces],
        [rows_block(hidden)] * 2,
        [like((count, hidden)), like((count, hidden), F32)],
        [normed, bias.reshape(1, hidden)] + pieces,
        2 * count * width * hidden,
    )


def slope_kernel(t_ref, g_ref, s_ref, *refs):
    pieces, (p_ref, sum_ref) = refs[:-2], refs[-2:]

    @pl.when(pl.program_id(0) == 0)
    def _():
        sum_ref[...] = jnp.zeros_like(sum_ref)

    grad = (times_pieces(g_ref[...], pieces) * s_ref[...]).astype(BF)
    p_ref[...] = grad
    sum_ref[...] += jnp.sum(grad.astype(F32), 0, keepdims=True)


def feed_slope(turns, grad, slope, pieces):
    count, width = grad.shape
    hidden = slope.shape[1]
    return call(
        slope_kernel,
        turns,
        count // BLOCK,
        [rows_block(width), rows_block(hidden)] + [whole(p) for p in pieces],
        [rows_block(hidden), pl.BlockSpec((1, hidden), lambda i, t: (0, 0))],
        [like((count, hidden)), like((1, hidden), F32)],
        [grad, slope] + pieces,
        2 * count * width * hidden,
    )


def lane_sum(field):
    return sum(field[:, i : i + LANES] for i in range(0, field.shape[1], LANES))


def weight_kernel(rows, with_sums, t_ref, l_ref, r_ref, *refs):
    step = pl.program_id(0)
    if with_sums:
        sum_ref, pieces, refs = refs[0], refs[1 : 1 + rows], refs[1 + rows :]
        parts_ref = refs[-1]
    grad = dot(l_ref[...], r_ref[...], 0, 0)
    for k in range(rows):

        @pl.when(step == k)
        def _(k=k):
            refs[k][...] = grad.astype(BF)
            if with_sums:
                piece = pieces[k][...].astype(F32)
                parts_ref[0] = lane_sum(piece * grad)
                parts_ref[1] = lane_sum(piece * sum_ref[...])


def weight_grad(turns, left, right, sums=None, pieces=()):
    rows = turns.shape[0]
    count, width = left.shape
    columns = right.shape[1]
    depth = width // rows
    out_shape = [like((depth, columns))] * rows
    out_specs = [whole(v) for v in out_shape]
    operands = [left, right]
    if pieces:
        operands += [sums] + pieces
        out_shape.append(like((2, width, LANES), F32))
        out_specs.append(pl.BlockSpec((2, depth, LANES), lambda k, t: (0, t[k], 0)))
    out = call(
        functools.partial(weight_kernel, rows, bool(pieces)),
        turns,
        rows,
        [pl.BlockSpec((count, depth), lambda k, t: (0, k))] + [whole(v) for v in operands[1:]],
        out_specs,
        out_shape,
        operands,
        2 * count * width * columns,
    )
    if pieces:
        return out[:-1], out[-1]
    return out


def out_kernel(rows, t_ref, o_ref, g_ref, *refs):
    *outs, grad_ref = refs
    depth = outs[0].shape[0]
    grad_ref[...] = dot(o_ref[...], g_ref[...], 0, 0)
    for j, out in enumerate(outs):
        at = pl.multiple_of(t_ref[rows + j] * depth, depth)
        out[...] = grad_ref[pl.ds(at, depth)].astype(BF)


def out_grad(turns, places, attended, grad):
    rows, group = turns.shape[0], places.shape[0]
    count, width = grad.shape
    part = width // rows
    depth = HD // group
    return pl.pallas_call(
        functools.partial(out_kernel, rows),
        name="out_kernel",
        grid_spec=pltpu.PrefetchScalarGridSpec(
            num_scalar_prefetch=1,
            grid=(rows,),
            in_specs=[whole(attended), pl.BlockSpec((count, part), lambda k, t: (0, k))],
            out_specs=[pl.BlockSpec((depth, part), lambda k, t: (0, t[k]))] * group,
            scratch_shapes=[pltpu.VMEM((HD, part), F32)],
        ),
        out_shape=[like((depth, width))] * group,
        compiler_params=pltpu.CompilerParams(vmem_limit_bytes=VMEM_LIMIT),
        cost_estimate=pl.CostEstimate(
            flops=2 * count * width * HD // COST,
            bytes_accessed=2 * (count * (width + HD) + width * HD) // COST,
            transcendentals=0,
        ),
    )(jnp.concatenate([turns, places]), attended, grad)


def turned_columns(t_ref, w_ref, start, size, depth):
    at = t_ref[start // depth] * depth + start % depth
    return w_ref[:, pl.ds(pl.multiple_of(at, LANES), size)]


def sum_kernel(depth, t_ref, h_ref, o_ref, w_ref, *refs):
    pieces, y_ref = refs[:-1], refs[-1]
    start = 0
    for piece in pieces:
        size = piece.shape[0]
        term = dot(h_ref[...], piece[...], 1, 1)
        term += dot(o_ref[...], turned_columns(t_ref, w_ref, start, size, depth), 1, 0)
        y_ref[:, start : start + size] = term.astype(BF)
        start += size


def out_sum(turns, hidden, pieces, attended, out_w):
    count = hidden.shape[0]
    width = out_w.shape[1]
    return call(
        functools.partial(sum_kernel, width // turns.shape[0]),
        turns,
        count // BLOCK,
        [rows_block(hidden.shape[1]), rows_block(HD), whole(out_w)] + [whole(p) for p in pieces],
        [rows_block(width)],
        [like((count, width))],
        [hidden, attended, out_w] + pieces,
        2 * count * width * (hidden.shape[1] + HD),
    )[0]


def back_kernel(t_ref, p_ref, q_ref, v_ref, *refs):
    pieces, c_ref = refs[:-1], refs[-1]
    count = len(pieces) // 2
    for k, (up, qkv) in enumerate(zip(pieces[:count], pieces[count:])):
        depth = up.shape[0]
        cols = slice(k * depth, (k + 1) * depth)
        term = dot(p_ref[...], up[...], 1, 1) * v_ref[2:3, cols]
        term += dot(q_ref[...], qkv[...], 1, 1) * v_ref[0:1, cols]
        c_ref[:, cols] = term.astype(BF)


def norm_back(turns, pre_grad, up_pieces, qkv_grad, qkv_pieces, vectors):
    count = pre_grad.shape[0]
    width = vectors.shape[1]
    columns = pre_grad.shape[1] + qkv_grad.shape[1]
    return call(
        back_kernel,
        turns,
        count // BLOCK,
        [rows_block(pre_grad.shape[1]), rows_block(qkv_grad.shape[1]), whole(vectors)]
        + [whole(p) for p in up_pieces + qkv_pieces],
        [rows_block(width)],
        [like((count, width))],
        [pre_grad, qkv_grad, vectors] + up_pieces + qkv_pieces,
        2 * count * width * columns,
    )[0]


def turned(field, cosine, minus, plus):
    head = field[:, :LANES]
    half = ROT // 2
    head = (
        head * cosine
        + pltpu.roll(head, LANES - half, 1) * minus
        + pltpu.roll(head, half, 1) * plus
    )
    return jnp.concatenate([head, field[:, LANES:]], 1)


def allowed_pairs(length, dq_ref, dk_ref):
    spot = lax.broadcasted_iota(jnp.int32, (length, length), 0)
    other = lax.broadcasted_iota(jnp.int32, (length, length), 1)
    return (dq_ref[0] == dk_ref[0]) & (other <= spot)


def forward_kernel(t_ref, a_ref, b_ref, c_ref, m_ref, p_ref, dq_ref, dk_ref, *refs):
    pieces, (qkv_ref, o_ref, lse_ref) = refs[:-3], refs[-3:]
    qkv = times_pieces(a_ref[...], pieces) + b_ref[...]
    tables = c_ref[0], m_ref[0], p_ref[0]
    queries = (turned(qkv[:, :HD], *tables) * HD ** (-0.5)).astype(BF)
    keys = turned(qkv[:, HD : 2 * HD], *tables).astype(BF)
    values = qkv[:, 2 * HD :].astype(BF)
    for i, field in enumerate((queries, keys, values)):
        qkv_ref[:, i * HD : (i + 1) * HD] = field
    allowed = allowed_pairs(a_ref.shape[0], dq_ref, dk_ref)
    scores = jnp.where(allowed, dot(queries, keys, 1, 1), MASKED)
    largest = jnp.max(scores, -1, keepdims=True)
    weights = jnp.where(allowed, jnp.exp(scores - largest), 0.0)
    mass = jnp.sum(weights, -1, keepdims=True)
    o_ref[...] = dot((weights / mass).astype(BF), values, 1, 0).astype(BF)
    lse_ref[...] = largest + jnp.log(mass)


def backward_kernel(
    parts, t_ref, g_ref, w_ref, qkv_ref, o_ref, lse_ref, c_ref, m_ref, p_ref, dq_ref, dk_ref,
    grad_ref, sum_ref,
):
    queries, keys, values = (qkv_ref[:, i * HD : (i + 1) * HD] for i in range(3))
    tables = c_ref[0], -m_ref[0], -p_ref[0]
    depth = w_ref.shape[1] // parts
    heads_grad = None
    for k in range(parts):
        cols = slice(k * depth, (k + 1) * depth)
        term = dot(g_ref[:, cols], turned_columns(t_ref, w_ref, k * depth, depth, depth), 1, 1)
        heads_grad = term if heads_grad is None else heads_grad + term
    heads_grad = heads_grad.astype(BF)
    allowed = allowed_pairs(g_ref.shape[0], dq_ref, dk_ref)
    scores = jnp.where(allowed, dot(queries, keys, 1, 1), MASKED)
    weights = jnp.where(allowed, jnp.exp(scores - lse_ref[...]), 0.0)
    deltas = jnp.sum(heads_grad.astype(F32) * o_ref[...].astype(F32), -1, keepdims=True)
    score_grad = (weights * (dot(heads_grad, values, 1, 1) - deltas)).astype(BF)
    query_grad = dot(score_grad, keys, 1, 0) * HD ** (-0.5)
    key_grad = dot(score_grad, queries, 0, 0)
    value_grad = dot(weights.astype(BF), heads_grad, 0, 0)
    fields = turned(query_grad, *tables), turned(key_grad, *tables), value_grad

    @pl.when(pl.program_id(0) == 0)
    def _():
        sum_ref[...] = jnp.zeros_like(sum_ref)

    for i, field in enumerate(fields):
        field = field.astype(BF)
        cols = slice(i * HD, (i + 1) * HD)
        grad_ref[:, cols] = field
        sum_ref[:, cols] += jnp.sum(field.astype(F32), 0, keepdims=True)


def pair_specs(length):
    table = pl.BlockSpec((1, length, LANES), lambda r, t: (r, 0, 0))
    return [table] * 3 + [
        pl.BlockSpec((1, length, 1), lambda r, t: (r, 0, 0)),
        pl.BlockSpec((1, 1, length), lambda r, t: (r, 0, 0)),
    ]


def head_forward(turns, normed, bias, pairs, pieces, length):
    count, width = normed.shape
    columns = 3 * HD
    return call(
        forward_kernel,
        turns,
        count // length,
        [rows_block(width, length), pl.BlockSpec((1, columns), lambda r, t: (0, 0))]
        + pair_specs(length)
        + [whole(p) for p in pieces],
        [rows_block(columns, length), rows_block(HD, length), rows_block(1, length)],
        [like((count, columns)), like((count, HD)), like((count, 1), F32)],
        [normed, bias.reshape(1, columns)] + pairs + pieces,
        2 * count * (width * columns + 2 * length * HD),
    )


def head_backward(turns, grad, out_w, qkv, attended, lse, pairs, length):
    count, width = grad.shape
    columns = 3 * HD
    return call(
        functools.partial(backward_kernel, turns.shape[0]),
        turns,
        count // length,
        [
            rows_block(width, length),
            whole(out_w),
            rows_block(columns, length),
            rows_block(HD, length),
            rows_block(1, length),
        ]
        + pair_specs(length),
        [rows_block(columns, length), pl.BlockSpec((1, columns), lambda r, t: (0, 0))],
        [like((count, columns)), like((1, columns), F32)],
        [grad, out_w, qkv, attended, lse] + pairs,
        2 * count * (width * HD + 5 * length * HD),
    )


def finish_kernel(rows, with_norm, t_ref, x_ref, s_ref, o_ref, out_ref):
    depth = x_ref.shape[1] // rows
    term = s_ref[...].astype(F32)
    if with_norm:
        centred = x_ref[...].astype(F32)
        centred = centred - jnp.mean(centred, -1, keepdims=True)
        rstd = lax.rsqrt(jnp.mean(centred * centred, -1, keepdims=True) + EPSILON)
        centred = centred * rstd
        term = term - jnp.mean(term, -1, keepdims=True) - centred * jnp.mean(
            term * centred, -1, keepdims=True
        )
        field = o_ref[...].astype(F32) + rstd * term
    else:
        field = x_ref[...].astype(F32) + term + o_ref[4:5]
    for k in range(rows):
        at = pl.multiple_of(t_ref[k] * depth, LANES)
        out_ref[:, pl.ds(at, depth)] = field[:, k * depth : (k + 1) * depth].astype(BF)


def finish(turns, x, term, other, with_norm):
    return call(
        functools.partial(finish_kernel, turns.shape[0], with_norm),
        turns,
        1,
        [whole(v) for v in (x, term, other)],
        [whole(x)],
        [like(x.shape)],
        [x, term, other],
    )[0]


def shards(
    plan,
    tokens,
    attn_weights,
    mlp_weights,
    ln1_gain,
    ln1_bias,
    ln2_gain,
    ln2_bias,
    qkv_bias,
    dense_bias,
    up_bias,
    down_bias,
    doc_lengths,
    cotangent,
):
    row_count, shard_len, width = tokens.shape
    depth = attn_weights.shape[0]
    heads = width // HD
    rows, blks = plan.rows, plan.blks
    own_hidden = mlp_weights.shape[-1] // blks
    me = lax.axis_index("blk")
    length = shard_len * blks
    count = row_count * length
    head_of = me % plan.group // plan.share * plan.per_row + me // plan.group
    part = me % plan.share
    own_rows = row_count // plan.share
    row = lax.axis_index("row")
    turns = row ^ jnp.arange(rows, dtype=jnp.int32)
    places = me % plan.group ^ jnp.arange(plan.group, dtype=jnp.int32)

    def exchange(field):
        return lax.all_to_all(field, "blk", 0, 0)

    def collect(field):
        return exchange(field.reshape(blks, -1, field.shape[-1]))

    def gather_blocks(field):
        field = field.reshape(row_count, shard_len, width)
        return lax.all_gather(field, "blk", axis=1, tiled=True).reshape(count, width)

    def sum_blocks(field):
        field = field.reshape(row_count, length, width)
        field = lax.psum_scatter(field, "blk", scatter_dimension=1, tiled=True)
        return field.reshape(row_count * shard_len, width)

    lengths = lax.dynamic_slice_in_dim(doc_lengths, part * own_rows, own_rows, 0)
    doc_ends = jnp.cumsum(lengths, axis=-1)
    starts = doc_ends - lengths
    spots = jnp.arange(length, dtype=jnp.int32)
    doc_ids = jnp.sum((spots[None, :, None] >= doc_ends[:, None, :]).astype(jnp.int32), -1)
    picked = doc_ids[:, :, None] == jnp.arange(lengths.shape[-1], dtype=jnp.int32)
    positions = spots - jnp.sum(jnp.where(picked, starts[:, None, :], 0), -1)
    lane = jnp.arange(LANES)
    inverse = 10000.0 ** (-2.0 * (lane % (ROT // 2)).astype(F32) / ROT)
    angles = positions.astype(F32)[..., None] * inverse
    sine = jnp.sin(angles)
    pairs = [
        jnp.where(lane < ROT, jnp.cos(angles), 1.0),
        jnp.where(lane < ROT // 2, -sine, 0.0),
        jnp.where((lane >= ROT // 2) & (lane < ROT), sine, 0.0),
        doc_ids[:, :, None],
        doc_ids[:, None, :],
    ]

    up_b = lax.dynamic_slice_in_dim(up_bias, me * own_hidden, own_hidden)
    qkv_b = lax.dynamic_index_in_dim(qkv_bias.reshape(3, heads, HD), head_of, 1, keepdims=False)
    qkv_b = qkv_b.reshape(-1)

    zeros = jnp.zeros((3, width), F32)
    vectors = jnp.stack([ln1_gain, ln1_bias, ln2_gain, ln2_bias, dense_bias + down_bias])
    x_own, g_own, vectors, g_sum = turn_in(
        turns,
        tokens.reshape(row_count * shard_len, width),
        cotangent.reshape(row_count * shard_len, width),
        jnp.concatenate([vectors, zeros]),
    )
    qkv_send, out_own = split_attn(turns, attn_weights, plan, width)
    qkv_mine = exchange(qkv_send)
    out_send = pick(
        row ^ places // plan.share,
        [out_own] + [swap(out_own, "row", rows, k) for k in range(1, rows)],
        plan.group,
    )
    up_send, down_send = split_mlp(turns, after(mlp_weights, qkv_send), blks)
    qkv_mine, up_send, *out_send = lax.optimization_barrier((qkv_mine, up_send, *out_send))
    up_mine = exchange(up_send)
    qkv_pieces = gather_row(qkv_mine.reshape(-1, 3 * HD), plan)
    out_got = [out_send[0]] + [swap_group(out_send[j], plan, j) for j in range(1, plan.group)]
    up_mine, x_own, down_send, *qkv_pieces = lax.optimization_barrier(
        (up_mine, x_own, down_send, *qkv_pieces, *out_got)
    )[: 3 + rows]
    x_all = gather_blocks(x_own)
    down_mine = exchange(down_send)
    up_pieces = gather_row(up_mine.reshape(-1, own_hidden), plan)
    out_w = place(places, out_got)
    down_mine, g_own, out_w, up_b, qkv_b, *pairs = lax.optimization_barrier(
        (down_mine, g_own, out_w, up_b, qkv_b, *pairs, *up_pieces)
    )
    pairs, up_pieces = pairs[: -len(up_pieces)], pairs[-len(up_pieces) :]
    g_all = gather_blocks(g_own)
    down_gather = Gather(down_mine.reshape(-1, own_hidden), plan)
    normed1, normed2 = norms(turns, x_all, vectors)

    def own(field):
        if plan.share == 1:
            return field
        return lax.dynamic_slice_in_dim(field, part * own_rows * length, own_rows * length, 0)

    def spread(field):
        if plan.share == 1:
            return field
        blank = jnp.zeros((count, field.shape[1]), field.dtype)
        return lax.dynamic_update_slice_in_dim(blank, field, part * own_rows * length, 0)

    own_normed1 = own(normed1)
    qkv, attended, lse = head_forward(
        turns, own_normed1, qkv_b, pairs, qkv_pieces, length
    )
    down_first = down_gather.first()
    hidden, slope = feed_up(turns, after(normed2, attended, *down_first), up_b, up_pieces)
    down_pieces = down_gather.finish(attended, *down_first)
    out_term = out_sum(turns, hidden, down_pieces, spread(attended), out_w)
    out_total = sum_blocks(out_term)

    g_all = after(g_all, out_term)
    down_g = weight_grad(turns, g_all, hidden)
    down_got = scatter_row(down_g, plan)
    own_grad = own(after(g_all, down_g[0]))
    out_g = out_grad(turns, places, attended, own_grad)
    out_got = [out_g[0]] + [swap_group(out_g[j], plan, j) for j in range(1, plan.group)]
    pre_grad, up_sum = feed_slope(turns, after(g_all, out_g[0]), slope, down_pieces)
    up_g, up_parts = weight_grad(turns, normed2, pre_grad, up_sum, up_pieces)
    qkv_grad, qkv_sum = head_backward(
        turns, after(own_grad, up_g[0]), out_w, qkv, attended, lse, pairs, length
    )
    down_total = add_pieces(turns, [after(down_g[0], qkv_grad, *out_got)] + down_got)
    down_back = collect(down_total)
    up_scatter = Scatter([after(v, down_total) for v in up_g], plan)
    norm_term = norm_back(
        turns,
        after(pre_grad, down_total),
        up_pieces,
        spread(qkv_grad),
        qkv_pieces,
        vectors,
    )
    up_near = up_scatter.second(turns, norm_term)
    up_got = up_scatter.finish()
    norm_total = sum_blocks(after(norm_term, *up_near))
    qkv_g, qkv_parts = weight_grad(
        turns,
        after(own_normed1, down_back, out_total, *up_near),
        qkv_grad,
        qkv_sum,
        qkv_pieces,
    )

    up_total = add_pieces(turns, [after(up_g[0], qkv_g[0])] + up_got)
    up_back = collect(up_total)
    qkv_got = scatter_row([after(v, up_total) for v in qkv_g], plan)

    terms = [jnp.sum(v, -1) for v in (qkv_parts, up_parts)]
    terms += [g_sum, qkv_sum, up_sum]
    terms = [v.reshape(-1) for v in terms]
    used = sum(v.size for v in terms)
    terms.append(jnp.zeros((-used % (8 * LANES),), F32))
    sums = jnp.concatenate(terms)
    sums = sums + sum(swap(sums, "row", rows, k) for k in range(1, rows))
    sums = after(sums, up_total)
    sums = jnp.stack([sums, swap(sums, "blk", blks, 1)])

    holders = turns[:, None] * plan.share + jnp.arange(plan.share, dtype=jnp.int32)
    holders = after((me % plan.group ^ holders).reshape(-1), sums)
    out_send = pick(holders, out_got, rows)
    layer_out = finish(turns, after(x_own, sums), out_total, vectors, False)

    joined = (up_back, layer_out, sums, out_send[0])
    qkv_total = add_pieces(turns, [after(qkv_g[0], *joined)] + qkv_got)
    qkv_back = collect(qkv_total)
    out_back = out_send[0].astype(F32) + sum(
        swap(after(out_send[k], qkv_total), "row", rows, k).astype(F32) for k in range(1, rows)
    )
    sums = after(sums, qkv_total)
    sums = jnp.concatenate([sums] + [swap(sums, "blk", blks, k) for k in range(2, blks, 2)])
    sums = sums[me ^ jnp.arange(blks, dtype=jnp.int32)]
    gain1, bias1, gain2, bias2, g_total = jnp.split(
        jnp.sum(sums[:, : 5 * width], 0), 5
    )
    sums = sums[:, 5 * width : used]
    qkv_bias_grad = sums[:, : 3 * HD].reshape(plan.per_row, rows, plan.share, 3, HD)
    qkv_bias_grad = jnp.sum(qkv_bias_grad, 2).transpose(2, 1, 0, 3).reshape(-1)
    up_bias_grad = sums[:, 3 * HD :].reshape(-1)

    tokens_grad = finish(turns, x_own, norm_total, g_own, True)
    return (
        layer_out.reshape(tokens.shape),
        tokens_grad.reshape(tokens.shape),
        join_attn(turns, qkv_back, after(out_back, tokens_grad), plan),
        join_mlp(turns, up_back, down_back),
        (gain1 - ln1_bias * bias1) / ln1_gain,
        bias1,
        (gain2 - ln2_bias * bias2) / ln2_gain,
        bias2,
        qkv_bias_grad,
        g_total,
        up_bias_grad,
        g_total,
    )


def solution(mesh):
    rows, blks = mesh.shape["row"], mesh.shape["blk"]
    vector = P()
    tokens = P("row", "blk", None)
    attn = P(("row", "blk"), None)
    mlp = P(("row", "blk"), None, None)

    def run(*arrays):
        plan = Plan(rows, blks, arrays[0].shape[-1] // HD)
        return jax.shard_map(
            functools.partial(shards, plan),
            mesh=mesh,
            in_specs=(tokens, attn, mlp) + (vector,) * 8 + (P("row", None), tokens),
            out_specs=(tokens, tokens, attn, mlp) + (vector,) * 8,
            check_vma=False,
        )(*arrays)

    return run
```
